32 devices in a mesh: fsdp: 16 (over z, y, x), dp: 2 (over core).
Axes of the slice: x: 2, y: 2, z: 4, core: 2. Of those that a mesh axis runs over, the one named last changes fastest.
Arguments:
- kmer_identifiers: int32 [32, 512], P(('fsdp', 'dp')), may hold values from 0 to 4100
- slot_fragment_ids: int32 [32, 512], P(('fsdp', 'dp')), may hold values from 0 to 32, never falling along the last dimension, each value on 1 to 32 neighbouring positions
- mirror_fragment_index: int32 [1024], P(('fsdp', 'dp')), may hold values from 0 to 1023, as said below
- fragment_weight: float32 [1024], P(('fsdp', 'dp')), may hold values from 0.15 to 4.8, as said below
- affinity_heat: float32 [], replicated, may hold values from 0.05 to 0.1
- optimizer_iteration: int32 [], replicated, may hold values from 2 to 20
- lexicon_table: float32 [4101, 768], P(None, 'fsdp'), may hold values from -6 to 6
- lexicon_first_moment: float32 [4101, 768], P(None, 'fsdp'), may hold values from -2.2351742e-08 to 2.2351742e-08
- lexicon_raw_moment: float32 [4101, 768], P(None, 'fsdp'), may hold values from 9.784441e-19 to 3.9137765e-18
- query_key_value_maps: float32 [768, 2304], P('fsdp'), may hold values from -0.21875 to 0.21875
- qkv_first_moment: float32 [768, 2304], P('fsdp'), may hold values from -2.0861626e-07 to 2.0861626e-07
- qkv_raw_moment: float32 [768, 2304], P('fsdp'), may hold values from 9.7844415e-17 to 3.9137766e-16
- attention_exit_map: float32 [768, 768], P('fsdp'), may hold values from -0.625 to 0.625
- exit_first_moment: float32 [768, 768], P('fsdp'), may hold values from -2.0861626e-07 to 2.0861626e-07
- exit_raw_moment: float32 [768, 768], P('fsdp'), may hold values from 9.7844415e-17 to 3.9137766e-16
- widening_matrix_in: float32 [768, 3072], P('fsdp'), may hold values from -0.21875 to 0.21875
- widening_first_moment: float32 [768, 3072], P('fsdp'), may hold values from -2.0861626e-07 to 2.0861626e-07
- widening_raw_moment: float32 [768, 3072], P('fsdp'), may hold values from 9.7844415e-17 to 3.9137766e-16
- narrowing_matrix_out: float32 [3072, 768], P('fsdp'), may hold values from -0.109375 to 0.109375
- narrowing_first_moment: float32 [3072, 768], P('fsdp'), may hold values from -4.4703484e-08 to 4.4703484e-08
- narrowing_raw_moment: float32 [3072, 768], P('fsdp'), may hold values from 3.9137765e-18 to 1.5655106e-17
- layernorm_scale_bias: float32 [4, 768], P(None, 'fsdp'), may hold values from -1.2 to 1.4, as said below
- layernorm_first_moment: float32 [4, 768], P(None, 'fsdp'), may hold values from -1.1920929e-06 to 1.1920929e-06
- layernorm_raw_moment: float32 [4, 768], P(None, 'fsdp'), may hold values from 3.51888e-15 to 1.407552e-14
Outputs:
- contrast_objective: float32 [], replicated
- grad_norm: float32 [], replicated
- embedding_out: float32 [4101, 768], P(None, 'fsdp')
- embed_first_out: float32 [4101, 768], P(None, 'fsdp')
- embed_second_out: float32 [4101, 768], P(None, 'fsdp')
- project_in_out: float32 [768, 2304], P('fsdp')
- in_first_out: float32 [768, 2304], P('fsdp')
- in_second_out: float32 [768, 2304], P('fsdp')
- project_out_out: float32 [768, 768], P('fsdp')
- out_first_out: float32 [768, 768], P('fsdp')
- out_second_out: float32 [768, 768], P('fsdp')
- ffn_up_out: float32 [768, 3072], P('fsdp')
- up_first_out: float32 [768, 3072], P('fsdp')
- up_second_out: float32 [768, 3072], P('fsdp')
- ffn_down_out: float32 [3072, 768], P('fsdp')
- down_first_out: float32 [3072, 768], P('fsdp')
- down_second_out: float32 [3072, 768], P('fsdp')
- norm_params_out: float32 [4, 768], P(None, 'fsdp')
- norm_first_out: float32 [4, 768], P(None, 'fsdp')
- norm_second_out: float32 [4, 768], P(None, 'fsdp')
The draws below stay inside these ranges and needn't reach their ends.
Inputs may be any that keep to these rules, and one draw needn't show every extreme that they name: `slot_fragment_ids`: within a row the segment numbers never fall; numbers 0 to 31 are fragments, 32 is the row's padding tail; each has 1 to 32 slots, and some has exactly 32. Fragments are paired: mirror_fragment_index[mirror_fragment_index[i]] = i and mirror_fragment_index[i] != i. `fragment_weight`: positive weights. `layernorm_scale_bias`: rows 0 and 2 are the two norms' gains, rows 1 and 3 their shifts.
All inputs are finite; a program needn't handle non-finite values.
Results may differ from the reference program's by a relative error of at most 0.015.
Values may be sent and summed in bfloat16 or wider, within the bound.
No kernel may reach another device: no remote copies, remote signals or barrier semaphores. Data moves between devices by JAX's collectives and lax.ppermute only.
A program may use at most 256 MiB of HBM per device.

```python
import math
import jax
import jax.numpy as jnp
import numpy as np
from jax import lax

MODEL_WIDTH = 768
H = 12
HD = 64
FF = 3072
V = 4101
ROW_TOKENS = 512
SEG_ROW = 32
MOST = 32
ROWS = 32
NSEG = 1024
NPARAM = 10230528


def draw_mirror_fragment_index(key, part):
    shuffled = jax.random.permutation(key, NSEG).astype(jnp.int32)
    paired = shuffled.reshape(-1, 2)
    result = jnp.zeros((NSEG,), jnp.int32)
    result = result.at[paired[:, 0]].set(paired[:, 1])
    return result.at[paired[:, 1]].set(paired[:, 0])


def draw_fragment_weight(key, part):
    place = jnp.arange(NSEG, dtype=jnp.float32) / (NSEG - 1) - 0.5
    rise = jnp.exp(jnp.log(5.0) * place)
    jitter = jax.random.uniform(jax.random.fold_in(key, 21), (NSEG,), jnp.float32, 0.7, 1.3)
    return rise * jitter


def draw_layernorm_scale_bias(key, part):
    gain_rows = jax.random.uniform(jax.random.fold_in(key, 11), (2, MODEL_WIDTH), jnp.float32, 0.6, 1.4)
    shifts = jnp.clip(0.3 * jax.random.normal(jax.random.fold_in(key, 12), (2, MODEL_WIDTH), jnp.float32), -1.2, 1.2)
    return jnp.stack([gain_rows[0], shifts[0], gain_rows[1], shifts[1]])


def plant(entries, own_key, low, high):
    longest = entries.shape.index(max(entries.shape))
    spots = []
    for shift in (0, 1):
        where = [jax.random.randint(jax.random.fold_in(own_key, axis), (), 0, length) for axis, length in enumerate(entries.shape)]
        where[longest] = (where[longest] + shift) % entries.shape[longest]
        spots.append(tuple(where))
    return entries.at[spots[0]].set(low).at[spots[1]].set(high)


def block_levels(rng, extent, cuts, least, high):
    factor_of = 1.0
    for position, blocks in cuts:
        steps = jax.random.uniform(jax.random.fold_in(jax.random.fold_in(rng, 6), position), (blocks,), jnp.float32, least / len(cuts), high / len(cuts))
        factor_of = factor_of * jnp.repeat(jnp.exp(steps), extent[position] // blocks).reshape((-1,) + (1,) * (len(extent) - 1 - position))
    return factor_of


def rank_table(amount, lean):
    weights = [(1 << 20) // math.isqrt(standing ** lean) + 1 for standing in range(1, amount + 1)]
    scale = 1 + sum(weights) // (1 << 30)
    return np.cumsum(np.array([max(1, weight // scale) for weight in weights]))


def skewed_ids(own_key, shape, number_of, slope):
    table = rank_table(number_of, slope)
    ticket = jax.random.randint(jax.random.fold_in(own_key, 1), shape, 0, int(table[number_of - 1]))
    grade = jnp.searchsorted(jnp.asarray(table, jnp.int32), ticket, side="right")
    return jax.random.permutation(jax.random.fold_in(own_key, 2), number_of)[grade].astype(jnp.int32)


def split_up(amount, total, limit, slope):
    weights = [(1 << 20) // math.isqrt(standing ** slope) + 1 for standing in range(2, amount + 1)]
    rest, counts = total - limit - (amount - 1), [1] * (amount - 1)
    while rest > 0:
        candidates = [i for i in range(amount - 1) if counts[i] < limit]
        whole, remaining = sum([weights[i] for i in candidates]), rest
        for i in candidates:
            more = min(limit - counts[i], max(1, remaining * weights[i] // whole), rest)
            counts[i] = counts[i] + more
            rest = rest - more
    return np.array([limit] + counts)


def uneven_parts(rng, number_of, total, most, lean):
    if number_of == 2:
        one = jax.random.randint(rng, (), max(1, total - most), min(most, total - 1) + 1)
        return jnp.stack([one, total - one])
    lengths = jnp.asarray(split_up(number_of, total, most, lean), jnp.int32)
    twos = (number_of - 1) // 2
    source_of, sink = lengths[1:1 + 2 * twos:2], lengths[2:2 + 2 * twos:2]
    margin = jnp.minimum(source_of - 1, most - sink)
    passed = jax.random.randint(jax.random.fold_in(rng, 1), (twos,), 0, 1 << 20) % (margin + 1)
    lengths = lengths.at[1:1 + 2 * twos:2].set(source_of - passed).at[2:2 + 2 * twos:2].set(sink + passed)
    return lengths[jax.random.permutation(jax.random.fold_in(rng, 2), number_of)]


def noise(own_key, dims, deviation, bound, shards=(), kind=jnp.bfloat16):
    values = deviation * jax.random.normal(own_key, dims, jnp.float32)
    if shards:
        values = values * block_levels(own_key, dims, shards, -0.22, 0.18)
    return jnp.clip(values, -bound, bound).astype(kind)


def setup_inputs(seed: int = 0) -> dict:
    streams_of = jax.random.split(jax.random.key(seed), 25)
    return {
        "kmer_identifiers": plant(skewed_ids(streams_of[0], (ROWS, ROW_TOKENS), V, 2), jax.random.fold_in(streams_of[0], 3), 0, V - 1).astype(jnp.int32),
        "slot_fragment_ids": jax.vmap(lambda own: jnp.searchsorted(jnp.cumsum(uneven_parts(own, SEG_ROW + 1, ROW_TOKENS, MOST, 1)), jnp.arange(ROW_TOKENS), side="right"))(jax.random.split(streams_of[1], ROWS)).reshape((ROWS, ROW_TOKENS)).astype(jnp.int32),
        "mirror_fragment_index": draw_mirror_fragment_index(jax.random.fold_in(streams_of[24], 71), 0),
        "fragment_weight": draw_fragment_weight(jax.random.fold_in(streams_of[24], 71), 0),
        "affinity_heat": jnp.clip(jax.random.uniform(streams_of[4], (), jnp.float32, 0.05, 0.1), 0.05, 0.1),
        "optimizer_iteration": jax.random.randint(streams_of[5], (), 2, 21).astype(jnp.int32),
        "lexicon_table": noise(streams_of[6], (V, MODEL_WIDTH), 1.0, 6.0, ((1, 16),), jnp.float32),
        "lexicon_first_moment": noise(streams_of[7], (V, MODEL_WIDTH), (0.0000111 / NPARAM ** 0.5), 2.2351741790771484e-08, ((1, 16),), jnp.float32),
        "lexicon_raw_moment": jnp.clip(jnp.exp(math.log(3.913776530563517e-18) - 1.3862944 * jax.random.uniform(streams_of[8], (V, MODEL_WIDTH), jnp.float32) ** block_levels(streams_of[8], (V, MODEL_WIDTH), ((1, 16),), -0.2, 0.2)), 9.784441326408793e-19, 3.913776530563517e-18),
        "query_key_value_maps": noise(streams_of[9], (MODEL_WIDTH, 3 * MODEL_WIDTH), MODEL_WIDTH ** -0.5, 0.21875, ((0, 16),), jnp.float32),
        "qkv_first_moment": noise(streams_of[10], (MODEL_WIDTH, 3 * MODEL_WIDTH), (0.000111 / NPARAM ** 0.5), 2.086162567138672e-07, ((0, 16),), jnp.float32),
        "qkv_raw_moment": jnp.clip(jnp.exp(math.log(3.9137766132815786e-16) - 1.3862944 * jax.random.uniform(streams_of[11], (MODEL_WIDTH, 3 * MODEL_WIDTH), jnp.float32) ** block_levels(streams_of[11], (MODEL_WIDTH, 3 * MODEL_WIDTH), ((0, 16),), -0.2, 0.2)), 9.784441533203947e-17, 3.9137766132815786e-16),
        "attention_exit_map": noise(streams_of[12], (MODEL_WIDTH, MODEL_WIDTH), (MODEL_WIDTH // 8) ** -0.5, 0.625, ((0, 16),), jnp.float32),
        "exit_first_moment": noise(streams_of[13], (MODEL_WIDTH, MODEL_WIDTH), (0.000111 / NPARAM ** 0.5), 2.086162567138672e-07, ((0, 16),), jnp.float32),
        "exit_raw_moment": jnp.clip(jnp.exp(math.log(3.9137766132815786e-16) - 1.3862944 * jax.random.uniform(streams_of[14], (MODEL_WIDTH, MODEL_WIDTH), jnp.float32) ** block_levels(streams_of[14], (MODEL_WIDTH, MODEL_WIDTH), ((0, 16),), -0.2, 0.2)), 9.784441533203947e-17, 3.9137766132815786e-16),
        "widening_matrix_in": noise(streams_of[15], (MODEL_WIDTH, FF), MODEL_WIDTH ** -0.5, 0.21875, ((0, 16),), jnp.float32),
        "widening_first_moment": noise(streams_of[16], (MODEL_WIDTH, FF), (0.000111 / NPARAM ** 0.5), 2.086162567138672e-07, ((0, 16),), jnp.float32),
        "widening_raw_moment": jnp.clip(jnp.exp(math.log(3.9137766132815786e-16) - 1.3862944 * jax.random.uniform(streams_of[17], (MODEL_WIDTH, FF), jnp.float32) ** block_levels(streams_of[17], (MODEL_WIDTH, FF), ((0, 16),), -0.2, 0.2)), 9.784441533203947e-17, 3.9137766132815786e-16),
        "narrowing_matrix_out": noise(streams_of[18], (FF, MODEL_WIDTH), FF ** -0.5, 0.109375, ((0, 16),), jnp.float32),
        "narrowing_first_moment": noise(streams_of[19], (FF, MODEL_WIDTH), (0.0000222 / NPARAM ** 0.5), 4.470348358154297e-08, ((0, 16),), jnp.float32),
        "narrowing_raw_moment": jnp.clip(jnp.exp(math.log(1.565510612225407e-17) - 1.3862944 * jax.random.uniform(streams_of[20], (FF, MODEL_WIDTH), jnp.float32) ** block_levels(streams_of[20], (FF, MODEL_WIDTH), ((0, 16),), -0.2, 0.2)), 3.913776530563517e-18, 1.565510612225407e-17),
        "layernorm_scale_bias": draw_layernorm_scale_bias(jax.random.fold_in(streams_of[24], 71), 0),
        "layernorm_first_moment": noise(streams_of[22], (4, MODEL_WIDTH), (0.000666 / NPARAM ** 0.5), 1.1920928955078125e-06, ((1, 16),), jnp.float32),
        "layernorm_raw_moment": jnp.clip(jnp.exp(math.log(1.4075520026054448e-14) - 1.3862944 * jax.random.uniform(streams_of[23], (4, MODEL_WIDTH), jnp.float32) ** block_levels(streams_of[23], (4, MODEL_WIDTH), ((1, 16),), -0.2, 0.2)), 3.518880006513612e-15, 1.4075520026054448e-14),
    }


@jax.custom_vjp
def low(v):
    return lax.optimization_barrier(v.astype(jnp.bfloat16)).astype(jnp.float32)

@jax.custom_vjp
def low_back(v):
    return v

def low_keep(v):
    return (low(v), None)

def low_pass(kept, grad):
    return (grad,)

def back_keep(v):
    return (v, None)

def back_low(kept, grad):
    return (low(grad),)
low.defvjp(low_keep, low_pass)
low_back.defvjp(back_keep, back_low)
largest_value = lax.Precision.HIGHEST
beta_one = 0.9
beta_two = 0.999
adam_eps = 1e-12
decay_rate = 0.01
rate_matrix = 0.1
rate_embed = 1.0
rate_norm = 1.0
clip_norm = 0.001
norm_eps = 1e-05
unit_eps = 1e-06
row_span = 128

def layer_norm(inputs, gain_row, shifts):
    center = inputs - lax.optimization_barrier(jnp.mean(inputs, -1, keepdims=True))
    return center * lax.rsqrt(lax.optimization_barrier(jnp.mean(center * center, -1, keepdims=True)) + norm_eps) * gain_row + shifts

def encode_rows(parameter_bundle, token_rows, segment_rows):
    lexicon_table, query_key_value_maps, attention_exit_map, widening_matrix_in, narrowing_matrix_out, layernorm_scale_bias = parameter_bundle
    batch_row_list = token_rows.shape[0]
    embedded = jnp.take(lexicon_table, token_rows.reshape(-1), axis=0)
    qkv_all = low(low_back(jnp.dot(embedded, query_key_value_maps, precision=largest_value)))
    qkv_all = qkv_all.reshape(batch_row_list, ROW_TOKENS, 3, H, HD)
    query_rows, key_rows, value_rows = (qkv_all[:, :, 0], qkv_all[:, :, 1], qkv_all[:, :, 2])
    raw_scores = jnp.einsum('bqhd,bkhd->bhqk', query_rows, key_rows, precision=largest_value)
    scores = low_back(raw_scores * HD ** (-0.5))
    same_segment = segment_rows[:, None, :, None] == segment_rows[:, None, None, :]
    scores = jnp.where(same_segment, scores, -1e+30)
    row_max = lax.optimization_barrier(jnp.max(scores, -1, keepdims=True))
    log_total = row_max + jnp.log(lax.optimization_barrier(jnp.sum(jnp.exp(scores - row_max), -1, keepdims=True)))
    attn_probs = low(jnp.exp(scores - log_total))
    mixed_heads = jnp.einsum('bhqk,bkhd->bqhd', attn_probs, value_rows, precision=largest_value)
    mixed_heads = low(low_back(mixed_heads.reshape(batch_row_list * ROW_TOKENS, MODEL_WIDTH)))
    attended = low_back(jnp.dot(mixed_heads, attention_exit_map, precision=largest_value))
    normed_one = layer_norm(embedded + attended, layernorm_scale_bias[0], layernorm_scale_bias[1])
    up_proj = low_back(jnp.dot(low(normed_one), widening_matrix_in, precision=largest_value))
    activated = low(jax.nn.gelu(up_proj, approximate=False))
    ffn_result = low_back(jnp.dot(activated, narrowing_matrix_out, precision=largest_value))
    second_normalized = layer_norm(normed_one + ffn_result, layernorm_scale_bias[2], layernorm_scale_bias[3])
    group_member = (segment_rows[:, None, :] == jnp.arange(SEG_ROW, dtype=jnp.int32)[None, :, None]).astype(jnp.float32)
    pooled_state = jnp.einsum('nkz,nzh->nkh', group_member, second_normalized.reshape(batch_row_list, ROW_TOKENS, MODEL_WIDTH), precision=largest_value)
    return pooled_state.reshape(batch_row_list * SEG_ROW, MODEL_WIDTH)

def affinity_rows(unit_rows, row_block, affinity_heat):
    row_units, row_numbers, partner_rows, weight_rows = row_block
    cosine_affinity_grid = low_back(jnp.dot(row_units, unit_rows.T, precision=largest_value))
    raw_affinity_values = cosine_affinity_grid / affinity_heat
    positions = jnp.arange(NSEG, dtype=jnp.int32)
    raw_affinity_values = jnp.where(row_numbers[:, None] == positions[None, :], -1e+30, raw_affinity_values)
    row_max = lax.optimization_barrier(jnp.max(raw_affinity_values, -1, keepdims=True))
    log_total = row_max[:, 0] + jnp.log(lax.optimization_barrier(jnp.sum(jnp.exp(raw_affinity_values - row_max), -1)))
    target = jnp.take_along_axis(raw_affinity_values, partner_rows[:, None], axis=1)[:, 0]
    return jnp.sum(weight_rows * (log_total - target))

def couple_objective(parameter_bundle, kmer_identifiers, slot_fragment_ids, mirror_fragment_index, fragment_weight, affinity_heat):
    rounded = tuple((low(piece) for piece in parameter_bundle))
    encode = jax.checkpoint(lambda block_pair: encode_rows(rounded, block_pair[0], block_pair[1]))
    pooled_state = lax.map(encode, (kmer_identifiers.reshape(-1, 8, ROW_TOKENS), slot_fragment_ids.reshape(-1, 8, ROW_TOKENS)))
    pooled_state = pooled_state.reshape(NSEG, MODEL_WIDTH)
    unit_rows = low(pooled_state * lax.rsqrt(lax.optimization_barrier(jnp.sum(pooled_state * pooled_state, -1, keepdims=True)) + unit_eps))
    row_blocks = (unit_rows.reshape(-1, row_span, MODEL_WIDTH), jnp.arange(NSEG, dtype=jnp.int32).reshape(-1, row_span), mirror_fragment_index.reshape(-1, row_span), fragment_weight.reshape(-1, row_span))
    totals = lax.map(jax.checkpoint(lambda row_block: affinity_rows(unit_rows, row_block, affinity_heat)), row_blocks)
    return jnp.sum(totals) / NSEG

def adam_update(weight, first, second, grad, fix_first, fix_second, rate, decay):
    first_new = beta_one * first + (1.0 - beta_one) * grad
    second_new = beta_two * second + (1.0 - beta_two) * grad * grad
    step_size = first_new / fix_first / (jnp.sqrt(second_new / fix_second) + adam_eps)
    return (weight - rate * (step_size + decay * weight), first_new, second_new)

def reference(kmer_identifiers, slot_fragment_ids, mirror_fragment_index, fragment_weight, affinity_heat, optimizer_iteration, lexicon_table, lexicon_first_moment, lexicon_raw_moment, query_key_value_maps, qkv_first_moment, qkv_raw_moment, attention_exit_map, exit_first_moment, exit_raw_moment, widening_matrix_in, widening_first_moment, widening_raw_moment, narrowing_matrix_out, narrowing_first_moment, narrowing_raw_moment, layernorm_scale_bias, layernorm_first_moment, layernorm_raw_moment):
    parameter_bundle = (lexicon_table, query_key_value_maps, attention_exit_map, widening_matrix_in, narrowing_matrix_out, layernorm_scale_bias)
    firsts = (lexicon_first_moment, qkv_first_moment, exit_first_moment, widening_first_moment, narrowing_first_moment, layernorm_first_moment)
    seconds = (lexicon_raw_moment, qkv_raw_moment, exit_raw_moment, widening_raw_moment, narrowing_raw_moment, layernorm_raw_moment)
    rates = (rate_embed, rate_matrix, rate_matrix, rate_matrix, rate_matrix, rate_norm)
    decays = (decay_rate, decay_rate, decay_rate, decay_rate, decay_rate, 0.0)
    contrast_objective, attraction_coefficient = jax.vjp(lambda *fragment_parts: couple_objective(fragment_parts, kmer_identifiers, slot_fragment_ids, mirror_fragment_index, fragment_weight, affinity_heat), *parameter_bundle)
    grads = attraction_coefficient(jnp.ones_like(contrast_objective))
    grad_norm = jnp.sqrt(sum((jnp.sum(piece * piece) for piece in grads)))
    factor = clip_norm / jnp.maximum(grad_norm, clip_norm)
    count_now = optimizer_iteration.astype(jnp.float32)
    fix_first = 1.0 - jnp.power(beta_one, count_now)
    fix_second = 1.0 - jnp.power(beta_two, count_now)
    updated = [adam_update(parameter_bundle[number], firsts[number], seconds[number], grads[number] * factor, fix_first, fix_second, rates[number], decays[number]) for number in range(6)]
    return (contrast_objective, grad_norm, updated[0][0], updated[0][1], updated[0][2], updated[1][0], updated[1][1], updated[1][2], updated[2][0], updated[2][1], updated[2][2], updated[3][0], updated[3][1], updated[3][2], updated[4][0], updated[4][1], updated[4][2], updated[5][0], updated[5][1], updated[5][2])
```

```python
import jax
import jax.numpy as jnp
from jax import lax
from jax.experimental import pallas as pl
from jax.experimental.pallas import tpu as pltpu
from jax.sharding import PartitionSpec as P

MODEL_WIDTH = 768
H = 12
HD = 64
SEG_ROW = 32


largest_value = lax.Precision.HIGHEST
beta_one = 0.9
beta_two = 0.999
adam_eps = 1e-12
decay_rate = 0.01
rate_matrix = 0.1
rate_embed = 1.0
rate_norm = 1.0
clip_norm = 0.001
norm_eps = 1e-05
unit_eps = 1e-06


def layer_norm(inputs, gain_row, shifts):
    center = inputs - jnp.mean(inputs, -1, keepdims=True)
    inv_std = lax.rsqrt(jnp.mean(center * center, -1, keepdims=True) + norm_eps)
    normed = center * inv_std
    return (normed * gain_row + shifts, normed, inv_std)


def norm_back(upstream, normed, inv_std, gain_row):
    scaled = upstream * gain_row
    grad_in = inv_std * (
        scaled
        - jnp.mean(scaled, -1, keepdims=True)
        - normed * jnp.mean(scaled * normed, -1, keepdims=True)
    )
    return (grad_in, jnp.sum(upstream * normed, 0), jnp.sum(upstream, 0))


def masked_scores(query_rows, key_rows, segment_rows):
    raw_scores = jnp.einsum(
        "bqhd,bkhd->bhqk", query_rows, key_rows, preferred_element_type=jnp.float32
    )
    same_segment = segment_rows[:, None, :, None] == segment_rows[:, None, None, :]
    return jnp.where(same_segment, raw_scores * HD ** (-0.5), -1e30)


def layer_forward(gathered, token_rows, segment_rows):
    (
        lexicon_table,
        query_key_value_maps,
        attention_exit_map,
        widening_matrix_in,
        narrowing_matrix_out,
        layernorm_scale_bias,
    ) = gathered
    batch_row_list, sequence_length = token_rows.shape
    embedded = jnp.take(lexicon_table, token_rows.reshape(-1), axis=0)
    qkv_all = jnp.dot(embedded, query_key_value_maps, preferred_element_type=jnp.float32).astype(
        jnp.bfloat16
    )
    qkv_all = qkv_all.reshape(batch_row_list, sequence_length, 3, H, HD)
    query_rows, key_rows, value_rows = (qkv_all[:, :, 0], qkv_all[:, :, 1], qkv_all[:, :, 2])
    scores = masked_scores(query_rows, key_rows, segment_rows)
    row_max = jnp.max(scores, -1, keepdims=True)
    log_total = row_max + jnp.log(jnp.sum(jnp.exp(scores - row_max), -1, keepdims=True))
    attn_probs = jnp.exp(scores - log_total).astype(jnp.bfloat16)
    mixed_heads = jnp.einsum(
        "bhqk,bkhd->bqhd", attn_probs, value_rows, preferred_element_type=jnp.float32
    )
    mixed_heads = mixed_heads.reshape(batch_row_list * sequence_length, MODEL_WIDTH).astype(
        jnp.bfloat16
    )
    attended = jnp.dot(mixed_heads, attention_exit_map, preferred_element_type=jnp.float32)
    normed_one, unit_one, inv_one = layer_norm(
        embedded.astype(jnp.float32) + attended, layernorm_scale_bias[0], layernorm_scale_bias[1]
    )
    normed_low = normed_one.astype(jnp.bfloat16)
    up_proj = jnp.dot(normed_low, widening_matrix_in, preferred_element_type=jnp.float32)
    activated = jax.nn.gelu(up_proj, approximate=False).astype(jnp.bfloat16)
    ffn_result = jnp.dot(activated, narrowing_matrix_out, preferred_element_type=jnp.float32)
    second_normalized, unit_two, inv_two = layer_norm(
        normed_one + ffn_result, layernorm_scale_bias[2], layernorm_scale_bias[3]
    )
    group_member = (
        segment_rows[:, None, :] == jnp.arange(SEG_ROW, dtype=jnp.int32)[None, :, None]
    ).astype(jnp.float32)
    pooled_state = jnp.einsum(
        "nkz,nzh->nkh",
        group_member,
        second_normalized.reshape(batch_row_list, sequence_length, MODEL_WIDTH),
        precision=largest_value,
    )
    saved_state = (
        embedded,
        query_rows,
        key_rows,
        value_rows,
        log_total,
        mixed_heads,
        unit_one,
        inv_one,
        normed_low,
        up_proj,
        activated,
        unit_two,
        inv_two,
        group_member,
    )
    return (pooled_state.reshape(batch_row_list * SEG_ROW, MODEL_WIDTH), saved_state)


def layer_backward(gathered, saved_state, token_rows, segment_rows, pooled_gradient):
    (
        lexicon_table,
        query_key_value_maps,
        attention_exit_map,
        widening_matrix_in,
        narrowing_matrix_out,
        layernorm_scale_bias,
    ) = gathered
    (
        embedded,
        query_rows,
        key_rows,
        value_rows,
        log_total,
        mixed_heads,
        unit_one,
        inv_one,
        normed_low,
        up_proj,
        activated,
        unit_two,
        inv_two,
        group_member,
    ) = saved_state
    batch_row_list, sequence_length = token_rows.shape
    pooled_gradient = pooled_gradient.reshape(batch_row_list, SEG_ROW, MODEL_WIDTH)
    second_gradient = jnp.einsum(
        "got,goy->gty", group_member, pooled_gradient, precision=largest_value
    ).reshape(batch_row_list * sequence_length, MODEL_WIDTH)
    grad_resid_two, grad_gain_two, grad_shift_two = norm_back(
        second_gradient, unit_two, inv_two, layernorm_scale_bias[2]
    )
    grad_result = grad_resid_two.astype(jnp.bfloat16)
    grad_ffn_down = jnp.einsum(
        "nf,nd->fd", activated, grad_result, preferred_element_type=jnp.float32
    )
    grad_act = jnp.einsum(
        "nd,fd->nf", grad_result, narrowing_matrix_out, preferred_element_type=jnp.float32
    )
    gelu_value, gelu_pull = jax.vjp(
        lambda pre_act: jax.nn.gelu(pre_act, approximate=False), up_proj
    )
    grad_up = gelu_pull(grad_act)[0].astype(jnp.bfloat16)
    grad_ffn_up = jnp.einsum("nd,nf->df", normed_low, grad_up, preferred_element_type=jnp.float32)
    grad_one = grad_resid_two + jnp.einsum(
        "nf,df->nd", grad_up, widening_matrix_in, preferred_element_type=jnp.float32
    )
    grad_resid_one, grad_gain_one, grad_shift_one = norm_back(
        grad_one, unit_one, inv_one, layernorm_scale_bias[0]
    )
    grad_attended = grad_resid_one.astype(jnp.bfloat16)
    grad_project_out = jnp.einsum(
        "nc,nd->cd", mixed_heads, grad_attended, preferred_element_type=jnp.float32
    )
    grad_mixed = jnp.einsum(
        "nd,cd->nc", grad_attended, attention_exit_map, preferred_element_type=jnp.float32
    )
    grad_mixed = grad_mixed.astype(jnp.bfloat16).reshape(batch_row_list, sequence_length, H, HD)
    scores = masked_scores(query_rows, key_rows, segment_rows)
    attn_probs = jnp.exp(scores - log_total)
    probs_low = attn_probs.astype(jnp.bfloat16)
    grad_values = jnp.einsum(
        "bhqk,bqhd->bkhd", probs_low, grad_mixed, preferred_element_type=jnp.float32
    )
    grad_probs = jnp.einsum(
        "bqhd,bkhd->bhqk", grad_mixed, value_rows, preferred_element_type=jnp.float32
    )
    grad_scores = attn_probs * (grad_probs - jnp.sum(grad_probs * attn_probs, -1, keepdims=True))
    grad_scores = grad_scores.astype(jnp.bfloat16)
    grad_query = jnp.einsum(
        "bhqk,bkhd->bqhd", grad_scores, key_rows, preferred_element_type=jnp.float32
    ) * HD ** (-0.5)
    grad_keys = jnp.einsum(
        "bhqk,bqhd->bkhd", grad_scores, query_rows, preferred_element_type=jnp.float32
    ) * HD ** (-0.5)
    grad_qkv = (
        jnp.stack([grad_query, grad_keys, grad_values], 2)
        .reshape(batch_row_list * sequence_length, 3 * MODEL_WIDTH)
        .astype(jnp.bfloat16)
    )
    grad_project_in = jnp.einsum(
        "nd,nc->dc", embedded, grad_qkv, preferred_element_type=jnp.float32
    )
    grad_embedded = grad_resid_one + jnp.einsum(
        "nc,dc->nd", grad_qkv, query_key_value_maps, preferred_element_type=jnp.float32
    )
    grad_norms = jnp.stack([grad_gain_one, grad_shift_one, grad_gain_two, grad_shift_two])
    return (
        grad_embedded,
        grad_project_in,
        grad_project_out,
        grad_ffn_up,
        grad_ffn_down,
        grad_norms,
    )


def adam_update(weight, first, second, grad, fix_first, fix_second, rate, decay):
    first_new = beta_one * first + (1.0 - beta_one) * grad
    second_new = beta_two * second + (1.0 - beta_two) * grad * grad
    step_size = first_new / fix_first / (jnp.sqrt(second_new / fix_second) + adam_eps)
    return (weight - rate * (step_size + decay * weight), first_new, second_new)


def per_device(
    kmer_identifiers,
    slot_fragment_ids,
    mirror_fragment_index,
    fragment_weight,
    affinity_heat,
    optimizer_iteration,
    lexicon_table,
    lexicon_first_moment,
    lexicon_raw_moment,
    query_key_value_maps,
    qkv_first_moment,
    qkv_raw_moment,
    attention_exit_map,
    exit_first_moment,
    exit_raw_moment,
    widening_matrix_in,
    widening_first_moment,
    widening_raw_moment,
    narrowing_matrix_out,
    narrowing_first_moment,
    narrowing_raw_moment,
    layernorm_scale_bias,
    layernorm_first_moment,
    layernorm_raw_moment,
):
    masters = (
        lexicon_table,
        query_key_value_maps,
        attention_exit_map,
        widening_matrix_in,
        narrowing_matrix_out,
        layernorm_scale_bias,
    )
    firsts = (
        lexicon_first_moment,
        qkv_first_moment,
        exit_first_moment,
        widening_first_moment,
        narrowing_first_moment,
        layernorm_first_moment,
    )
    seconds = (
        lexicon_raw_moment,
        qkv_raw_moment,
        exit_raw_moment,
        widening_raw_moment,
        narrowing_raw_moment,
        layernorm_raw_moment,
    )
    rates = (rate_embed, rate_matrix, rate_matrix, rate_matrix, rate_matrix, rate_norm)
    decays = (decay_rate, decay_rate, decay_rate, decay_rate, decay_rate, 0.0)
    lowered = tuple((piece.astype(jnp.bfloat16) for piece in masters))
    gathered = (
        lax.all_gather(lowered[0], "fsdp", axis=1, tiled=True),
        lax.all_gather(lowered[1], "fsdp", axis=0, tiled=True),
        lax.all_gather(lowered[2], "fsdp", axis=0, tiled=True),
        lax.all_gather(lowered[3], "fsdp", axis=0, tiled=True),
        lax.all_gather(lowered[4], "fsdp", axis=0, tiled=True),
        lax.all_gather(lowered[5], "fsdp", axis=1, tiled=True),
    )
    pooled_state, saved_state = layer_forward(gathered, kmer_identifiers, slot_fragment_ids)
    unit_scale = lax.rsqrt(jnp.sum(pooled_state * pooled_state, -1, keepdims=True) + unit_eps)
    unit_rows = pooled_state * unit_scale
    unit_low = unit_rows.astype(jnp.bfloat16)
    every_unit = lax.all_gather(unit_low, ("fsdp", "dp"), axis=0, tiled=True)
    cosine_affinity_grid = jnp.einsum(
        "sd,td->st", unit_low, every_unit, preferred_element_type=jnp.float32
    )
    seg_local = pooled_state.shape[0]
    fragment_tally = every_unit.shape[0]
    shard_fragment_lines = lax.axis_index(("fsdp", "dp")) * seg_local + jnp.arange(
        seg_local, dtype=jnp.int32
    )
    field_sequence_array = jnp.arange(fragment_tally, dtype=jnp.int32)
    raw_affinity_values = jnp.where(
        shard_fragment_lines[:, None] == field_sequence_array[None, :],
        -1e30,
        cosine_affinity_grid / affinity_heat,
    )
    row_max = jnp.max(raw_affinity_values, -1, keepdims=True)
    log_total = row_max[:, 0] + jnp.log(jnp.sum(jnp.exp(raw_affinity_values - row_max), -1))
    chosen = mirror_fragment_index[:, None] == field_sequence_array[None, :]
    chosen_real_entry = chosen.astype(jnp.float32)
    target = jnp.sum(jnp.where(chosen, raw_affinity_values, 0.0), -1)
    contrast_objective = (
        lax.psum(jnp.sum(fragment_weight * (log_total - target)), ("fsdp", "dp")) / fragment_tally
    )
    exponent_probabilities = jnp.exp(raw_affinity_values - log_total[:, None])
    similarity_gradient = (
        (exponent_probabilities - chosen_real_entry)
        * fragment_weight[:, None]
        / (fragment_tally * affinity_heat)
    ).astype(jnp.bfloat16)
    grad_rows = jnp.dot(similarity_gradient, every_unit, preferred_element_type=jnp.float32)
    column_terms = jnp.einsum(
        "st,sd->td", similarity_gradient, unit_low, preferred_element_type=jnp.float32
    )
    grad_cols = lax.psum_scatter(column_terms, ("fsdp", "dp"), scatter_dimension=0, tiled=True)
    grad_unit = grad_rows + grad_cols
    pooled_gradient = unit_scale * (
        grad_unit - unit_rows * jnp.sum(grad_unit * unit_rows, -1, keepdims=True)
    )
    again = (
        lax.all_gather(lowered[0], "fsdp", axis=1, tiled=True),
        lax.all_gather(lowered[1], "fsdp", axis=0, tiled=True),
        lax.all_gather(lowered[2], "fsdp", axis=0, tiled=True),
        lax.all_gather(lowered[3], "fsdp", axis=0, tiled=True),
        lax.all_gather(lowered[4], "fsdp", axis=0, tiled=True),
        lax.all_gather(lowered[5], "fsdp", axis=1, tiled=True),
    )
    grads = layer_backward(again, saved_state, kmer_identifiers, slot_fragment_ids, pooled_gradient)
    vocab = lexicon_table.shape[0]
    rest = (
        lax.psum_scatter(grads[1], "fsdp", scatter_dimension=0, tiled=True),
        lax.psum_scatter(grads[2], "fsdp", scatter_dimension=0, tiled=True),
        lax.psum_scatter(grads[3], "fsdp", scatter_dimension=0, tiled=True),
        lax.psum_scatter(grads[4], "fsdp", scatter_dimension=0, tiled=True),
        lax.psum_scatter(grads[5], "fsdp", scatter_dimension=1, tiled=True),
    )
    column_rows = lax.all_to_all(
        grads[0].astype(jnp.bfloat16), "fsdp", split_axis=1, concat_axis=0, tiled=True
    ).astype(jnp.float32)
    all_tokens = lax.all_gather(kmer_identifiers.reshape(-1), "fsdp", axis=0, tiled=True)
    table_shard = jax.ops.segment_sum(column_rows, all_tokens, num_segments=vocab)
    shards = (table_shard, rest[0], rest[1], rest[2], rest[3], rest[4])
    shards = (
        lax.psum(shards[0].astype(jnp.bfloat16), "dp").astype(jnp.float32),
        lax.psum(shards[1].astype(jnp.bfloat16), "dp").astype(jnp.float32),
        lax.psum(shards[2].astype(jnp.bfloat16), "dp").astype(jnp.float32),
        lax.psum(shards[3].astype(jnp.bfloat16), "dp").astype(jnp.float32),
        lax.psum(shards[4].astype(jnp.bfloat16), "dp").astype(jnp.float32),
        lax.psum(shards[5].astype(jnp.bfloat16), "dp").astype(jnp.float32),
    )
    squares = sum((jnp.sum(piece * piece) for piece in shards))
    grad_norm = jnp.sqrt(lax.psum(squares, "fsdp"))
    factor = clip_norm / jnp.maximum(grad_norm, clip_norm)
    count_now = optimizer_iteration.astype(jnp.float32)
    fix_first = 1.0 - jnp.power(beta_one, count_now)
    fix_second = 1.0 - jnp.power(beta_two, count_now)
    updated = [
        adam_update(
            masters[number],
            firsts[number],
            seconds[number],
            shards[number] * factor,
            fix_first,
            fix_second,
            rates[number],
            decays[number],
        )
        for number in range(6)
    ]
    return (
        contrast_objective,
        grad_norm,
        updated[0][0],
        updated[0][1],
        updated[0][2],
        updated[1][0],
        updated[1][1],
        updated[1][2],
        updated[2][0],
        updated[2][1],
        updated[2][2],
        updated[3][0],
        updated[3][1],
        updated[3][2],
        updated[4][0],
        updated[4][1],
        updated[4][2],
        updated[5][0],
        updated[5][1],
        updated[5][2],
    )


AXES = ("fsdp", "dp")
VOCAB_PAD = 4352
VOCAB_HALF = VOCAB_PAD // 2
BIG_VMEM = pltpu.CompilerParams(vmem_limit_bytes=60 * 1024 * 1024)
bf16 = jnp.bfloat16
f32 = jnp.float32


def pairs_of(moved):
    spots = [(z, y, x, c) for z in range(4) for y in range(2) for x in range(2) for c in range(2)]

    def linear(spot):
        z, y, x, c = spot
        return ((z * 2 + y) * 2 + x) * 2 + c

    return [(linear(spot), linear(moved(*spot))) for spot in spots]


FIRST = pairs_of(lambda z, y, x, c: (z, y, x ^ 1, c) if c == 0 else (z, y ^ 1, x, c))
SECOND = pairs_of(lambda z, y, x, c: (z, y ^ 1, x, c) if c == 0 else (z, y, x ^ 1, c))
BOTH = pairs_of(lambda z, y, x, c: (z, y ^ 1, x ^ 1, c))
CORE = pairs_of(lambda z, y, x, c: (z, y, x, 1 - c))
ZS = [None] + [pairs_of(lambda z, y, x, c, j=j: (z ^ j, y, x, c)) for j in (1, 2, 3)]


def send(array, pairs):
    return lax.ppermute(array, AXES, pairs)


class Place:
    def __init__(self):
        f = lax.axis_index("fsdp")
        self.core = lax.axis_index("dp")
        self.z, self.y, self.x = f // 4, (f // 2) % 2, f % 2

    def plane_slot(self, core, a, b):
        dy = jnp.where(core == 0, b, a)
        dx = jnp.where(core == 0, a, b)
        return (self.y ^ dy) * 2 + (self.x ^ dx)

    def chip(self, core, j, a, b):
        return (self.z ^ j) * 4 + self.plane_slot(core, a, b)


def gather_blocks(piece):
    column = jnp.stack([piece] + [send(piece, ZS[j]) for j in (1, 2, 3)])
    one = send(column, FIRST)
    two = send(column, SECOND)
    three = send(one, SECOND)
    return [column, one, two, three]


def move_kernel(plan, n_in, idx_ref, *refs):
    ins, outs, sems = refs[:n_in], refs[n_in:-1], refs[-1]
    copies = []
    for number, (source, source_at, target, target_at) in enumerate(plan):
        src = ins[source].at[idx_ref[source_at[1]] if source_at[0] else source_at[1]]
        dst = outs[target].at[idx_ref[target_at[1]] if target_at[0] else target_at[1]]
        copies.append(pltpu.make_async_copy(src, dst, sems.at[number]))
    for copy in copies:
        copy.start()
    for copy in copies:
        copy.wait()


def move(plan, index, arrays, shapes):
    return pl.pallas_call(
        lambda *refs: move_kernel(plan, len(arrays), *refs),
        out_shape=shapes,
        in_specs=[pl.BlockSpec(memory_space=pltpu.SMEM)]
        + [pl.BlockSpec(memory_space=pl.ANY)] * len(arrays),
        out_specs=[pl.BlockSpec(memory_space=pltpu.VMEM)] * len(shapes),
        scratch_shapes=[pltpu.SemaphoreType.DMA((len(plan),))],
        compiler_params=BIG_VMEM,
    )(index, *arrays)


def gather_halves(piece, place):
    rows, width = piece.shape
    mine = gather_blocks(piece)
    theirs = [send(block, CORE) for block in mine]
    index, plan = [], []
    for side, blocks in enumerate((mine, theirs)):
        core = place.core if side == 0 else 1 - place.core
        for b in (0, 1):
            for a in (0, 1):
                for j in range(4):
                    plan.append((side * 4 + a + 2 * b, (False, j), 0, (True, len(index))))
                    index.append(core * 16 + place.chip(core, j, a, b))
    shape = jax.ShapeDtypeStruct((32, rows, width), piece.dtype)
    (out,) = move(plan, jnp.stack(index).astype(jnp.int32), mine + theirs, [shape])
    return out.reshape(2, 16 * rows, width)


def scatter_sum(grad, place):
    chunks = grad.reshape(16, grad.shape[0] // 16, grad.shape[1])
    index, plan = [], []
    for b in (0, 1):
        for a in (0, 1):
            for j in range(4):
                plan.append((0, (True, len(index)), 1 - b, (False, a * 4 + j)))
                index.append(place.chip(place.core, j, a, b))
    shape = jax.ShapeDtypeStruct((8,) + chunks.shape[1:], bf16)
    away, keep = move(plan, jnp.stack(index).astype(jnp.int32), [chunks], [shape, shape])
    came = send(away, SECOND)
    across = (keep[4:].astype(f32) + came[4:].astype(f32)).astype(bf16)
    came_two = send(across, FIRST)
    here = [
        keep[j].astype(f32) + came[j].astype(f32) + came_two[j].astype(f32) for j in range(4)
    ]
    far = [send(here[j].astype(bf16), ZS[j]) for j in (1, 2, 3)]
    return here[0] + far[0].astype(f32) + far[1].astype(f32) + far[2].astype(f32)


def one_hot(ids_row, start, count):
    spots = lax.broadcasted_iota(jnp.int32, (count, ids_row.shape[1]), 0) + start
    return jnp.where(spots == ids_row, 1.0, 0.0).astype(bf16)


def lookup_kernel(idx_ref, ids_ref, *refs):
    ins, outs, table, sems = refs[:7], refs[7:11], refs[11], refs[12]
    copies = [
        pltpu.make_async_copy(
            ins[0], table.at[pl.ds(pl.multiple_of(idx_ref[0], 16), 48), :], sems.at[0]
        )
    ]
    for number in range(1, 7):
        column = pl.multiple_of(idx_ref[7 + (number - 1) // 3], 128)
        row = pl.multiple_of(idx_ref[number], 16)
        copies.append(
            pltpu.make_async_copy(
                ins[number],
                table.at[pl.ds(row, 48), pl.ds(column, VOCAB_HALF)],
                sems.at[number],
            )
        )
    for copy in copies:
        copy.start()
    for copy in copies:
        copy.wait()
    for j in range(4):
        total = jnp.zeros((192, 512), f32)
        for k in range(VOCAB_PAD // 256):
            total += jnp.dot(
                table[:, k * 256 : (k + 1) * 256],
                one_hot(ids_ref[j], k * 256, 256),
                preferred_element_type=f32,
            )
        outs[j][...] = total.astype(bf16)


def lookup(index, ids_z, arrays):
    vmem = pl.BlockSpec(memory_space=pltpu.VMEM)
    return pl.pallas_call(
        lookup_kernel,
        out_shape=[jax.ShapeDtypeStruct((192, 512), bf16)] * 4,
        in_specs=[pl.BlockSpec(memory_space=pltpu.SMEM), vmem]
        + [pl.BlockSpec(memory_space=pl.ANY)] * 7,
        out_specs=[vmem] * 4,
        scratch_shapes=[pltpu.VMEM((192, VOCAB_PAD), bf16), pltpu.SemaphoreType.DMA((7,))],
        compiler_params=BIG_VMEM,
    )(index, ids_z, *arrays)


def token_sum_kernel(idx_ref, ids_ref, other_ids_ref, mine_ref, other_ref, out_ref):
    start = idx_ref[0]
    for low in range(0, VOCAB_HALF, 256):
        count = min(256, VOCAB_HALF - low)
        total = jnp.zeros((192, count), f32)
        for ids, block in ((ids_ref, mine_ref), (other_ids_ref, other_ref)):
            for j in range(4):
                total += lax.dot_general(
                    block[j],
                    one_hot(ids[j], start + low, count),
                    (((1,), (1,)), ((), ())),
                    preferred_element_type=f32,
                )
        out_ref[:, low : low + count] = total.astype(bf16)


def token_sum(index, ids_z, other_ids, mine, other):
    vmem = pl.BlockSpec(memory_space=pltpu.VMEM)
    return pl.pallas_call(
        token_sum_kernel,
        out_shape=jax.ShapeDtypeStruct((192, VOCAB_HALF), bf16),
        in_specs=[pl.BlockSpec(memory_space=pltpu.SMEM)] + [vmem] * 4,
        out_specs=vmem,
        compiler_params=BIG_VMEM,
    )(index, ids_z, other_ids, mine, other)


def my_half(array, core, width):
    return lax.dynamic_slice_in_dim(array, core * width, width, axis=1)


def both_halves(own, other, core, axis):
    return jnp.where(
        core == 0,
        jnp.concatenate([own, other], axis),
        jnp.concatenate([other, own], axis),
    )


def in_three(value):
    high = value.astype(bf16)
    rest = value - high.astype(f32)
    middle = rest.astype(bf16)
    return high, middle, (rest - middle.astype(f32)).astype(bf16)


def all_sum(value):
    for pairs in (ZS[1:], [FIRST, SECOND, BOTH]):
        one, two, three = (send(value, p) for p in pairs)
        value = (value + one) + (two + three)
    return value


def per_device_links(
    kmer_identifiers,
    slot_fragment_ids,
    mirror_fragment_index,
    fragment_weight,
    affinity_heat,
    optimizer_iteration,
    lexicon_table,
    lexicon_first_moment,
    lexicon_raw_moment,
    query_key_value_maps,
    qkv_first_moment,
    qkv_raw_moment,
    attention_exit_map,
    exit_first_moment,
    exit_raw_moment,
    widening_matrix_in,
    widening_first_moment,
    widening_raw_moment,
    narrowing_matrix_out,
    narrowing_first_moment,
    narrowing_raw_moment,
    layernorm_scale_bias,
    layernorm_first_moment,
    layernorm_raw_moment,
):
    place = Place()
    core = place.core
    vocab = lexicon_table.shape[0]
    table_cut = jnp.pad(lexicon_table.T.astype(bf16), ((0, 0), (0, VOCAB_PAD - vocab)))
    table_half = my_half(table_cut, core, VOCAB_HALF)
    t_one = send(table_half, FIRST)
    t_two = send(table_half, SECOND)
    t_three = send(t_one, SECOND)
    others = [send(t, CORE) for t in (t_one, t_two, t_three)]
    ids_z = jnp.stack([kmer_identifiers] + [send(kmer_identifiers, ZS[j]) for j in (1, 2, 3)])
    norm_cut = layernorm_scale_bias.T.astype(bf16)
    heavy = jnp.stack(in_three(fragment_weight), 1)
    partner = jnp.stack([mirror_fragment_index // 32, mirror_fragment_index % 32], 1).astype(bf16)
    extra = jnp.concatenate(
        [
            norm_cut,
            jnp.pad(jnp.concatenate([heavy, partner], 1), ((0, 16), (0, 0))),
            jnp.zeros((48, 119), bf16),
        ],
        1,
    )
    low_in = query_key_value_maps.astype(bf16)
    low_out = attention_exit_map.astype(bf16)
    low_up = widening_matrix_in.astype(bf16)
    low_down = narrowing_matrix_out.astype(bf16)
    in_out_cut = jnp.concatenate(
        [my_half(low_in[:, k * 768 : (k + 1) * 768], core, 384) for k in range(3)]
        + [my_half(low_out, core, 384), extra],
        1,
    )
    in_out = gather_halves(in_out_cut, place)
    up_w = gather_halves(my_half(low_up, core, 1536), place)
    down_w = gather_halves(my_half(low_down, core, 384), place)
    slots = [place.y * 2 + place.x]
    for side in (core, 1 - core):
        slots += [place.plane_slot(side, a, b) for a, b in ((1, 0), (0, 1), (1, 1))]
    index = jnp.stack(
        [s * 48 for s in slots] + [core * VOCAB_HALF, (1 - core) * VOCAB_HALF]
    ).astype(jnp.int32)
    found = lookup(index, ids_z, [table_cut, t_one, t_two, t_three] + others)
    columns = [found[0]] + [send(found[j], ZS[j]) for j in (1, 2, 3)]
    z_index = jnp.stack([place.z ^ j for j in range(4)]).astype(jnp.int32)
    (embedded_t,) = move(
        [(j, (False, 0), 0, (True, j)) for j in range(4)],
        z_index,
        [col.reshape(1, 192, 512) for col in columns],
        [jax.ShapeDtypeStruct((4, 192, 512), bf16)],
    )
    embedded = embedded_t.reshape(768, 512).T
    side_data = in_out[:, :, 1536:1664]
    params = side_data[0, :, :4].T.astype(f32)
    segments = slot_fragment_ids
    qkv = jnp.concatenate(
        [jnp.dot(embedded, in_out[k, :, :1152], preferred_element_type=f32) for k in (0, 1)], 1
    ).astype(bf16)
    qkv = qkv.reshape(1, 512, 2, 3, H // 2, HD)
    query_rows, key_rows, value_rows = (
        qkv[:, :, :, k].reshape(1, 512, H, HD) for k in range(3)
    )
    scores = masked_scores(query_rows, key_rows, segments)
    row_max = jnp.max(scores, -1, keepdims=True)
    log_total = row_max + jnp.log(jnp.sum(jnp.exp(scores - row_max), -1, keepdims=True))
    attn_probs = jnp.exp(scores - log_total).astype(bf16)
    mixed = jnp.einsum("bhqk,bkhd->bqhd", attn_probs, value_rows, preferred_element_type=f32)
    mixed = mixed.reshape(512, MODEL_WIDTH).astype(bf16)
    out_w = jnp.concatenate([in_out[0, :, 1152:1536], in_out[1, :, 1152:1536]], 1)
    attended = jnp.dot(mixed, out_w, preferred_element_type=f32)
    normed_one, unit_one, inv_one = layer_norm(
        embedded.astype(f32) + attended, params[0], params[1]
    )
    normed_low = normed_one.astype(bf16)
    up_proj = jnp.concatenate(
        [jnp.dot(normed_low, up_w[k], preferred_element_type=f32) for k in (0, 1)], 1
    )
    activated = jax.nn.gelu(up_proj, approximate=False).astype(bf16)
    ffn_result = jnp.concatenate(
        [jnp.dot(activated, down_w[k], preferred_element_type=f32) for k in (0, 1)], 1
    )
    normed_two, unit_two, inv_two = layer_norm(normed_one + ffn_result, params[2], params[3])
    member = (segments == jnp.arange(SEG_ROW, dtype=jnp.int32)[:, None]).astype(f32)
    pooled = jnp.dot(member, normed_two, precision=largest_value)
    unit_scale = lax.rsqrt(jnp.sum(pooled * pooled, -1, keepdims=True) + unit_eps)
    unit_rows = pooled * unit_scale
    unit_low = unit_rows.astype(bf16)
    embedded_o, mixed_o, normed_o, activated_o = (
        send(a, CORE) for a in (embedded, mixed, normed_low, activated)
    )
    column = jnp.stack([unit_low] + [send(unit_low, ZS[j]) for j in (1, 2, 3)])
    blocks = [column, send(column, FIRST), send(column, SECOND), send(column, BOTH)]
    blocks = blocks + [send(block, CORE) for block in blocks]
    plan, index = [], []
    for side, who in enumerate((core, 1 - core)):
        for b in (0, 1):
            for a in (0, 1):
                for j in range(4):
                    plan.append((side * 4 + a + 2 * b, (False, j), 0, (True, len(index))))
                    index.append(place.chip(who, j, a, b) * 2 + who)
    (every,) = move(
        plan,
        jnp.stack(index).astype(jnp.int32),
        blocks,
        [jax.ShapeDtypeStruct((32, 32, MODEL_WIDTH), bf16)],
    )
    every_unit = every.reshape(1024, MODEL_WIDTH)
    tally = 1024
    about = side_data.reshape(2, 16, 48, 128)[:, :, :32, 4:9].astype(f32)
    about = about.transpose(1, 0, 2, 3).reshape(tally, 5)
    weights = about[:, 0] + about[:, 1] + about[:, 2]
    partners = (about[:, 3] * 32.0 + about[:, 4]).astype(jnp.int32)
    numbers = jnp.arange(tally, dtype=jnp.int32)
    grid = (
        jnp.einsum("sd,td->st", every_unit, every_unit, preferred_element_type=f32)
        / affinity_heat
    )
    grid = jnp.where(numbers[:, None] == numbers[None, :], -1e30, grid)
    top = jnp.max(grid, -1, keepdims=True)
    log_sum = top + jnp.log(jnp.sum(jnp.exp(grid - top), -1, keepdims=True))
    chosen = partners[:, None] == numbers[None, :]
    target = jnp.sum(jnp.where(chosen, grid, 0.0), -1, keepdims=True)
    contrast_objective = jnp.sum(weights[:, None] * (log_sum - target)) / tally
    grid_gradient = (
        (jnp.exp(grid - log_sum) - chosen.astype(f32))
        * weights[:, None]
        / (tally * affinity_heat)
    ).astype(bf16)
    base = (lax.axis_index("fsdp") * 2 + core) * 32
    my_rows = lax.dynamic_slice_in_dim(grid_gradient, base, 32, axis=0)
    my_cols = lax.dynamic_slice_in_dim(grid_gradient, base, 32, axis=1)
    grad_unit = jnp.dot(my_rows, every_unit, preferred_element_type=f32) + jnp.einsum(
        "st,sd->td", my_cols, every_unit, preferred_element_type=f32
    )
    pooled_gradient = unit_scale * (
        grad_unit - unit_rows * jnp.sum(grad_unit * unit_rows, -1, keepdims=True)
    )
    second_gradient = jnp.einsum("ot,oy->ty", member, pooled_gradient, precision=largest_value)
    grad_two, gain_two, shift_two = norm_back(second_gradient, unit_two, inv_two, params[2])
    grad_result = grad_two.astype(bf16)
    grad_result_o = send(my_half(grad_result, 1 - core, 384), CORE)
    grad_down = jnp.einsum(
        "nf,nd->fd",
        jnp.concatenate([activated, activated_o], 0),
        jnp.concatenate([my_half(grad_result, core, 384), grad_result_o], 0),
        preferred_element_type=f32,
    ).astype(bf16)
    down_sum = scatter_sum(grad_down, place)
    down_all = jnp.concatenate([down_w[0], down_w[1]], 1)
    grad_act = jnp.einsum("nd,fd->nf", grad_result, down_all, preferred_element_type=f32)
    _, gelu_pull = jax.vjp(lambda pre: jax.nn.gelu(pre, approximate=False), up_proj)
    grad_up = gelu_pull(grad_act)[0].astype(bf16)
    grad_up_o = send(my_half(grad_up, 1 - core, 1536), CORE)
    grad_ffn_up = jnp.einsum(
        "nd,nf->df",
        jnp.concatenate([normed_low, normed_o], 0),
        jnp.concatenate([my_half(grad_up, core, 1536), grad_up_o], 0),
        preferred_element_type=f32,
    ).astype(bf16)
    up_all = jnp.concatenate([up_w[0], up_w[1]], 1)
    grad_one = grad_two + jnp.einsum("nf,df->nd", grad_up, up_all, preferred_element_type=f32)
    grad_resid, gain_one, shift_one = norm_back(grad_one, unit_one, inv_one, params[0])
    grad_attended = grad_resid.astype(bf16)
    grad_att_o = send(my_half(grad_attended, 1 - core, 384), CORE)
    grad_out = jnp.einsum(
        "nc,nd->cd",
        jnp.concatenate([mixed, mixed_o], 0),
        jnp.concatenate([my_half(grad_attended, core, 384), grad_att_o], 0),
        preferred_element_type=f32,
    ).astype(bf16)
    norms = jnp.stack([gain_one, shift_one, gain_two, shift_two])
    norms = norms + send(norms, CORE)
    up_out_sum = scatter_sum(
        jnp.concatenate(
            [grad_ffn_up, grad_out, jnp.pad(norms.T.astype(bf16), ((0, 0), (0, 124)))], 1
        ),
        place,
    )
    grad_mixed = jnp.einsum("nd,cd->nc", grad_attended, out_w, preferred_element_type=f32)
    grad_mixed = grad_mixed.astype(bf16).reshape(1, 512, H, HD)
    scores = masked_scores(query_rows, key_rows, segments)
    attn_probs = jnp.exp(scores - log_total)
    probs_low = attn_probs.astype(bf16)
    grad_values = jnp.einsum(
        "bhqk,bqhd->bkhd", probs_low, grad_mixed, preferred_element_type=f32
    )
    grad_probs = jnp.einsum(
        "bqhd,bkhd->bhqk", grad_mixed, value_rows, preferred_element_type=f32
    )
    grad_scores = attn_probs * (grad_probs - jnp.sum(grad_probs * attn_probs, -1, keepdims=True))
    grad_scores = grad_scores.astype(bf16)
    grad_query = jnp.einsum(
        "bhqk,bkhd->bqhd", grad_scores, key_rows, preferred_element_type=f32
    ) * HD ** (-0.5)
    grad_keys = jnp.einsum(
        "bhqk,bqhd->bkhd", grad_scores, query_rows, preferred_element_type=f32
    ) * HD ** (-0.5)
    grad_qkv = jnp.stack(
        [g.reshape(512, 2, 384) for g in (grad_query, grad_keys, grad_values)], 2
    ).astype(bf16)
    grad_qkv = grad_qkv.reshape(512, 2304)
    grad_embedded = grad_resid + sum(
        jnp.einsum(
            "nc,dc->nd",
            grad_qkv[:, k * 1152 : (k + 1) * 1152],
            in_out[k, :, :1152],
            preferred_element_type=f32,
        )
        for k in (0, 1)
    )
    rows_t = grad_embedded.astype(bf16).T.reshape(4, 192, 512)
    outs = move(
        [(0, (True, j), j, (False, 0)) for j in range(4)],
        z_index,
        [rows_t],
        [jax.ShapeDtypeStruct((1, 192, 512), bf16)] * 4,
    )
    token_cols = jnp.concatenate([outs[0]] + [send(outs[j], ZS[j]) for j in (1, 2, 3)], 0)
    token_cols_o = send(token_cols, CORE)
    ids_o = send(ids_z, CORE)
    grad_qkv_o = send(my_half(grad_qkv, 1 - core, 1152), CORE)
    grad_in = jnp.einsum(
        "nd,nc->dc",
        jnp.concatenate([embedded, embedded_o], 0),
        jnp.concatenate([my_half(grad_qkv, core, 1152), grad_qkv_o], 0),
        preferred_element_type=f32,
    ).astype(bf16)
    in_sum = scatter_sum(grad_in, place)
    table_part = token_sum(
        (core * VOCAB_HALF).astype(jnp.int32).reshape(1), ids_z, ids_o, token_cols, token_cols_o
    ).reshape(4, 48, VOCAB_HALF)
    slots = [place.plane_slot(core, a, b) for a, b in ((0, 0), (1, 0), (0, 1), (1, 1))]
    pair = jax.ShapeDtypeStruct((2, 48, VOCAB_HALF), bf16)
    keep, away = move(
        [(0, (True, k), k // 2, (False, k % 2)) for k in range(4)],
        jnp.stack(slots).astype(jnp.int32),
        [table_part],
        [pair, pair],
    )
    came = send(away, SECOND)
    across = (keep[1].astype(f32) + came[1].astype(f32)).astype(bf16)
    table_sum = keep[0].astype(f32) + came[0].astype(f32) + send(across, FIRST).astype(f32)
    sums = [s.astype(bf16) for s in (table_sum, in_sum, up_out_sum, down_sum)]
    table_o, in_o, up_out_o, down_o = (send(s, CORE) for s in sums)
    table_g, in_g, up_out_g, down_g = sums
    norm_own = up_out_g[:, 1920:1924].astype(f32)
    squares = sum(
        jnp.sum(jnp.square(p.astype(f32)))
        for p in (table_g, in_g, up_out_g[:, :1920], down_g)
    ) + jnp.where(core == 0, jnp.sum(norm_own * norm_own), 0.0)
    squares = all_sum(squares.reshape(1, 1))
    squares = squares + send(squares, CORE)
    grad_norm = jnp.sqrt(squares[0, 0])
    in_both = both_halves(in_g.reshape(48, 3, 384), in_o.reshape(48, 3, 384), core, 2)
    shards = (
        both_halves(table_g, table_o, core, 1)[:, :vocab],
        in_both.reshape(48, 2304),
        both_halves(up_out_g[:, 1536:1920], up_out_o[:, 1536:1920], core, 1),
        both_halves(up_out_g[:, :1536], up_out_o[:, :1536], core, 1),
        both_halves(down_g, down_o, core, 1),
        jnp.where(core == 0, up_out_g[:, 1920:1924], up_out_o[:, 1920:1924]).T,
    )
    masters = (
        lexicon_table.T,
        query_key_value_maps,
        attention_exit_map,
        widening_matrix_in,
        narrowing_matrix_out,
        layernorm_scale_bias,
    )
    firsts = (
        lexicon_first_moment.T,
        qkv_first_moment,
        exit_first_moment,
        widening_first_moment,
        narrowing_first_moment,
        layernorm_first_moment,
    )
    seconds = (
        lexicon_raw_moment.T,
        qkv_raw_moment,
        exit_raw_moment,
        widening_raw_moment,
        narrowing_raw_moment,
        layernorm_raw_moment,
    )
    rates = (rate_embed, rate_matrix, rate_matrix, rate_matrix, rate_matrix, rate_norm)
    decays = (decay_rate, decay_rate, decay_rate, decay_rate, decay_rate, 0.0)
    factor = clip_norm / jnp.maximum(grad_norm, clip_norm)
    count_now = optimizer_iteration.astype(f32)
    fix_first = 1.0 - jnp.power(beta_one, count_now)
    fix_second = 1.0 - jnp.power(beta_two, count_now)
    results = [contrast_objective, grad_norm]
    for number in range(6):
        updated = adam_update(
            masters[number],
            firsts[number],
            seconds[number],
            shards[number].astype(f32) * factor,
            fix_first,
            fix_second,
            rates[number],
            decays[number],
        )
        results += [u.T for u in updated] if number == 0 else list(updated)
    return tuple(results)


def solution(mesh):
    in_specs = (
        P(("fsdp", "dp"), None),
        P(("fsdp", "dp"), None),
        P(("fsdp", "dp")),
        P(("fsdp", "dp")),
        P(),
        P(),
        P(None, "fsdp"),
        P(None, "fsdp"),
        P(None, "fsdp"),
        P("fsdp", None),
        P("fsdp", None),
        P("fsdp", None),
        P("fsdp", None),
        P("fsdp", None),
        P("fsdp", None),
        P("fsdp", None),
        P("fsdp", None),
        P("fsdp", None),
        P("fsdp", None),
        P("fsdp", None),
        P("fsdp", None),
        P(None, "fsdp"),
        P(None, "fsdp"),
        P(None, "fsdp"),
    )
    out_specs = (
        P(),
        P(),
        P(None, "fsdp"),
        P(None, "fsdp"),
        P(None, "fsdp"),
        P("fsdp", None),
        P("fsdp", None),
        P("fsdp", None),
        P("fsdp", None),
        P("fsdp", None),
        P("fsdp", None),
        P("fsdp", None),
        P("fsdp", None),
        P("fsdp", None),
        P("fsdp", None),
        P("fsdp", None),
        P("fsdp", None),
        P(None, "fsdp"),
        P(None, "fsdp"),
        P(None, "fsdp"),
    )
    own_plan = dict(mesh.shape) == {"fsdp": 16, "dp": 2}
    return jax.shard_map(
        per_device_links if own_plan else per_device, mesh=mesh, in_specs=in_specs, out_specs=out_specs, check_vma=False
    )
```

```python
import jax
import jax.numpy as jnp
from jax import lax
from jax.experimental import pallas as pl
from jax.experimental.pallas import tpu as pltpu
from jax.sharding import PartitionSpec as P

MODEL_WIDTH = 768
H = 12
HD = 64
SEG_ROW = 32


largest_value = lax.Precision.HIGHEST
beta_one = 0.9
beta_two = 0.999
adam_eps = 1e-12
decay_rate = 0.01
rate_matrix = 0.1
rate_embed = 1.0
rate_norm = 1.0
clip_norm = 0.001
norm_eps = 1e-05
unit_eps = 1e-06


def layer_norm(inputs, gain_row, shifts):
    center = inputs - jnp.mean(inputs, -1, keepdims=True)
    inv_std = lax.rsqrt(jnp.mean(center * center, -1, keepdims=True) + norm_eps)
    normed = center * inv_std
    return (normed * gain_row + shifts, normed, inv_std)


def norm_back(upstream, normed, inv_std, gain_row):
    scaled = upstream * gain_row
    grad_in = inv_std * (
        scaled
        - jnp.mean(scaled, -1, keepdims=True)
        - normed * jnp.mean(scaled * normed, -1, keepdims=True)
    )
    return (grad_in, jnp.sum(upstream * normed, 0), jnp.sum(upstream, 0))


def masked_scores(query_rows, key_rows, segment_rows):
    raw_scores = jnp.einsum(
        "bqhd,bkhd->bhqk", query_rows, key_rows, preferred_element_type=jnp.float32
    )
    same_segment = segment_rows[:, None, :, None] == segment_rows[:, None, None, :]
    return jnp.where(same_segment, raw_scores * HD ** (-0.5), -1e30)


def layer_forward(gathered, token_rows, segment_rows):
    (
        lexicon_table,
        query_key_value_maps,
        attention_exit_map,
        widening_matrix_in,
        narrowing_matrix_out,
        layernorm_scale_bias,
    ) = gathered
    batch_row_list, sequence_length = token_rows.shape
    embedded = jnp.take(lexicon_table, token_rows.reshape(-1), axis=0)
    qkv_all = jnp.dot(embedded, query_key_value_maps, preferred_element_type=jnp.float32).astype(
        jnp.bfloat16
    )
    qkv_all = qkv_all.reshape(batch_row_list, sequence_length, 3, H, HD)
    query_rows, key_rows, value_rows = (qkv_all[:, :, 0], qkv_all[:, :, 1], qkv_all[:, :, 2])
    scores = masked_scores(query_rows, key_rows, segment_rows)
    row_max = jnp.max(scores, -1, keepdims=True)
    log_total = row_max + jnp.log(jnp.sum(jnp.exp(scores - row_max), -1, keepdims=True))
    attn_probs = jnp.exp(scores - log_total).astype(jnp.bfloat16)
    mixed_heads = jnp.einsum(
        "bhqk,bkhd->bqhd", attn_probs, value_rows, preferred_element_type=jnp.float32
    )
    mixed_heads = mixed_heads.reshape(batch_row_list * sequence_length, MODEL_WIDTH).astype(
        jnp.bfloat16
    )
    attended = jnp.dot(mixed_heads, attention_exit_map, preferred_element_type=jnp.float32)
    normed_one, unit_one, inv_one = layer_norm(
        embedded.astype(jnp.float32) + attended, layernorm_scale_bias[0], layernorm_scale_bias[1]
    )
    normed_low = normed_one.astype(jnp.bfloat16)
    up_proj = jnp.dot(normed_low, widening_matrix_in, preferred_element_type=jnp.float32)
    activated = jax.nn.gelu(up_proj, approximate=False).astype(jnp.bfloat16)
    ffn_result = jnp.dot(activated, narrowing_matrix_out, preferred_element_type=jnp.float32)
    second_normalized, unit_two, inv_two = layer_norm(
        normed_one + ffn_result, layernorm_scale_bias[2], layernorm_scale_bias[3]
    )
    group_member = (
        segment_rows[:, None, :] == jnp.arange(SEG_ROW, dtype=jnp.int32)[None, :, None]
    ).astype(jnp.float32)
    pooled_state = jnp.einsum(
        "nkz,nzh->nkh",
        group_member,
        second_normalized.reshape(batch_row_list, sequence_length, MODEL_WIDTH),
        precision=largest_value,
    )
    saved_state = (
        embedded,
        query_rows,
        key_rows,
        value_rows,
        log_total,
        mixed_heads,
        unit_one,
        inv_one,
        normed_low,
        up_proj,
        activated,
        unit_two,
        inv_two,
        group_member,
    )
    return (pooled_state.reshape(batch_row_list * SEG_ROW, MODEL_WIDTH), saved_state)


def layer_backward(gathered, saved_state, token_rows, segment_rows, pooled_gradient):
    (
        lexicon_table,
        query_key_value_maps,
        attention_exit_map,
        widening_matrix_in,
        narrowing_matrix_out,
        layernorm_scale_bias,
    ) = gathered
    (
        embedded,
        query_rows,
        key_rows,
        value_rows,
        log_total,
        mixed_heads,
        unit_one,
        inv_one,
        normed_low,
        up_proj,
        activated,
        unit_two,
        inv_two,
        group_member,
    ) = saved_state
    batch_row_list, sequence_length = token_rows.shape
    pooled_gradient = pooled_gradient.reshape(batch_row_list, SEG_ROW, MODEL_WIDTH)
    second_gradient = jnp.einsum(
        "got,goy->gty", group_member, pooled_gradient, precision=largest_value
    ).reshape(batch_row_list * sequence_length, MODEL_WIDTH)
    grad_resid_two, grad_gain_two, grad_shift_two = norm_back(
        second_gradient, unit_two, inv_two, layernorm_scale_bias[2]
    )
    grad_result = grad_resid_two.astype(jnp.bfloat16)
    grad_ffn_down = jnp.einsum(
        "nf,nd->fd", activated, grad_result, preferred_element_type=jnp.float32
    )
    grad_act = jnp.einsum(
        "nd,fd->nf", grad_result, narrowing_matrix_out, preferred_element_type=jnp.float32
    )
    gelu_value, gelu_pull = jax.vjp(
        lambda pre_act: jax.nn.gelu(pre_act, approximate=False), up_proj
    )
    grad_up = gelu_pull(grad_act)[0].astype(jnp.bfloat16)
    grad_ffn_up = jnp.einsum("nd,nf->df", normed_low, grad_up, preferred_element_type=jnp.float32)
    grad_one = grad_resid_two + jnp.einsum(
        "nf,df->nd", grad_up, widening_matrix_in, preferred_element_type=jnp.float32
    )
    grad_resid_one, grad_gain_one, grad_shift_one = norm_back(
        grad_one, unit_one, inv_one, layernorm_scale_bias[0]
    )
    grad_attended = grad_resid_one.astype(jnp.bfloat16)
    grad_project_out = jnp.einsum(
        "nc,nd->cd", mixed_heads, grad_attended, preferred_element_type=jnp.float32
    )
    grad_mixed = jnp.einsum(
        "nd,cd->nc", grad_attended, attention_exit_map, preferred_element_type=jnp.float32
    )
    grad_mixed = grad_mixed.astype(jnp.bfloat16).reshape(batch_row_list, sequence_length, H, HD)
    scores = masked_scores(query_rows, key_rows, segment_rows)
    attn_probs = jnp.exp(scores - log_total)
    probs_low = attn_probs.astype(jnp.bfloat16)
    grad_values = jnp.einsum(
        "bhqk,bqhd->bkhd", probs_low, grad_mixed, preferred_element_type=jnp.float32
    )
    grad_probs = jnp.einsum(
        "bqhd,bkhd->bhqk", grad_mixed, value_rows, preferred_element_type=jnp.float32
    )
    grad_scores = attn_probs * (grad_probs - jnp.sum(grad_probs * attn_probs, -1, keepdims=True))
    grad_scores = grad_scores.astype(jnp.bfloat16)
    grad_query = jnp.einsum(
        "bhqk,bkhd->bqhd", grad_scores, key_rows, preferred_element_type=jnp.float32
    ) * HD ** (-0.5)
    grad_keys = jnp.einsum(
        "bhqk,bqhd->bkhd", grad_scores, query_rows, preferred_element_type=jnp.float32
    ) * HD ** (-0.5)
    grad_qkv = (
        jnp.stack([grad_query, grad_keys, grad_values], 2)
        .reshape(batch_row_list * sequence_length, 3 * MODEL_WIDTH)
        .astype(jnp.bfloat16)
    )
    grad_project_in = jnp.einsum(
        "nd,nc->dc", embedded, grad_qkv, preferred_element_type=jnp.float32
    )
    grad_embedded = grad_resid_one + jnp.einsum(
        "nc,dc->nd", grad_qkv, query_key_value_maps, preferred_element_type=jnp.float32
    )
    grad_norms = jnp.stack([grad_gain_one, grad_shift_one, grad_gain_two, grad_shift_two])
    return (
        grad_embedded,
        grad_project_in,
        grad_project_out,
        grad_ffn_up,
        grad_ffn_down,
        grad_norms,
    )


def adam_update(weight, first, second, grad, fix_first, fix_second, rate, decay):
    first_new = beta_one * first + (1.0 - beta_one) * grad
    second_new = beta_two * second + (1.0 - beta_two) * grad * grad
    step_size = first_new / fix_first / (jnp.sqrt(second_new / fix_second) + adam_eps)
    return (weight - rate * (step_size + decay * weight), first_new, second_new)


def per_device(
    kmer_identifiers,
    slot_fragment_ids,
    mirror_fragment_index,
    fragment_weight,
    affinity_heat,
    optimizer_iteration,
    lexicon_table,
    lexicon_first_moment,
    lexicon_raw_moment,
    query_key_value_maps,
    qkv_first_moment,
    qkv_raw_moment,
    attention_exit_map,
    exit_first_moment,
    exit_raw_moment,
    widening_matrix_in,
    widening_first_moment,
    widening_raw_moment,
    narrowing_matrix_out,
    narrowing_first_moment,
    narrowing_raw_moment,
    layernorm_scale_bias,
    layernorm_first_moment,
    layernorm_raw_moment,
):
    masters = (
        lexicon_table,
        query_key_value_maps,
        attention_exit_map,
        widening_matrix_in,
        narrowing_matrix_out,
        layernorm_scale_bias,
    )
    firsts = (
        lexicon_first_moment,
        qkv_first_moment,
        exit_first_moment,
        widening_first_moment,
        narrowing_first_moment,
        layernorm_first_moment,
    )
    seconds = (
        lexicon_raw_moment,
        qkv_raw_moment,
        exit_raw_moment,
        widening_raw_moment,
        narrowing_raw_moment,
        layernorm_raw_moment,
    )
    rates = (rate_embed, rate_matrix, rate_matrix, rate_matrix, rate_matrix, rate_norm)
    decays = (decay_rate, decay_rate, decay_rate, decay_rate, decay_rate, 0.0)
    lowered = tuple((piece.astype(jnp.bfloat16) for piece in masters))
    gathered = (
        lax.all_gather(lowered[0], "fsdp", axis=1, tiled=True),
        lax.all_gather(lowered[1], "fsdp", axis=0, tiled=True),
        lax.all_gather(lowered[2], "fsdp", axis=0, tiled=True),
        lax.all_gather(lowered[3], "fsdp", axis=0, tiled=True),
        lax.all_gather(lowered[4], "fsdp", axis=0, tiled=True),
        lax.all_gather(lowered[5], "fsdp", axis=1, tiled=True),
    )
    pooled_state, saved_state = layer_forward(gathered, kmer_identifiers, slot_fragment_ids)
    unit_scale = lax.rsqrt(jnp.sum(pooled_state * pooled_state, -1, keepdims=True) + unit_eps)
    unit_rows = pooled_state * unit_scale
    unit_low = unit_rows.astype(jnp.bfloat16)
    every_unit = lax.all_gather(unit_low, ("fsdp", "dp"), axis=0, tiled=True)
    cosine_affinity_grid = jnp.einsum(
        "sd,td->st", unit_low, every_unit, preferred_element_type=jnp.float32
    )
    seg_local = pooled_state.shape[0]
    fragment_tally = every_unit.shape[0]
    shard_fragment_lines = lax.axis_index(("fsdp", "dp")) * seg_local + jnp.arange(
        seg_local, dtype=jnp.int32
    )
    field_sequence_array = jnp.arange(fragment_tally, dtype=jnp.int32)
    raw_affinity_values = jnp.where(
        shard_fragment_lines[:, None] == field_sequence_array[None, :],
        -1e30,
        cosine_affinity_grid / affinity_heat,
    )
    row_max = jnp.max(raw_affinity_values, -1, keepdims=True)
    log_total = row_max[:, 0] + jnp.log(jnp.sum(jnp.exp(raw_affinity_values - row_max), -1))
    chosen = mirror_fragment_index[:, None] == field_sequence_array[None, :]
    chosen_real_entry = chosen.astype(jnp.float32)
    target = jnp.sum(jnp.where(chosen, raw_affinity_values, 0.0), -1)
    contrast_objective = (
        lax.psum(jnp.sum(fragment_weight * (log_total - target)), ("fsdp", "dp")) / fragment_tally
    )
    exponent_probabilities = jnp.exp(raw_affinity_values - log_total[:, None])
    similarity_gradient = (
        (exponent_probabilities - chosen_real_entry)
        * fragment_weight[:, None]
        / (fragment_tally * affinity_heat)
    ).astype(jnp.bfloat16)
    grad_rows = jnp.dot(similarity_gradient, every_unit, preferred_element_type=jnp.float32)
    column_terms = jnp.einsum(
        "st,sd->td", similarity_gradient, unit_low, preferred_element_type=jnp.float32
    )
    grad_cols = lax.psum_scatter(column_terms, ("fsdp", "dp"), scatter_dimension=0, tiled=True)
    grad_unit = grad_rows + grad_cols
    pooled_gradient = unit_scale * (
        grad_unit - unit_rows * jnp.sum(grad_unit * unit_rows, -1, keepdims=True)
    )
    again = (
        lax.all_gather(lowered[0], "fsdp", axis=1, tiled=True),
        lax.all_gather(lowered[1], "fsdp", axis=0, tiled=True),
        lax.all_gather(lowered[2], "fsdp", axis=0, tiled=True),
        lax.all_gather(lowered[3], "fsdp", axis=0, tiled=True),
        lax.all_gather(lowered[4], "fsdp", axis=0, tiled=True),
        lax.all_gather(lowered[5], "fsdp", axis=1, tiled=True),
    )
    grads = layer_backward(again, saved_state, kmer_identifiers, slot_fragment_ids, pooled_gradient)
    vocab = lexicon_table.shape[0]
    rest = (
        lax.psum_scatter(grads[1], "fsdp", scatter_dimension=0, tiled=True),
        lax.psum_scatter(grads[2], "fsdp", scatter_dimension=0, tiled=True),
        lax.psum_scatter(grads[3], "fsdp", scatter_dimension=0, tiled=True),
        lax.psum_scatter(grads[4], "fsdp", scatter_dimension=0, tiled=True),
        lax.psum_scatter(grads[5], "fsdp", scatter_dimension=1, tiled=True),
    )
    column_rows = lax.all_to_all(
        grads[0].astype(jnp.bfloat16), "fsdp", split_axis=1, concat_axis=0, tiled=True
    ).astype(jnp.float32)
    all_tokens = lax.all_gather(kmer_identifiers.reshape(-1), "fsdp", axis=0, tiled=True)
    table_shard = jax.ops.segment_sum(column_rows, all_tokens, num_segments=vocab)
    shards = (table_shard, rest[0], rest[1], rest[2], rest[3], rest[4])
    shards = (
        lax.psum(shards[0].astype(jnp.bfloat16), "dp").astype(jnp.float32),
        lax.psum(shards[1].astype(jnp.bfloat16), "dp").astype(jnp.float32),
        lax.psum(shards[2].astype(jnp.bfloat16), "dp").astype(jnp.float32),
        lax.psum(shards[3].astype(jnp.bfloat16), "dp").astype(jnp.float32),
        lax.psum(shards[4].astype(jnp.bfloat16), "dp").astype(jnp.float32),
        lax.psum(shards[5].astype(jnp.bfloat16), "dp").astype(jnp.float32),
    )
    squares = sum((jnp.sum(piece * piece) for piece in shards))
    grad_norm = jnp.sqrt(lax.psum(squares, "fsdp"))
    factor = clip_norm / jnp.maximum(grad_norm, clip_norm)
    count_now = optimizer_iteration.astype(jnp.float32)
    fix_first = 1.0 - jnp.power(beta_one, count_now)
    fix_second = 1.0 - jnp.power(beta_two, count_now)
    updated = [
        adam_update(
            masters[number],
            firsts[number],
            seconds[number],
            shards[number] * factor,
            fix_first,
            fix_second,
            rates[number],
            decays[number],
        )
        for number in range(6)
    ]
    return (
        contrast_objective,
        grad_norm,
        updated[0][0],
        updated[0][1],
        updated[0][2],
        updated[1][0],
        updated[1][1],
        updated[1][2],
        updated[2][0],
        updated[2][1],
        updated[2][2],
        updated[3][0],
        updated[3][1],
        updated[3][2],
        updated[4][0],
        updated[4][1],
        updated[4][2],
        updated[5][0],
        updated[5][1],
        updated[5][2],
    )


AXES = ("fsdp", "dp")
VOCAB_PAD = 4352
VOCAB_HALF = VOCAB_PAD // 2
BIG_VMEM = pltpu.CompilerParams(vmem_limit_bytes=60 * 1024 * 1024)
bf16 = jnp.bfloat16
f32 = jnp.float32


def pairs_of(moved):
    spots = [(z, y, x, c) for z in range(4) for y in range(2) for x in range(2) for c in range(2)]

    def linear(spot):
        z, y, x, c = spot
        return ((z * 2 + y) * 2 + x) * 2 + c

    return [(linear(spot), linear(moved(*spot))) for spot in spots]


FIRST = pairs_of(lambda z, y, x, c: (z, y, x ^ 1, c) if c == 0 else (z, y ^ 1, x, c))
SECOND = pairs_of(lambda z, y, x, c: (z, y ^ 1, x, c) if c == 0 else (z, y, x ^ 1, c))
BOTH = pairs_of(lambda z, y, x, c: (z, y ^ 1, x ^ 1, c))
CORE = pairs_of(lambda z, y, x, c: (z, y, x, 1 - c))
ZS = [None] + [pairs_of(lambda z, y, x, c, j=j: (z ^ j, y, x, c)) for j in (1, 2, 3)]


def send(array, pairs):
    return lax.ppermute(array, AXES, pairs)


def after(array, *others):
    return lax.optimization_barrier((array,) + others)[0]


def together(arrays, *others):
    arrays = list(arrays)
    return list(lax.optimization_barrier((*arrays, *others)))[: len(arrays)]


class Place:
    def __init__(self):
        f = lax.axis_index("fsdp")
        self.core = lax.axis_index("dp")
        self.z, self.y, self.x = f // 4, (f // 2) % 2, f % 2

    def plane_slot(self, core, a, b):
        dy = jnp.where(core == 0, b, a)
        dx = jnp.where(core == 0, a, b)
        return (self.y ^ dy) * 2 + (self.x ^ dx)

    def chip(self, core, j, a, b):
        return (self.z ^ j) * 4 + self.plane_slot(core, a, b)


def z_sends(piece):
    return [piece] + [send(piece, ZS[j]) for j in (1, 2, 3)]


def z_column(piece):
    return jnp.stack(z_sends(piece))


def plane_sends(column, direct=False, gate=()):
    one = send(column, FIRST)
    two = send(column, SECOND)
    three = send(column, BOTH) if direct else send(after(one, *gate), SECOND)
    return [column, one, two, three]


def both_cores(mine):
    return mine + [send(block, CORE) for block in mine]


def piece_index(place, rows):
    halves, starts = [], []
    for core in (place.core, 1 - place.core):
        for a, b in ((0, 0), (1, 0), (0, 1), (1, 1)):
            for j in range(4):
                halves.append(core)
                starts.append(place.chip(core, j, a, b) * rows)
    return jnp.stack(halves + starts).astype(jnp.int32)


def slot_index(place):
    chips = [
        place.chip(place.core, j, a, b) for b in (0, 1) for a in (0, 1) for j in range(4)
    ]
    return jnp.stack(chips).astype(jnp.int32)


def scatter_add(keep, came):
    return (keep[4:].astype(f32) + came[4:].astype(f32)).astype(bf16)


def scatter_here(keep, came, came_two):
    here = [
        keep[j].astype(f32) + came[j].astype(f32) + came_two[j].astype(f32) for j in range(4)
    ]
    return here[0], [h.astype(bf16) for h in here[1:]]


def line_sends(far):
    return [send(h, ZS[j]) for h, j in zip(far, (1, 2, 3))]


def line_sum(here, far):
    return (here + far[0].astype(f32) + far[1].astype(f32) + far[2].astype(f32)).astype(bf16)


def whole_copies(sources, targets, sems):
    return [
        pltpu.make_async_copy(source, target, sems.at[number])
        for number, (source, target) in enumerate(zip(sources, targets))
    ]


def staged_call(body, scalars, arrays, pieces, shapes, scratch, cost):
    n_s, n_a, n_p, n_o = len(scalars), len(arrays), len(pieces), len(shapes)

    def kernel(*refs):
        smem, refs = refs[:n_s], refs[n_s:]
        hbm, refs = refs[:n_a], refs[n_a:]
        far, refs = refs[:n_p], refs[n_p:]
        out, refs = refs[:n_o], refs[n_o:]
        near_in, refs = refs[:n_a], refs[n_a:]
        near_out, refs = refs[:n_o], refs[n_o:]
        in_sems, out_sems, refs = refs[0], refs[1], refs[2:]
        copies = whole_copies(hbm, near_in, in_sems)
        for copy in copies:
            copy.start()

        def ready():
            for copy in copies:
                copy.wait()

        body(ready, *smem, *near_in, *far, *near_out, *refs)
        copies_out = whole_copies(near_out, out, out_sems)
        for copy in copies_out:
            copy.start()
        for copy in copies_out:
            copy.wait()

    in_hbm = pl.BlockSpec(memory_space=pltpu.HBM)
    return pl.pallas_call(
        kernel,
        out_shape=shapes,
        in_specs=[pl.BlockSpec(memory_space=pltpu.SMEM)] * n_s + [in_hbm] * (n_a + n_p),
        out_specs=[in_hbm] * n_o,
        scratch_shapes=[pltpu.VMEM(a.shape, a.dtype) for a in arrays]
        + [pltpu.VMEM(s.shape, s.dtype) for s in shapes]
        + [pltpu.SemaphoreType.DMA((n_a,)), pltpu.SemaphoreType.DMA((n_o,))]
        + scratch,
        cost_estimate=pl.CostEstimate(flops=int(cost * 1e9), bytes_accessed=0, transcendentals=0),
        compiler_params=BIG_VMEM,
    )(*scalars, *arrays, *pieces)


def shaped(dtype, *dims):
    return jax.ShapeDtypeStruct(dims, dtype)


def one_hot(ids_row, start, count):
    spots = lax.broadcasted_iota(jnp.int32, (count, ids_row.shape[1]), 0) + start
    return jnp.where(spots == ids_row, 1.0, 0.0).astype(bf16)


def lookup_kernel(ready, idx_ref, ids_ref, *refs):
    ins = list(refs[:4]) + [refs[4].at[k] for k in range(3)]
    outs, table, sems = refs[5:9], refs[9], refs[10]
    copies = [
        pltpu.make_async_copy(
            ins[0], table.at[pl.ds(pl.multiple_of(idx_ref[0], 16), 48), :], sems.at[0]
        )
    ]
    for number in range(1, 7):
        column = pl.multiple_of(idx_ref[7 + (number - 1) // 3], 128)
        row = pl.multiple_of(idx_ref[number], 16)
        copies.append(
            pltpu.make_async_copy(
                ins[number],
                table.at[pl.ds(row, 48), pl.ds(column, VOCAB_HALF)],
                sems.at[number],
            )
        )
    for copy in copies:
        copy.start()
    ready()
    for copy in copies:
        copy.wait()
    for j in range(4):
        total = jnp.zeros((192, 512), f32)
        for k in range(VOCAB_PAD // 256):
            total += jnp.dot(
                table[:, k * 256 : (k + 1) * 256],
                one_hot(ids_ref[j], k * 256, 256),
                preferred_element_type=f32,
            )
        outs[j][...] = total.astype(bf16)


def lookup(index, ids_z, arrays):
    return staged_call(
        lookup_kernel,
        [index],
        [ids_z],
        arrays,
        [
            shaped(bf16, 192, 512),
            shaped(bf16, 192, 512),
            shaped(bf16, 192, 512),
            shaped(bf16, 192, 512),
        ],
        [
            pltpu.VMEM((192, VOCAB_PAD), bf16),
            pltpu.SemaphoreType.DMA((7,)),
        ],
        6,
    )


def token_sum_kernel(ready, idx_ref, ids_ref, other_ids_ref, mine_ref, other_ref, keep_ref, away_ref, whole_ref
):
    ready()
    start = idx_ref[0]
    for low in range(0, VOCAB_HALF, 256):
        count = min(256, VOCAB_HALF - low)
        total = jnp.zeros((192, count), f32)
        for ids, block in ((ids_ref, mine_ref), (other_ids_ref, other_ref)):
            for j in range(4):
                total += lax.dot_general(
                    block[j],
                    one_hot(ids[j], start + low, count),
                    (((1,), (1,)), ((), ())),
                    preferred_element_type=f32,
                )
        whole_ref[:, low : low + count] = total.astype(bf16)
    for k in range(2):
        keep_ref[k] = whole_ref[pl.ds(pl.multiple_of(idx_ref[1 + k], 16), 48), :]
        away_ref[k] = whole_ref[pl.ds(pl.multiple_of(idx_ref[3 + k], 16), 48), :]


def token_sum(index, ids_z, other_ids, mine, other):
    return staged_call(
        token_sum_kernel,
        [index],
        [ids_z, other_ids, mine, other],
        [],
        [
            shaped(bf16, 2, 48, VOCAB_HALF),
            shaped(bf16, 2, 48, VOCAB_HALF),
        ],
        [
            pltpu.VMEM((192, VOCAB_HALF), bf16),
        ],
        8,
    )


def my_half(array, core, width):
    return lax.dynamic_slice_in_dim(array, core * width, width, axis=1)


def all_sum(value):
    one, two, three = (send(value, p) for p in ZS[1:])
    value = (value + one) + (two + three)
    value = value + send(value, FIRST)
    return value + send(value, SECOND)


WINDOWS = (0, 64, 192, 256)
SCALE = HD ** (-0.5)


def piece_copies(idx_ref, base, pieces, target, rows, sems, first_sem, cut=None):
    copies = []
    for number in range(32):
        half = idx_ref[base + number]
        row = pl.multiple_of(idx_ref[base + 32 + number], 16)
        source = pieces[number // 4].at[number % 4]
        if cut is not None:
            source = source.at[:, cut]
        copies.append(
            pltpu.make_async_copy(
                source, target.at[half, pl.ds(row, rows), :], sems.at[first_sem + number]
            )
        )
    return copies


def window_bias(seg_row, seg_col, b):
    w = WINDOWS[b]
    same = seg_col[b * 128 : (b + 1) * 128, :] == seg_row[:, w : w + 256]
    bias = jnp.where(same, 0.0, -1e30)
    return jnp.concatenate([bias, bias], 0)


def two_heads(block):
    left = lax.broadcasted_iota(jnp.int32, block.shape, 1) < HD
    none = jnp.zeros_like(block)
    return jnp.concatenate([jnp.where(left, block, none), jnp.where(left, none, block)], 0)


def nt_dot(a, b):
    return lax.dot_general(a, b, (((1,), (1,)), ((), ())), preferred_element_type=f32)


def tn_dot(a, b):
    return lax.dot_general(a, b, (((0,), (0,)), ((), ())), preferred_element_type=f32)


def nn_dot(a, b):
    return jnp.dot(a, b, preferred_element_type=f32)


def row_norm(v):
    center = v - jnp.mean(v, -1, keepdims=True)
    inv = lax.rsqrt(jnp.mean(center * center, -1, keepdims=True) + norm_eps)
    return center * inv, inv


def attention_kernel(ready, idx_ref, seg_row_ref, seg_col_ref, *refs):
    e_in, pieces = refs[:4], refs[4:12]
    (e_ref, qkv_ref, lse_ref, mixed_ref, unit_ref, inv_ref, low_ref, par_ref, side_ref) = refs[12:21]
    et_ref, w_ref, bias_ref, attended_ref, sems = refs[21:]
    e_copies = [
        pltpu.make_async_copy(
            e_in[j],
            et_ref.at[pl.ds(pl.multiple_of(idx_ref[j], 16), 192), :],
            sems.at[j],
        )
        for j in range(4)
    ]
    w_copies = piece_copies(idx_ref, 4, pieces, w_ref, 48, sems, 4)
    for copy in e_copies + w_copies:
        copy.start()
    ready()
    for b in range(4):
        bias_ref[b] = window_bias(seg_row_ref[...], seg_col_ref[...], b)
    for copy in e_copies:
        copy.wait()
    e_ref[...] = et_ref[...].T
    for copy in w_copies:
        copy.wait()
    par_ref[...] = w_ref[0, :, 1536:1664].T.astype(f32)[:8]
    side_ref[...] = w_ref[:, :, 1536:1664]
    for k in range(2):
        for t in range(3):
            part = nn_dot(e_ref[...], w_ref[k, :, t * 384 : (t + 1) * 384])
            if t == 0:
                part = part.astype(bf16).astype(f32) * SCALE
            part = part.astype(bf16)
            for i in range(3):
                qkv_ref[t * 6 + k * 3 + i] = part[:, i * 128 : (i + 1) * 128]
    lse_ref[...] = jnp.zeros_like(lse_ref)
    lane = lax.broadcasted_iota(jnp.int32, (128, 128), 1)
    left = lane < HD

    @pl.loop(0, 6)
    def _(pair):
        for b in range(4):
            rows = pl.ds(b * 128, 128)
            keys = pl.ds(WINDOWS[b], 256)
            q = qkv_ref[pair, rows, :]
            k = qkv_ref[pair + 6, keys, :]
            v = qkv_ref[pair + 12, keys, :]
            s = nt_dot(two_heads(q), k) + bias_ref[b]
            top = jnp.max(s, -1, keepdims=True)
            e = jnp.exp(s - top)
            total = jnp.sum(e, -1, keepdims=True)
            log = top + jnp.log(total)
            lse = jnp.where(lane == pair * 2, log[:128], lse_ref[rows, :])
            lse_ref[rows, :] = jnp.where(lane == pair * 2 + 1, log[128:], lse)
            mixed = nn_dot((e * (1.0 / total)).astype(bf16), v)
            cols = pl.ds(pl.multiple_of(pair * 128, 128), 128)
            mixed_ref[rows, cols] = jnp.where(left, mixed[:128], mixed[128:]).astype(bf16)

    for k in range(2):
        attended_ref[:, k * 384 : (k + 1) * 384] = nn_dot(mixed_ref[...], w_ref[k, :, 1152:1536])
    for b in range(4):
        rows = slice(b * 128, (b + 1) * 128)
        unit, inv = row_norm(e_ref[rows, :].astype(f32) + attended_ref[rows, :])
        unit_ref[rows, :] = unit
        inv_ref[rows, :] = jnp.broadcast_to(inv, (128, 128))
        low_ref[rows, :] = (unit * par_ref[0:1, :] + par_ref[1:2, :]).astype(bf16)


def attention_forward(index, seg_row, seg_col, columns, pieces):
    return staged_call(
        attention_kernel,
        [index],
        [seg_row, seg_col],
        [*columns, *pieces],
        [
            shaped(bf16, 512, 768),
            shaped(bf16, 18, 512, 128),
            shaped(f32, 512, 128),
            shaped(bf16, 512, 768),
            shaped(f32, 512, 768),
            shaped(f32, 512, 128),
            shaped(bf16, 512, 768),
            shaped(f32, 8, 768),
            shaped(bf16, 2, 768, 128),
        ],
        [
            pltpu.VMEM((768, 512), bf16),
            pltpu.VMEM((2, 768, 1664), bf16),
            pltpu.VMEM((4, 256, 256), f32),
            pltpu.VMEM((512, 768), f32),
            pltpu.SemaphoreType.DMA((36,)),
        ],
        17,
    )


def gelu_and_slope(u):
    square = 0.5 * u * u
    t = 1.0 / (1.0 + (0.5 * 0.5**0.5) * jnp.abs(u))
    poly = 0.17087277
    for factor in (
        -0.82215223,
        1.48851587,
        -1.13520398,
        0.27886807,
        -0.18628806,
        0.09678418,
        0.37409196,
        1.00002368,
        -1.26551223,
    ):
        poly = factor + t * poly
    tail = (0.5 * t) * jnp.exp(poly - square)
    phi = jnp.where(u < 0, tail, 1.0 - tail)
    return u * phi, phi + (u * 0.3989422804014327) * jnp.exp(-square)


def up_kernel(ready, idx_ref, low_ref, *refs):
    pieces, act_ref, slope_ref, w_ref, sems = refs[:8], refs[8], refs[9], refs[10], refs[11]
    copies = piece_copies(idx_ref, 0, pieces, w_ref, 48, sems, 0)
    for copy in copies:
        copy.start()
    ready()
    for copy in copies:
        copy.wait()
    for k in range(2):

        @pl.loop(0, 6)
        def _(n):
            cols = pl.ds(pl.multiple_of(n * 256, 256), 256)
            u = nn_dot(low_ref[...], w_ref[k, :, cols])
            value, slope = gelu_and_slope(u)
            out_cols = pl.ds(pl.multiple_of(k * 1536 + n * 256, 256), 256)
            act_ref[:, out_cols] = value.astype(bf16)
            slope_ref[:, out_cols] = slope.astype(bf16)


def up_forward(index, low, pieces):
    return staged_call(
        up_kernel,
        [index],
        [low],
        pieces,
        [
            shaped(bf16, 512, 3072),
            shaped(bf16, 512, 3072),
        ],
        [
            pltpu.VMEM((2, 768, 1536), bf16),
            pltpu.SemaphoreType.DMA((32,)),
        ],
        18,
    )


def thirds(v):
    high = v.astype(bf16)
    rest = v - high.astype(f32)
    middle = rest.astype(bf16)
    return high, middle, (rest - middle.astype(f32)).astype(bf16)


def half_copies(core, own, other, target, sems):
    return [
        pltpu.make_async_copy(own, target.at[core], sems.at[0]),
        pltpu.make_async_copy(other, target.at[1 - core], sems.at[1]),
    ]


def down_kernel(ready, idx_ref, seg_row_ref, act_ref, unit_one_ref, par_ref, *refs):
    unit_ref, inv_ref, frag_ref, frag_low_ref, size_ref, w_ref, result_ref, sems = refs[2:]
    copies = half_copies(idx_ref[0], refs[0], refs[1], w_ref, sems)
    for copy in copies:
        copy.start()
    ready()
    for copy in copies:
        copy.wait()
    for k in range(2):
        result_ref[:, k * 384 : (k + 1) * 384] = nn_dot(act_ref[...], w_ref[k])
    pooled = jnp.zeros((32, 768), f32)
    for b in range(4):
        rows = slice(b * 128, (b + 1) * 128)
        one = unit_one_ref[rows, :] * par_ref[0:1, :] + par_ref[1:2, :]
        unit, inv = row_norm(one + result_ref[rows, :])
        unit_ref[rows, :] = unit
        inv_ref[rows, :] = jnp.broadcast_to(inv, (128, 128))
        two = unit * par_ref[2:3, :] + par_ref[3:4, :]
        member = lax.broadcasted_iota(jnp.int32, (32, 128), 0) == seg_row_ref[:, rows]
        member = jnp.where(member, 1.0, 0.0).astype(bf16)
        for part in thirds(two):
            pooled += nn_dot(member, part)
    size = lax.rsqrt(jnp.sum(pooled * pooled, -1, keepdims=True) + unit_eps)
    frag = pooled * size
    frag_ref[...] = frag
    frag_low_ref[...] = frag.astype(bf16)
    size_ref[...] = jnp.broadcast_to(size, (32, 128))


def down_forward(index, seg_row, act, unit_one, params, pieces):
    return staged_call(
        down_kernel,
        [index],
        [seg_row, act, unit_one, params],
        pieces,
        [
            shaped(f32, 512, 768),
            shaped(f32, 512, 128),
            shaped(f32, 32, 768),
            shaped(bf16, 32, 768),
            shaped(f32, 32, 128),
        ],
        [
            pltpu.VMEM((2, 3072, 384), bf16),
            pltpu.VMEM((512, 768), f32),
            pltpu.SemaphoreType.DMA((2,)),
        ],
        10,
    )


def back_norm(upstream, unit, inv, gain):
    scaled = upstream * gain
    return inv * (
        scaled
        - jnp.mean(scaled, -1, keepdims=True)
        - unit * jnp.mean(scaled * unit, -1, keepdims=True)
    )


def loss_kernel(
    ready, idx_ref, heat_ref, seg_col_ref, partner_ref, own_weight_ref, partner_row_ref, side_ref,
    frag_ref, size_ref, unit_ref, inv_ref, par_ref, slope_ref, *refs
):
    blocks, down_pieces = refs[:8], refs[8:10]
    loss_ref, low_own_ref, low_other_ref, gup_own_ref, gup_other_ref, two_ref, gains_ref = refs[10:17]
    all_ref, down_ref, low_ref, spread_ref, sems, w_sems = refs[17:]
    copies = []
    for number in range(32):
        row = pl.multiple_of(idx_ref[1 + number], 16)
        copies.append(
            pltpu.make_async_copy(
                blocks[number // 4].at[number % 4], all_ref.at[pl.ds(row, 32), :], sems.at[number]
            )
        )
    core = idx_ref[33]
    down_copies = half_copies(core, down_pieces[0], down_pieces[1], down_ref, w_sems)
    for copy in copies + down_copies:
        copy.start()
    ready()
    for copy in copies:
        copy.wait()
    base = idx_ref[0]
    inv_heat = 1.0 / heat_ref[0]
    tally = 1024
    mine = all_ref[pl.ds(pl.multiple_of(base, 16), 32), :]
    grid = (nt_dot(mine, all_ref[...]) - 1.0) * inv_heat
    across = lax.broadcasted_iota(jnp.int32, (32, tally), 1)
    down = lax.broadcasted_iota(jnp.int32, (32, tally), 0) + base
    powers = jnp.where(across == down, 0.0, jnp.exp(grid))
    total = jnp.sum(powers, -1, keepdims=True)
    chosen = across == partner_ref[...]
    target = jnp.sum(jnp.where(chosen, grid, 0.0), -1, keepdims=True)
    terms = own_weight_ref[...] * (jnp.log(total) - target)
    loss_ref[...] = jnp.broadcast_to(jnp.sum(terms, 0, keepdims=True) / tally, (8, 128))
    pull = powers / total - jnp.where(chosen, 1.0, 0.0)
    pull = (pull * (own_weight_ref[...] * (inv_heat / tally))).astype(bf16)
    grad = nn_dot(pull, all_ref[...])
    for big in range(2):
        many = all_ref[big * 512 : (big + 1) * 512, :]
        spread_ref[...] = nt_dot(many, all_ref[...])
        close = nt_dot(many, mine)
        parts = []
        for b in range(big * 4, big * 4 + 4):
            inside = slice((b - big * 4) * 128, (b - big * 4 + 1) * 128)
            spread = jnp.exp((spread_ref[inside, :] - 1.0) * inv_heat)
            number = lax.broadcasted_iota(jnp.int32, (128, 128), 0)
            same = number == lax.broadcasted_iota(jnp.int32, (128, 128), 1)
            spread_total = sum(
                jnp.where(same, 0.0, spread[:, n * 128 : (n + 1) * 128])
                if n == b
                else spread[:, n * 128 : (n + 1) * 128]
                for n in range(8)
            )
            spread_total = jnp.sum(spread_total, -1, keepdims=True)
            part = jnp.exp((close[inside, :] - 1.0) * inv_heat)
            here = lax.broadcasted_iota(jnp.int32, (128, 32), 0) + b * 128
            column = lax.broadcasted_iota(jnp.int32, (128, 32), 1) + base
            part = jnp.where(here == column, 0.0, part) / spread_total
            part = part - jnp.where(here == partner_row_ref[...], 1.0, 0.0)
            side = jnp.concatenate(
                [
                    side_ref[n % 2, (n // 2) * 48 : (n // 2) * 48 + 32, :].astype(f32)
                    for n in range(b * 4, b * 4 + 4)
                ],
                0,
            )
            lanes = lax.broadcasted_iota(jnp.int32, (128, 128), 1)
            wanted = jnp.logical_and(lanes >= 4, lanes < 7)
            weight = jnp.sum(jnp.where(wanted, side, 0.0), -1, keepdims=True)
            parts.append((part * (weight * (inv_heat / tally))).astype(bf16))
        grad += tn_dot(jnp.concatenate(parts, 0), many)
    frag = frag_ref[...]
    pooled = size_ref[:, 0:1] * (grad - frag * jnp.sum(grad * frag, -1, keepdims=True))
    stacked = jnp.concatenate(thirds(pooled), 0)
    gain_two = jnp.zeros((1, 768), f32)
    shift_two = jnp.zeros((1, 768), f32)
    for b in range(4):
        rows = slice(b * 128, (b + 1) * 128)
        slot = lax.broadcasted_iota(jnp.int32, (128, 96), 1) % 32
        member = jnp.where(slot == seg_col_ref[rows, :], 1.0, 0.0).astype(bf16)
        upstream = nn_dot(member, stacked)
        unit = unit_ref[rows, :]
        back = back_norm(upstream, unit, inv_ref[rows, 0:1], par_ref[2:3, :])
        two_ref[rows, :] = back
        low_ref[rows, :] = back.astype(bf16)
        gain_two += jnp.sum(upstream * unit, 0, keepdims=True)
        shift_two += jnp.sum(upstream, 0, keepdims=True)
    halves = (core, 1 - core)
    for half, ref in zip(halves, (low_own_ref, low_other_ref)):
        ref[...] = low_ref[:, pl.ds(pl.multiple_of(half * 384, 128), 384)]
    for copy in down_copies:
        copy.wait()
    for half, gup_ref in zip(halves, (gup_own_ref, gup_other_ref)):

        @pl.loop(0, 6)
        def _(n):
            cols = pl.ds(pl.multiple_of(n * 256, 256), 256)
            wide = pl.ds(pl.multiple_of(half * 1536 + n * 256, 256), 256)
            g = sum(
                nt_dot(low_ref[:, k * 384 : (k + 1) * 384], down_ref[k, wide, :])
                for k in range(2)
            )
            gup_ref[:, cols] = (g * slope_ref[:, wide].astype(f32)).astype(bf16)

    gains_ref[...] = jnp.concatenate([gain_two, shift_two, jnp.zeros((6, 768), f32)], 0)


def loss_backward(index, heat, arrays, pieces):
    return staged_call(
        loss_kernel,
        [index, heat],
        arrays,
        pieces,
        [
            shaped(f32, 8, 128),
            shaped(bf16, 512, 384),
            shaped(bf16, 512, 384),
            shaped(bf16, 512, 1536),
            shaped(bf16, 512, 1536),
            shaped(f32, 512, 768),
            shaped(f32, 8, 768),
        ],
        [
            pltpu.VMEM((1024, 768), bf16),
            pltpu.VMEM((2, 3072, 384), bf16),
            pltpu.VMEM((512, 768), bf16),
            pltpu.VMEM((512, 1024), f32),
            pltpu.SemaphoreType.DMA((32,)),
            pltpu.SemaphoreType.DMA((2,)),
        ],
        18,
    )


def ffn_back_kernel(
    ready, idx_ref, gup_own_ref, gup_other_ref, two_ref, unit_ref, inv_ref, par_ref, *refs
):
    pieces = refs[:8]
    resid_ref, att_ref, own_ref, other_ref, gains_ref, up_ref, sems = refs[8:]
    copies = piece_copies(idx_ref, 0, pieces, up_ref, 48, sems, 0)
    for copy in copies:
        copy.start()
    ready()
    for copy in copies:
        copy.wait()
    core = idx_ref[0]
    for n in range(3):
        cols = slice(n * 256, (n + 1) * 256)
        resid_ref[:, cols] = (
            two_ref[:, cols]
            + nt_dot(gup_own_ref[...], up_ref[core, cols, :])
            + nt_dot(gup_other_ref[...], up_ref[1 - core, cols, :])
        )
    gain_sum = jnp.zeros((1, 768), f32)
    shift_sum = jnp.zeros((1, 768), f32)
    for b in range(4):
        rows = slice(b * 128, (b + 1) * 128)
        one = resid_ref[rows, :]
        unit = unit_ref[rows, :]
        back = back_norm(one, unit, inv_ref[rows, 0:1], par_ref[0:1, :])
        resid_ref[rows, :] = back
        att_ref[rows, :] = back.astype(bf16)
        gain_sum += jnp.sum(one * unit, 0, keepdims=True)
        shift_sum += jnp.sum(one, 0, keepdims=True)
    for half, ref in ((core, own_ref), (1 - core, other_ref)):
        ref[...] = att_ref[:, pl.ds(pl.multiple_of(half * 384, 128), 384)]
    gains_ref[...] = jnp.concatenate([gain_sum, shift_sum, jnp.zeros((6, 768), f32)], 0)


def ffn_backward(index, arrays, pieces):
    return staged_call(
        ffn_back_kernel,
        [index],
        arrays,
        pieces,
        [
            shaped(f32, 512, 768),
            shaped(bf16, 512, 768),
            shaped(bf16, 512, 384),
            shaped(bf16, 512, 384),
            shaped(f32, 8, 768),
        ],
        [pltpu.VMEM((2, 768, 1536), bf16), pltpu.SemaphoreType.DMA((32,))],
        9,
    )


def heads_back(half, gm_ref, qkv_ref, lse_ref, bias_ref, gqkv_ref, gk_ref, gv_ref):
    lane = lax.broadcasted_iota(jnp.int32, (128, 128), 1)
    left = lane < HD
    gk_ref[...] = jnp.zeros_like(gk_ref)
    gv_ref[...] = jnp.zeros_like(gv_ref)

    @pl.loop(0, 3)
    def _(spot):
        pair = half * 3 + spot
        for b in range(4):
            rows = pl.ds(b * 128, 128)
            keys = pl.ds(WINDOWS[b], 256)
            q = qkv_ref[pair, rows, :]
            k = qkv_ref[pair + 6, keys, :]
            v = qkv_ref[pair + 12, keys, :]
            gm = gm_ref[rows, pl.ds(pl.multiple_of(spot * 128, 128), 128)]
            q, gm = two_heads(q), two_heads(gm)
            stats = lse_ref[rows, :]
            lse = jnp.concatenate(
                [
                    jnp.sum(jnp.where(lane == pair * 2 + h, stats, 0.0), -1, keepdims=True)
                    for h in range(2)
                ],
                0,
            )
            p = jnp.exp(nt_dot(q, k) + bias_ref[b] - lse)
            gp = nt_dot(gm, v)
            gs = (p * (gp - jnp.sum(gp * p, -1, keepdims=True))).astype(bf16)
            gq = nn_dot(gs, k)
            gq = (jnp.where(left, gq[:128], gq[128:]) * SCALE).astype(bf16)
            gqkv_ref[rows, pl.ds(pl.multiple_of(spot * 128, 128), 128)] = gq
            gk_ref[spot, keys, :] += tn_dot(gs, q)
            gv_ref[spot, keys, :] += tn_dot(p.astype(bf16), gm)
        for third, ref in ((1, gk_ref), (2, gv_ref)):
            cols = pl.ds(pl.multiple_of(third * 384 + spot * 128, 128), 128)
            gqkv_ref[:, cols] = ref[spot].astype(bf16)


def other_heads_kernel(ready, idx_ref, seg_row_ref, seg_col_ref, qkv_ref, lse_ref, att_ref, resid_ref, *refs
):
    pieces = refs[:8]
    gqkv_ref, gm_own_ref, part_ref = refs[8:11]
    w_ref, bias_ref, gm_ref, gk_ref, gv_ref, sems = refs[11:]
    copies = piece_copies(idx_ref, 4, pieces, w_ref, 48, sems, 0)
    for copy in copies:
        copy.start()
    ready()
    for b in range(4):
        bias_ref[b] = window_bias(seg_row_ref[...], seg_col_ref[...], b)
    for copy in copies:
        copy.wait()
    core = idx_ref[4]
    half = 1 - core
    for side, ref in ((half, gm_ref), (core, gm_own_ref)):
        rows = pl.ds(pl.multiple_of(side * 384, 128), 384)
        ref[...] = sum(
            nt_dot(att_ref[:, k * 384 : (k + 1) * 384], w_ref[k, rows, 1152:1536])
            for k in range(2)
        ).astype(bf16)
    heads_back(half, gm_ref, qkv_ref, lse_ref, bias_ref, gqkv_ref, gk_ref, gv_ref)
    for n in range(3):
        cols = slice(n * 256, (n + 1) * 256)
        part_ref[:, cols] = resid_ref[:, cols] + nt_dot(gqkv_ref[...], w_ref[half, cols, :1152])


def other_heads(index, arrays, pieces):
    return staged_call(
        other_heads_kernel,
        [index],
        arrays,
        pieces,
        [
            shaped(bf16, 512, 1152),
            shaped(bf16, 512, 384),
            shaped(f32, 512, 768),
        ],
        [
            pltpu.VMEM((2, 768, 1664), bf16),
            pltpu.VMEM((4, 256, 256), f32),
            pltpu.VMEM((512, 384), bf16),
            pltpu.VMEM((3, 512, 128), f32),
            pltpu.VMEM((3, 512, 128), f32),
            pltpu.SemaphoreType.DMA((32,)),
        ],
        17,
    )


def own_heads_kernel(ready, idx_ref, seg_row_ref, seg_col_ref, qkv_ref, lse_ref, gm_ref, part_ref, *refs
):
    pieces = refs[:4]
    gqkv_ref, outs = refs[4], refs[5:9]
    w_ref, bias_ref, gk_ref, gv_ref, et_ref, sems = refs[9:]
    copies = []
    for number in range(16):
        row = pl.multiple_of(idx_ref[36 + number], 16)
        copies.append(
            pltpu.make_async_copy(
                pieces[number // 4].at[number % 4], w_ref.at[pl.ds(row, 48), :], sems.at[number]
            )
        )
    for copy in copies:
        copy.start()
    ready()
    for b in range(4):
        bias_ref[b] = window_bias(seg_row_ref[...], seg_col_ref[...], b)
    core = idx_ref[4]
    heads_back(core, gm_ref, qkv_ref, lse_ref, bias_ref, gqkv_ref, gk_ref, gv_ref)
    for copy in copies:
        copy.wait()
    for n in range(3):
        cols = slice(n * 256, (n + 1) * 256)
        total = part_ref[:, cols] + nt_dot(gqkv_ref[...], w_ref[cols, :1152])
        et_ref[cols, :] = total.astype(bf16).T
    for j in range(4):
        outs[j][...] = et_ref[pl.ds(pl.multiple_of(idx_ref[j], 16), 192), :]


def own_heads(index, arrays, pieces):
    return staged_call(
        own_heads_kernel,
        [index],
        arrays,
        pieces,
        [
            shaped(bf16, 512, 1152),
            shaped(bf16, 192, 512),
            shaped(bf16, 192, 512),
            shaped(bf16, 192, 512),
            shaped(bf16, 192, 512),
        ],
        [
            pltpu.VMEM((768, 1664), bf16),
            pltpu.VMEM((4, 256, 256), f32),
            pltpu.VMEM((3, 512, 128), f32),
            pltpu.VMEM((3, 512, 128), f32),
            pltpu.VMEM((768, 512), bf16),
            pltpu.SemaphoreType.DMA((16,)),
        ],
        15,
    )


def to_slots(idx_ref, whole_ref, keep_ref, away_ref):
    for slot in range(8):
        keep_ref[slot] = whole_ref[idx_ref[slot]]
        away_ref[slot] = whole_ref[idx_ref[8 + slot]]


def down_grad_kernel(ready, idx_ref, act_ref, act_o_ref, g_ref, g_o_ref, keep_ref, away_ref, whole_ref):
    ready()
    for n in range(8):
        cols = slice(n * 384, (n + 1) * 384)
        total = tn_dot(act_ref[:, cols], g_ref[...]) + tn_dot(act_o_ref[:, cols], g_o_ref[...])
        total = total.astype(bf16)
        whole_ref[2 * n] = total[:192]
        whole_ref[2 * n + 1] = total[192:]
    to_slots(idx_ref, whole_ref, keep_ref, away_ref)


def down_grad(index, arrays):
    return staged_call(
        down_grad_kernel,
        [index],
        arrays,
        [],
        [shaped(bf16, 8, 192, 384)] * 2,
        [pltpu.VMEM((16, 192, 384), bf16)],
        7,
    )


def store_chunks(whole_ref, cols, total):
    for f in range(16):
        whole_ref[f, :, cols] = total[f * 48 : (f + 1) * 48]


def up_out_grad_kernel(
    ready, idx_ref, low_ref, low_o_ref, g_ref, g_o_ref, mixed_ref, mixed_o_ref, ga_ref, ga_o_ref, norms_ref,
    keep_ref, away_ref, whole_ref, t_ref,
):
    ready()
    t_ref[0] = low_ref[...].T
    t_ref[1] = low_o_ref[...].T
    for n in range(3):
        cols = slice(n * 512, (n + 1) * 512)
        total = nn_dot(t_ref[0], g_ref[:, cols]) + nn_dot(t_ref[1], g_o_ref[:, cols])
        store_chunks(whole_ref, cols, total.astype(bf16))
    t_ref[0] = mixed_ref[...].T
    t_ref[1] = mixed_o_ref[...].T
    total = nn_dot(t_ref[0], ga_ref[...]) + nn_dot(t_ref[1], ga_o_ref[...])
    store_chunks(whole_ref, slice(1536, 1920), total.astype(bf16))
    norms = norms_ref[...].T.astype(bf16)
    norms = jnp.concatenate([norms, jnp.zeros((768, 120), bf16)], 1)
    store_chunks(whole_ref, slice(1920, 2048), norms)
    to_slots(idx_ref, whole_ref, keep_ref, away_ref)


def up_out_grad(index, arrays):
    return staged_call(
        up_out_grad_kernel,
        [index],
        arrays,
        [],
        [
            shaped(bf16, 8, 48, 2048),
            shaped(bf16, 8, 48, 2048),
        ],
        [
            pltpu.VMEM((16, 48, 2048), bf16),
            pltpu.VMEM((2, 768, 512), bf16),
        ],
        8,
    )


def in_grad_kernel(ready, idx_ref, e_ref, e_o_ref, g_ref, g_o_ref, keep_ref, away_ref, whole_ref, t_ref):
    ready()
    t_ref[0] = e_ref[...].T
    t_ref[1] = e_o_ref[...].T
    for t in range(3):
        cols = slice(t * 384, (t + 1) * 384)
        total = nn_dot(t_ref[0], g_ref[:, cols]) + nn_dot(t_ref[1], g_o_ref[:, cols])
        store_chunks(whole_ref, cols, total.astype(bf16))
    to_slots(idx_ref, whole_ref, keep_ref, away_ref)


def in_grad(index, arrays):
    return staged_call(
        in_grad_kernel,
        [index],
        arrays,
        [],
        [
            shaped(bf16, 8, 48, 1152),
            shaped(bf16, 8, 48, 1152),
        ],
        [
            pltpu.VMEM((16, 48, 1152), bf16),
            pltpu.VMEM((2, 768, 512), bf16),
        ],
        6,
    )


def optimizer_kernel(ready, core_ref, fix_ref, totals_ref, totals_o_ref, *refs):
    ready()
    own, other = refs[:4], refs[4:8]
    params, outs = refs[8:26], refs[26:46]
    table_ref = refs[46]
    core = core_ref[0]
    totals = totals_ref[...] + totals_o_ref[...]
    norm = jnp.sqrt(totals[:, 0:1])
    outs[0][...] = totals[:, 1:2]
    outs[1][...] = norm
    factor = clip_norm / jnp.maximum(norm, clip_norm)
    fix_one, fix_two = 1.0 / fix_ref[0], 1.0 / fix_ref[1]

    def update(number, spot, grad, rate, decay):
        w_ref, first_ref, second_ref = params[3 * number : 3 * number + 3]
        grad = grad.astype(f32) * factor
        weight = w_ref[spot]
        first = beta_one * first_ref[spot] + (1.0 - beta_one) * grad
        second = beta_two * second_ref[spot] + (1.0 - beta_two) * grad * grad
        step = (first * fix_one) / (jnp.sqrt(second * fix_two) + adam_eps)
        outs[2 + 3 * number][spot] = weight - rate * (step + decay * weight)
        outs[3 + 3 * number][spot] = first
        outs[4 + 3 * number][spot] = second

    every = slice(None)
    for side, (table, into, up_out, down) in enumerate((own, other)):
        half = core if side == 0 else 1 - core

        def columns(width, start=0):
            return pl.ds(pl.multiple_of(half * width + start, 128), width)

        table_ref[:, columns(VOCAB_HALF)] = table[...]
        for t in range(3):
            update(
                1,
                (every, columns(384, t * 768)),
                into[:, t * 384 : (t + 1) * 384],
                rate_matrix,
                decay_rate,
            )
        update(2, (every, columns(384)), up_out[:, 1536:1920], rate_matrix, decay_rate)
        for t in range(3):
            spot = pl.ds(pl.multiple_of(half * 1536 + t * 512, 128), 512)
            update(3, (every, spot), up_out[:, t * 512 : (t + 1) * 512], rate_matrix, decay_rate)
        for t in range(4):
            rows = slice(t * 48, (t + 1) * 48)
            update(4, (rows, columns(384)), down[rows, :], rate_matrix, decay_rate)
    vocab = params[0].shape[1]
    for low in range(0, vocab, 512):
        spot = slice(low, min(vocab, low + 512))
        update(0, (every, spot), table_ref[:, spot], rate_embed, decay_rate)
    norms = jnp.where(core == 0, own[2][:, 1920:].astype(f32), other[2][:, 1920:].astype(f32))
    update(5, (every, every), norms.T[:4], rate_norm, 0.0)


def optimizer(core, fixes, totals, totals_o, own, other, params):
    return staged_call(
        optimizer_kernel,
        [core, fixes],
        [totals, totals_o, *own, *other, *params],
        [],
        [
            shaped(f32, 1, 1),
            shaped(f32, 1, 1),
            *[shaped(f32, *p.shape) for p in params],
        ],
        [
            pltpu.VMEM((48, VOCAB_PAD), bf16),
        ],
        8,
    )


def per_device_links(
    kmer_identifiers,
    slot_fragment_ids,
    mirror_fragment_index,
    fragment_weight,
    affinity_heat,
    optimizer_iteration,
    lexicon_table,
    lexicon_first_moment,
    lexicon_raw_moment,
    query_key_value_maps,
    qkv_first_moment,
    qkv_raw_moment,
    attention_exit_map,
    exit_first_moment,
    exit_raw_moment,
    widening_matrix_in,
    widening_first_moment,
    widening_raw_moment,
    narrowing_matrix_out,
    narrowing_first_moment,
    narrowing_raw_moment,
    layernorm_scale_bias,
    layernorm_first_moment,
    layernorm_raw_moment,
):
    place = Place()
    core = place.core
    vocab = lexicon_table.shape[0]
    table_cut = jnp.pad(lexicon_table.T.astype(bf16), ((0, 0), (0, VOCAB_PAD - vocab)))
    table_half = my_half(table_cut, core, VOCAB_HALF)
    near = [send(table_half, FIRST), send(table_half, SECOND)]
    near.append(send(near[0], SECOND))
    ids_z = jnp.stack(
        [kmer_identifiers] + [send(kmer_identifiers, ZS[j]) for j in (1, 2, 3)]
    )
    others = send(after(jnp.stack(near), ids_z), CORE)
    norm_cut = layernorm_scale_bias.T.astype(bf16)
    heavy = jnp.stack(thirds(fragment_weight), 1)
    extra = jnp.concatenate(
        [
            norm_cut,
            jnp.pad(heavy, ((0, 16), (0, 0))),
            jnp.zeros((48, 121), bf16),
        ],
        1,
    )
    low_in = query_key_value_maps.astype(bf16)
    low_out = attention_exit_map.astype(bf16)
    low_up = widening_matrix_in.astype(bf16)
    low_down = narrowing_matrix_out.astype(bf16)
    in_out_cut = jnp.concatenate(
        [my_half(low_in[:, k * 768 : (k + 1) * 768], core, 384) for k in range(3)]
        + [my_half(low_out, core, 384), extra],
        1,
    )
    both_cut = jnp.concatenate([in_out_cut, my_half(low_up, core, 1536)], 1)
    both_far = z_sends(after(both_cut, table_half))
    down_half = my_half(low_down, core, 384)
    down_own = lax.all_gather(after(down_half, *near), "fsdp", axis=0, tiled=True)
    slots = [place.y * 2 + place.x]
    for side in (core, 1 - core):
        slots += [place.plane_slot(side, a, b) for a, b in ((1, 0), (0, 1), (1, 1))]
    index = jnp.stack(
        [s * 48 for s in slots] + [core * VOCAB_HALF, (1 - core) * VOCAB_HALF]
    ).astype(jnp.int32)
    found = lookup(index, ids_z, [table_cut] + near + [others])
    both_far = together(both_far, *found)
    in_out_column = jnp.stack([p[:, :1664] for p in both_far])
    up_column = jnp.stack([p[:, 1664:] for p in both_far])
    columns = [found[0]] + [send(found[j], ZS[j]) for j in (1, 2, 3)]
    in_out_mine = plane_sends(in_out_column, False, columns)
    in_out = both_cores(together(in_out_mine, in_out_mine[3]))
    up_mine = plane_sends(after(up_column, in_out_mine[3]), True)
    seg_row = slot_fragment_ids
    seg_col = slot_fragment_ids.reshape(512, 1)
    index_48 = piece_index(place, 48)
    z_index = jnp.stack([(place.z ^ j) * 192 for j in range(4)]).astype(jnp.int32)
    attention_index = jnp.concatenate([z_index, index_48])
    embedded, qkv, lse, mixed, unit_one, inv_one, normed_low, params, side = attention_forward(
        attention_index, seg_row, seg_col, columns, in_out
    )
    up_w = both_cores(together(up_mine, normed_low))
    activated, slope = up_forward(index_48, normed_low, up_w)
    down_w = [down_own, send(after(down_own, normed_low), CORE)]
    core_index = core.astype(jnp.int32).reshape(1)
    unit_two, inv_two, unit_rows, unit_low, unit_scale = down_forward(
        core_index, seg_row, activated, unit_one, params, down_w
    )
    embedded_o, mixed_o, normed_o, activated_o = (
        send(a, CORE) for a in (embedded, mixed, normed_low, activated)
    )
    column = jnp.stack([unit_low] + [send(unit_low, ZS[j]) for j in (1, 2, 3)])
    blocks = [column, send(column, FIRST), send(column, SECOND), send(column, BOTH)]
    blocks = blocks + [send(block, CORE) for block in blocks]
    base = (lax.axis_index("fsdp") * 2 + core) * 32
    index = [base]
    for who in (core, 1 - core):
        for a, b in ((0, 0), (1, 0), (0, 1), (1, 1)):
            index += [(place.chip(who, j, a, b) * 2 + who) * 32 for j in range(4)]
    index += [core]
    (
        loss_tile, grad_result_own, grad_result_x, grad_up_own, grad_up_x, grad_two, gains_two,
    ) = loss_backward(
        jnp.stack(index).astype(jnp.int32),
        affinity_heat.reshape(1),
        [
            seg_col,
            mirror_fragment_index.reshape(32, 1),
            fragment_weight.reshape(32, 1),
            mirror_fragment_index.reshape(1, 32),
            side,
            unit_rows,
            unit_scale,
            unit_two,
            inv_two,
            params,
            slope,
        ],
        blocks + down_w,
    )
    slots = slot_index(place)
    grad_result_o = send(grad_result_x, CORE)
    ids_o = send(ids_z, CORE)
    grad_up_o = send(grad_up_x, CORE)
    spare = [embedded_o, mixed_o, normed_o, ids_o]
    down_keep, down_away = down_grad(
        slots, [after(activated, *spare), activated_o, grad_result_own, grad_result_o]
    )
    down_came = send(down_away, SECOND)
    grad_resid, grad_attended, grad_att_own, grad_att_x, gains_one = ffn_backward(
        index_48,
        [after(grad_up_own, down_away), grad_up_x, grad_two, unit_one, inv_one, params],
        up_w,
    )
    grad_att_o = send(grad_att_x, CORE)
    norms = jnp.concatenate([gains_one[:2], gains_two[:2], jnp.zeros((4, 768), f32)], 0)
    norms = norms + send(norms, CORE)
    up_out_keep, up_out_away = up_out_grad(
        slots,
        [
            normed_low,
            normed_o,
            grad_up_own,
            grad_up_o,
            mixed,
            mixed_o,
            grad_att_own,
            grad_att_o,
            norms,
        ],
    )
    up_out_came = send(up_out_away, SECOND)
    down_came = after(down_came, up_out_away)
    down_across = scatter_add(down_keep, down_came)
    down_came_two = send(down_across, FIRST)
    grad_qkv_x, grad_mixed_own, part = other_heads(
        attention_index,
        [seg_row, seg_col, qkv, lse, after(grad_attended, down_across), grad_resid],
        in_out,
    )
    grad_qkv_o = send(grad_qkv_x, CORE)
    down_came_two, up_out_came = together([down_came_two, up_out_came], part)
    down_here, down_far = scatter_here(down_keep, down_came, down_came_two)
    up_out_across = scatter_add(up_out_keep, up_out_came)
    up_out_came_two = send(up_out_across, FIRST)
    down_far_came = line_sends(down_far)
    grad_qkv_own, *outs = own_heads(
        attention_index,
        [seg_row, seg_col, qkv, lse, grad_mixed_own, after(part, up_out_across, *down_far)],
        in_out[:4],
    )
    far_cols = [send(outs[j], ZS[j]) for j in (1, 2, 3)]
    *down_far_came, up_out_came_two, grad_qkv_o = together(
        down_far_came + [up_out_came_two, grad_qkv_o], grad_qkv_own
    )
    down_sum = line_sum(down_here, down_far_came)
    in_keep, in_away = in_grad(slots, [embedded, embedded_o, grad_qkv_own, grad_qkv_o])
    far_cols = together(far_cols, in_away)
    in_came = send(after(in_away, *far_cols), SECOND)
    token_cols = jnp.stack([outs[0]] + far_cols)
    token_cols_o = send(token_cols, CORE)
    up_out_here, up_out_far = scatter_here(
        up_out_keep, up_out_came, after(up_out_came_two, token_cols)
    )
    up_out_far_came = line_sends(up_out_far)
    plane = [place.plane_slot(core, a, b) * 48 for a, b in ((0, 0), (1, 0), (0, 1), (1, 1))]
    keep, away = token_sum(
        jnp.stack([core * VOCAB_HALF] + plane).astype(jnp.int32),
        after(ids_z, *up_out_far),
        ids_o,
        token_cols,
        token_cols_o,
    )
    came = send(away, SECOND)
    in_came = after(in_came, away)
    in_across = scatter_add(in_keep, in_came)
    in_came_two = send(in_across, FIRST)
    across = (keep[1].astype(f32) + came[1].astype(f32)).astype(bf16)
    came_two = send(across, FIRST)
    in_here, in_far = scatter_here(in_keep, in_came, after(in_came_two, across))
    in_far_came = line_sends(in_far)
    up_out_sum = line_sum(up_out_here, together(up_out_far_came, across))
    table_sum = keep[0].astype(f32) + came[0].astype(f32) + came_two.astype(f32)
    table_sum = table_sum.astype(bf16)
    in_sum = line_sum(in_here, together(in_far_came, table_sum))
    sums = [table_sum, in_sum, up_out_sum, down_sum]
    sums_o = [send(s, CORE) for s in sums]
    squares = sum(
        jnp.sum(jnp.square(p.astype(f32)))
        for p in (sums[0], sums[1], sums[2][:, :1920], sums[3])
    )
    norm_own = sums[2][:, 1920:1924].astype(f32)
    squares += jnp.where(core == 0, jnp.sum(norm_own * norm_own), 0.0)
    totals = jnp.concatenate([squares.reshape(1, 1), loss_tile[:1, :1]], 1)
    totals = all_sum(after(totals, *sums_o))
    count_now = optimizer_iteration.astype(f32)
    fixes = jnp.stack([1.0 - jnp.power(beta_one, count_now), 1.0 - jnp.power(beta_two, count_now)])
    results = optimizer(
        core_index,
        fixes,
        totals,
        send(totals, CORE),
        sums,
        sums_o,
        [
            lexicon_table.T,
            lexicon_first_moment.T,
            lexicon_raw_moment.T,
            query_key_value_maps,
            qkv_first_moment,
            qkv_raw_moment,
            attention_exit_map,
            exit_first_moment,
            exit_raw_moment,
            widening_matrix_in,
            widening_first_moment,
            widening_raw_moment,
            narrowing_matrix_out,
            narrowing_first_moment,
            narrowing_raw_moment,
            layernorm_scale_bias,
            layernorm_first_moment,
            layernorm_raw_moment,
        ],
    )
    results = list(results)
    results[:2] = [r[0, 0] for r in results[:2]]
    results[2:5] = [r.T for r in results[2:5]]
    return tuple(results)


def solution(mesh):
    in_specs = (
        P(("fsdp", "dp"), None),
        P(("fsdp", "dp"), None),
        P(("fsdp", "dp")),
        P(("fsdp", "dp")),
        P(),
        P(),
        P(None, "fsdp"),
        P(None, "fsdp"),
        P(None, "fsdp"),
        P("fsdp", None),
        P("fsdp", None),
        P("fsdp", None),
        P("fsdp", None),
        P("fsdp", None),
        P("fsdp", None),
        P("fsdp", None),
        P("fsdp", None),
        P("fsdp", None),
        P("fsdp", None),
        P("fsdp", None),
        P("fsdp", None),
        P(None, "fsdp"),
        P(None, "fsdp"),
        P(None, "fsdp"),
    )
    out_specs = (
        P(),
        P(),
        P(None, "fsdp"),
        P(None, "fsdp"),
        P(None, "fsdp"),
        P("fsdp", None),
        P("fsdp", None),
        P("fsdp", None),
        P("fsdp", None),
        P("fsdp", None),
        P("fsdp", None),
        P("fsdp", None),
        P("fsdp", None),
        P("fsdp", None),
        P("fsdp", None),
        P("fsdp", None),
        P("fsdp", None),
        P(None, "fsdp"),
        P(None, "fsdp"),
        P(None, "fsdp"),
    )
    own_plan = dict(mesh.shape) == {"fsdp": 16, "dp": 2}
    return jax.shard_map(
        per_device_links if own_plan else per_device, mesh=mesh, in_specs=in_specs, out_specs=out_specs, check_vma=False
    )
```

```python
import jax
import jax.numpy as jnp
from jax import lax
from jax.experimental import pallas as pl
from jax.experimental.pallas import tpu as pltpu
from jax.sharding import PartitionSpec as P

MODEL_WIDTH = 768
H = 12
HD = 64
SEG_ROW = 32


largest_value = lax.Precision.HIGHEST
beta_one = 0.9
beta_two = 0.999
adam_eps = 1e-12
decay_rate = 0.01
rate_matrix = 0.1
rate_embed = 1.0
rate_norm = 1.0
clip_norm = 0.001
norm_eps = 1e-05
unit_eps = 1e-06


def layer_norm(inputs, gain_row, shifts):
    center = inputs - jnp.mean(inputs, -1, keepdims=True)
    inv_std = lax.rsqrt(jnp.mean(center * center, -1, keepdims=True) + norm_eps)
    normed = center * inv_std
    return (normed * gain_row + shifts, normed, inv_std)


def norm_back(upstream, normed, inv_std, gain_row):
    scaled = upstream * gain_row
    grad_in = inv_std * (
        scaled
        - jnp.mean(scaled, -1, keepdims=True)
        - normed * jnp.mean(scaled * normed, -1, keepdims=True)
    )
    return (grad_in, jnp.sum(upstream * normed, 0), jnp.sum(upstream, 0))


def masked_scores(query_rows, key_rows, segment_rows):
    raw_scores = jnp.einsum(
        "bqhd,bkhd->bhqk", query_rows, key_rows, preferred_element_type=jnp.float32
    )
    same_segment = segment_rows[:, None, :, None] == segment_rows[:, None, None, :]
    return jnp.where(same_segment, raw_scores * HD ** (-0.5), -1e30)


def layer_forward(gathered, token_rows, segment_rows):
    (
        lexicon_table,
        query_key_value_maps,
        attention_exit_map,
        widening_matrix_in,
        narrowing_matrix_out,
        layernorm_scale_bias,
    ) = gathered
    batch_row_list, sequence_length = token_rows.shape
    embedded = jnp.take(lexicon_table, token_rows.reshape(-1), axis=0)
    qkv_all = jnp.dot(embedded, query_key_value_maps, preferred_element_type=jnp.float32).astype(
        jnp.bfloat16
    )
    qkv_all = qkv_all.reshape(batch_row_list, sequence_length, 3, H, HD)
    query_rows, key_rows, value_rows = (qkv_all[:, :, 0], qkv_all[:, :, 1], qkv_all[:, :, 2])
    scores = masked_scores(query_rows, key_rows, segment_rows)
    row_max = jnp.max(scores, -1, keepdims=True)
    log_total = row_max + jnp.log(jnp.sum(jnp.exp(scores - row_max), -1, keepdims=True))
    attn_probs = jnp.exp(scores - log_total).astype(jnp.bfloat16)
    mixed_heads = jnp.einsum(
        "bhqk,bkhd->bqhd", attn_probs, value_rows, preferred_element_type=jnp.float32
    )
    mixed_heads = mixed_heads.reshape(batch_row_list * sequence_length, MODEL_WIDTH).astype(
        jnp.bfloat16
    )
    attended = jnp.dot(mixed_heads, attention_exit_map, preferred_element_type=jnp.float32)
    normed_one, unit_one, inv_one = layer_norm(
        embedded.astype(jnp.float32) + attended, layernorm_scale_bias[0], layernorm_scale_bias[1]
    )
    normed_low = normed_one.astype(jnp.bfloat16)
    up_proj = jnp.dot(normed_low, widening_matrix_in, preferred_element_type=jnp.float32)
    activated = jax.nn.gelu(up_proj, approximate=False).astype(jnp.bfloat16)
    ffn_result = jnp.dot(activated, narrowing_matrix_out, preferred_element_type=jnp.float32)
    second_normalized, unit_two, inv_two = layer_norm(
        normed_one + ffn_result, layernorm_scale_bias[2], layernorm_scale_bias[3]
    )
    group_member = (
        segment_rows[:, None, :] == jnp.arange(SEG_ROW, dtype=jnp.int32)[None, :, None]
    ).astype(jnp.float32)
    pooled_state = jnp.einsum(
        "nkz,nzh->nkh",
        group_member,
        second_normalized.reshape(batch_row_list, sequence_length, MODEL_WIDTH),
        precision=largest_value,
    )
    saved_state = (
        embedded,
        query_rows,
        key_rows,
        value_rows,
        log_total,
        mixed_heads,
        unit_one,
        inv_one,
        normed_low,
        up_proj,
        activated,
        unit_two,
        inv_two,
        group_member,
    )
    return (pooled_state.reshape(batch_row_list * SEG_ROW, MODEL_WIDTH), saved_state)


def layer_backward(gathered, saved_state, token_rows, segment_rows, pooled_gradient):
    (
        lexicon_table,
        query_key_value_maps,
        attention_exit_map,
        widening_matrix_in,
        narrowing_matrix_out,
        layernorm_scale_bias,
    ) = gathered
    (
        embedded,
        query_rows,
        key_rows,
        value_rows,
        log_total,
        mixed_heads,
        unit_one,
        inv_one,
        normed_low,
        up_proj,
        activated,
        unit_two,
        inv_two,
        group_member,
    ) = saved_state
    batch_row_list, sequence_length = token_rows.shape
    pooled_gradient = pooled_gradient.reshape(batch_row_list, SEG_ROW, MODEL_WIDTH)
    second_gradient = jnp.einsum(
        "got,goy->gty", group_member, pooled_gradient, precision=largest_value
    ).reshape(batch_row_list * sequence_length, MODEL_WIDTH)
    grad_resid_two, grad_gain_two, grad_shift_two = norm_back(
        second_gradient, unit_two, inv_two, layernorm_scale_bias[2]
    )
    grad_result = grad_resid_two.astype(jnp.bfloat16)
    grad_ffn_down = jnp.einsum(
        "nf,nd->fd", activated, grad_result, preferred_element_type=jnp.float32
    )
    grad_act = jnp.einsum(
        "nd,fd->nf", grad_result, narrowing_matrix_out, preferred_element_type=jnp.float32
    )
    gelu_value, gelu_pull = jax.vjp(
        lambda pre_act: jax.nn.gelu(pre_act, approximate=False), up_proj
    )
    grad_up = gelu_pull(grad_act)[0].astype(jnp.bfloat16)
    grad_ffn_up = jnp.einsum("nd,nf->df", normed_low, grad_up, preferred_element_type=jnp.float32)
    grad_one = grad_resid_two + jnp.einsum(
        "nf,df->nd", grad_up, widening_matrix_in, preferred_element_type=jnp.float32
    )
    grad_resid_one, grad_gain_one, grad_shift_one = norm_back(
        grad_one, unit_one, inv_one, layernorm_scale_bias[0]
    )
    grad_attended = grad_resid_one.astype(jnp.bfloat16)
    grad_project_out = jnp.einsum(
        "nc,nd->cd", mixed_heads, grad_attended, preferred_element_type=jnp.float32
    )
    grad_mixed = jnp.einsum(
        "nd,cd->nc", grad_attended, attention_exit_map, preferred_element_type=jnp.float32
    )
    grad_mixed = grad_mixed.astype(jnp.bfloat16).reshape(batch_row_list, sequence_length, H, HD)
    scores = masked_scores(query_rows, key_rows, segment_rows)
    attn_probs = jnp.exp(scores - log_total)
    probs_low = attn_probs.astype(jnp.bfloat16)
    grad_values = jnp.einsum(
        "bhqk,bqhd->bkhd", probs_low, grad_mixed, preferred_element_type=jnp.float32
    )
    grad_probs = jnp.einsum(
        "bqhd,bkhd->bhqk", grad_mixed, value_rows, preferred_element_type=jnp.float32
    )
    grad_scores = attn_probs * (grad_probs - jnp.sum(grad_probs * attn_probs, -1, keepdims=True))
    grad_scores = grad_scores.astype(jnp.bfloat16)
    grad_query = jnp.einsum(
        "bhqk,bkhd->bqhd", grad_scores, key_rows, preferred_element_type=jnp.float32
    ) * HD ** (-0.5)
    grad_keys = jnp.einsum(
        "bhqk,bqhd->bkhd", grad_scores, query_rows, preferred_element_type=jnp.float32
    ) * HD ** (-0.5)
    grad_qkv = (
        jnp.stack([grad_query, grad_keys, grad_values], 2)
        .reshape(batch_row_list * sequence_length, 3 * MODEL_WIDTH)
        .astype(jnp.bfloat16)
    )
    grad_project_in = jnp.einsum(
        "nd,nc->dc", embedded, grad_qkv, preferred_element_type=jnp.float32
    )
    grad_embedded = grad_resid_one + jnp.einsum(
        "nc,dc->nd", grad_qkv, query_key_value_maps, preferred_element_type=jnp.float32
    )
    grad_norms = jnp.stack([grad_gain_one, grad_shift_one, grad_gain_two, grad_shift_two])
    return (
        grad_embedded,
        grad_project_in,
        grad_project_out,
        grad_ffn_up,
        grad_ffn_down,
        grad_norms,
    )


def adam_update(weight, first, second, grad, fix_first, fix_second, rate, decay):
    first_new = beta_one * first + (1.0 - beta_one) * grad
    second_new = beta_two * second + (1.0 - beta_two) * grad * grad
    step_size = first_new / fix_first / (jnp.sqrt(second_new / fix_second) + adam_eps)
    return (weight - rate * (step_size + decay * weight), first_new, second_new)


def per_device(
    kmer_identifiers,
    slot_fragment_ids,
    mirror_fragment_index,
    fragment_weight,
    affinity_heat,
    optimizer_iteration,
    lexicon_table,
    lexicon_first_moment,
    lexicon_raw_moment,
    query_key_value_maps,
    qkv_first_moment,
    qkv_raw_moment,
    attention_exit_map,
    exit_first_moment,
    exit_raw_moment,
    widening_matrix_in,
    widening_first_moment,
    widening_raw_moment,
    narrowing_matrix_out,
    narrowing_first_moment,
    narrowing_raw_moment,
    layernorm_scale_bias,
    layernorm_first_moment,
    layernorm_raw_moment,
):
    masters = (
        lexicon_table,
        query_key_value_maps,
        attention_exit_map,
        widening_matrix_in,
        narrowing_matrix_out,
        layernorm_scale_bias,
    )
    firsts = (
        lexicon_first_moment,
        qkv_first_moment,
        exit_first_moment,
        widening_first_moment,
        narrowing_first_moment,
        layernorm_first_moment,
    )
    seconds = (
        lexicon_raw_moment,
        qkv_raw_moment,
        exit_raw_moment,
        widening_raw_moment,
        narrowing_raw_moment,
        layernorm_raw_moment,
    )
    rates = (rate_embed, rate_matrix, rate_matrix, rate_matrix, rate_matrix, rate_norm)
    decays = (decay_rate, decay_rate, decay_rate, decay_rate, decay_rate, 0.0)
    lowered = tuple((piece.astype(jnp.bfloat16) for piece in masters))
    gathered = (
        lax.all_gather(lowered[0], "fsdp", axis=1, tiled=True),
        lax.all_gather(lowered[1], "fsdp", axis=0, tiled=True),
        lax.all_gather(lowered[2], "fsdp", axis=0, tiled=True),
        lax.all_gather(lowered[3], "fsdp", axis=0, tiled=True),
        lax.all_gather(lowered[4], "fsdp", axis=0, tiled=True),
        lax.all_gather(lowered[5], "fsdp", axis=1, tiled=True),
    )
    pooled_state, saved_state = layer_forward(gathered, kmer_identifiers, slot_fragment_ids)
    unit_scale = lax.rsqrt(jnp.sum(pooled_state * pooled_state, -1, keepdims=True) + unit_eps)
    unit_rows = pooled_state * unit_scale
    unit_low = unit_rows.astype(jnp.bfloat16)
    every_unit = lax.all_gather(unit_low, ("fsdp", "dp"), axis=0, tiled=True)
    cosine_affinity_grid = jnp.einsum(
        "sd,td->st", unit_low, every_unit, preferred_element_type=jnp.float32
    )
    seg_local = pooled_state.shape[0]
    fragment_tally = every_unit.shape[0]
    shard_fragment_lines = lax.axis_index(("fsdp", "dp")) * seg_local + jnp.arange(
        seg_local, dtype=jnp.int32
    )
    field_sequence_array = jnp.arange(fragment_tally, dtype=jnp.int32)
    raw_affinity_values = jnp.where(
        shard_fragment_lines[:, None] == field_sequence_array[None, :],
        -1e30,
        cosine_affinity_grid / affinity_heat,
    )
    row_max = jnp.max(raw_affinity_values, -1, keepdims=True)
    log_total = row_max[:, 0] + jnp.log(jnp.sum(jnp.exp(raw_affinity_values - row_max), -1))
    chosen = mirror_fragment_index[:, None] == field_sequence_array[None, :]
    chosen_real_entry = chosen.astype(jnp.float32)
    target = jnp.sum(jnp.where(chosen, raw_affinity_values, 0.0), -1)
    contrast_objective = (
        lax.psum(jnp.sum(fragment_weight * (log_total - target)), ("fsdp", "dp")) / fragment_tally
    )
    exponent_probabilities = jnp.exp(raw_affinity_values - log_total[:, None])
    similarity_gradient = (
        (exponent_probabilities - chosen_real_entry)
        * fragment_weight[:, None]
        / (fragment_tally * affinity_heat)
    ).astype(jnp.bfloat16)
    grad_rows = jnp.dot(similarity_gradient, every_unit, preferred_element_type=jnp.float32)
    column_terms = jnp.einsum(
        "st,sd->td", similarity_gradient, unit_low, preferred_element_type=jnp.float32
    )
    grad_cols = lax.psum_scatter(column_terms, ("fsdp", "dp"), scatter_dimension=0, tiled=True)
    grad_unit = grad_rows + grad_cols
    pooled_gradient = unit_scale * (
        grad_unit - unit_rows * jnp.sum(grad_unit * unit_rows, -1, keepdims=True)
    )
    again = (
        lax.all_gather(lowered[0], "fsdp", axis=1, tiled=True),
        lax.all_gather(lowered[1], "fsdp", axis=0, tiled=True),
        lax.all_gather(lowered[2], "fsdp", axis=0, tiled=True),
        lax.all_gather(lowered[3], "fsdp", axis=0, tiled=True),
        lax.all_gather(lowered[4], "fsdp", axis=0, tiled=True),
        lax.all_gather(lowered[5], "fsdp", axis=1, tiled=True),
    )
    grads = layer_backward(again, saved_state, kmer_identifiers, slot_fragment_ids, pooled_gradient)
    vocab = lexicon_table.shape[0]
    rest = (
        lax.psum_scatter(grads[1], "fsdp", scatter_dimension=0, tiled=True),
        lax.psum_scatter(grads[2], "fsdp", scatter_dimension=0, tiled=True),
        lax.psum_scatter(grads[3], "fsdp", scatter_dimension=0, tiled=True),
        lax.psum_scatter(grads[4], "fsdp", scatter_dimension=0, tiled=True),
        lax.psum_scatter(grads[5], "fsdp", scatter_dimension=1, tiled=True),
    )
    column_rows = lax.all_to_all(
        grads[0].astype(jnp.bfloat16), "fsdp", split_axis=1, concat_axis=0, tiled=True
    ).astype(jnp.float32)
    all_tokens = lax.all_gather(kmer_identifiers.reshape(-1), "fsdp", axis=0, tiled=True)
    table_shard = jax.ops.segment_sum(column_rows, all_tokens, num_segments=vocab)
    shards = (table_shard, rest[0], rest[1], rest[2], rest[3], rest[4])
    shards = (
        lax.psum(shards[0].astype(jnp.bfloat16), "dp").astype(jnp.float32),
        lax.psum(shards[1].astype(jnp.bfloat16), "dp").astype(jnp.float32),
        lax.psum(shards[2].astype(jnp.bfloat16), "dp").astype(jnp.float32),
        lax.psum(shards[3].astype(jnp.bfloat16), "dp").astype(jnp.float32),
        lax.psum(shards[4].astype(jnp.bfloat16), "dp").astype(jnp.float32),
        lax.psum(shards[5].astype(jnp.bfloat16), "dp").astype(jnp.float32),
    )
    squares = sum((jnp.sum(piece * piece) for piece in shards))
    grad_norm = jnp.sqrt(lax.psum(squares, "fsdp"))
    factor = clip_norm / jnp.maximum(grad_norm, clip_norm)
    count_now = optimizer_iteration.astype(jnp.float32)
    fix_first = 1.0 - jnp.power(beta_one, count_now)
    fix_second = 1.0 - jnp.power(beta_two, count_now)
    updated = [
        adam_update(
            masters[number],
            firsts[number],
            seconds[number],
            shards[number] * factor,
            fix_first,
            fix_second,
            rates[number],
            decays[number],
        )
        for number in range(6)
    ]
    return (
        contrast_objective,
        grad_norm,
        updated[0][0],
        updated[0][1],
        updated[0][2],
        updated[1][0],
        updated[1][1],
        updated[1][2],
        updated[2][0],
        updated[2][1],
        updated[2][2],
        updated[3][0],
        updated[3][1],
        updated[3][2],
        updated[4][0],
        updated[4][1],
        updated[4][2],
        updated[5][0],
        updated[5][1],
        updated[5][2],
    )


AXES = ("fsdp", "dp")
VOCAB_PAD = 4352
VOCAB_HALF = VOCAB_PAD // 2
BIG_VMEM = pltpu.CompilerParams(vmem_limit_bytes=60 * 1024 * 1024)
bf16 = jnp.bfloat16
f32 = jnp.float32


def pairs_of(moved):
    spots = [(z, y, x, c) for z in range(4) for y in range(2) for x in range(2) for c in range(2)]

    def linear(spot):
        z, y, x, c = spot
        return ((z * 2 + y) * 2 + x) * 2 + c

    return [(linear(spot), linear(moved(*spot))) for spot in spots]


FIRST = pairs_of(lambda z, y, x, c: (z, y, x ^ 1, c) if c == 0 else (z, y ^ 1, x, c))
SECOND = pairs_of(lambda z, y, x, c: (z, y ^ 1, x, c) if c == 0 else (z, y, x ^ 1, c))
BOTH = pairs_of(lambda z, y, x, c: (z, y ^ 1, x ^ 1, c))
CORE = pairs_of(lambda z, y, x, c: (z, y, x, 1 - c))
ZS = [None] + [pairs_of(lambda z, y, x, c, j=j: (z ^ j, y, x, c)) for j in (1, 2, 3)]


def send(array, pairs):
    return lax.ppermute(array, AXES, pairs)


def after(array, *others):
    return lax.optimization_barrier((array,) + others)[0]


def together(arrays, *others):
    arrays = list(arrays)
    return list(lax.optimization_barrier((*arrays, *others)))[: len(arrays)]


class Place:
    def __init__(self):
        f = lax.axis_index("fsdp")
        self.core = lax.axis_index("dp")
        self.z, self.y, self.x = f // 4, (f // 2) % 2, f % 2

    def plane_slot(self, core, a, b):
        dy = jnp.where(core == 0, b, a)
        dx = jnp.where(core == 0, a, b)
        return (self.y ^ dy) * 2 + (self.x ^ dx)

    def chip(self, core, j, a, b):
        return (self.z ^ j) * 4 + self.plane_slot(core, a, b)


def z_sends(piece):
    return [piece] + [send(piece, ZS[j]) for j in (1, 2, 3)]


def z_column(piece):
    return jnp.stack(z_sends(piece))


def plane_sends(column, direct=False, gate=()):
    one = send(column, FIRST)
    two = send(column, SECOND)
    three = send(column, BOTH) if direct else send(after(one, *gate), SECOND)
    return [column, one, two, three]


def both_cores(mine):
    return mine + [send(block, CORE) for block in mine]


def piece_index(place, rows):
    halves, starts = [], []
    for core in (place.core, 1 - place.core):
        for a, b in ((0, 0), (1, 0), (0, 1), (1, 1)):
            for j in range(4):
                halves.append(core)
                starts.append(place.chip(core, j, a, b) * rows)
    return jnp.stack(halves + starts).astype(jnp.int32)


def pair_index(place, rows):
    halves, starts = [], []
    for core in (place.core, 1 - place.core):
        for b in (0, 1):
            for j in range(4):
                for a in (0, 1):
                    halves.append(core)
                    starts.append(place.chip(core, j, a, b) * rows)
    return jnp.stack(halves + starts).astype(jnp.int32)


def slot_index(place):
    chips = [
        place.chip(place.core, j, a, b) for b in (0, 1) for a in (0, 1) for j in range(4)
    ]
    return jnp.stack(chips).astype(jnp.int32)


def scatter_add(keep, came):
    return (keep[4:].astype(f32) + came[4:].astype(f32)).astype(bf16)


def scatter_here(keep, came, came_two):
    here = [
        keep[j].astype(f32) + came[j].astype(f32) + came_two[j].astype(f32) for j in range(4)
    ]
    return here[0], [h.astype(bf16) for h in here[1:]]


def line_sends(far):
    return [send(h, ZS[j]) for h, j in zip(far, (1, 2, 3))]


def line_sum(here, far):
    return (here + far[0].astype(f32) + far[1].astype(f32) + far[2].astype(f32)).astype(bf16)


def whole_copies(sources, targets, sems):
    return [
        pltpu.make_async_copy(source, target, sems.at[number])
        for number, (source, target) in enumerate(zip(sources, targets))
    ]


class Stage:
    def __init__(self, copies_in, copies_out):
        self.copies_in, self.copies_out = dict(enumerate(copies_in)), dict(enumerate(copies_out))
        self.started = []

    def __call__(self, *which):
        for number in which or tuple(self.copies_in):
            self.copies_in.pop(number).wait()

    def put(self, *which):
        for number in which or tuple(self.copies_out):
            copy = self.copies_out.pop(number)
            copy.start()
            self.started.append(copy)

    def finish(self):
        self.put(*tuple(self.copies_out))
        for copy in self.started:
            copy.wait()


def staged_call(body, scalars, arrays, pieces, shapes, scratch, cost, late=()):
    n_s, n_a, n_p, n_o = len(scalars), len(arrays), len(pieces), len(shapes)

    def kernel(*refs):
        smem, refs = refs[:n_s], refs[n_s:]
        hbm, refs = refs[:n_a], refs[n_a:]
        far, refs = refs[:n_p], refs[n_p:]
        out, refs = refs[:n_o], refs[n_o:]
        near_in, refs = refs[:n_a], refs[n_a:]
        near_out, refs = refs[:n_o], refs[n_o:]
        in_sems, out_sems, refs = refs[0], refs[1], refs[2:]
        copies = whole_copies(hbm, near_in, in_sems)
        for number, copy in enumerate(copies):
            if number not in late:
                copy.start()
        stage = Stage(copies, whole_copies(near_out, out, out_sems))
        body(stage, *smem, *near_in, *far, *near_out, *refs)
        stage.finish()

    in_hbm = pl.BlockSpec(memory_space=pltpu.HBM)
    return pl.pallas_call(
        kernel,
        out_shape=shapes,
        in_specs=[pl.BlockSpec(memory_space=pltpu.SMEM)] * n_s + [in_hbm] * (n_a + n_p),
        out_specs=[in_hbm] * n_o,
        scratch_shapes=[pltpu.VMEM(a.shape, a.dtype) for a in arrays]
        + [pltpu.VMEM(s.shape, s.dtype) for s in shapes]
        + [pltpu.SemaphoreType.DMA((n_a,)), pltpu.SemaphoreType.DMA((n_o,))]
        + scratch,
        cost_estimate=pl.CostEstimate(flops=int(cost * 1e9), bytes_accessed=0, transcendentals=0),
        compiler_params=BIG_VMEM,
    )(*scalars, *arrays, *pieces)


def shaped(dtype, *dims):
    return jax.ShapeDtypeStruct(dims, dtype)


def one_hot(ids_row, start, count):
    spots = lax.broadcasted_iota(jnp.int32, (count, ids_row.shape[1]), 0) + start
    return jnp.where(spots == ids_row, 1.0, 0.0).astype(bf16)


def prepare_kernel(
    ready, core_ref, table_ref, in_ref, out_ref, up_ref, down_ref, norm_ref, ids_ref, weight_ref,
    both_ref, cut_ref, half_ref, down_half_ref,
):
    core = core_ref[0]

    def mine(ref, width, start=0):
        return ref[:, pl.ds(pl.multiple_of(start + core * width, 128), width)].astype(bf16)

    ready(1, 2, 3, 5, 6, 7)
    for t in range(3):
        both_ref[:, t * 384 : (t + 1) * 384] = mine(in_ref, 384, t * 768)
    both_ref[:, 1152:1536] = mine(out_ref, 384)
    rest = jnp.zeros((1, 16), f32)
    heavy = [jnp.concatenate([w.astype(f32), rest], 1) for w in thirds(weight_ref[...])]
    extra = jnp.concatenate([norm_ref[...]] + heavy + [jnp.zeros((121, 48), f32)], 0)
    both_ref[:, 1536:1664] = extra.T.astype(bf16)
    both_ref[:, 1664:3200] = mine(up_ref, 1536)
    ids = jnp.concatenate([ids_ref[:, k * 128 : (k + 1) * 128] for k in range(4)], 0)
    high = lax.shift_right_logical(ids, 6)
    ids = jnp.concatenate([high, ids - high * 64], 0).astype(f32).astype(bf16)
    both_ref[:, 3200:3328] = jnp.concatenate([ids, jnp.zeros((40, 128), bf16)], 0)
    ready.put(0)
    ready(0, 4)
    vocab = table_ref.shape[1]
    even = vocab - vocab % 128
    cut_ref[:, :even] = table_ref[:, :even].astype(bf16)
    last = [table_ref[:, even:], jnp.zeros((48, VOCAB_PAD - vocab), f32)]
    cut_ref[:, even:] = jnp.concatenate(last, 1).astype(bf16)
    half_ref[...] = cut_ref[:, pl.ds(pl.multiple_of(core * VOCAB_HALF, 128), VOCAB_HALF)]
    down_half_ref[...] = mine(down_ref, 384)


def prepare(core, arrays):
    return staged_call(
        prepare_kernel,
        [core],
        arrays,
        [],
        [
            shaped(bf16, 48, 3328),
            shaped(bf16, 48, VOCAB_PAD),
            shaped(bf16, 48, VOCAB_HALF),
            shaped(bf16, 192, 384),
        ],
        [],
        3,
    )


def id_row(ids_ref, j):
    rows = ids_ref[j]
    return jnp.concatenate([rows[k : k + 1] for k in range(4)], 1)


def lookup_kernel(ready, idx_ref, ids_ref, *refs):
    ins = list(refs[:4]) + [refs[4].at[k] for k in range(3)]
    outs, table, sems = refs[5:9], refs[9], refs[10]
    copies = [
        pltpu.make_async_copy(
            ins[0], table.at[pl.ds(pl.multiple_of(idx_ref[0], 16), 48), :], sems.at[0]
        )
    ]
    for number in range(1, 7):
        column = pl.multiple_of(idx_ref[7 + (number - 1) // 3], 128)
        row = pl.multiple_of(idx_ref[number], 16)
        copies.append(
            pltpu.make_async_copy(
                ins[number],
                table.at[pl.ds(row, 48), pl.ds(column, VOCAB_HALF)],
                sems.at[number],
            )
        )
    for copy in copies:
        copy.start()
    ready()
    for copy in copies:
        copy.wait()
    for j in range(4):
        total = jnp.zeros((192, 512), f32)
        for k in range(VOCAB_PAD // 256):
            total += jnp.dot(
                table[:, k * 256 : (k + 1) * 256],
                one_hot(id_row(ids_ref, j), k * 256, 256),
                preferred_element_type=f32,
            )
        outs[j][...] = total.astype(bf16)


def lookup(index, ids_z, arrays):
    return staged_call(
        lookup_kernel,
        [index],
        [ids_z],
        arrays,
        [
            shaped(bf16, 192, 512),
            shaped(bf16, 192, 512),
            shaped(bf16, 192, 512),
            shaped(bf16, 192, 512),
        ],
        [
            pltpu.VMEM((192, VOCAB_PAD), bf16),
            pltpu.SemaphoreType.DMA((7,)),
        ],
        6,
    )


def token_sum_kernel(ready, idx_ref, ids_ref, other_ids_ref, mine_ref, other_ref, keep_ref, away_ref, whole_ref
):
    ready()
    start = idx_ref[0]
    for low in range(0, VOCAB_HALF, 256):
        count = min(256, VOCAB_HALF - low)
        total = jnp.zeros((192, count), f32)
        for ids, block in ((ids_ref, mine_ref), (other_ids_ref, other_ref)):
            for j in range(4):
                total += lax.dot_general(
                    block[j],
                    one_hot(id_row(ids, j), start + low, count),
                    (((1,), (1,)), ((), ())),
                    preferred_element_type=f32,
                )
        whole_ref[:, low : low + count] = total.astype(bf16)
    for k in range(2):
        keep_ref[k] = whole_ref[pl.ds(pl.multiple_of(idx_ref[1 + k], 16), 48), :]
        away_ref[k] = whole_ref[pl.ds(pl.multiple_of(idx_ref[3 + k], 16), 48), :]


def token_sum(index, ids_z, other_ids, mine, other):
    return staged_call(
        token_sum_kernel,
        [index],
        [ids_z, other_ids, mine, other],
        [],
        [
            shaped(bf16, 2, 48, VOCAB_HALF),
            shaped(bf16, 2, 48, VOCAB_HALF),
        ],
        [
            pltpu.VMEM((192, VOCAB_HALF), bf16),
        ],
        8,
    )


def my_half(array, core, width):
    return lax.dynamic_slice_in_dim(array, core * width, width, axis=1)


def all_sum(value):
    for pairs in (ZS[1:], [FIRST, SECOND, BOTH]):
        one, two, three = (send(value, p) for p in pairs)
        value = (value + one) + (two + three)
    return value


WINDOWS = (0, 64, 192, 256)
SCALE = HD ** (-0.5)


def piece_copies(idx_ref, base, pieces, target, rows, sems, first_sem):
    copies = []
    for number in range(32):
        half = idx_ref[base + number]
        row = pl.multiple_of(idx_ref[base + 32 + number], 16)
        each = 32 // len(pieces)
        source = pieces[number // each].at[number % each]
        copies.append(
            pltpu.make_async_copy(
                source, target.at[half, pl.ds(row, rows), :], sems.at[first_sem + number]
            )
        )
    return copies


def window_bias(seg_row, seg_col, b):
    w = WINDOWS[b]
    same = seg_col[b * 128 : (b + 1) * 128, :] == seg_row[:, w : w + 256]
    bias = jnp.where(same, 0.0, -1e30)
    return jnp.concatenate([bias, bias], 0)


def two_heads(block):
    left = lax.broadcasted_iota(jnp.int32, block.shape, 1) < HD
    none = jnp.zeros_like(block)
    return jnp.concatenate([jnp.where(left, block, none), jnp.where(left, none, block)], 0)


def nt_dot(a, b):
    return lax.dot_general(a, b, (((1,), (1,)), ((), ())), preferred_element_type=f32)


def tn_dot(a, b):
    return lax.dot_general(a, b, (((0,), (0,)), ((), ())), preferred_element_type=f32)


def nn_dot(a, b):
    return jnp.dot(a, b, preferred_element_type=f32)


def row_norm(v):
    center = v - jnp.mean(v, -1, keepdims=True)
    inv = lax.rsqrt(jnp.mean(center * center, -1, keepdims=True) + norm_eps)
    return center * inv, inv


def attention_kernel(ready, idx_ref, seg_row_ref, seg_col_ref, *refs):
    e_in, pieces = refs[:4], refs[4:12]
    (e_ref, qkv_ref, lse_ref, mixed_ref, unit_ref, inv_ref, low_ref, par_ref, side_ref) = refs[12:21]
    et_ref, w_ref, bias_ref, attended_ref, sems = refs[21:]
    e_copies = [
        pltpu.make_async_copy(
            e_in[j],
            et_ref.at[pl.ds(pl.multiple_of(idx_ref[j], 16), 192), :],
            sems.at[j],
        )
        for j in range(4)
    ]
    w_copies = piece_copies(idx_ref, 4, pieces, w_ref, 48, sems, 4)
    for copy in e_copies + w_copies:
        copy.start()
    ready()
    for b in range(4):
        bias_ref[b] = window_bias(seg_row_ref[...], seg_col_ref[...], b)
    for copy in e_copies:
        copy.wait()
    e_ref[...] = et_ref[...].T
    ready.put(0)
    for copy in w_copies:
        copy.wait()
    par_ref[...] = w_ref[0, :, 1536:1664].T.astype(f32)[:8]
    side_ref[...] = w_ref[:, :, 1536:1664]
    for k in range(2):
        for t in range(3):
            part = nn_dot(e_ref[...], w_ref[k, :, t * 384 : (t + 1) * 384])
            if t == 0:
                part = part.astype(bf16).astype(f32) * SCALE
            part = part.astype(bf16)
            for i in range(3):
                qkv_ref[t * 6 + k * 3 + i] = part[:, i * 128 : (i + 1) * 128]
    ready.put(1, 7, 8)
    lse_ref[...] = jnp.zeros_like(lse_ref)
    lane = lax.broadcasted_iota(jnp.int32, (128, 128), 1)
    left = lane < HD

    @pl.loop(0, 6)
    def _(pair):
        for b in range(4):
            rows = pl.ds(b * 128, 128)
            keys = pl.ds(WINDOWS[b], 256)
            q = qkv_ref[pair, rows, :]
            k = qkv_ref[pair + 6, keys, :]
            v = qkv_ref[pair + 12, keys, :]
            s = nt_dot(two_heads(q), k) + bias_ref[b]
            top = jnp.max(s, -1, keepdims=True)
            e = jnp.exp(s - top)
            total = jnp.sum(e, -1, keepdims=True)
            log = top + jnp.log(total)
            lse = jnp.where(lane == pair * 2, log[:128], lse_ref[rows, :])
            lse_ref[rows, :] = jnp.where(lane == pair * 2 + 1, log[128:], lse)
            mixed = nn_dot((e * (1.0 / total)).astype(bf16), v)
            cols = pl.ds(pl.multiple_of(pair * 128, 128), 128)
            mixed_ref[rows, cols] = jnp.where(left, mixed[:128], mixed[128:]).astype(bf16)

    ready.put(2, 3)
    for k in range(2):
        attended_ref[:, k * 384 : (k + 1) * 384] = nn_dot(mixed_ref[...], w_ref[k, :, 1152:1536])
    for b in range(4):
        rows = slice(b * 128, (b + 1) * 128)
        unit, inv = row_norm(e_ref[rows, :].astype(f32) + attended_ref[rows, :])
        unit_ref[rows, :] = unit
        inv_ref[rows, :] = jnp.broadcast_to(inv, (128, 128))
        low_ref[rows, :] = (unit * par_ref[0:1, :] + par_ref[1:2, :]).astype(bf16)


def attention_forward(index, seg_row, seg_col, columns, pieces):
    return staged_call(
        attention_kernel,
        [index],
        [seg_row, seg_col],
        [*columns, *pieces],
        [
            shaped(bf16, 512, 768),
            shaped(bf16, 18, 512, 128),
            shaped(f32, 512, 128),
            shaped(bf16, 512, 768),
            shaped(f32, 512, 768),
            shaped(f32, 512, 128),
            shaped(bf16, 512, 768),
            shaped(f32, 8, 768),
            shaped(bf16, 2, 768, 128),
        ],
        [
            pltpu.VMEM((768, 512), bf16),
            pltpu.VMEM((2, 768, 1664), bf16),
            pltpu.VMEM((4, 256, 256), f32),
            pltpu.VMEM((512, 768), f32),
            pltpu.SemaphoreType.DMA((36,)),
        ],
        17,
    )


def gelu_and_slope(u):
    bell = jnp.exp(-0.5 * u * u)
    base = 1.0 + (0.3275911 * 0.5**0.5) * jnp.abs(u)
    t = pl.reciprocal(base, approx=True)
    t = t * (2.0 - base * t)
    poly = -0.07032334059476852
    for factor in (
        0.24725385010242462,
        -0.2008872926235199,
        0.2245105654001236,
        0.013965459540486336,
        0.10251718759536743,
        0.09044301509857178,
        0.09252061694860458,
    ):
        poly = factor + t * poly
    tail = (t * poly) * bell
    phi = jnp.where(u < 0, tail, 1.0 - tail)
    return u * phi, phi + (u * 0.3989422804014327) * bell


def up_kernel(ready, idx_ref, low_ref, *refs):
    pieces, act_ref, slope_ref, w_ref, sems = refs[:8], refs[8], refs[9], refs[10], refs[11]
    copies = piece_copies(idx_ref, 0, pieces, w_ref, 48, sems, 0)
    for copy in copies:
        copy.start()
    ready()
    for copy in copies:
        copy.wait()
    for k in range(2):

        @pl.loop(0, 6)
        def _(n):
            cols = pl.ds(pl.multiple_of(n * 256, 256), 256)
            u = nn_dot(low_ref[...], w_ref[k, :, cols])
            value, slope = gelu_and_slope(u)
            out_cols = pl.ds(pl.multiple_of(k * 1536 + n * 256, 256), 256)
            act_ref[:, out_cols] = value.astype(bf16)
            slope_ref[:, out_cols] = slope.astype(bf16)


def up_forward(index, low, pieces):
    return staged_call(
        up_kernel,
        [index],
        [low],
        pieces,
        [
            shaped(bf16, 512, 3072),
            shaped(bf16, 512, 3072),
        ],
        [
            pltpu.VMEM((2, 768, 1536), bf16),
            pltpu.SemaphoreType.DMA((32,)),
        ],
        18,
    )


def thirds(v):
    high = v.astype(bf16)
    rest = v - high.astype(f32)
    middle = rest.astype(bf16)
    return high, middle, (rest - middle.astype(f32)).astype(bf16)


def down_kernel(ready, idx_ref, seg_row_ref, act_ref, unit_one_ref, par_ref, *refs):
    unit_ref, inv_ref, frag_ref, frag_low_ref, size_ref, w_ref, result_ref, sems = refs[4:]
    copies = piece_copies(idx_ref, 0, refs[:4], w_ref, 192, sems, 0)
    for copy in copies:
        copy.start()
    ready()
    for copy in copies:
        copy.wait()
    for k in range(2):
        result_ref[:, k * 384 : (k + 1) * 384] = nn_dot(act_ref[...], w_ref[k])
    pooled = jnp.zeros((32, 768), f32)
    for b in range(4):
        rows = slice(b * 128, (b + 1) * 128)
        one = unit_one_ref[rows, :] * par_ref[0:1, :] + par_ref[1:2, :]
        unit, inv = row_norm(one + result_ref[rows, :])
        unit_ref[rows, :] = unit
        inv_ref[rows, :] = jnp.broadcast_to(inv, (128, 128))
        two = unit * par_ref[2:3, :] + par_ref[3:4, :]
        member = lax.broadcasted_iota(jnp.int32, (32, 128), 0) == seg_row_ref[:, rows]
        member = jnp.where(member, 1.0, 0.0).astype(bf16)
        for part in thirds(two):
            pooled += nn_dot(member, part)
    size = lax.rsqrt(jnp.sum(pooled * pooled, -1, keepdims=True) + unit_eps)
    frag = pooled * size
    frag_ref[...] = frag
    frag_low_ref[...] = frag.astype(bf16)
    size_ref[...] = jnp.broadcast_to(size, (32, 128))


def down_forward(index, seg_row, act, unit_one, params, pieces):
    return staged_call(
        down_kernel,
        [index],
        [seg_row, act, unit_one, params],
        pieces,
        [
            shaped(f32, 512, 768),
            shaped(f32, 512, 128),
            shaped(f32, 32, 768),
            shaped(bf16, 32, 768),
            shaped(f32, 32, 128),
        ],
        [
            pltpu.VMEM((2, 3072, 384), bf16),
            pltpu.VMEM((512, 768), f32),
            pltpu.SemaphoreType.DMA((32,)),
        ],
        10,
    )


def back_norm(upstream, unit, inv, gain):
    scaled = upstream * gain
    return inv * (
        scaled
        - jnp.mean(scaled, -1, keepdims=True)
        - unit * jnp.mean(scaled * unit, -1, keepdims=True)
    )


def loss_kernel(
    ready, idx_ref, heat_ref, seg_col_ref, partner_ref, own_weight_ref, side_ref,
    frag_ref, size_ref, unit_ref, inv_ref, par_ref, slope_ref, *refs
):
    blocks, down_pieces = refs[:8], refs[8:12]
    loss_ref, low_own_ref, low_other_ref, gup_own_ref, gup_other_ref, two_ref, gains_ref = refs[12:19]
    all_ref, down_ref, low_ref, spread_ref, sems, w_sems = refs[19:]
    copies = []
    for number in range(32):
        row = pl.multiple_of(idx_ref[1 + number], 16)
        copies.append(
            pltpu.make_async_copy(
                blocks[number // 4].at[number % 4], all_ref.at[pl.ds(row, 32), :], sems.at[number]
            )
        )
    core = idx_ref[33]
    down_copies = piece_copies(idx_ref, 34, down_pieces, down_ref, 192, w_sems, 0)
    for copy in copies:
        copy.start()
    for copy in copies:
        copy.wait()
    ready(1, 2, 3)
    ready.copies_in[9].start()
    for copy in down_copies:
        copy.start()
    base = idx_ref[0]
    inv_heat = 1.0 / heat_ref[0]
    tally = 1024
    mine = all_ref[pl.ds(pl.multiple_of(base, 16), 32), :]
    grid = (nt_dot(mine, all_ref[...]) - 1.0) * inv_heat
    across = lax.broadcasted_iota(jnp.int32, (32, tally), 1)
    down = lax.broadcasted_iota(jnp.int32, (32, tally), 0) + base
    powers = jnp.where(across == down, 0.0, jnp.exp(grid))
    total = jnp.sum(powers, -1, keepdims=True)
    eye = lax.broadcasted_iota(jnp.int32, (32, 32), 0) == lax.broadcasted_iota(jnp.int32, (32, 32), 1)
    partner = jnp.sum(jnp.where(eye, partner_ref[...].astype(f32), 0.0), -1, keepdims=True)
    own_weight = jnp.sum(jnp.where(eye, own_weight_ref[...], 0.0), -1, keepdims=True)
    chosen = across == partner.astype(jnp.int32)
    target = jnp.sum(jnp.where(chosen, grid, 0.0), -1, keepdims=True)
    terms = own_weight * (jnp.log(total) - target)
    loss_ref[...] = jnp.broadcast_to(jnp.sum(terms, 0, keepdims=True) / tally, (8, 128))
    picked = jnp.where(chosen, 1.0, 0.0)
    pull = (powers / total - picked) * (own_weight * (inv_heat / tally))
    totals = [jnp.zeros((1, 128), f32) for _ in range(8)]
    number = lax.broadcasted_iota(jnp.int32, (128, 128), 0)
    same = number == lax.broadcasted_iota(jnp.int32, (128, 128), 1)
    weights = []
    for big in range(2):
        spread_ref[...] = nt_dot(all_ref[big * 512 : (big + 1) * 512, :], all_ref[...])
        for b in range(big * 4, big * 4 + 4):
            inside = slice((b - big * 4) * 128, (b - big * 4 + 1) * 128)
            for n in range(8):
                spread = jnp.exp((spread_ref[inside, n * 128 : (n + 1) * 128] - 1.0) * inv_heat)
                if n == b:
                    spread = jnp.where(same, 0.0, spread)
                totals[n] += jnp.sum(spread, 0, keepdims=True)
            side = jnp.concatenate(
                [
                    side_ref[n % 2, (n // 2) * 48 : (n // 2) * 48 + 32, :].astype(f32)
                    for n in range(b * 4, b * 4 + 4)
                ],
                0,
            ).T
            weights.append(side[4:5] + side[5:6] + side[6:7])
    totals, weights = jnp.concatenate(totals, 1), jnp.concatenate(weights, 1)
    column_pull = (powers / totals - picked) * (weights * (inv_heat / tally))
    both = jnp.concatenate([pull.astype(bf16), column_pull.astype(bf16)], 0)
    both = nn_dot(both, all_ref[...])
    grad = both[:32] + both[32:]
    ready(0, 4, 5, 6, 7, 8)
    frag = frag_ref[...]
    pooled = size_ref[:, 0:1] * (grad - frag * jnp.sum(grad * frag, -1, keepdims=True))
    stacked = jnp.concatenate(thirds(pooled), 0)
    gain_two = jnp.zeros((1, 768), f32)
    shift_two = jnp.zeros((1, 768), f32)
    for b in range(4):
        rows = slice(b * 128, (b + 1) * 128)
        slot = lax.broadcasted_iota(jnp.int32, (128, 96), 1) % 32
        member = jnp.where(slot == seg_col_ref[rows, :], 1.0, 0.0).astype(bf16)
        upstream = nn_dot(member, stacked)
        unit = unit_ref[rows, :]
        back = back_norm(upstream, unit, inv_ref[rows, 0:1], par_ref[2:3, :])
        two_ref[rows, :] = back
        low_ref[rows, :] = back.astype(bf16)
        gain_two += jnp.sum(upstream * unit, 0, keepdims=True)
        shift_two += jnp.sum(upstream, 0, keepdims=True)
    halves = (core, 1 - core)
    for half, ref in zip(halves, (low_own_ref, low_other_ref)):
        ref[...] = low_ref[:, pl.ds(pl.multiple_of(half * 384, 128), 384)]
    ready.put(0, 1, 2, 5)
    ready(9)
    for copy in down_copies:
        copy.wait()
    for half, gup_ref in zip(halves, (gup_own_ref, gup_other_ref)):

        @pl.loop(0, 6)
        def _(n):
            cols = pl.ds(pl.multiple_of(n * 256, 256), 256)
            wide = pl.ds(pl.multiple_of(half * 1536 + n * 256, 256), 256)
            g = sum(
                nt_dot(low_ref[:, k * 384 : (k + 1) * 384], down_ref[k, wide, :])
                for k in range(2)
            )
            gup_ref[:, cols] = (g * slope_ref[:, wide].astype(f32)).astype(bf16)

        if gup_ref is gup_own_ref:
            ready.put(3)

    gains_ref[...] = jnp.concatenate([gain_two, shift_two, jnp.zeros((6, 768), f32)], 0)


def loss_backward(index, heat, arrays, pieces):
    return staged_call(
        loss_kernel,
        [index, heat],
        arrays,
        pieces,
        [
            shaped(f32, 8, 128),
            shaped(bf16, 512, 384),
            shaped(bf16, 512, 384),
            shaped(bf16, 512, 1536),
            shaped(bf16, 512, 1536),
            shaped(f32, 512, 768),
            shaped(f32, 8, 768),
        ],
        [
            pltpu.VMEM((1024, 768), bf16),
            pltpu.VMEM((2, 3072, 384), bf16),
            pltpu.VMEM((512, 768), bf16),
            pltpu.VMEM((512, 1024), f32),
            pltpu.SemaphoreType.DMA((32,)),
            pltpu.SemaphoreType.DMA((32,)),
        ],
        18,
        (9,),
    )


def ffn_back_kernel(
    ready, idx_ref, gup_own_ref, gup_other_ref, two_ref, unit_ref, inv_ref, par_ref, *refs
):
    pieces = refs[:8]
    resid_ref, att_ref, own_ref, other_ref, gains_ref, up_ref, sems = refs[8:]
    copies = piece_copies(idx_ref, 0, pieces, up_ref, 48, sems, 0)
    for copy in copies:
        copy.start()
    ready()
    for copy in copies:
        copy.wait()
    core = idx_ref[0]
    for n in range(3):
        cols = slice(n * 256, (n + 1) * 256)
        resid_ref[:, cols] = (
            two_ref[:, cols]
            + nt_dot(gup_own_ref[...], up_ref[core, cols, :])
            + nt_dot(gup_other_ref[...], up_ref[1 - core, cols, :])
        )
    gain_sum = jnp.zeros((1, 768), f32)
    shift_sum = jnp.zeros((1, 768), f32)
    for b in range(4):
        rows = slice(b * 128, (b + 1) * 128)
        one = resid_ref[rows, :]
        unit = unit_ref[rows, :]
        back = back_norm(one, unit, inv_ref[rows, 0:1], par_ref[0:1, :])
        resid_ref[rows, :] = back
        att_ref[rows, :] = back.astype(bf16)
        gain_sum += jnp.sum(one * unit, 0, keepdims=True)
        shift_sum += jnp.sum(one, 0, keepdims=True)
    for half, ref in ((core, own_ref), (1 - core, other_ref)):
        ref[...] = att_ref[:, pl.ds(pl.multiple_of(half * 384, 128), 384)]
    gains_ref[...] = jnp.concatenate([gain_sum, shift_sum, jnp.zeros((6, 768), f32)], 0)


def ffn_backward(index, arrays, pieces):
    return staged_call(
        ffn_back_kernel,
        [index],
        arrays,
        pieces,
        [
            shaped(f32, 512, 768),
            shaped(bf16, 512, 768),
            shaped(bf16, 512, 384),
            shaped(bf16, 512, 384),
            shaped(f32, 8, 768),
        ],
        [pltpu.VMEM((2, 768, 1536), bf16), pltpu.SemaphoreType.DMA((32,))],
        9,
    )


def heads_back(half, gm_ref, qkv_ref, lse_ref, bias_ref, gqkv_ref, gk_ref, gv_ref):
    lane = lax.broadcasted_iota(jnp.int32, (128, 128), 1)
    left = lane < HD
    gk_ref[...] = jnp.zeros_like(gk_ref)
    gv_ref[...] = jnp.zeros_like(gv_ref)

    @pl.loop(0, 3)
    def _(spot):
        pair = half * 3 + spot
        for b in range(4):
            rows = pl.ds(b * 128, 128)
            keys = pl.ds(WINDOWS[b], 256)
            q = qkv_ref[pair, rows, :]
            k = qkv_ref[pair + 6, keys, :]
            v = qkv_ref[pair + 12, keys, :]
            gm = gm_ref[rows, pl.ds(pl.multiple_of(spot * 128, 128), 128)]
            q, gm = two_heads(q), two_heads(gm)
            stats = lse_ref[rows, :]
            lse = jnp.concatenate(
                [
                    jnp.sum(jnp.where(lane == pair * 2 + h, stats, 0.0), -1, keepdims=True)
                    for h in range(2)
                ],
                0,
            )
            p = jnp.exp(nt_dot(q, k) + bias_ref[b] - lse)
            gp = nt_dot(gm, v)
            gs = (p * (gp - jnp.sum(gp * p, -1, keepdims=True))).astype(bf16)
            gq = nn_dot(gs, k)
            gq = (jnp.where(left, gq[:128], gq[128:]) * SCALE).astype(bf16)
            gqkv_ref[rows, pl.ds(pl.multiple_of(spot * 128, 128), 128)] = gq
            gk_ref[spot, keys, :] += tn_dot(gs, q)
            gv_ref[spot, keys, :] += tn_dot(p.astype(bf16), gm)
        for third, ref in ((1, gk_ref), (2, gv_ref)):
            cols = pl.ds(pl.multiple_of(third * 384 + spot * 128, 128), 128)
            gqkv_ref[:, cols] = ref[spot].astype(bf16)


def other_heads_kernel(ready, idx_ref, seg_row_ref, seg_col_ref, qkv_ref, lse_ref, att_ref, resid_ref, *refs
):
    pieces = refs[:8]
    gqkv_ref, gm_own_ref, part_ref = refs[8:11]
    w_ref, bias_ref, gm_ref, gk_ref, gv_ref, sems = refs[11:]
    copies = piece_copies(idx_ref, 4, pieces, w_ref, 48, sems, 0)
    for copy in copies:
        copy.start()
    ready()
    for b in range(4):
        bias_ref[b] = window_bias(seg_row_ref[...], seg_col_ref[...], b)
    for copy in copies:
        copy.wait()
    core = idx_ref[4]
    half = 1 - core
    for side, ref in ((half, gm_ref), (core, gm_own_ref)):
        rows = pl.ds(pl.multiple_of(side * 384, 128), 384)
        ref[...] = sum(
            nt_dot(att_ref[:, k * 384 : (k + 1) * 384], w_ref[k, rows, 1152:1536])
            for k in range(2)
        ).astype(bf16)
    heads_back(half, gm_ref, qkv_ref, lse_ref, bias_ref, gqkv_ref, gk_ref, gv_ref)
    ready.put(0, 1)
    for n in range(3):
        cols = slice(n * 256, (n + 1) * 256)
        part_ref[:, cols] = resid_ref[:, cols] + nt_dot(gqkv_ref[...], w_ref[half, cols, :1152])


def other_heads(index, arrays, pieces):
    return staged_call(
        other_heads_kernel,
        [index],
        arrays,
        pieces,
        [
            shaped(bf16, 512, 1152),
            shaped(bf16, 512, 384),
            shaped(f32, 512, 768),
        ],
        [
            pltpu.VMEM((2, 768, 1664), bf16),
            pltpu.VMEM((4, 256, 256), f32),
            pltpu.VMEM((512, 384), bf16),
            pltpu.VMEM((3, 512, 128), f32),
            pltpu.VMEM((3, 512, 128), f32),
            pltpu.SemaphoreType.DMA((32,)),
        ],
        17,
    )


def own_heads_kernel(ready, idx_ref, seg_row_ref, seg_col_ref, qkv_ref, lse_ref, gm_ref, part_ref, *refs
):
    pieces = refs[:4]
    gqkv_ref, outs = refs[4], refs[5:9]
    w_ref, bias_ref, gk_ref, gv_ref, et_ref, sems = refs[9:]
    copies = []
    for number in range(16):
        row = pl.multiple_of(idx_ref[36 + number], 16)
        copies.append(
            pltpu.make_async_copy(
                pieces[number // 4].at[number % 4], w_ref.at[pl.ds(row, 48), :], sems.at[number]
            )
        )
    for copy in copies:
        copy.start()
    ready()
    for b in range(4):
        bias_ref[b] = window_bias(seg_row_ref[...], seg_col_ref[...], b)
    core = idx_ref[4]
    heads_back(core, gm_ref, qkv_ref, lse_ref, bias_ref, gqkv_ref, gk_ref, gv_ref)
    ready.put(0)
    for copy in copies:
        copy.wait()
    for n in range(3):
        cols = slice(n * 256, (n + 1) * 256)
        total = part_ref[:, cols] + nt_dot(gqkv_ref[...], w_ref[cols, :1152])
        et_ref[cols, :] = total.astype(bf16).T
    for j in range(4):
        outs[j][...] = et_ref[pl.ds(pl.multiple_of(idx_ref[j], 16), 192), :]


def own_heads(index, arrays, pieces):
    return staged_call(
        own_heads_kernel,
        [index],
        arrays,
        pieces,
        [
            shaped(bf16, 512, 1152),
            shaped(bf16, 192, 512),
            shaped(bf16, 192, 512),
            shaped(bf16, 192, 512),
            shaped(bf16, 192, 512),
        ],
        [
            pltpu.VMEM((768, 1664), bf16),
            pltpu.VMEM((4, 256, 256), f32),
            pltpu.VMEM((3, 512, 128), f32),
            pltpu.VMEM((3, 512, 128), f32),
            pltpu.VMEM((768, 512), bf16),
            pltpu.SemaphoreType.DMA((16,)),
        ],
        15,
    )


def to_slots(idx_ref, whole_ref, keep_ref, away_ref):
    for slot in range(8):
        keep_ref[slot] = whole_ref[idx_ref[slot]]
        away_ref[slot] = whole_ref[idx_ref[8 + slot]]


def down_grad_kernel(ready, idx_ref, act_ref, act_o_ref, g_ref, g_o_ref, keep_ref, away_ref, whole_ref):
    ready()
    for n in range(8):
        cols = slice(n * 384, (n + 1) * 384)
        total = tn_dot(act_ref[:, cols], g_ref[...]) + tn_dot(act_o_ref[:, cols], g_o_ref[...])
        total = total.astype(bf16)
        whole_ref[2 * n] = total[:192]
        whole_ref[2 * n + 1] = total[192:]
    to_slots(idx_ref, whole_ref, keep_ref, away_ref)


def down_grad(index, arrays):
    return staged_call(
        down_grad_kernel,
        [index],
        arrays,
        [],
        [shaped(bf16, 8, 192, 384)] * 2,
        [pltpu.VMEM((16, 192, 384), bf16)],
        7,
    )


def store_chunks(whole_ref, cols, total):
    for f in range(16):
        whole_ref[f, :, cols] = total[f * 48 : (f + 1) * 48]


def up_out_grad_kernel(
    ready, idx_ref, low_ref, low_o_ref, g_ref, g_o_ref, mixed_ref, mixed_o_ref, ga_ref, ga_o_ref, norms_ref,
    keep_ref, away_ref, whole_ref, t_ref,
):
    ready()
    t_ref[0] = low_ref[...].T
    t_ref[1] = low_o_ref[...].T
    for n in range(3):
        cols = slice(n * 512, (n + 1) * 512)
        total = nn_dot(t_ref[0], g_ref[:, cols]) + nn_dot(t_ref[1], g_o_ref[:, cols])
        store_chunks(whole_ref, cols, total.astype(bf16))
    t_ref[0] = mixed_ref[...].T
    t_ref[1] = mixed_o_ref[...].T
    total = nn_dot(t_ref[0], ga_ref[...]) + nn_dot(t_ref[1], ga_o_ref[...])
    store_chunks(whole_ref, slice(1536, 1920), total.astype(bf16))
    norms = norms_ref[...].T.astype(bf16)
    norms = jnp.concatenate([norms, jnp.zeros((768, 120), bf16)], 1)
    store_chunks(whole_ref, slice(1920, 2048), norms)
    to_slots(idx_ref, whole_ref, keep_ref, away_ref)


def up_out_grad(index, arrays):
    return staged_call(
        up_out_grad_kernel,
        [index],
        arrays,
        [],
        [
            shaped(bf16, 8, 48, 2048),
            shaped(bf16, 8, 48, 2048),
        ],
        [
            pltpu.VMEM((16, 48, 2048), bf16),
            pltpu.VMEM((2, 768, 512), bf16),
        ],
        8,
    )


def in_grad_kernel(ready, idx_ref, e_ref, e_o_ref, g_ref, g_o_ref, keep_ref, away_ref, whole_ref, t_ref):
    ready()
    t_ref[0] = e_ref[...].T
    t_ref[1] = e_o_ref[...].T
    for t in range(3):
        cols = slice(t * 384, (t + 1) * 384)
        total = nn_dot(t_ref[0], g_ref[:, cols]) + nn_dot(t_ref[1], g_o_ref[:, cols])
        store_chunks(whole_ref, cols, total.astype(bf16))
    to_slots(idx_ref, whole_ref, keep_ref, away_ref)


def in_grad(index, arrays):
    return staged_call(
        in_grad_kernel,
        [index],
        arrays,
        [],
        [
            shaped(bf16, 8, 48, 1152),
            shaped(bf16, 8, 48, 1152),
        ],
        [
            pltpu.VMEM((16, 48, 1152), bf16),
            pltpu.VMEM((2, 768, 512), bf16),
        ],
        6,
    )


def optimizer_kernel(ready, core_ref, fix_ref, totals_ref, totals_o_ref, *refs):
    ready(*range(10))
    own, other = refs[:4], refs[4:8]
    params, outs = refs[8:26], refs[26:46]
    table_ref = refs[46]
    core = core_ref[0]
    totals = totals_ref[...] + totals_o_ref[...]
    norm = jnp.sqrt(totals[:, 0:1])
    outs[0][...] = totals[:, 1:2]
    outs[1][...] = norm
    factor = clip_norm / jnp.maximum(norm, clip_norm)
    fix_one, fix_two = 1.0 / fix_ref[0], 1.0 / fix_ref[1]

    def update(number, spot, grad, rate, decay):
        w_ref, first_ref, second_ref = params[3 * number : 3 * number + 3]
        grad = grad.astype(f32) * factor
        weight = w_ref[spot]
        first = beta_one * first_ref[spot] + (1.0 - beta_one) * grad
        second = beta_two * second_ref[spot] + (1.0 - beta_two) * grad * grad
        step = (first * fix_one) / (jnp.sqrt(second * fix_two) + adam_eps)
        outs[2 + 3 * number][spot] = weight - rate * (step + decay * weight)
        outs[3 + 3 * number][spot] = first
        outs[4 + 3 * number][spot] = second

    every = slice(None)
    halves = ((core, own), (1 - core, other))

    def columns(half, width, start=0):
        return pl.ds(pl.multiple_of(half * width + start, 128), width)

    def opened(number):
        ready(*range(10 + 3 * number, 13 + 3 * number))

    def done(number):
        ready.put(*range(2 + 3 * number, 5 + 3 * number))

    opened(3)
    for half, (_, _, up_out, _) in halves:
        for t in range(3):
            spot = pl.ds(pl.multiple_of(half * 1536 + t * 512, 128), 512)
            update(3, (every, spot), up_out[:, t * 512 : (t + 1) * 512], rate_matrix, decay_rate)
    done(3)
    opened(4)
    for half, (_, _, _, down) in halves:
        for t in range(4):
            rows = slice(t * 48, (t + 1) * 48)
            update(4, (rows, columns(half, 384)), down[rows, :], rate_matrix, decay_rate)
    done(4)
    opened(1)
    for half, (_, into, _, _) in halves:
        for t in range(3):
            update(
                1,
                (every, columns(half, 384, t * 768)),
                into[:, t * 384 : (t + 1) * 384],
                rate_matrix,
                decay_rate,
            )
    done(1)
    opened(0)
    for half, (table, _, _, _) in halves:
        table_ref[:, columns(half, VOCAB_HALF)] = table[...]
    vocab = params[0].shape[1]
    for low in range(0, vocab, 512):
        spot = slice(low, min(vocab, low + 512))
        update(0, (every, spot), table_ref[:, spot], rate_embed, decay_rate)
    done(0)
    opened(2)
    for half, (_, _, up_out, _) in halves:
        update(2, (every, columns(half, 384)), up_out[:, 1536:1920], rate_matrix, decay_rate)
    done(2)
    opened(5)
    norms = jnp.where(core == 0, own[2][:, 1920:].astype(f32), other[2][:, 1920:].astype(f32))
    update(5, (every, every), norms.T[:4], rate_norm, 0.0)


def optimizer(core, fixes, totals, totals_o, own, other, params):
    return staged_call(
        optimizer_kernel,
        [core, fixes],
        [totals, totals_o, *own, *other, *params],
        [],
        [
            shaped(f32, 1, 1),
            shaped(f32, 1, 1),
            *[shaped(f32, *p.shape) for p in params],
        ],
        [
            pltpu.VMEM((48, VOCAB_PAD), bf16),
        ],
        8,
    )


def per_device_links(
    kmer_identifiers,
    slot_fragment_ids,
    mirror_fragment_index,
    fragment_weight,
    affinity_heat,
    optimizer_iteration,
    lexicon_table,
    lexicon_first_moment,
    lexicon_raw_moment,
    query_key_value_maps,
    qkv_first_moment,
    qkv_raw_moment,
    attention_exit_map,
    exit_first_moment,
    exit_raw_moment,
    widening_matrix_in,
    widening_first_moment,
    widening_raw_moment,
    narrowing_matrix_out,
    narrowing_first_moment,
    narrowing_raw_moment,
    layernorm_scale_bias,
    layernorm_first_moment,
    layernorm_raw_moment,
):
    place = Place()
    core = place.core
    vocab = lexicon_table.shape[0]
    core_index = core.astype(jnp.int32).reshape(1)
    both_cut, table_cut, table_half, down_half = prepare(
        core_index,
        [
            lexicon_table.T,
            query_key_value_maps,
            attention_exit_map,
            widening_matrix_in,
            narrowing_matrix_out,
            layernorm_scale_bias,
            kmer_identifiers,
            fragment_weight.reshape(1, 32),
        ],
    )
    near = [send(table_half, FIRST), send(table_half, SECOND)]
    near.append(send(near[0], SECOND))
    both_far = z_sends(both_cut)
    slots = [place.y * 2 + place.x]
    for side in (core, 1 - core):
        slots += [place.plane_slot(side, a, b) for a, b in ((1, 0), (0, 1), (1, 1))]
    index = jnp.stack(
        [s * 48 for s in slots] + [core * VOCAB_HALF, (1 - core) * VOCAB_HALF]
    ).astype(jnp.int32)
    down_first = send(after(down_half, near[0]), FIRST)
    others = send(after(jnp.stack(near), down_first, *both_far), CORE)
    id_parts = jnp.stack([p[:8, 3200:] for p in both_far]).astype(f32)
    ids_z = (id_parts[:, :4] * 64.0 + id_parts[:, 4:]).astype(jnp.int32)
    in_out_column = jnp.stack([p[:, :1664] for p in both_far])
    in_out_mine = plane_sends(in_out_column, True)
    found = lookup(index, ids_z, [table_cut] + near + [others])
    up_column = after(jnp.stack([p[:, 1664:3200] for p in both_far]), *found)
    columns = [found[0]] + [send(found[j], ZS[j]) for j in (1, 2, 3)]
    in_out = both_cores(together(in_out_mine, *columns))
    up_column = after(up_column, in_out_mine[3])
    up_mine = [up_column, send(up_column, FIRST), send(up_column, SECOND)]
    down_pair = jnp.stack([down_half, after(down_first, *found)])
    down_far = z_sends(after(down_pair, *columns))
    seg_row = slot_fragment_ids
    seg_col = slot_fragment_ids.reshape(512, 1)
    index_48 = piece_index(place, 48)
    z_index = jnp.stack([(place.z ^ j) * 192 for j in range(4)]).astype(jnp.int32)
    attention_index = jnp.concatenate([z_index, index_48])
    embedded, qkv, lse, mixed, unit_one, inv_one, normed_low, params, side = attention_forward(
        attention_index, seg_row, seg_col, columns, in_out
    )
    *up_mine, d_one, d_two, d_three = together(up_mine + down_far[1:], normed_low)
    up_mine.append(send(up_mine[1], SECOND))
    down_one = jnp.stack([down_far[0], d_one, d_two, d_three]).reshape(8, 192, 384)
    down_two = send(down_one, SECOND)
    down_one_o = send(down_one, CORE)
    up_w = both_cores(up_mine)
    activated, slope = up_forward(index_48, normed_low, up_w)
    down_two, down_one_o = together([down_two, down_one_o], activated)
    down_w = [down_one, down_two, down_one_o, send(down_two, CORE)]
    index_192 = pair_index(place, 192)
    base = (lax.axis_index("fsdp") * 2 + core) * 32
    unit_two, inv_two, unit_rows, unit_low, unit_scale = down_forward(
        index_192, seg_row, activated, unit_one, params, down_w
    )
    embedded_o, mixed_o, normed_o, activated_o = (
        send(a, CORE) for a in (embedded, mixed, normed_low, activated)
    )
    column = jnp.stack([unit_low] + [send(unit_low, ZS[j]) for j in (1, 2, 3)])
    blocks = [column, send(column, FIRST), send(column, SECOND), send(column, BOTH)]
    blocks = blocks + [send(block, CORE) for block in blocks]
    index = [base]
    for who in (core, 1 - core):
        for a, b in ((0, 0), (1, 0), (0, 1), (1, 1)):
            index += [(place.chip(who, j, a, b) * 2 + who) * 32 for j in range(4)]
    index += [core]
    (
        loss_tile, grad_result_own, grad_result_x, grad_up_own, grad_up_x, grad_two, gains_two,
    ) = loss_backward(
        jnp.concatenate([jnp.stack(index).astype(jnp.int32), index_192]),
        affinity_heat.reshape(1),
        [
            seg_col,
            mirror_fragment_index.reshape(1, 32),
            fragment_weight.reshape(1, 32),
            side,
            unit_rows,
            unit_scale,
            unit_two,
            inv_two,
            params,
            slope,
        ],
        blocks + down_w,
    )
    slots = slot_index(place)
    grad_result_o = send(grad_result_x, CORE)
    ids_o = send(ids_z, CORE)
    grad_up_o = send(grad_up_x, CORE)
    spare = [embedded_o, mixed_o, normed_o, ids_o]
    down_keep, down_away = down_grad(
        slots, [after(activated, *spare), activated_o, grad_result_own, grad_result_o]
    )
    down_came = send(down_away, SECOND)
    grad_resid, grad_attended, grad_att_own, grad_att_x, gains_one = ffn_backward(
        index_48,
        [after(grad_up_own, down_away), grad_up_x, grad_two, unit_one, inv_one, params],
        up_w,
    )
    grad_att_o = send(grad_att_x, CORE)
    norms = jnp.concatenate([gains_one[:2], gains_two[:2], jnp.zeros((4, 768), f32)], 0)
    norms = norms + send(norms, CORE)
    up_out_keep, up_out_away = up_out_grad(
        slots,
        [
            normed_low,
            normed_o,
            grad_up_own,
            grad_up_o,
            mixed,
            mixed_o,
            grad_att_own,
            grad_att_o,
            norms,
        ],
    )
    up_out_came = send(up_out_away, SECOND)
    down_came = after(down_came, up_out_away)
    down_across = scatter_add(down_keep, down_came)
    down_came_two = send(down_across, FIRST)
    grad_qkv_x, grad_mixed_own, part = other_heads(
        attention_index,
        [seg_row, seg_col, qkv, lse, after(grad_attended, down_across), grad_resid],
        in_out,
    )
    grad_qkv_o = send(grad_qkv_x, CORE)
    down_came_two = after(down_came_two, part)
    down_here, down_far = scatter_here(down_keep, down_came, down_came_two)
    down_far_came = line_sends(down_far)
    grad_qkv_own, *outs = own_heads(
        attention_index,
        [seg_row, seg_col, qkv, lse, grad_mixed_own, after(part, *down_far)],
        in_out[:4],
    )
    far_cols = [send(outs[j], ZS[j]) for j in (1, 2, 3)]
    *down_far_came, up_out_came, grad_qkv_o = together(
        down_far_came + [up_out_came, grad_qkv_o], grad_qkv_own
    )
    up_out_across = scatter_add(up_out_keep, up_out_came)
    up_out_came_two = send(up_out_across, FIRST)
    in_keep, in_away = in_grad(
        slots, [embedded, embedded_o, after(grad_qkv_own, up_out_across), grad_qkv_o]
    )
    far_cols = together(far_cols, in_away)
    in_came = send(after(in_away, *far_cols), SECOND)
    token_cols = jnp.stack([outs[0]] + far_cols)
    token_cols_o = send(token_cols, CORE)
    up_out_here, up_out_far = scatter_here(
        up_out_keep, up_out_came, after(up_out_came_two, token_cols)
    )
    up_out_far_came = line_sends(up_out_far)
    plane = [place.plane_slot(core, a, b) * 48 for a, b in ((0, 0), (1, 0), (0, 1), (1, 1))]
    keep, away = token_sum(
        jnp.stack([core * VOCAB_HALF] + plane).astype(jnp.int32),
        after(ids_z, *up_out_far),
        ids_o,
        token_cols,
        token_cols_o,
    )
    came = send(away, SECOND)
    down_sum = line_sum(after(down_here, away), down_far_came)
    in_came = after(in_came, away)
    in_across = scatter_add(in_keep, in_came)
    in_came_two = send(in_across, FIRST)
    across = (keep[1].astype(f32) + came[1].astype(f32)).astype(bf16)
    came_two = send(across, FIRST)
    in_here, in_far = scatter_here(in_keep, in_came, after(in_came_two, across))
    in_far_came = line_sends(in_far)
    up_out_sum = line_sum(up_out_here, together(up_out_far_came, across))
    table_sum = keep[0].astype(f32) + came[0].astype(f32) + came_two.astype(f32)
    table_sum = table_sum.astype(bf16)
    in_sum = line_sum(in_here, together(in_far_came, table_sum))
    sums = [table_sum, in_sum, up_out_sum, down_sum]
    sums_o = [send(s, CORE) for s in together(sums, table_sum)]
    squares = sum(
        jnp.sum(jnp.square(p.astype(f32)))
        for p in (sums[0], sums[1], sums[2][:, :1920], sums[3])
    )
    norm_own = sums[2][:, 1920:1924].astype(f32)
    squares += jnp.where(core == 0, jnp.sum(norm_own * norm_own), 0.0)
    totals = jnp.concatenate([squares.reshape(1, 1), loss_tile[:1, :1]], 1)
    totals = all_sum(after(totals, *sums_o))
    count_now = optimizer_iteration.astype(f32)
    fixes = jnp.stack([1.0 - jnp.power(beta_one, count_now), 1.0 - jnp.power(beta_two, count_now)])
    results = optimizer(
        core_index,
        fixes,
        totals,
        send(totals, CORE),
        sums,
        sums_o,
        [
            lexicon_table.T,
            lexicon_first_moment.T,
            lexicon_raw_moment.T,
            query_key_value_maps,
            qkv_first_moment,
            qkv_raw_moment,
            attention_exit_map,
            exit_first_moment,
            exit_raw_moment,
            widening_matrix_in,
            widening_first_moment,
            widening_raw_moment,
            narrowing_matrix_out,
            narrowing_first_moment,
            narrowing_raw_moment,
            layernorm_scale_bias,
            layernorm_first_moment,
            layernorm_raw_moment,
        ],
    )
    results = list(results)
    results[:2] = [r[0, 0] for r in results[:2]]
    results[2:5] = [r.T for r in results[2:5]]
    return tuple(results)


def solution(mesh):
    in_specs = (
        P(("fsdp", "dp"), None),
        P(("fsdp", "dp"), None),
        P(("fsdp", "dp")),
        P(("fsdp", "dp")),
        P(),
        P(),
        P(None, "fsdp"),
        P(None, "fsdp"),
        P(None, "fsdp"),
        P("fsdp", None),
        P("fsdp", None),
        P("fsdp", None),
        P("fsdp", None),
        P("fsdp", None),
        P("fsdp", None),
        P("fsdp", None),
        P("fsdp", None),
        P("fsdp", None),
        P("fsdp", None),
        P("fsdp", None),
        P("fsdp", None),
        P(None, "fsdp"),
        P(None, "fsdp"),
        P(None, "fsdp"),
    )
    out_specs = (
        P(),
        P(),
        P(None, "fsdp"),
        P(None, "fsdp"),
        P(None, "fsdp"),
        P("fsdp", None),
        P("fsdp", None),
        P("fsdp", None),
        P("fsdp", None),
        P("fsdp", None),
        P("fsdp", None),
        P("fsdp", None),
        P("fsdp", None),
        P("fsdp", None),
        P("fsdp", None),
        P("fsdp", None),
        P("fsdp", None),
        P(None, "fsdp"),
        P(None, "fsdp"),
        P(None, "fsdp"),
    )
    own_plan = dict(mesh.shape) == {"fsdp": 16, "dp": 2}
    return jax.shard_map(
        per_device_links if own_plan else per_device, mesh=mesh, in_specs=in_specs, out_specs=out_specs, check_vma=False
    )
```

```python
import jax
import jax.numpy as jnp
from jax import lax
from jax.experimental import pallas as pl
from jax.experimental.pallas import tpu as pltpu
from jax.sharding import PartitionSpec as P

MODEL_WIDTH = 768
H = 12
HD = 64
SEG_ROW = 32


largest_value = lax.Precision.HIGHEST
beta_one = 0.9
beta_two = 0.999
adam_eps = 1e-12
decay_rate = 0.01
rate_matrix = 0.1
rate_embed = 1.0
rate_norm = 1.0
clip_norm = 0.001
norm_eps = 1e-05
unit_eps = 1e-06


def layer_norm(inputs, gain_row, shifts):
    center = inputs - jnp.mean(inputs, -1, keepdims=True)
    inv_std = lax.rsqrt(jnp.mean(center * center, -1, keepdims=True) + norm_eps)
    normed = center * inv_std
    return (normed * gain_row + shifts, normed, inv_std)


def norm_back(upstream, normed, inv_std, gain_row):
    scaled = upstream * gain_row
    grad_in = inv_std * (
        scaled
        - jnp.mean(scaled, -1, keepdims=True)
        - normed * jnp.mean(scaled * normed, -1, keepdims=True)
    )
    return (grad_in, jnp.sum(upstream * normed, 0), jnp.sum(upstream, 0))


def masked_scores(query_rows, key_rows, segment_rows):
    raw_scores = jnp.einsum(
        "bqhd,bkhd->bhqk", query_rows, key_rows, preferred_element_type=jnp.float32
    )
    same_segment = segment_rows[:, None, :, None] == segment_rows[:, None, None, :]
    return jnp.where(same_segment, raw_scores * HD ** (-0.5), -1e30)


def layer_forward(gathered, token_rows, segment_rows):
    (
        lexicon_table,
        query_key_value_maps,
        attention_exit_map,
        widening_matrix_in,
        narrowing_matrix_out,
        layernorm_scale_bias,
    ) = gathered
    batch_row_list, sequence_length = token_rows.shape
    embedded = jnp.take(lexicon_table, token_rows.reshape(-1), axis=0)
    qkv_all = jnp.dot(embedded, query_key_value_maps, preferred_element_type=jnp.float32).astype(
        jnp.bfloat16
    )
    qkv_all = qkv_all.reshape(batch_row_list, sequence_length, 3, H, HD)
    query_rows, key_rows, value_rows = (qkv_all[:, :, 0], qkv_all[:, :, 1], qkv_all[:, :, 2])
    scores = masked_scores(query_rows, key_rows, segment_rows)
    row_max = jnp.max(scores, -1, keepdims=True)
    log_total = row_max + jnp.log(jnp.sum(jnp.exp(scores - row_max), -1, keepdims=True))
    attn_probs = jnp.exp(scores - log_total).astype(jnp.bfloat16)
    mixed_heads = jnp.einsum(
        "bhqk,bkhd->bqhd", attn_probs, value_rows, preferred_element_type=jnp.float32
    )
    mixed_heads = mixed_heads.reshape(batch_row_list * sequence_length, MODEL_WIDTH).astype(
        jnp.bfloat16
    )
    attended = jnp.dot(mixed_heads, attention_exit_map, preferred_element_type=jnp.float32)
    normed_one, unit_one, inv_one = layer_norm(
        embedded.astype(jnp.float32) + attended, layernorm_scale_bias[0], layernorm_scale_bias[1]
    )
    normed_low = normed_one.astype(jnp.bfloat16)
    up_proj = jnp.dot(normed_low, widening_matrix_in, preferred_element_type=jnp.float32)
    activated = jax.nn.gelu(up_proj, approximate=False).astype(jnp.bfloat16)
    ffn_result = jnp.dot(activated, narrowing_matrix_out, preferred_element_type=jnp.float32)
    second_normalized, unit_two, inv_two = layer_norm(
        normed_one + ffn_result, layernorm_scale_bias[2], layernorm_scale_bias[3]
    )
    group_member = (
        segment_rows[:, None, :] == jnp.arange(SEG_ROW, dtype=jnp.int32)[None, :, None]
    ).astype(jnp.float32)
    pooled_state = jnp.einsum(
        "nkz,nzh->nkh",
        group_member,
        second_normalized.reshape(batch_row_list, sequence_length, MODEL_WIDTH),
        precision=largest_value,
    )
    saved_state = (
        embedded,
        query_rows,
        key_rows,
        value_rows,
        log_total,
        mixed_heads,
        unit_one,
        inv_one,
        normed_low,
        up_proj,
        activated,
        unit_two,
        inv_two,
        group_member,
    )
    return (pooled_state.reshape(batch_row_list * SEG_ROW, MODEL_WIDTH), saved_state)


def layer_backward(gathered, saved_state, token_rows, segment_rows, pooled_gradient):
    (
        lexicon_table,
        query_key_value_maps,
        attention_exit_map,
        widening_matrix_in,
        narrowing_matrix_out,
        layernorm_scale_bias,
    ) = gathered
    (
        embedded,
        query_rows,
        key_rows,
        value_rows,
        log_total,
        mixed_heads,
        unit_one,
        inv_one,
        normed_low,
        up_proj,
        activated,
        unit_two,
        inv_two,
        group_member,
    ) = saved_state
    batch_row_list, sequence_length = token_rows.shape
    pooled_gradient = pooled_gradient.reshape(batch_row_list, SEG_ROW, MODEL_WIDTH)
    second_gradient = jnp.einsum(
        "got,goy->gty", group_member, pooled_gradient, precision=largest_value
    ).reshape(batch_row_list * sequence_length, MODEL_WIDTH)
    grad_resid_two, grad_gain_two, grad_shift_two = norm_back(
        second_gradient, unit_two, inv_two, layernorm_scale_bias[2]
    )
    grad_result = grad_resid_two.astype(jnp.bfloat16)
    grad_ffn_down = jnp.einsum(
        "nf,nd->fd", activated, grad_result, preferred_element_type=jnp.float32
    )
    grad_act = jnp.einsum(
        "nd,fd->nf", grad_result, narrowing_matrix_out, preferred_element_type=jnp.float32
    )
    gelu_value, gelu_pull = jax.vjp(
        lambda pre_act: jax.nn.gelu(pre_act, approximate=False), up_proj
    )
    grad_up = gelu_pull(grad_act)[0].astype(jnp.bfloat16)
    grad_ffn_up = jnp.einsum("nd,nf->df", normed_low, grad_up, preferred_element_type=jnp.float32)
    grad_one = grad_resid_two + jnp.einsum(
        "nf,df->nd", grad_up, widening_matrix_in, preferred_element_type=jnp.float32
    )
    grad_resid_one, grad_gain_one, grad_shift_one = norm_back(
        grad_one, unit_one, inv_one, layernorm_scale_bias[0]
    )
    grad_attended = grad_resid_one.astype(jnp.bfloat16)
    grad_project_out = jnp.einsum(
        "nc,nd->cd", mixed_heads, grad_attended, preferred_element_type=jnp.float32
    )
    grad_mixed = jnp.einsum(
        "nd,cd->nc", grad_attended, attention_exit_map, preferred_element_type=jnp.float32
    )
    grad_mixed = grad_mixed.astype(jnp.bfloat16).reshape(batch_row_list, sequence_length, H, HD)
    scores = masked_scores(query_rows, key_rows, segment_rows)
    attn_probs = jnp.exp(scores - log_total)
    probs_low = attn_probs.astype(jnp.bfloat16)
    grad_values = jnp.einsum(
        "bhqk,bqhd->bkhd", probs_low, grad_mixed, preferred_element_type=jnp.float32
    )
    grad_probs = jnp.einsum(
        "bqhd,bkhd->bhqk", grad_mixed, value_rows, preferred_element_type=jnp.float32
    )
    grad_scores = attn_probs * (grad_probs - jnp.sum(grad_probs * attn_probs, -1, keepdims=True))
    grad_scores = grad_scores.astype(jnp.bfloat16)
    grad_query = jnp.einsum(
        "bhqk,bkhd->bqhd", grad_scores, key_rows, preferred_element_type=jnp.float32
    ) * HD ** (-0.5)
    grad_keys = jnp.einsum(
        "bhqk,bqhd->bkhd", grad_scores, query_rows, preferred_element_type=jnp.float32
    ) * HD ** (-0.5)
    grad_qkv = (
        jnp.stack([grad_query, grad_keys, grad_values], 2)
        .reshape(batch_row_list * sequence_length, 3 * MODEL_WIDTH)
        .astype(jnp.bfloat16)
    )
    grad_project_in = jnp.einsum(
        "nd,nc->dc", embedded, grad_qkv, preferred_element_type=jnp.float32
    )
    grad_embedded = grad_resid_one + jnp.einsum(
        "nc,dc->nd", grad_qkv, query_key_value_maps, preferred_element_type=jnp.float32
    )
    grad_norms = jnp.stack([grad_gain_one, grad_shift_one, grad_gain_two, grad_shift_two])
    return (
        grad_embedded,
        grad_project_in,
        grad_project_out,
        grad_ffn_up,
        grad_ffn_down,
        grad_norms,
    )


def adam_update(weight, first, second, grad, fix_first, fix_second, rate, decay):
    first_new = beta_one * first + (1.0 - beta_one) * grad
    second_new = beta_two * second + (1.0 - beta_two) * grad * grad
    step_size = first_new / fix_first / (jnp.sqrt(second_new / fix_second) + adam_eps)
    return (weight - rate * (step_size + decay * weight), first_new, second_new)


def per_device(
    kmer_identifiers,
    slot_fragment_ids,
    mirror_fragment_index,
    fragment_weight,
    affinity_heat,
    optimizer_iteration,
    lexicon_table,
    lexicon_first_moment,
    lexicon_raw_moment,
    query_key_value_maps,
    qkv_first_moment,
    qkv_raw_moment,
    attention_exit_map,
    exit_first_moment,
    exit_raw_moment,
    widening_matrix_in,
    widening_first_moment,
    widening_raw_moment,
    narrowing_matrix_out,
    narrowing_first_moment,
    narrowing_raw_moment,
    layernorm_scale_bias,
    layernorm_first_moment,
    layernorm_raw_moment,
):
    masters = (
        lexicon_table,
        query_key_value_maps,
        attention_exit_map,
        widening_matrix_in,
        narrowing_matrix_out,
        layernorm_scale_bias,
    )
    firsts = (
        lexicon_first_moment,
        qkv_first_moment,
        exit_first_moment,
        widening_first_moment,
        narrowing_first_moment,
        layernorm_first_moment,
    )
    seconds = (
        lexicon_raw_moment,
        qkv_raw_moment,
        exit_raw_moment,
        widening_raw_moment,
        narrowing_raw_moment,
        layernorm_raw_moment,
    )
    rates = (rate_embed, rate_matrix, rate_matrix, rate_matrix, rate_matrix, rate_norm)
    decays = (decay_rate, decay_rate, decay_rate, decay_rate, decay_rate, 0.0)
    lowered = tuple((piece.astype(jnp.bfloat16) for piece in masters))
    gathered = (
        lax.all_gather(lowered[0], "fsdp", axis=1, tiled=True),
        lax.all_gather(lowered[1], "fsdp", axis=0, tiled=True),
        lax.all_gather(lowered[2], "fsdp", axis=0, tiled=True),
        lax.all_gather(lowered[3], "fsdp", axis=0, tiled=True),
        lax.all_gather(lowered[4], "fsdp", axis=0, tiled=True),
        lax.all_gather(lowered[5], "fsdp", axis=1, tiled=True),
    )
    pooled_state, saved_state = layer_forward(gathered, kmer_identifiers, slot_fragment_ids)
    unit_scale = lax.rsqrt(jnp.sum(pooled_state * pooled_state, -1, keepdims=True) + unit_eps)
    unit_rows = pooled_state * unit_scale
    unit_low = unit_rows.astype(jnp.bfloat16)
    every_unit = lax.all_gather(unit_low, ("fsdp", "dp"), axis=0, tiled=True)
    cosine_affinity_grid = jnp.einsum(
        "sd,td->st", unit_low, every_unit, preferred_element_type=jnp.float32
    )
    seg_local = pooled_state.shape[0]
    fragment_tally = every_unit.shape[0]
    shard_fragment_lines = lax.axis_index(("fsdp", "dp")) * seg_local + jnp.arange(
        seg_local, dtype=jnp.int32
    )
    field_sequence_array = jnp.arange(fragment_tally, dtype=jnp.int32)
    raw_affinity_values = jnp.where(
        shard_fragment_lines[:, None] == field_sequence_array[None, :],
        -1e30,
        cosine_affinity_grid / affinity_heat,
    )
    row_max = jnp.max(raw_affinity_values, -1, keepdims=True)
    log_total = row_max[:, 0] + jnp.log(jnp.sum(jnp.exp(raw_affinity_values - row_max), -1))
    chosen = mirror_fragment_index[:, None] == field_sequence_array[None, :]
    chosen_real_entry = chosen.astype(jnp.float32)
    target = jnp.sum(jnp.where(chosen, raw_affinity_values, 0.0), -1)
    contrast_objective = (
        lax.psum(jnp.sum(fragment_weight * (log_total - target)), ("fsdp", "dp")) / fragment_tally
    )
    exponent_probabilities = jnp.exp(raw_affinity_values - log_total[:, None])
    similarity_gradient = (
        (exponent_probabilities - chosen_real_entry)
        * fragment_weight[:, None]
        / (fragment_tally * affinity_heat)
    ).astype(jnp.bfloat16)
    grad_rows = jnp.dot(similarity_gradient, every_unit, preferred_element_type=jnp.float32)
    column_terms = jnp.einsum(
        "st,sd->td", similarity_gradient, unit_low, preferred_element_type=jnp.float32
    )
    grad_cols = lax.psum_scatter(column_terms, ("fsdp", "dp"), scatter_dimension=0, tiled=True)
    grad_unit = grad_rows + grad_cols
    pooled_gradient = unit_scale * (
        grad_unit - unit_rows * jnp.sum(grad_unit * unit_rows, -1, keepdims=True)
    )
    again = (
        lax.all_gather(lowered[0], "fsdp", axis=1, tiled=True),
        lax.all_gather(lowered[1], "fsdp", axis=0, tiled=True),
        lax.all_gather(lowered[2], "fsdp", axis=0, tiled=True),
        lax.all_gather(lowered[3], "fsdp", axis=0, tiled=True),
        lax.all_gather(lowered[4], "fsdp", axis=0, tiled=True),
        lax.all_gather(lowered[5], "fsdp", axis=1, tiled=True),
    )
    grads = layer_backward(again, saved_state, kmer_identifiers, slot_fragment_ids, pooled_gradient)
    vocab = lexicon_table.shape[0]
    rest = (
        lax.psum_scatter(grads[1], "fsdp", scatter_dimension=0, tiled=True),
        lax.psum_scatter(grads[2], "fsdp", scatter_dimension=0, tiled=True),
        lax.psum_scatter(grads[3], "fsdp", scatter_dimension=0, tiled=True),
        lax.psum_scatter(grads[4], "fsdp", scatter_dimension=0, tiled=True),
        lax.psum_scatter(grads[5], "fsdp", scatter_dimension=1, tiled=True),
    )
    column_rows = lax.all_to_all(
        grads[0].astype(jnp.bfloat16), "fsdp", split_axis=1, concat_axis=0, tiled=True
    ).astype(jnp.float32)
    all_tokens = lax.all_gather(kmer_identifiers.reshape(-1), "fsdp", axis=0, tiled=True)
    table_shard = jax.ops.segment_sum(column_rows, all_tokens, num_segments=vocab)
    shards = (table_shard, rest[0], rest[1], rest[2], rest[3], rest[4])
    shards = (
        lax.psum(shards[0].astype(jnp.bfloat16), "dp").astype(jnp.float32),
        lax.psum(shards[1].astype(jnp.bfloat16), "dp").astype(jnp.float32),
        lax.psum(shards[2].astype(jnp.bfloat16), "dp").astype(jnp.float32),
        lax.psum(shards[3].astype(jnp.bfloat16), "dp").astype(jnp.float32),
        lax.psum(shards[4].astype(jnp.bfloat16), "dp").astype(jnp.float32),
        lax.psum(shards[5].astype(jnp.bfloat16), "dp").astype(jnp.float32),
    )
    squares = sum((jnp.sum(piece * piece) for piece in shards))
    grad_norm = jnp.sqrt(lax.psum(squares, "fsdp"))
    factor = clip_norm / jnp.maximum(grad_norm, clip_norm)
    count_now = optimizer_iteration.astype(jnp.float32)
    fix_first = 1.0 - jnp.power(beta_one, count_now)
    fix_second = 1.0 - jnp.power(beta_two, count_now)
    updated = [
        adam_update(
            masters[number],
            firsts[number],
            seconds[number],
            shards[number] * factor,
            fix_first,
            fix_second,
            rates[number],
            decays[number],
        )
        for number in range(6)
    ]
    return (
        contrast_objective,
        grad_norm,
        updated[0][0],
        updated[0][1],
        updated[0][2],
        updated[1][0],
        updated[1][1],
        updated[1][2],
        updated[2][0],
        updated[2][1],
        updated[2][2],
        updated[3][0],
        updated[3][1],
        updated[3][2],
        updated[4][0],
        updated[4][1],
        updated[4][2],
        updated[5][0],
        updated[5][1],
        updated[5][2],
    )


AXES = ("fsdp", "dp")
VOCAB_PAD = 4352
VOCAB_HALF = VOCAB_PAD // 2
BIG_VMEM = pltpu.CompilerParams(vmem_limit_bytes=60 * 1024 * 1024)
bf16 = jnp.bfloat16
f32 = jnp.float32


def pairs_of(moved):
    spots = [(z, y, x, c) for z in range(4) for y in range(2) for x in range(2) for c in range(2)]

    def linear(spot):
        z, y, x, c = spot
        return ((z * 2 + y) * 2 + x) * 2 + c

    return [(linear(spot), linear(moved(*spot))) for spot in spots]


FIRST = pairs_of(lambda z, y, x, c: (z, y, x ^ 1, c) if c == 0 else (z, y ^ 1, x, c))
SECOND = pairs_of(lambda z, y, x, c: (z, y ^ 1, x, c) if c == 0 else (z, y, x ^ 1, c))
BOTH = pairs_of(lambda z, y, x, c: (z, y ^ 1, x ^ 1, c))
CORE = pairs_of(lambda z, y, x, c: (z, y, x, 1 - c))
ZS = [None] + [pairs_of(lambda z, y, x, c, j=j: (z ^ j, y, x, c)) for j in (1, 2, 3)]


def send(array, pairs):
    return lax.ppermute(array, AXES, pairs)


def after(array, *others):
    return lax.optimization_barrier((array,) + others)[0]


def together(arrays, *others):
    arrays = list(arrays)
    return list(lax.optimization_barrier((*arrays, *others)))[: len(arrays)]


class Place:
    def __init__(self):
        f = lax.axis_index("fsdp")
        self.core = lax.axis_index("dp")
        self.z, self.y, self.x = f // 4, (f // 2) % 2, f % 2

    def plane_slot(self, core, a, b):
        dy = jnp.where(core == 0, b, a)
        dx = jnp.where(core == 0, a, b)
        return (self.y ^ dy) * 2 + (self.x ^ dx)

    def chip(self, core, j, a, b):
        return (self.z ^ j) * 4 + self.plane_slot(core, a, b)


def z_sends(piece):
    return [piece] + [send(piece, ZS[j]) for j in (1, 2, 3)]


def z_column(piece):
    return jnp.stack(z_sends(piece))


def plane_sends(column, direct=False, gate=()):
    one = send(column, FIRST)
    two = send(column, SECOND)
    three = send(column, BOTH) if direct else send(after(one, *gate), SECOND)
    return [column, one, two, three]


def both_cores(mine):
    return mine + [send(block, CORE) for block in mine]


Z_ROWS, BY_FLIP, FRAGMENTS, BY_PAIR, SLOTS, LOOKUP, PLANE = 0, 4, 68, 102, 166, 182, 191
MY_CORE = FRAGMENTS + 33


def index_vector(place):
    core, other = place.core, 1 - place.core
    n = jnp.arange(32, dtype=jnp.int32)
    who, m = jnp.where(n < 16, core, other), n % 16
    chips = place.chip(who, m % 4, (m // 4) % 2, m // 8)
    pairs = place.chip(who, (m // 2) % 4, m % 2, m // 8)
    base = (lax.axis_index("fsdp") * 2 + core) * 32
    k = jnp.arange(7, dtype=jnp.int32)
    side, flips = jnp.where(k < 4, core, other), jnp.where(k < 4, k, k - 3)
    reached = place.plane_slot(side, flips % 2, flips // 2)
    parts = [
        (place.z ^ jnp.arange(4, dtype=jnp.int32)) * 192,
        who,
        chips * 48,
        base,
        (chips * 2 + who) * 32,
        core,
        who,
        pairs * 192,
        chips[:16],
        reached * 48,
        core * VOCAB_HALF,
        other * VOCAB_HALF,
        core * VOCAB_HALF,
        reached[:4] * 48,
    ]
    return jnp.concatenate([jnp.atleast_1d(p).astype(jnp.int32) for p in parts])


class Part:
    def __init__(self, ref, start):
        self.ref, self.start = ref, start

    def __getitem__(self, number):
        return self.ref[self.start + number]


def scatter_add(keep, came):
    return (keep[4:].astype(f32) + came[4:].astype(f32)).astype(bf16)


def scatter_here(keep, came, came_two):
    here = [
        keep[j].astype(f32) + came[j].astype(f32) + came_two[j].astype(f32) for j in range(4)
    ]
    return here[0], [h.astype(bf16) for h in here[1:]]


def line_sends(far):
    return [send(h, ZS[j]) for h, j in zip(far, (1, 2, 3))]


def line_sum(here, far):
    return (here + far[0].astype(f32) + far[1].astype(f32) + far[2].astype(f32)).astype(bf16)


def whole_copies(sources, targets, sems):
    return [
        pltpu.make_async_copy(source, target, sems.at[number])
        for number, (source, target) in enumerate(zip(sources, targets))
    ]


class Stage:
    def __init__(self, copies_in, copies_out, pairs, sems):
        self.copies_in, self.copies_out = dict(enumerate(copies_in)), dict(enumerate(copies_out))
        self.started, self.pairs, self.sems = [], pairs, sems

    def __call__(self, *which):
        for number in which or tuple(self.copies_in):
            self.copies_in.pop(number).wait()

    def put(self, *which):
        for number in which or tuple(self.copies_out):
            copy = self.copies_out.pop(number)
            copy.start()
            self.started.append(copy)

    def put_half(self, side, half, which, width):
        cols = pl.ds(pl.multiple_of(half * width, 128), width)
        for number in which:
            self.copies_out.pop(number, None)
            source, target = self.pairs[number]
            copy = pltpu.make_async_copy(
                source.at[:, cols], target.at[:, cols], self.sems.at[side * len(which) + number]
            )
            copy.start()
            self.started.append(copy)

    def finish(self):
        self.put(*tuple(self.copies_out))
        for copy in self.started:
            copy.wait()


def staged_call(body, scalars, arrays, pieces, shapes, scratch, cost, late=()):
    n_s, n_a, n_p, n_o = len(scalars), len(arrays), len(pieces), len(shapes)

    def kernel(*refs):
        smem, refs = [Part(r, s) for r, (_, s) in zip(refs, scalars)], refs[n_s:]
        hbm, refs = refs[:n_a], refs[n_a:]
        far, refs = refs[:n_p], refs[n_p:]
        out, refs = refs[:n_o], refs[n_o:]
        near_in, refs = refs[:n_a], refs[n_a:]
        near_out, refs = refs[:n_o], refs[n_o:]
        in_sems, out_sems, half_sems, refs = refs[0], refs[1], refs[2], refs[3:]
        copies = whole_copies(hbm, near_in, in_sems)
        for number, copy in enumerate(copies):
            if number not in late:
                copy.start()
        pairs = list(zip(near_out, out))
        stage = Stage(copies, whole_copies(near_out, out, out_sems), pairs, half_sems)
        body(stage, *smem, *near_in, *far, *near_out, *refs)
        stage.finish()

    in_hbm = pl.BlockSpec(memory_space=pltpu.HBM)
    return pl.pallas_call(
        kernel,
        out_shape=shapes,
        in_specs=[pl.BlockSpec(memory_space=pltpu.SMEM)] * n_s + [in_hbm] * (n_a + n_p),
        out_specs=[in_hbm] * n_o,
        scratch_shapes=[pltpu.VMEM(a.shape, a.dtype) for a in arrays]
        + [pltpu.VMEM(s.shape, s.dtype) for s in shapes]
        + [pltpu.SemaphoreType.DMA((n,)) for n in (n_a, n_o, 4)]
        + scratch,
        cost_estimate=pl.CostEstimate(flops=int(cost * 1e9), bytes_accessed=0, transcendentals=0),
        compiler_params=BIG_VMEM,
    )(*[vector for vector, _ in scalars], *arrays, *pieces)


def shaped(dtype, *dims):
    return jax.ShapeDtypeStruct(dims, dtype)


def one_hot(ids_row, start, count):
    spots = lax.broadcasted_iota(jnp.int32, (count, ids_row.shape[1]), 0) + start
    return jnp.where(spots == ids_row, 1.0, 0.0).astype(bf16)


def prepare_kernel(
    ready, core_ref, table_ref, in_ref, out_ref, up_ref, down_ref, norm_ref, ids_ref, weight_ref,
    both_ref, cut_ref, half_ref, down_half_ref,
):
    core = core_ref[0]

    def mine(ref, width, start=0):
        return ref[:, pl.ds(pl.multiple_of(start + core * width, 128), width)].astype(bf16)

    ready(1, 2, 3, 5, 6, 7)
    for t in range(3):
        both_ref[:, t * 384 : (t + 1) * 384] = mine(in_ref, 384, t * 768)
    both_ref[:, 1152:1536] = mine(out_ref, 384)
    rest = jnp.zeros((1, 16), f32)
    heavy = [jnp.concatenate([w.astype(f32), rest], 1) for w in thirds(weight_ref[...])]
    extra = jnp.concatenate([norm_ref[...]] + heavy + [jnp.zeros((121, 48), f32)], 0)
    both_ref[:, 1536:1664] = extra.T.astype(bf16)
    both_ref[:, 1664:3200] = mine(up_ref, 1536)
    ids = jnp.concatenate([ids_ref[:, k * 128 : (k + 1) * 128] for k in range(4)], 0)
    high = lax.shift_right_logical(ids, 6)
    ids = jnp.concatenate([high, ids - high * 64], 0).astype(f32).astype(bf16)
    both_ref[:, 3200:3328] = jnp.concatenate([ids, jnp.zeros((40, 128), bf16)], 0)
    ready.put(0)
    ready(0, 4)
    vocab = table_ref.shape[1]
    even = vocab - vocab % 128
    cut_ref[:, :even] = table_ref[:, :even].astype(bf16)
    last = [table_ref[:, even:], jnp.zeros((48, VOCAB_PAD - vocab), f32)]
    cut_ref[:, even:] = jnp.concatenate(last, 1).astype(bf16)
    half_ref[...] = cut_ref[:, pl.ds(pl.multiple_of(core * VOCAB_HALF, 128), VOCAB_HALF)]
    down_half_ref[...] = mine(down_ref, 384)


def prepare(core, arrays):
    return staged_call(
        prepare_kernel,
        [(core, MY_CORE)],
        arrays,
        [],
        [
            shaped(bf16, 48, 3328),
            shaped(bf16, 48, VOCAB_PAD),
            shaped(bf16, 48, VOCAB_HALF),
            shaped(bf16, 192, 384),
        ],
        [],
        3,
    )


def id_row(ids_ref, j):
    rows = ids_ref[j]
    return jnp.concatenate([rows[k : k + 1] for k in range(4)], 1)


def lookup_kernel(ready, idx_ref, ids_ref, *refs):
    ins = list(refs[:4]) + [refs[4].at[k] for k in range(3)]
    outs, table, sems = refs[5:9], refs[9], refs[10]
    copies = [
        pltpu.make_async_copy(
            ins[0], table.at[pl.ds(pl.multiple_of(idx_ref[0], 16), 48), :], sems.at[0]
        )
    ]
    for number in range(1, 7):
        column = pl.multiple_of(idx_ref[7 + (number - 1) // 3], 128)
        row = pl.multiple_of(idx_ref[number], 16)
        copies.append(
            pltpu.make_async_copy(
                ins[number],
                table.at[pl.ds(row, 48), pl.ds(column, VOCAB_HALF)],
                sems.at[number],
            )
        )
    for copy in copies:
        copy.start()
    ready()
    for copy in copies:
        copy.wait()
    for j in range(4):
        total = jnp.zeros((192, 512), f32)
        for k in range(VOCAB_PAD // 256):
            total += jnp.dot(
                table[:, k * 256 : (k + 1) * 256],
                one_hot(id_row(ids_ref, j), k * 256, 256),
                preferred_element_type=f32,
            )
        outs[j][...] = total.astype(bf16)


def lookup(index, ids_z, arrays):
    return staged_call(
        lookup_kernel,
        [(index, LOOKUP)],
        [ids_z],
        arrays,
        [
            shaped(bf16, 192, 512),
            shaped(bf16, 192, 512),
            shaped(bf16, 192, 512),
            shaped(bf16, 192, 512),
        ],
        [
            pltpu.VMEM((192, VOCAB_PAD), bf16),
            pltpu.SemaphoreType.DMA((7,)),
        ],
        6,
    )


def token_sum_kernel(ready, idx_ref, ids_ref, other_ids_ref, mine_ref, other_ref, keep_ref, away_ref, whole_ref
):
    ready()
    start = idx_ref[0]
    for low in range(0, VOCAB_HALF, 256):
        count = min(256, VOCAB_HALF - low)
        total = jnp.zeros((192, count), f32)
        for ids, block in ((ids_ref, mine_ref), (other_ids_ref, other_ref)):
            for j in range(4):
                total += lax.dot_general(
                    block[j],
                    one_hot(id_row(ids, j), start + low, count),
                    (((1,), (1,)), ((), ())),
                    preferred_element_type=f32,
                )
        whole_ref[:, low : low + count] = total.astype(bf16)
    for k in range(2):
        keep_ref[k] = whole_ref[pl.ds(pl.multiple_of(idx_ref[1 + k], 16), 48), :]
        away_ref[k] = whole_ref[pl.ds(pl.multiple_of(idx_ref[3 + k], 16), 48), :]


def token_sum(index, ids_z, other_ids, mine, other):
    return staged_call(
        token_sum_kernel,
        [(index, PLANE)],
        [ids_z, other_ids, mine, other],
        [],
        [
            shaped(bf16, 2, 48, VOCAB_HALF),
            shaped(bf16, 2, 48, VOCAB_HALF),
        ],
        [
            pltpu.VMEM((192, VOCAB_HALF), bf16),
        ],
        8,
    )


def my_half(array, core, width):
    return lax.dynamic_slice_in_dim(array, core * width, width, axis=1)


def all_sum(value):
    for pairs in (ZS[1:], [FIRST, SECOND, BOTH]):
        one, two, three = (send(value, p) for p in pairs)
        value = (value + one) + (two + three)
    return value


WINDOWS = (0, 64, 192, 256)
SCALE = HD ** (-0.5)


def piece_copies(idx_ref, base, pieces, target, rows, sems, first_sem):
    copies = []
    for number in range(32):
        half = idx_ref[base + number]
        row = pl.multiple_of(idx_ref[base + 32 + number], 16)
        each = 32 // len(pieces)
        source = pieces[number // each].at[number % each]
        copies.append(
            pltpu.make_async_copy(
                source, target.at[half, pl.ds(row, rows), :], sems.at[first_sem + number]
            )
        )
    return copies


def window_bias(seg_row, seg_col, b):
    w = WINDOWS[b]
    same = seg_col[b * 128 : (b + 1) * 128, :] == seg_row[:, w : w + 256]
    bias = jnp.where(same, 0.0, -1e30)
    return jnp.concatenate([bias, bias], 0)


def two_heads(block):
    left = lax.broadcasted_iota(jnp.int32, block.shape, 1) < HD
    none = jnp.zeros_like(block)
    return jnp.concatenate([jnp.where(left, block, none), jnp.where(left, none, block)], 0)


def nt_dot(a, b):
    return lax.dot_general(a, b, (((1,), (1,)), ((), ())), preferred_element_type=f32)


def tn_dot(a, b):
    return lax.dot_general(a, b, (((0,), (0,)), ((), ())), preferred_element_type=f32)


def nn_dot(a, b):
    return jnp.dot(a, b, preferred_element_type=f32)


def row_norm(v):
    center = v - jnp.mean(v, -1, keepdims=True)
    inv = lax.rsqrt(jnp.mean(center * center, -1, keepdims=True) + norm_eps)
    return center * inv, inv


def attention_kernel(ready, idx_ref, seg_row_ref, seg_col_ref, *refs):
    e_in, pieces = refs[:4], refs[4:12]
    (e_ref, qkv_ref, lse_ref, mixed_ref, unit_ref, inv_ref, low_ref, par_ref, side_ref) = refs[12:21]
    et_ref, w_ref, bias_ref, attended_ref, sems = refs[21:]
    e_copies = [
        pltpu.make_async_copy(
            e_in[j],
            et_ref.at[pl.ds(pl.multiple_of(idx_ref[j], 16), 192), :],
            sems.at[j],
        )
        for j in range(4)
    ]
    w_copies = piece_copies(idx_ref, 4, pieces, w_ref, 48, sems, 4)
    for copy in e_copies + w_copies:
        copy.start()
    ready()
    for b in range(4):
        bias_ref[b] = window_bias(seg_row_ref[...], seg_col_ref[...], b)
    for copy in e_copies:
        copy.wait()
    e_ref[...] = et_ref[...].T
    ready.put(0)
    for copy in w_copies:
        copy.wait()
    par_ref[...] = w_ref[0, :, 1536:1664].T.astype(f32)[:8]
    side_ref[...] = w_ref[:, :, 1536:1664]
    for k in range(2):
        for t in range(3):
            part = nn_dot(e_ref[...], w_ref[k, :, t * 384 : (t + 1) * 384])
            if t == 0:
                part = part.astype(bf16).astype(f32) * SCALE
            part = part.astype(bf16)
            for i in range(3):
                qkv_ref[t * 6 + k * 3 + i] = part[:, i * 128 : (i + 1) * 128]
    ready.put(1, 7, 8)
    lse_ref[...] = jnp.zeros_like(lse_ref)
    lane = lax.broadcasted_iota(jnp.int32, (128, 128), 1)
    left = lane < HD

    @pl.loop(0, 6, unroll=3)
    def _(pair):
        for b in range(4):
            rows = pl.ds(b * 128, 128)
            keys = pl.ds(WINDOWS[b], 256)
            q = qkv_ref[pair, rows, :]
            k = qkv_ref[pair + 6, keys, :]
            v = qkv_ref[pair + 12, keys, :]
            s = nt_dot(two_heads(q), k) + bias_ref[b]
            top = jnp.max(s, -1, keepdims=True)
            e = jnp.exp(s - top)
            total = jnp.sum(e, -1, keepdims=True)
            log = top + jnp.log(total)
            lse = jnp.where(lane == pair * 2, log[:128], lse_ref[rows, :])
            lse_ref[rows, :] = jnp.where(lane == pair * 2 + 1, log[128:], lse)
            mixed = nn_dot((e * (1.0 / total)).astype(bf16), v)
            cols = pl.ds(pl.multiple_of(pair * 128, 128), 128)
            mixed_ref[rows, cols] = jnp.where(left, mixed[:128], mixed[128:]).astype(bf16)

    ready.put(2, 3)
    for k in range(2):
        attended_ref[:, k * 384 : (k + 1) * 384] = nn_dot(mixed_ref[...], w_ref[k, :, 1152:1536])
    for b in range(4):
        rows = slice(b * 128, (b + 1) * 128)
        unit, inv = row_norm(e_ref[rows, :].astype(f32) + attended_ref[rows, :])
        unit_ref[rows, :] = unit
        inv_ref[rows, :] = jnp.broadcast_to(inv, (128, 128))
        low_ref[rows, :] = (unit * par_ref[0:1, :] + par_ref[1:2, :]).astype(bf16)


def attention_forward(index, seg_row, seg_col, columns, pieces):
    return staged_call(
        attention_kernel,
        [(index, Z_ROWS)],
        [seg_row, seg_col],
        [*columns, *pieces],
        [
            shaped(bf16, 512, 768),
            shaped(bf16, 18, 512, 128),
            shaped(f32, 512, 128),
            shaped(bf16, 512, 768),
            shaped(f32, 512, 768),
            shaped(f32, 512, 128),
            shaped(bf16, 512, 768),
            shaped(f32, 8, 768),
            shaped(bf16, 2, 768, 128),
        ],
        [
            pltpu.VMEM((768, 512), bf16),
            pltpu.VMEM((2, 768, 1664), bf16),
            pltpu.VMEM((4, 256, 256), f32),
            pltpu.VMEM((512, 768), f32),
            pltpu.SemaphoreType.DMA((36,)),
        ],
        17,
    )


def gelu_and_slope(u):
    bell = jnp.exp(-0.5 * u * u)
    base = 1.0 + (0.3275911 * 0.5**0.5) * jnp.abs(u)
    t = pl.reciprocal(base, approx=True)
    t = t * (2.0 - base * t)
    poly = -0.07032334059476852
    for factor in (
        0.24725385010242462,
        -0.2008872926235199,
        0.2245105654001236,
        0.013965459540486336,
        0.10251718759536743,
        0.09044301509857178,
        0.09252061694860458,
    ):
        poly = factor + t * poly
    tail = (t * poly) * bell
    phi = jnp.where(u < 0, tail, 1.0 - tail)
    return u * phi, phi + (u * 0.3989422804014327) * bell


def up_kernel(ready, idx_ref, low_ref, *refs):
    pieces, act_ref, slope_ref, w_ref, sems = refs[:8], refs[8], refs[9], refs[10], refs[11]
    copies = piece_copies(idx_ref, 0, pieces, w_ref, 48, sems, 0)
    for copy in copies:
        copy.start()
    ready()
    core = idx_ref[0]
    for side in range(2):
        half = core if side == 0 else 1 - core
        for copy in copies[side * 16 : side * 16 + 16]:
            copy.wait()

        @pl.loop(0, 6, unroll=3)
        def _(n):
            cols = pl.ds(pl.multiple_of(n * 256, 256), 256)
            u = nn_dot(low_ref[...], w_ref[half, :, cols])
            value, slope = gelu_and_slope(u)
            out_cols = pl.ds(pl.multiple_of(half * 1536 + n * 256, 256), 256)
            act_ref[:, out_cols] = value.astype(bf16)
            slope_ref[:, out_cols] = slope.astype(bf16)

        ready.put_half(side, half, (0, 1), 1536)


def up_forward(index, low, pieces):
    return staged_call(
        up_kernel,
        [(index, BY_FLIP)],
        [low],
        pieces,
        [
            shaped(bf16, 512, 3072),
            shaped(bf16, 512, 3072),
        ],
        [
            pltpu.VMEM((2, 768, 1536), bf16),
            pltpu.SemaphoreType.DMA((32,)),
        ],
        18,
    )


def thirds(v):
    high = v.astype(bf16)
    rest = v - high.astype(f32)
    middle = rest.astype(bf16)
    return high, middle, (rest - middle.astype(f32)).astype(bf16)


def down_kernel(ready, idx_ref, seg_row_ref, act_ref, unit_one_ref, par_ref, *refs):
    unit_ref, inv_ref, frag_ref, frag_low_ref, size_ref, w_ref, result_ref, sems = refs[4:]
    copies = piece_copies(idx_ref, 0, refs[:4], w_ref, 192, sems, 0)
    for copy in copies:
        copy.start()
    ready()
    for copy in copies:
        copy.wait()
    for k in range(2):
        result_ref[:, k * 384 : (k + 1) * 384] = nn_dot(act_ref[...], w_ref[k])
    pooled = jnp.zeros((32, 768), f32)
    for b in range(4):
        rows = slice(b * 128, (b + 1) * 128)
        one = unit_one_ref[rows, :] * par_ref[0:1, :] + par_ref[1:2, :]
        unit, inv = row_norm(one + result_ref[rows, :])
        unit_ref[rows, :] = unit
        inv_ref[rows, :] = jnp.broadcast_to(inv, (128, 128))
        two = unit * par_ref[2:3, :] + par_ref[3:4, :]
        member = lax.broadcasted_iota(jnp.int32, (32, 128), 0) == seg_row_ref[:, rows]
        member = jnp.where(member, 1.0, 0.0).astype(bf16)
        for part in thirds(two):
            pooled += nn_dot(member, part)
    size = lax.rsqrt(jnp.sum(pooled * pooled, -1, keepdims=True) + unit_eps)
    frag = pooled * size
    frag_ref[...] = frag
    frag_low_ref[...] = frag.astype(bf16)
    size_ref[...] = jnp.broadcast_to(size, (32, 128))


def down_forward(index, seg_row, act, unit_one, params, pieces):
    return staged_call(
        down_kernel,
        [(index, BY_PAIR)],
        [seg_row, act, unit_one, params],
        pieces,
        [
            shaped(f32, 512, 768),
            shaped(f32, 512, 128),
            shaped(f32, 32, 768),
            shaped(bf16, 32, 768),
            shaped(f32, 32, 128),
        ],
        [
            pltpu.VMEM((2, 3072, 384), bf16),
            pltpu.VMEM((512, 768), f32),
            pltpu.SemaphoreType.DMA((32,)),
        ],
        10,
    )


def back_norm(upstream, unit, inv, gain):
    scaled = upstream * gain
    return inv * (
        scaled
        - jnp.mean(scaled, -1, keepdims=True)
        - unit * jnp.mean(scaled * unit, -1, keepdims=True)
    )


def loss_kernel(
    ready, idx_ref, heat_ref, seg_col_ref, partner_ref, own_weight_ref, side_ref,
    frag_ref, size_ref, unit_ref, inv_ref, par_ref, slope_ref, *refs
):
    blocks, down_pieces = refs[:8], refs[8:12]
    loss_ref, low_own_ref, low_other_ref, gup_own_ref, gup_other_ref, two_ref, gains_ref = refs[12:19]
    all_ref, down_ref, low_ref, spread_ref, sems, w_sems = refs[19:]
    copies = []
    for number in range(32):
        row = pl.multiple_of(idx_ref[1 + number], 16)
        copies.append(
            pltpu.make_async_copy(
                blocks[number // 4].at[number % 4], all_ref.at[pl.ds(row, 32), :], sems.at[number]
            )
        )
    core = idx_ref[33]
    down_copies = piece_copies(idx_ref, 34, down_pieces, down_ref, 192, w_sems, 0)
    for copy in copies:
        copy.start()
    for copy in copies:
        copy.wait()
    ready(1, 2, 3)
    ready.copies_in[9].start()
    for copy in down_copies:
        copy.start()
    base = idx_ref[0]
    inv_heat = 1.0 / heat_ref[0]
    tally = 1024
    mine = all_ref[pl.ds(pl.multiple_of(base, 16), 32), :]
    grid = (nt_dot(mine, all_ref[...]) - 1.0) * inv_heat
    across = lax.broadcasted_iota(jnp.int32, (32, tally), 1)
    down = lax.broadcasted_iota(jnp.int32, (32, tally), 0) + base
    powers = jnp.where(across == down, 0.0, jnp.exp(grid))
    total = jnp.sum(powers, -1, keepdims=True)
    eye = lax.broadcasted_iota(jnp.int32, (32, 32), 0) == lax.broadcasted_iota(jnp.int32, (32, 32), 1)
    partner = jnp.sum(jnp.where(eye, partner_ref[...].astype(f32), 0.0), -1, keepdims=True)
    own_weight = jnp.sum(jnp.where(eye, own_weight_ref[...], 0.0), -1, keepdims=True)
    chosen = across == partner.astype(jnp.int32)
    target = jnp.sum(jnp.where(chosen, grid, 0.0), -1, keepdims=True)
    terms = own_weight * (jnp.log(total) - target)
    loss_ref[...] = jnp.broadcast_to(jnp.sum(terms, 0, keepdims=True) / tally, (8, 128))
    picked = jnp.where(chosen, 1.0, 0.0)
    pull = (powers / total - picked) * (own_weight * (inv_heat / tally))
    totals = [jnp.zeros((1, 128), f32) for _ in range(8)]
    number = lax.broadcasted_iota(jnp.int32, (128, 128), 0)
    same = number == lax.broadcasted_iota(jnp.int32, (128, 128), 1)
    weights = []
    for big in range(2):
        spread_ref[...] = nt_dot(all_ref[big * 512 : (big + 1) * 512, :], all_ref[...])
        for b in range(big * 4, big * 4 + 4):
            inside = slice((b - big * 4) * 128, (b - big * 4 + 1) * 128)
            for n in range(8):
                spread = jnp.exp((spread_ref[inside, n * 128 : (n + 1) * 128] - 1.0) * inv_heat)
                if n == b:
                    spread = jnp.where(same, 0.0, spread)
                totals[n] += jnp.sum(spread, 0, keepdims=True)
            side = jnp.concatenate(
                [
                    side_ref[n % 2, (n // 2) * 48 : (n // 2) * 48 + 32, :].astype(f32)
                    for n in range(b * 4, b * 4 + 4)
                ],
                0,
            ).T
            weights.append(side[4:5] + side[5:6] + side[6:7])
    totals, weights = jnp.concatenate(totals, 1), jnp.concatenate(weights, 1)
    column_pull = (powers / totals - picked) * (weights * (inv_heat / tally))
    both = jnp.concatenate([pull.astype(bf16), column_pull.astype(bf16)], 0)
    both = nn_dot(both, all_ref[...])
    grad = both[:32] + both[32:]
    ready(0, 4, 5, 6, 7, 8)
    frag = frag_ref[...]
    pooled = size_ref[:, 0:1] * (grad - frag * jnp.sum(grad * frag, -1, keepdims=True))
    stacked = jnp.concatenate(thirds(pooled), 0)
    gain_two = jnp.zeros((1, 768), f32)
    shift_two = jnp.zeros((1, 768), f32)
    for b in range(4):
        rows = slice(b * 128, (b + 1) * 128)
        slot = lax.broadcasted_iota(jnp.int32, (128, 96), 1) % 32
        member = jnp.where(slot == seg_col_ref[rows, :], 1.0, 0.0).astype(bf16)
        upstream = nn_dot(member, stacked)
        unit = unit_ref[rows, :]
        back = back_norm(upstream, unit, inv_ref[rows, 0:1], par_ref[2:3, :])
        two_ref[rows, :] = back
        low_ref[rows, :] = back.astype(bf16)
        gain_two += jnp.sum(upstream * unit, 0, keepdims=True)
        shift_two += jnp.sum(upstream, 0, keepdims=True)
    halves = (core, 1 - core)
    for half, ref in zip(halves, (low_own_ref, low_other_ref)):
        ref[...] = low_ref[:, pl.ds(pl.multiple_of(half * 384, 128), 384)]
    ready.put(0, 1, 2, 5)
    ready(9)
    for copy in down_copies:
        copy.wait()
    for half, gup_ref in zip(halves, (gup_own_ref, gup_other_ref)):

        @pl.loop(0, 6, unroll=3)
        def _(n):
            cols = pl.ds(pl.multiple_of(n * 256, 256), 256)
            wide = pl.ds(pl.multiple_of(half * 1536 + n * 256, 256), 256)
            g = sum(
                nt_dot(low_ref[:, k * 384 : (k + 1) * 384], down_ref[k, wide, :])
                for k in range(2)
            )
            gup_ref[:, cols] = (g * slope_ref[:, wide].astype(f32)).astype(bf16)

        if gup_ref is gup_own_ref:
            ready.put(3)

    gains_ref[...] = jnp.concatenate([gain_two, shift_two, jnp.zeros((6, 768), f32)], 0)


def loss_backward(index, heat, arrays, pieces):
    return staged_call(
        loss_kernel,
        [(index, FRAGMENTS), (heat, 0)],
        arrays,
        pieces,
        [
            shaped(f32, 8, 128),
            shaped(bf16, 512, 384),
            shaped(bf16, 512, 384),
            shaped(bf16, 512, 1536),
            shaped(bf16, 512, 1536),
            shaped(f32, 512, 768),
            shaped(f32, 8, 768),
        ],
        [
            pltpu.VMEM((1024, 768), bf16),
            pltpu.VMEM((2, 3072, 384), bf16),
            pltpu.VMEM((512, 768), bf16),
            pltpu.VMEM((512, 1024), f32),
            pltpu.SemaphoreType.DMA((32,)),
            pltpu.SemaphoreType.DMA((32,)),
        ],
        18,
        (9,),
    )


def ffn_back_kernel(
    ready, idx_ref, gup_own_ref, gup_other_ref, two_ref, unit_ref, inv_ref, par_ref, gains_two_ref, *refs
):
    pieces = refs[:8]
    resid_ref, att_ref, own_ref, other_ref, gains_ref, up_ref, sems = refs[8:]
    copies = piece_copies(idx_ref, 0, pieces, up_ref, 48, sems, 0)
    for copy in copies:
        copy.start()
    ready()
    for copy in copies:
        copy.wait()
    core = idx_ref[0]
    for n in range(3):
        cols = slice(n * 256, (n + 1) * 256)
        resid_ref[:, cols] = (
            two_ref[:, cols]
            + nt_dot(gup_own_ref[...], up_ref[core, cols, :])
            + nt_dot(gup_other_ref[...], up_ref[1 - core, cols, :])
        )
    gain_sum = jnp.zeros((1, 768), f32)
    shift_sum = jnp.zeros((1, 768), f32)
    for b in range(4):
        rows = slice(b * 128, (b + 1) * 128)
        one = resid_ref[rows, :]
        unit = unit_ref[rows, :]
        back = back_norm(one, unit, inv_ref[rows, 0:1], par_ref[0:1, :])
        resid_ref[rows, :] = back
        att_ref[rows, :] = back.astype(bf16)
        gain_sum += jnp.sum(one * unit, 0, keepdims=True)
        shift_sum += jnp.sum(one, 0, keepdims=True)
    for half, ref in ((core, own_ref), (1 - core, other_ref)):
        ref[...] = att_ref[:, pl.ds(pl.multiple_of(half * 384, 128), 384)]
    gains_ref[...] = jnp.concatenate(
        [gain_sum, shift_sum, gains_two_ref[0:2, :], jnp.zeros((4, 768), f32)], 0
    )


def ffn_backward(index, arrays, pieces):
    return staged_call(
        ffn_back_kernel,
        [(index, BY_FLIP)],
        arrays,
        pieces,
        [
            shaped(f32, 512, 768),
            shaped(bf16, 512, 768),
            shaped(bf16, 512, 384),
            shaped(bf16, 512, 384),
            shaped(f32, 8, 768),
        ],
        [pltpu.VMEM((2, 768, 1536), bf16), pltpu.SemaphoreType.DMA((32,))],
        9,
    )


def heads_back(half, gm_ref, qkv_ref, lse_ref, bias_ref, gqkv_ref, gk_ref, gv_ref):
    lane = lax.broadcasted_iota(jnp.int32, (128, 128), 1)
    left = lane < HD
    gk_ref[...] = jnp.zeros_like(gk_ref)
    gv_ref[...] = jnp.zeros_like(gv_ref)

    @pl.loop(0, 3, unroll=3)
    def _(spot):
        pair = half * 3 + spot
        for b in range(4):
            rows = pl.ds(b * 128, 128)
            keys = pl.ds(WINDOWS[b], 256)
            q = qkv_ref[pair, rows, :]
            k = qkv_ref[pair + 6, keys, :]
            v = qkv_ref[pair + 12, keys, :]
            gm = gm_ref[rows, pl.ds(pl.multiple_of(spot * 128, 128), 128)]
            q, gm = two_heads(q), two_heads(gm)
            stats = lse_ref[rows, :]
            lse = jnp.concatenate(
                [
                    jnp.sum(jnp.where(lane == pair * 2 + h, stats, 0.0), -1, keepdims=True)
                    for h in range(2)
                ],
                0,
            )
            p = jnp.exp(nt_dot(q, k) + bias_ref[b] - lse)
            gp = nt_dot(gm, v)
            gs = (p * (gp - jnp.sum(gp * p, -1, keepdims=True))).astype(bf16)
            gq = nn_dot(gs, k)
            gq = (jnp.where(left, gq[:128], gq[128:]) * SCALE).astype(bf16)
            gqkv_ref[rows, pl.ds(pl.multiple_of(spot * 128, 128), 128)] = gq
            gk_ref[spot, keys, :] += tn_dot(gs, q)
            gv_ref[spot, keys, :] += tn_dot(p.astype(bf16), gm)
        for third, ref in ((1, gk_ref), (2, gv_ref)):
            cols = pl.ds(pl.multiple_of(third * 384 + spot * 128, 128), 128)
            gqkv_ref[:, cols] = ref[spot].astype(bf16)


def other_heads_kernel(ready, idx_ref, seg_row_ref, seg_col_ref, qkv_ref, lse_ref, att_ref, resid_ref, *refs
):
    pieces = refs[:8]
    gqkv_ref, gm_own_ref, part_ref = refs[8:11]
    w_ref, bias_ref, gm_ref, gk_ref, gv_ref, sems = refs[11:]
    copies = piece_copies(idx_ref, 4, pieces, w_ref, 48, sems, 0)
    for copy in copies:
        copy.start()
    ready()
    for b in range(4):
        bias_ref[b] = window_bias(seg_row_ref[...], seg_col_ref[...], b)
    for copy in copies:
        copy.wait()
    core = idx_ref[4]
    half = 1 - core
    for side, ref in ((half, gm_ref), (core, gm_own_ref)):
        rows = pl.ds(pl.multiple_of(side * 384, 128), 384)
        ref[...] = sum(
            nt_dot(att_ref[:, k * 384 : (k + 1) * 384], w_ref[k, rows, 1152:1536])
            for k in range(2)
        ).astype(bf16)
    heads_back(half, gm_ref, qkv_ref, lse_ref, bias_ref, gqkv_ref, gk_ref, gv_ref)
    ready.put(0, 1)
    for n in range(3):
        cols = slice(n * 256, (n + 1) * 256)
        part_ref[:, cols] = resid_ref[:, cols] + nt_dot(gqkv_ref[...], w_ref[half, cols, :1152])


def other_heads(index, arrays, pieces):
    return staged_call(
        other_heads_kernel,
        [(index, Z_ROWS)],
        arrays,
        pieces,
        [
            shaped(bf16, 512, 1152),
            shaped(bf16, 512, 384),
            shaped(f32, 512, 768),
        ],
        [
            pltpu.VMEM((2, 768, 1664), bf16),
            pltpu.VMEM((4, 256, 256), f32),
            pltpu.VMEM((512, 384), bf16),
            pltpu.VMEM((3, 512, 128), f32),
            pltpu.VMEM((3, 512, 128), f32),
            pltpu.SemaphoreType.DMA((32,)),
        ],
        17,
    )


def own_heads_kernel(ready, idx_ref, seg_row_ref, seg_col_ref, qkv_ref, lse_ref, gm_ref, part_ref, *refs
):
    pieces = refs[:4]
    gqkv_ref, outs = refs[4], refs[5:9]
    w_ref, bias_ref, gk_ref, gv_ref, et_ref, sems = refs[9:]
    copies = []
    for number in range(16):
        row = pl.multiple_of(idx_ref[36 + number], 16)
        copies.append(
            pltpu.make_async_copy(
                pieces[number // 4].at[number % 4], w_ref.at[pl.ds(row, 48), :], sems.at[number]
            )
        )
    for copy in copies:
        copy.start()
    ready()
    for b in range(4):
        bias_ref[b] = window_bias(seg_row_ref[...], seg_col_ref[...], b)
    core = idx_ref[4]
    heads_back(core, gm_ref, qkv_ref, lse_ref, bias_ref, gqkv_ref, gk_ref, gv_ref)
    ready.put(0)
    for copy in copies:
        copy.wait()
    for n in range(3):
        cols = slice(n * 256, (n + 1) * 256)
        total = part_ref[:, cols] + nt_dot(gqkv_ref[...], w_ref[cols, :1152])
        et_ref[cols, :] = total.astype(bf16).T
    for j in range(4):
        outs[j][...] = et_ref[pl.ds(pl.multiple_of(idx_ref[j], 16), 192), :]


def own_heads(index, arrays, pieces):
    return staged_call(
        own_heads_kernel,
        [(index, Z_ROWS)],
        arrays,
        pieces,
        [
            shaped(bf16, 512, 1152),
            shaped(bf16, 192, 512),
            shaped(bf16, 192, 512),
            shaped(bf16, 192, 512),
            shaped(bf16, 192, 512),
        ],
        [
            pltpu.VMEM((768, 1664), bf16),
            pltpu.VMEM((4, 256, 256), f32),
            pltpu.VMEM((3, 512, 128), f32),
            pltpu.VMEM((3, 512, 128), f32),
            pltpu.VMEM((768, 512), bf16),
            pltpu.SemaphoreType.DMA((16,)),
        ],
        15,
    )


def to_slots(idx_ref, whole_ref, keep_ref, away_ref):
    for slot in range(8):
        keep_ref[slot] = whole_ref[idx_ref[slot]]
        away_ref[slot] = whole_ref[idx_ref[8 + slot]]


def down_grad_kernel(ready, idx_ref, act_ref, act_o_ref, g_ref, g_o_ref, keep_ref, away_ref, whole_ref):
    ready()
    for n in range(8):
        cols = slice(n * 384, (n + 1) * 384)
        total = tn_dot(act_ref[:, cols], g_ref[...]) + tn_dot(act_o_ref[:, cols], g_o_ref[...])
        total = total.astype(bf16)
        whole_ref[2 * n] = total[:192]
        whole_ref[2 * n + 1] = total[192:]
    to_slots(idx_ref, whole_ref, keep_ref, away_ref)


def down_grad(index, arrays):
    return staged_call(
        down_grad_kernel,
        [(index, SLOTS)],
        arrays,
        [],
        [shaped(bf16, 8, 192, 384)] * 2,
        [pltpu.VMEM((16, 192, 384), bf16)],
        7,
    )


def store_chunks(whole_ref, cols, total):
    for f in range(16):
        whole_ref[f, :, cols] = total[f * 48 : (f + 1) * 48]


def up_out_grad_kernel(
    ready, idx_ref, low_ref, low_o_ref, g_ref, g_o_ref, mixed_ref, mixed_o_ref, ga_ref, ga_o_ref, norms_ref,
    norms_o_ref, keep_ref, away_ref, whole_ref, t_ref,
):
    ready()
    t_ref[0] = low_ref[...].T
    t_ref[1] = low_o_ref[...].T
    for n in range(3):
        cols = slice(n * 512, (n + 1) * 512)
        total = nn_dot(t_ref[0], g_ref[:, cols]) + nn_dot(t_ref[1], g_o_ref[:, cols])
        store_chunks(whole_ref, cols, total.astype(bf16))
    t_ref[0] = mixed_ref[...].T
    t_ref[1] = mixed_o_ref[...].T
    total = nn_dot(t_ref[0], ga_ref[...]) + nn_dot(t_ref[1], ga_o_ref[...])
    store_chunks(whole_ref, slice(1536, 1920), total.astype(bf16))
    norms = (norms_ref[...] + norms_o_ref[...]).T.astype(bf16)
    norms = jnp.concatenate([norms, jnp.zeros((768, 120), bf16)], 1)
    store_chunks(whole_ref, slice(1920, 2048), norms)
    to_slots(idx_ref, whole_ref, keep_ref, away_ref)


def up_out_grad(index, arrays):
    return staged_call(
        up_out_grad_kernel,
        [(index, SLOTS)],
        arrays,
        [],
        [
            shaped(bf16, 8, 48, 2048),
            shaped(bf16, 8, 48, 2048),
        ],
        [
            pltpu.VMEM((16, 48, 2048), bf16),
            pltpu.VMEM((2, 768, 512), bf16),
        ],
        8,
    )


def in_grad_kernel(ready, idx_ref, e_ref, e_o_ref, g_ref, g_o_ref, keep_ref, away_ref, whole_ref, t_ref):
    ready()
    t_ref[0] = e_ref[...].T
    t_ref[1] = e_o_ref[...].T
    for t in range(3):
        cols = slice(t * 384, (t + 1) * 384)
        total = nn_dot(t_ref[0], g_ref[:, cols]) + nn_dot(t_ref[1], g_o_ref[:, cols])
        store_chunks(whole_ref, cols, total.astype(bf16))
    to_slots(idx_ref, whole_ref, keep_ref, away_ref)


def in_grad(index, arrays):
    return staged_call(
        in_grad_kernel,
        [(index, SLOTS)],
        arrays,
        [],
        [
            shaped(bf16, 8, 48, 1152),
            shaped(bf16, 8, 48, 1152),
        ],
        [
            pltpu.VMEM((16, 48, 1152), bf16),
            pltpu.VMEM((2, 768, 512), bf16),
        ],
        6,
    )


def optimizer_kernel(ready, core_ref, fix_ref, totals_ref, totals_o_ref, *refs):
    ready(*range(10))
    own, other = refs[:4], refs[4:8]
    params, outs = refs[8:26], refs[26:46]
    table_ref = refs[46]
    core = core_ref[0]
    totals = totals_ref[...] + totals_o_ref[...]
    norm = jnp.sqrt(totals[:, 0:1])
    outs[0][...] = totals[:, 1:2]
    outs[1][...] = norm
    factor = clip_norm / jnp.maximum(norm, clip_norm)
    fix_one, fix_two = 1.0 / fix_ref[0], 1.0 / fix_ref[1]

    def update(number, spot, grad, rate, decay):
        w_ref, first_ref, second_ref = params[3 * number : 3 * number + 3]
        grad = grad.astype(f32) * factor
        weight = w_ref[spot]
        first = beta_one * first_ref[spot] + (1.0 - beta_one) * grad
        second = beta_two * second_ref[spot] + (1.0 - beta_two) * grad * grad
        step = (first * fix_one) / (jnp.sqrt(second * fix_two) + adam_eps)
        outs[2 + 3 * number][spot] = weight - rate * (step + decay * weight)
        outs[3 + 3 * number][spot] = first
        outs[4 + 3 * number][spot] = second

    every = slice(None)
    halves = ((core, own), (1 - core, other))

    def columns(half, width, start=0):
        return pl.ds(pl.multiple_of(half * width + start, 128), width)

    def opened(number):
        ready(*range(10 + 3 * number, 13 + 3 * number))

    def done(number):
        ready.put(*range(2 + 3 * number, 5 + 3 * number))

    opened(3)
    for half, (_, _, up_out, _) in halves:
        for t in range(3):
            spot = pl.ds(pl.multiple_of(half * 1536 + t * 512, 128), 512)
            update(3, (every, spot), up_out[:, t * 512 : (t + 1) * 512], rate_matrix, decay_rate)
    done(3)
    opened(4)
    for half, (_, _, _, down) in halves:
        for t in range(4):
            rows = slice(t * 48, (t + 1) * 48)
            update(4, (rows, columns(half, 384)), down[rows, :], rate_matrix, decay_rate)
    done(4)
    opened(1)
    for half, (_, into, _, _) in halves:
        for t in range(3):
            update(
                1,
                (every, columns(half, 384, t * 768)),
                into[:, t * 384 : (t + 1) * 384],
                rate_matrix,
                decay_rate,
            )
    done(1)
    opened(0)
    for half, (table, _, _, _) in halves:
        table_ref[:, columns(half, VOCAB_HALF)] = table[...]
    vocab = params[0].shape[1]
    for low in range(0, vocab, 512):
        spot = slice(low, min(vocab, low + 512))
        update(0, (every, spot), table_ref[:, spot], rate_embed, decay_rate)
    done(0)
    opened(2)
    for half, (_, _, up_out, _) in halves:
        update(2, (every, columns(half, 384)), up_out[:, 1536:1920], rate_matrix, decay_rate)
    done(2)
    opened(5)
    norms = jnp.where(core == 0, own[2][:, 1920:].astype(f32), other[2][:, 1920:].astype(f32))
    update(5, (every, every), norms.T[:4], rate_norm, 0.0)


def optimizer(core, fixes, totals, totals_o, own, other, params):
    return staged_call(
        optimizer_kernel,
        [(core, MY_CORE), (fixes, 0)],
        [totals, totals_o, *own, *other, *params],
        [],
        [
            shaped(f32, 1, 1),
            shaped(f32, 1, 1),
            *[shaped(f32, *p.shape) for p in params],
        ],
        [
            pltpu.VMEM((48, VOCAB_PAD), bf16),
        ],
        8,
    )


def per_device_links(
    kmer_identifiers,
    slot_fragment_ids,
    mirror_fragment_index,
    fragment_weight,
    affinity_heat,
    optimizer_iteration,
    lexicon_table,
    lexicon_first_moment,
    lexicon_raw_moment,
    query_key_value_maps,
    qkv_first_moment,
    qkv_raw_moment,
    attention_exit_map,
    exit_first_moment,
    exit_raw_moment,
    widening_matrix_in,
    widening_first_moment,
    widening_raw_moment,
    narrowing_matrix_out,
    narrowing_first_moment,
    narrowing_raw_moment,
    layernorm_scale_bias,
    layernorm_first_moment,
    layernorm_raw_moment,
):
    place = Place()
    core = place.core
    vocab = lexicon_table.shape[0]
    index = index_vector(place)
    both_cut, table_cut, table_half, down_half = prepare(
        index,
        [
            lexicon_table.T,
            query_key_value_maps,
            attention_exit_map,
            widening_matrix_in,
            narrowing_matrix_out,
            layernorm_scale_bias,
            kmer_identifiers,
            fragment_weight.reshape(1, 32),
        ],
    )
    near = [send(table_half, FIRST), send(table_half, SECOND)]
    near.append(send(near[0], SECOND))
    both_far = z_sends(both_cut)
    down_first = send(after(down_half, near[0]), FIRST)
    others = send(after(jnp.stack(near), down_first, *both_far), CORE)
    id_parts = jnp.stack([p[:8, 3200:] for p in both_far]).astype(f32)
    ids_z = (id_parts[:, :4] * 64.0 + id_parts[:, 4:]).astype(jnp.int32)
    in_out_column = jnp.stack([p[:, :1664] for p in both_far])
    in_out_mine = plane_sends(in_out_column, True)
    found = lookup(index, ids_z, [table_cut] + near + [others])
    up_column = after(jnp.stack([p[:, 1664:3200] for p in both_far]), *found)
    columns = [found[0]] + [send(found[j], ZS[j]) for j in (1, 2, 3)]
    in_out = both_cores(together(in_out_mine, *columns))
    up_column = after(up_column, in_out_mine[3])
    up_mine = [up_column, send(up_column, FIRST), send(up_column, SECOND)]
    down_pair = jnp.stack([down_half, after(down_first, *found)])
    down_far = z_sends(after(down_pair, *columns))
    seg_row = slot_fragment_ids
    seg_col = slot_fragment_ids.reshape(512, 1)
    embedded, qkv, lse, mixed, unit_one, inv_one, normed_low, params, side = attention_forward(
        index, seg_row, seg_col, columns, in_out
    )
    *up_mine, d_one, d_two, d_three = together(up_mine + down_far[1:], normed_low)
    up_mine.append(send(up_mine[1], SECOND))
    down_one = jnp.stack([down_far[0], d_one, d_two, d_three]).reshape(8, 192, 384)
    down_two = send(down_one, SECOND)
    down_one_o = send(down_one, CORE)
    up_w = both_cores(up_mine)
    activated, slope = up_forward(index, normed_low, up_w)
    down_two, down_one_o = together([down_two, down_one_o], activated)
    down_w = [down_one, down_two, down_one_o, send(down_two, CORE)]
    unit_two, inv_two, unit_rows, unit_low, unit_scale = down_forward(
        index, seg_row, activated, unit_one, params, down_w
    )
    embedded_o, mixed_o, normed_o, activated_o = (
        send(a, CORE) for a in (embedded, mixed, normed_low, activated)
    )
    column = jnp.stack([unit_low] + [send(unit_low, ZS[j]) for j in (1, 2, 3)])
    blocks = [column, send(column, FIRST), send(column, SECOND), send(column, BOTH)]
    blocks = blocks + [send(block, CORE) for block in blocks]
    (
        loss_tile, grad_result_own, grad_result_x, grad_up_own, grad_up_x, grad_two, gains_two,
    ) = loss_backward(
        index,
        affinity_heat.reshape(1),
        [
            seg_col,
            mirror_fragment_index.reshape(1, 32),
            fragment_weight.reshape(1, 32),
            side,
            unit_rows,
            unit_scale,
            unit_two,
            inv_two,
            params,
            slope,
        ],
        blocks + down_w,
    )
    grad_result_o = send(grad_result_x, CORE)
    ids_o = send(ids_z, CORE)
    grad_up_o = send(grad_up_x, CORE)
    spare = [embedded_o, mixed_o, normed_o, ids_o]
    down_keep, down_away = down_grad(
        index, [after(activated, *spare), activated_o, grad_result_own, grad_result_o]
    )
    down_came = send(down_away, SECOND)
    grad_resid, grad_attended, grad_att_own, grad_att_x, norms = ffn_backward(
        index,
        [after(grad_up_own, down_away), grad_up_x, grad_two, unit_one, inv_one, params, gains_two],
        up_w,
    )
    grad_att_o = send(grad_att_x, CORE)
    norms_o = send(norms, CORE)
    up_out_keep, up_out_away = up_out_grad(
        index,
        [
            normed_low,
            normed_o,
            grad_up_own,
            grad_up_o,
            mixed,
            mixed_o,
            grad_att_own,
            grad_att_o,
            norms,
            norms_o,
        ],
    )
    up_out_came = send(up_out_away, SECOND)
    down_came = after(down_came, up_out_away)
    down_across = scatter_add(down_keep, down_came)
    down_came_two = send(down_across, FIRST)
    grad_qkv_x, grad_mixed_own, part = other_heads(
        index,
        [seg_row, seg_col, qkv, lse, after(grad_attended, down_across), grad_resid],
        in_out,
    )
    grad_qkv_o = send(grad_qkv_x, CORE)
    down_came_two = after(down_came_two, part)
    down_here, down_far = scatter_here(down_keep, down_came, down_came_two)
    down_far_came = line_sends(down_far)
    grad_qkv_own, *outs = own_heads(
        index,
        [seg_row, seg_col, qkv, lse, grad_mixed_own, after(part, *down_far)],
        in_out[:4],
    )
    far_cols = [send(outs[j], ZS[j]) for j in (1, 2, 3)]
    *down_far_came, up_out_came, grad_qkv_o = together(
        down_far_came + [up_out_came, grad_qkv_o], grad_qkv_own
    )
    up_out_across = scatter_add(up_out_keep, up_out_came)
    up_out_came_two = send(up_out_across, FIRST)
    in_keep, in_away = in_grad(
        index, [embedded, embedded_o, after(grad_qkv_own, up_out_across), grad_qkv_o]
    )
    far_cols = together(far_cols, in_away)
    in_came = send(in_away, SECOND)
    token_cols = jnp.stack([outs[0]] + far_cols)
    token_cols_o = send(token_cols, CORE)
    up_out_here, up_out_far = scatter_here(
        up_out_keep, up_out_came, after(up_out_came_two, token_cols)
    )
    up_out_far_came = line_sends(up_out_far)
    keep, away = token_sum(
        index,
        after(ids_z, *up_out_far),
        ids_o,
        token_cols,
        token_cols_o,
    )
    came = send(away, SECOND)
    in_came = after(in_came, away)
    in_across = scatter_add(in_keep, in_came)
    in_came_two = send(in_across, FIRST)
    across = (keep[1].astype(f32) + came[1].astype(f32)).astype(bf16)
    came_two = send(across, FIRST)
    up_out_far_came = together(up_out_far_came, across)
    in_here, in_far = scatter_here(
        in_keep, in_came, after(in_came_two, across, *up_out_far_came)
    )
    in_far_came = line_sends(in_far)
    down_sum = line_sum(after(down_here, *in_far), down_far_came)
    up_out_sum = line_sum(up_out_here, together(up_out_far_came, *in_far))
    table_sum = keep[0].astype(f32) + came[0].astype(f32) + came_two.astype(f32)
    table_sum = table_sum.astype(bf16)
    early = [table_sum, up_out_sum, down_sum]
    norm_own = up_out_sum[:, 1920:1924].astype(f32)
    squares = sum(
        jnp.sum(jnp.square(p.astype(f32))) for p in (table_sum, up_out_sum[:, :1920], down_sum)
    ) + jnp.where(core == 0, jnp.sum(norm_own * norm_own), 0.0)
    early_o = [send(s, CORE) for s in early]
    in_sum = line_sum(in_here, together(in_far_came, squares))
    in_o = send(in_sum, CORE)
    squares += jnp.sum(jnp.square(in_sum.astype(f32)))
    lane = lax.broadcasted_iota(jnp.int32, (1, 128), 1)
    totals = jnp.where(lane == 0, squares, loss_tile[0:1])
    totals = all_sum(after(totals, *early_o))
    sums = [table_sum, in_sum, up_out_sum, down_sum]
    sums_o = [early_o[0], in_o, early_o[1], early_o[2]]
    count_now = optimizer_iteration.astype(f32)
    fixes = jnp.stack([1.0 - jnp.power(beta_one, count_now), 1.0 - jnp.power(beta_two, count_now)])
    results = optimizer(
        index,
        fixes,
        totals,
        send(totals, CORE),
        sums,
        sums_o,
        [
            lexicon_table.T,
            lexicon_first_moment.T,
            lexicon_raw_moment.T,
            query_key_value_maps,
            qkv_first_moment,
            qkv_raw_moment,
            attention_exit_map,
            exit_first_moment,
            exit_raw_moment,
            widening_matrix_in,
            widening_first_moment,
            widening_raw_moment,
            narrowing_matrix_out,
            narrowing_first_moment,
            narrowing_raw_moment,
            layernorm_scale_bias,
            layernorm_first_moment,
            layernorm_raw_moment,
        ],
    )
    results = list(results)
    results[:2] = [r[0, 0] for r in results[:2]]
    results[2:5] = [r.T for r in results[2:5]]
    return tuple(results)


def solution(mesh):
    in_specs = (
        P(("fsdp", "dp"), None),
        P(("fsdp", "dp"), None),
        P(("fsdp", "dp")),
        P(("fsdp", "dp")),
        P(),
        P(),
        P(None, "fsdp"),
        P(None, "fsdp"),
        P(None, "fsdp"),
        P("fsdp", None),
        P("fsdp", None),
        P("fsdp", None),
        P("fsdp", None),
        P("fsdp", None),
        P("fsdp", None),
        P("fsdp", None),
        P("fsdp", None),
        P("fsdp", None),
        P("fsdp", None),
        P("fsdp", None),
        P("fsdp", None),
        P(None, "fsdp"),
        P(None, "fsdp"),
        P(None, "fsdp"),
    )
    out_specs = (
        P(),
        P(),
        P(None, "fsdp"),
        P(None, "fsdp"),
        P(None, "fsdp"),
        P("fsdp", None),
        P("fsdp", None),
        P("fsdp", None),
        P("fsdp", None),
        P("fsdp", None),
        P("fsdp", None),
        P("fsdp", None),
        P("fsdp", None),
        P("fsdp", None),
        P("fsdp", None),
        P("fsdp", None),
        P("fsdp", None),
        P(None, "fsdp"),
        P(None, "fsdp"),
        P(None, "fsdp"),
    )
    own_plan = dict(mesh.shape) == {"fsdp": 16, "dp": 2}
    return jax.shard_map(
        per_device_links if own_plan else per_device, mesh=mesh, in_specs=in_specs, out_specs=out_specs, check_vma=False
    )
```

```python
import jax
import jax.numpy as jnp
from jax import lax
from jax.experimental import pallas as pl
from jax.experimental.pallas import tpu as pltpu
from jax.sharding import PartitionSpec as P

MODEL_WIDTH = 768
H = 12
HD = 64
SEG_ROW = 32


largest_value = lax.Precision.HIGHEST
beta_one = 0.9
beta_two = 0.999
adam_eps = 1e-12
decay_rate = 0.01
rate_matrix = 0.1
rate_embed = 1.0
rate_norm = 1.0
clip_norm = 0.001
norm_eps = 1e-05
unit_eps = 1e-06


def layer_norm(inputs, gain_row, shifts):
    center = inputs - jnp.mean(inputs, -1, keepdims=True)
    inv_std = lax.rsqrt(jnp.mean(center * center, -1, keepdims=True) + norm_eps)
    normed = center * inv_std
    return (normed * gain_row + shifts, normed, inv_std)


def norm_back(upstream, normed, inv_std, gain_row):
    scaled = upstream * gain_row
    grad_in = inv_std * (
        scaled
        - jnp.mean(scaled, -1, keepdims=True)
        - normed * jnp.mean(scaled * normed, -1, keepdims=True)
    )
    return (grad_in, jnp.sum(upstream * normed, 0), jnp.sum(upstream, 0))


def masked_scores(query_rows, key_rows, segment_rows):
    raw_scores = jnp.einsum(
        "bqhd,bkhd->bhqk", query_rows, key_rows, preferred_element_type=jnp.float32
    )
    same_segment = segment_rows[:, None, :, None] == segment_rows[:, None, None, :]
    return jnp.where(same_segment, raw_scores * HD ** (-0.5), -1e30)


def layer_forward(gathered, token_rows, segment_rows):
    (
        lexicon_table,
        query_key_value_maps,
        attention_exit_map,
        widening_matrix_in,
        narrowing_matrix_out,
        layernorm_scale_bias,
    ) = gathered
    batch_row_list, sequence_length = token_rows.shape
    embedded = jnp.take(lexicon_table, token_rows.reshape(-1), axis=0)
    qkv_all = jnp.dot(embedded, query_key_value_maps, preferred_element_type=jnp.float32).astype(
        jnp.bfloat16
    )
    qkv_all = qkv_all.reshape(batch_row_list, sequence_length, 3, H, HD)
    query_rows, key_rows, value_rows = (qkv_all[:, :, 0], qkv_all[:, :, 1], qkv_all[:, :, 2])
    scores = masked_scores(query_rows, key_rows, segment_rows)
    row_max = jnp.max(scores, -1, keepdims=True)
    log_total = row_max + jnp.log(jnp.sum(jnp.exp(scores - row_max), -1, keepdims=True))
    attn_probs = jnp.exp(scores - log_total).astype(jnp.bfloat16)
    mixed_heads = jnp.einsum(
        "bhqk,bkhd->bqhd", attn_probs, value_rows, preferred_element_type=jnp.float32
    )
    mixed_heads = mixed_heads.reshape(batch_row_list * sequence_length, MODEL_WIDTH).astype(
        jnp.bfloat16
    )
    attended = jnp.dot(mixed_heads, attention_exit_map, preferred_element_type=jnp.float32)
    normed_one, unit_one, inv_one = layer_norm(
        embedded.astype(jnp.float32) + attended, layernorm_scale_bias[0], layernorm_scale_bias[1]
    )
    normed_low = normed_one.astype(jnp.bfloat16)
    up_proj = jnp.dot(normed_low, widening_matrix_in, preferred_element_type=jnp.float32)
    activated = jax.nn.gelu(up_proj, approximate=False).astype(jnp.bfloat16)
    ffn_result = jnp.dot(activated, narrowing_matrix_out, preferred_element_type=jnp.float32)
    second_normalized, unit_two, inv_two = layer_norm(
        normed_one + ffn_result, layernorm_scale_bias[2], layernorm_scale_bias[3]
    )
    group_member = (
        segment_rows[:, None, :] == jnp.arange(SEG_ROW, dtype=jnp.int32)[None, :, None]
    ).astype(jnp.float32)
    pooled_state = jnp.einsum(
        "nkz,nzh->nkh",
        group_member,
        second_normalized.reshape(batch_row_list, sequence_length, MODEL_WIDTH),
        precision=largest_value,
    )
    saved_state = (
        embedded,
        query_rows,
        key_rows,
        value_rows,
        log_total,
        mixed_heads,
        unit_one,
        inv_one,
        normed_low,
        up_proj,
        activated,
        unit_two,
        inv_two,
        group_member,
    )
    return (pooled_state.reshape(batch_row_list * SEG_ROW, MODEL_WIDTH), saved_state)


def layer_backward(gathered, saved_state, token_rows, segment_rows, pooled_gradient):
    (
        lexicon_table,
        query_key_value_maps,
        attention_exit_map,
        widening_matrix_in,
        narrowing_matrix_out,
        layernorm_scale_bias,
    ) = gathered
    (
        embedded,
        query_rows,
        key_rows,
        value_rows,
        log_total,
        mixed_heads,
        unit_one,
        inv_one,
        normed_low,
        up_proj,
        activated,
        unit_two,
        inv_two,
        group_member,
    ) = saved_state
    batch_row_list, sequence_length = token_rows.shape
    pooled_gradient = pooled_gradient.reshape(batch_row_list, SEG_ROW, MODEL_WIDTH)
    second_gradient = jnp.einsum(
        "got,goy->gty", group_member, pooled_gradient, precision=largest_value
    ).reshape(batch_row_list * sequence_length, MODEL_WIDTH)
    grad_resid_two, grad_gain_two, grad_shift_two = norm_back(
        second_gradient, unit_two, inv_two, layernorm_scale_bias[2]
    )
    grad_result = grad_resid_two.astype(jnp.bfloat16)
    grad_ffn_down = jnp.einsum(
        "nf,nd->fd", activated, grad_result, preferred_element_type=jnp.float32
    )
    grad_act = jnp.einsum(
        "nd,fd->nf", grad_result, narrowing_matrix_out, preferred_element_type=jnp.float32
    )
    gelu_value, gelu_pull = jax.vjp(
        lambda pre_act: jax.nn.gelu(pre_act, approximate=False), up_proj
    )
    grad_up = gelu_pull(grad_act)[0].astype(jnp.bfloat16)
    grad_ffn_up = jnp.einsum("nd,nf->df", normed_low, grad_up, preferred_element_type=jnp.float32)
    grad_one = grad_resid_two + jnp.einsum(
        "nf,df->nd", grad_up, widening_matrix_in, preferred_element_type=jnp.float32
    )
    grad_resid_one, grad_gain_one, grad_shift_one = norm_back(
        grad_one, unit_one, inv_one, layernorm_scale_bias[0]
    )
    grad_attended = grad_resid_one.astype(jnp.bfloat16)
    grad_project_out = jnp.einsum(
        "nc,nd->cd", mixed_heads, grad_attended, preferred_element_type=jnp.float32
    )
    grad_mixed = jnp.einsum(
        "nd,cd->nc", grad_attended, attention_exit_map, preferred_element_type=jnp.float32
    )
    grad_mixed = grad_mixed.astype(jnp.bfloat16).reshape(batch_row_list, sequence_length, H, HD)
    scores = masked_scores(query_rows, key_rows, segment_rows)
    attn_probs = jnp.exp(scores - log_total)
    probs_low = attn_probs.astype(jnp.bfloat16)
    grad_values = jnp.einsum(
        "bhqk,bqhd->bkhd", probs_low, grad_mixed, preferred_element_type=jnp.float32
    )
    grad_probs = jnp.einsum(
        "bqhd,bkhd->bhqk", grad_mixed, value_rows, preferred_element_type=jnp.float32
    )
    grad_scores = attn_probs * (grad_probs - jnp.sum(grad_probs * attn_probs, -1, keepdims=True))
    grad_scores = grad_scores.astype(jnp.bfloat16)
    grad_query = jnp.einsum(
        "bhqk,bkhd->bqhd", grad_scores, key_rows, preferred_element_type=jnp.float32
    ) * HD ** (-0.5)
    grad_keys = jnp.einsum(
        "bhqk,bqhd->bkhd", grad_scores, query_rows, preferred_element_type=jnp.float32
    ) * HD ** (-0.5)
    grad_qkv = (
        jnp.stack([grad_query, grad_keys, grad_values], 2)
        .reshape(batch_row_list * sequence_length, 3 * MODEL_WIDTH)
        .astype(jnp.bfloat16)
    )
    grad_project_in = jnp.einsum(
        "nd,nc->dc", embedded, grad_qkv, preferred_element_type=jnp.float32
    )
    grad_embedded = grad_resid_one + jnp.einsum(
        "nc,dc->nd", grad_qkv, query_key_value_maps, preferred_element_type=jnp.float32
    )
    grad_norms = jnp.stack([grad_gain_one, grad_shift_one, grad_gain_two, grad_shift_two])
    return (
        grad_embedded,
        grad_project_in,
        grad_project_out,
        grad_ffn_up,
        grad_ffn_down,
        grad_norms,
    )


def adam_update(weight, first, second, grad, fix_first, fix_second, rate, decay):
    first_new = beta_one * first + (1.0 - beta_one) * grad
    second_new = beta_two * second + (1.0 - beta_two) * grad * grad
    step_size = first_new / fix_first / (jnp.sqrt(second_new / fix_second) + adam_eps)
    return (weight - rate * (step_size + decay * weight), first_new, second_new)


def per_device(
    kmer_identifiers,
    slot_fragment_ids,
    mirror_fragment_index,
    fragment_weight,
    affinity_heat,
    optimizer_iteration,
    lexicon_table,
    lexicon_first_moment,
    lexicon_raw_moment,
    query_key_value_maps,
    qkv_first_moment,
    qkv_raw_moment,
    attention_exit_map,
    exit_first_moment,
    exit_raw_moment,
    widening_matrix_in,
    widening_first_moment,
    widening_raw_moment,
    narrowing_matrix_out,
    narrowing_first_moment,
    narrowing_raw_moment,
    layernorm_scale_bias,
    layernorm_first_moment,
    layernorm_raw_moment,
):
    masters = (
        lexicon_table,
        query_key_value_maps,
        attention_exit_map,
        widening_matrix_in,
        narrowing_matrix_out,
        layernorm_scale_bias,
    )
    firsts = (
        lexicon_first_moment,
        qkv_first_moment,
        exit_first_moment,
        widening_first_moment,
        narrowing_first_moment,
        layernorm_first_moment,
    )
    seconds = (
        lexicon_raw_moment,
        qkv_raw_moment,
        exit_raw_moment,
        widening_raw_moment,
        narrowing_raw_moment,
        layernorm_raw_moment,
    )
    rates = (rate_embed, rate_matrix, rate_matrix, rate_matrix, rate_matrix, rate_norm)
    decays = (decay_rate, decay_rate, decay_rate, decay_rate, decay_rate, 0.0)
    lowered = tuple((piece.astype(jnp.bfloat16) for piece in masters))
    gathered = (
        lax.all_gather(lowered[0], "fsdp", axis=1, tiled=True),
        lax.all_gather(lowered[1], "fsdp", axis=0, tiled=True),
        lax.all_gather(lowered[2], "fsdp", axis=0, tiled=True),
        lax.all_gather(lowered[3], "fsdp", axis=0, tiled=True),
        lax.all_gather(lowered[4], "fsdp", axis=0, tiled=True),
        lax.all_gather(lowered[5], "fsdp", axis=1, tiled=True),
    )
    pooled_state, saved_state = layer_forward(gathered, kmer_identifiers, slot_fragment_ids)
    unit_scale = lax.rsqrt(jnp.sum(pooled_state * pooled_state, -1, keepdims=True) + unit_eps)
    unit_rows = pooled_state * unit_scale
    unit_low = unit_rows.astype(jnp.bfloat16)
    every_unit = lax.all_gather(unit_low, ("fsdp", "dp"), axis=0, tiled=True)
    cosine_affinity_grid = jnp.einsum(
        "sd,td->st", unit_low, every_unit, preferred_element_type=jnp.float32
    )
    seg_local = pooled_state.shape[0]
    fragment_tally = every_unit.shape[0]
    shard_fragment_lines = lax.axis_index(("fsdp", "dp")) * seg_local + jnp.arange(
        seg_local, dtype=jnp.int32
    )
    field_sequence_array = jnp.arange(fragment_tally, dtype=jnp.int32)
    raw_affinity_values = jnp.where(
        shard_fragment_lines[:, None] == field_sequence_array[None, :],
        -1e30,
        cosine_affinity_grid / affinity_heat,
    )
    row_max = jnp.max(raw_affinity_values, -1, keepdims=True)
    log_total = row_max[:, 0] + jnp.log(jnp.sum(jnp.exp(raw_affinity_values - row_max), -1))
    chosen = mirror_fragment_index[:, None] == field_sequence_array[None, :]
    chosen_real_entry = chosen.astype(jnp.float32)
    target = jnp.sum(jnp.where(chosen, raw_affinity_values, 0.0), -1)
    contrast_objective = (
        lax.psum(jnp.sum(fragment_weight * (log_total - target)), ("fsdp", "dp")) / fragment_tally
    )
    exponent_probabilities = jnp.exp(raw_affinity_values - log_total[:, None])
    similarity_gradient = (
        (exponent_probabilities - chosen_real_entry)
        * fragment_weight[:, None]
        / (fragment_tally * affinity_heat)
    ).astype(jnp.bfloat16)
    grad_rows = jnp.dot(similarity_gradient, every_unit, preferred_element_type=jnp.float32)
    column_terms = jnp.einsum(
        "st,sd->td", similarity_gradient, unit_low, preferred_element_type=jnp.float32
    )
    grad_cols = lax.psum_scatter(column_terms, ("fsdp", "dp"), scatter_dimension=0, tiled=True)
    grad_unit = grad_rows + grad_cols
    pooled_gradient = unit_scale * (
        grad_unit - unit_rows * jnp.sum(grad_unit * unit_rows, -1, keepdims=True)
    )
    again = (
        lax.all_gather(lowered[0], "fsdp", axis=1, tiled=True),
        lax.all_gather(lowered[1], "fsdp", axis=0, tiled=True),
        lax.all_gather(lowered[2], "fsdp", axis=0, tiled=True),
        lax.all_gather(lowered[3], "fsdp", axis=0, tiled=True),
        lax.all_gather(lowered[4], "fsdp", axis=0, tiled=True),
        lax.all_gather(lowered[5], "fsdp", axis=1, tiled=True),
    )
    grads = layer_backward(again, saved_state, kmer_identifiers, slot_fragment_ids, pooled_gradient)
    vocab = lexicon_table.shape[0]
    rest = (
        lax.psum_scatter(grads[1], "fsdp", scatter_dimension=0, tiled=True),
        lax.psum_scatter(grads[2], "fsdp", scatter_dimension=0, tiled=True),
        lax.psum_scatter(grads[3], "fsdp", scatter_dimension=0, tiled=True),
        lax.psum_scatter(grads[4], "fsdp", scatter_dimension=0, tiled=True),
        lax.psum_scatter(grads[5], "fsdp", scatter_dimension=1, tiled=True),
    )
    column_rows = lax.all_to_all(
        grads[0].astype(jnp.bfloat16), "fsdp", split_axis=1, concat_axis=0, tiled=True
    ).astype(jnp.float32)
    all_tokens = lax.all_gather(kmer_identifiers.reshape(-1), "fsdp", axis=0, tiled=True)
    table_shard = jax.ops.segment_sum(column_rows, all_tokens, num_segments=vocab)
    shards = (table_shard, rest[0], rest[1], rest[2], rest[3], rest[4])
    shards = (
        lax.psum(shards[0].astype(jnp.bfloat16), "dp").astype(jnp.float32),
        lax.psum(shards[1].astype(jnp.bfloat16), "dp").astype(jnp.float32),
        lax.psum(shards[2].astype(jnp.bfloat16), "dp").astype(jnp.float32),
        lax.psum(shards[3].astype(jnp.bfloat16), "dp").astype(jnp.float32),
        lax.psum(shards[4].astype(jnp.bfloat16), "dp").astype(jnp.float32),
        lax.psum(shards[5].astype(jnp.bfloat16), "dp").astype(jnp.float32),
    )
    squares = sum((jnp.sum(piece * piece) for piece in shards))
    grad_norm = jnp.sqrt(lax.psum(squares, "fsdp"))
    factor = clip_norm / jnp.maximum(grad_norm, clip_norm)
    count_now = optimizer_iteration.astype(jnp.float32)
    fix_first = 1.0 - jnp.power(beta_one, count_now)
    fix_second = 1.0 - jnp.power(beta_two, count_now)
    updated = [
        adam_update(
            masters[number],
            firsts[number],
            seconds[number],
            shards[number] * factor,
            fix_first,
            fix_second,
            rates[number],
            decays[number],
        )
        for number in range(6)
    ]
    return (
        contrast_objective,
        grad_norm,
        updated[0][0],
        updated[0][1],
        updated[0][2],
        updated[1][0],
        updated[1][1],
        updated[1][2],
        updated[2][0],
        updated[2][1],
        updated[2][2],
        updated[3][0],
        updated[3][1],
        updated[3][2],
        updated[4][0],
        updated[4][1],
        updated[4][2],
        updated[5][0],
        updated[5][1],
        updated[5][2],
    )


AXES = ("fsdp", "dp")
VOCAB_PAD = 4352
VOCAB_HALF = VOCAB_PAD // 2
BIG_VMEM = pltpu.CompilerParams(vmem_limit_bytes=60 * 1024 * 1024)
bf16 = jnp.bfloat16
f32 = jnp.float32


def pairs_of(moved):
    spots = [(z, y, x, c) for z in range(4) for y in range(2) for x in range(2) for c in range(2)]

    def linear(spot):
        z, y, x, c = spot
        return ((z * 2 + y) * 2 + x) * 2 + c

    return [(linear(spot), linear(moved(*spot))) for spot in spots]


FIRST = pairs_of(lambda z, y, x, c: (z, y, x ^ 1, c) if c == 0 else (z, y ^ 1, x, c))
SECOND = pairs_of(lambda z, y, x, c: (z, y ^ 1, x, c) if c == 0 else (z, y, x ^ 1, c))
BOTH = pairs_of(lambda z, y, x, c: (z, y ^ 1, x ^ 1, c))
CORE = pairs_of(lambda z, y, x, c: (z, y, x, 1 - c))
ZS = [None] + [pairs_of(lambda z, y, x, c, j=j: (z ^ j, y, x, c)) for j in (1, 2, 3)]


def send(array, pairs):
    return lax.ppermute(array, AXES, pairs)


def after(array, *others):
    return lax.optimization_barrier((array,) + others)[0]


def together(arrays, *others):
    arrays = list(arrays)
    return list(lax.optimization_barrier((*arrays, *others)))[: len(arrays)]


class Place:
    def __init__(self):
        f = lax.axis_index("fsdp")
        self.core = lax.axis_index("dp")
        self.z, self.y, self.x = f // 4, (f // 2) % 2, f % 2

    def plane_slot(self, core, a, b):
        dy = jnp.where(core == 0, b, a)
        dx = jnp.where(core == 0, a, b)
        return (self.y ^ dy) * 2 + (self.x ^ dx)

    def chip(self, core, j, a, b):
        return (self.z ^ j) * 4 + self.plane_slot(core, a, b)


def z_sends(piece):
    return [piece] + [send(piece, ZS[j]) for j in (1, 2, 3)]


def z_column(piece):
    return jnp.stack(z_sends(piece))


def plane_sends(column, direct=False, gate=()):
    one = send(column, FIRST)
    two = send(column, SECOND)
    three = send(column, BOTH) if direct else send(after(one, *gate), SECOND)
    return [column, one, two, three]


def both_cores(mine):
    return mine + [send(block, CORE) for block in mine]


Z_ROWS, BY_FLIP, FRAGMENTS, BY_PAIR, SLOTS, LOOKUP, PLANE = 0, 4, 68, 102, 166, 182, 191
MY_CORE = FRAGMENTS + 33


def index_vector(place):
    core, other = place.core, 1 - place.core
    n = jnp.arange(32, dtype=jnp.int32)
    who, m = jnp.where(n < 16, core, other), n % 16
    chips = place.chip(who, m % 4, (m // 4) % 2, m // 8)
    pairs = place.chip(who, (m // 2) % 4, m % 2, m // 8)
    base = (lax.axis_index("fsdp") * 2 + core) * 32
    k = jnp.arange(7, dtype=jnp.int32)
    side, flips = jnp.where(k < 4, core, other), jnp.where(k < 4, k, k - 3)
    reached = place.plane_slot(side, flips % 2, flips // 2)
    parts = [
        (place.z ^ jnp.arange(4, dtype=jnp.int32)) * 192,
        who,
        chips * 48,
        base,
        (chips * 2 + who) * 32,
        core,
        who,
        pairs * 192,
        chips[:16],
        reached * 48,
        core * VOCAB_HALF,
        other * VOCAB_HALF,
        core * VOCAB_HALF,
        reached[:4] * 48,
    ]
    return jnp.concatenate([jnp.atleast_1d(p).astype(jnp.int32) for p in parts])


class Part:
    def __init__(self, ref, start):
        self.ref, self.start = ref, start

    def __getitem__(self, number):
        return self.ref[self.start + number]


def scatter_add(keep, came):
    return (keep[4:].astype(f32) + came[4:].astype(f32)).astype(bf16)


def scatter_here(keep, came, came_two):
    here = [
        keep[j].astype(f32) + came[j].astype(f32) + came_two[j].astype(f32) for j in range(4)
    ]
    return here[0], [h.astype(bf16) for h in here[1:]]


def line_sends(far):
    return [send(h, ZS[j]) for h, j in zip(far, (1, 2, 3))]


def line_sum(here, far):
    return (here + far[0].astype(f32) + far[1].astype(f32) + far[2].astype(f32)).astype(bf16)


def whole_copies(sources, targets, sems):
    return [
        pltpu.make_async_copy(source, target, sems.at[number])
        for number, (source, target) in enumerate(zip(sources, targets))
    ]


class Stage:
    def __init__(self, copies_in, copies_out, pairs, sems):
        self.copies_in, self.copies_out = dict(enumerate(copies_in)), dict(enumerate(copies_out))
        self.started, self.pairs, self.sems = [], pairs, sems

    def __call__(self, *which):
        for number in which or tuple(self.copies_in):
            self.copies_in.pop(number).wait()

    def put(self, *which):
        for number in which or tuple(self.copies_out):
            copy = self.copies_out.pop(number)
            copy.start()
            self.started.append(copy)

    def put_half(self, side, half, which, width):
        cols = pl.ds(pl.multiple_of(half * width, 128), width)
        for number in which:
            self.copies_out.pop(number, None)
            source, target = self.pairs[number]
            copy = pltpu.make_async_copy(
                source.at[:, cols], target.at[:, cols], self.sems.at[side * len(which) + number]
            )
            copy.start()
            self.started.append(copy)

    def finish(self):
        self.put(*tuple(self.copies_out))
        for copy in self.started:
            copy.wait()


def staged_call(body, scalars, arrays, pieces, shapes, scratch, cost, late=(), staged_out=True):
    n_s, n_a, n_p, n_o = len(scalars), len(arrays), len(pieces), len(shapes)

    def kernel(*refs):
        smem, refs = [Part(r, s) for r, (_, s) in zip(refs, scalars)], refs[n_s:]
        hbm, refs = refs[:n_a], refs[n_a:]
        far, refs = refs[:n_p], refs[n_p:]
        out, refs = refs[:n_o], refs[n_o:]
        near_in, refs = refs[:n_a], refs[n_a:]
        if staged_out:
            near_out, refs = refs[:n_o], refs[n_o:]
        else:
            near_out, out = out, []
        in_sems, out_sems, half_sems, refs = refs[0], refs[1], refs[2], refs[3:]
        copies = whole_copies(hbm, near_in, in_sems)
        for number, copy in enumerate(copies):
            if number not in late:
                copy.start()
        pairs = list(zip(near_out, out))
        stage = Stage(copies, whole_copies(near_out, out, out_sems), pairs, half_sems)
        body(stage, *smem, *near_in, *far, *near_out, *refs)
        stage.finish()

    in_hbm = pl.BlockSpec(memory_space=pltpu.HBM)
    return pl.pallas_call(
        kernel,
        out_shape=shapes,
        in_specs=[pl.BlockSpec(memory_space=pltpu.SMEM)] * n_s + [in_hbm] * (n_a + n_p),
        out_specs=[in_hbm] * n_o,
        scratch_shapes=[pltpu.VMEM(a.shape, a.dtype) for a in arrays]
        + [pltpu.VMEM(s.shape, s.dtype) for s in shapes if staged_out]
        + [pltpu.SemaphoreType.DMA((n,)) for n in (n_a, n_o, 4)]
        + scratch,
        cost_estimate=pl.CostEstimate(flops=int(cost * 1e9), bytes_accessed=0, transcendentals=0),
        compiler_params=BIG_VMEM,
    )(*[vector for vector, _ in scalars], *arrays, *pieces)


def shaped(dtype, *dims):
    return jax.ShapeDtypeStruct(dims, dtype)


def one_hot(ids_row, start, count):
    spots = lax.broadcasted_iota(jnp.int32, (count, ids_row.shape[1]), 0) + start
    return jnp.where(spots == ids_row, 1.0, 0.0).astype(bf16)


def prepare_kernel(
    ready, core_ref, table_ref, in_ref, out_ref, up_ref, down_ref, norm_ref, ids_ref, weight_ref,
    both_ref, cut_ref, half_ref, down_half_ref,
):
    core = core_ref[0]

    def mine(ref, width, start=0):
        return ref[:, pl.ds(pl.multiple_of(start + core * width, 128), width)].astype(bf16)

    ready(1, 2, 3, 5, 6, 7)
    for t in range(3):
        both_ref[:, t * 384 : (t + 1) * 384] = mine(in_ref, 384, t * 768)
    both_ref[:, 1152:1536] = mine(out_ref, 384)
    rest = jnp.zeros((1, 16), f32)
    heavy = [jnp.concatenate([w.astype(f32), rest], 1) for w in thirds(weight_ref[...])]
    extra = jnp.concatenate([norm_ref[...]] + heavy + [jnp.zeros((121, 48), f32)], 0)
    both_ref[:, 1536:1664] = extra.T.astype(bf16)
    both_ref[:, 1664:3200] = mine(up_ref, 1536)
    ids = jnp.concatenate([ids_ref[:, k * 128 : (k + 1) * 128] for k in range(4)], 0)
    high = lax.shift_right_logical(ids, 6)
    ids = jnp.concatenate([high, ids - high * 64], 0).astype(f32).astype(bf16)
    both_ref[:, 3200:3328] = jnp.concatenate([ids, jnp.zeros((40, 128), bf16)], 0)
    ready.put(0)
    ready(0, 4)
    vocab = table_ref.shape[1]
    even = vocab - vocab % 128
    cut_ref[:, :even] = table_ref[:, :even].astype(bf16)
    last = [table_ref[:, even:], jnp.zeros((48, VOCAB_PAD - vocab), f32)]
    cut_ref[:, even:] = jnp.concatenate(last, 1).astype(bf16)
    half_ref[...] = cut_ref[:, pl.ds(pl.multiple_of(core * VOCAB_HALF, 128), VOCAB_HALF)]
    down_half_ref[...] = mine(down_ref, 384)


def prepare(core, arrays):
    return staged_call(
        prepare_kernel,
        [(core, MY_CORE)],
        arrays,
        [],
        [
            shaped(bf16, 48, 3328),
            shaped(bf16, 48, VOCAB_PAD),
            shaped(bf16, 48, VOCAB_HALF),
            shaped(bf16, 192, 384),
        ],
        [],
        3,
    )


def id_row(ids_ref, j):
    rows = ids_ref[j]
    return jnp.concatenate([rows[k : k + 1] for k in range(4)], 1)


def lookup_kernel(ready, idx_ref, ids_ref, down_ref, down_first_ref, *refs):
    ins = list(refs[:4]) + [refs[4].at[k] for k in range(3)]
    outs, table, sems = refs[5:9], refs[9], refs[10]
    copies = [
        pltpu.make_async_copy(
            ins[0], table.at[pl.ds(pl.multiple_of(idx_ref[0], 16), 48), :], sems.at[0]
        )
    ]
    for number in range(1, 7):
        column = pl.multiple_of(idx_ref[7 + (number - 1) // 3], 128)
        row = pl.multiple_of(idx_ref[number], 16)
        copies.append(
            pltpu.make_async_copy(
                ins[number],
                table.at[pl.ds(row, 48), pl.ds(column, VOCAB_HALF)],
                sems.at[number],
            )
        )
    for copy in copies:
        copy.start()
    ready()
    for copy in copies:
        copy.wait()
    for j in range(4):
        total = jnp.zeros((192, 512), f32)
        for k in range(VOCAB_PAD // 256):
            total += jnp.dot(
                table[:, k * 256 : (k + 1) * 256],
                one_hot(id_row(ids_ref, j), k * 256, 256),
                preferred_element_type=f32,
            )
        outs[j][:, :512] = total.astype(bf16)
    outs[1][:, 512:896] = down_ref[...]
    outs[1][:, 896:] = down_first_ref[...]


def lookup(index, ids_z, down_pair, arrays):
    return staged_call(
        lookup_kernel,
        [(index, LOOKUP)],
        [ids_z, *down_pair],
        arrays,
        [
            shaped(bf16, 192, 512),
            shaped(bf16, 192, 1280),
            shaped(bf16, 192, 512),
            shaped(bf16, 192, 512),
        ],
        [
            pltpu.VMEM((192, VOCAB_PAD), bf16),
            pltpu.SemaphoreType.DMA((7,)),
        ],
        6,
    )


def token_sum_kernel(
    ready, idx_ref, ids_ref, other_ids_ref, mine_ref, other_ref, keep_ref, away_ref, whole_ref, sems
):
    ready()
    start = idx_ref[0]
    for low in range(0, VOCAB_HALF, 256):
        count = min(256, VOCAB_HALF - low)
        total = jnp.zeros((192, count), f32)
        for ids, block in ((ids_ref, mine_ref), (other_ids_ref, other_ref)):
            for j in range(4):
                total += lax.dot_general(
                    block[j],
                    one_hot(id_row(ids, j), start + low, count),
                    (((1,), (1,)), ((), ())),
                    preferred_element_type=f32,
                )
        whole_ref[:, low : low + count] = total.astype(bf16)
    copies = []
    for k in range(4):
        rows = pl.ds(pl.multiple_of(idx_ref[1 + k], 16), 48)
        ref = keep_ref if k < 2 else away_ref
        copies.append(pltpu.make_async_copy(whole_ref.at[rows, :], ref.at[k % 2], sems.at[k]))
    for copy in copies[::-1]:
        copy.start()
    for copy in copies:
        copy.wait()


def token_sum(index, ids_z, other_ids, mine, other):
    return staged_call(
        token_sum_kernel,
        [(index, PLANE)],
        [ids_z, other_ids, mine, other],
        [],
        [
            shaped(bf16, 2, 48, VOCAB_HALF),
            shaped(bf16, 2, 48, VOCAB_HALF),
        ],
        [
            pltpu.VMEM((192, VOCAB_HALF), bf16),
            pltpu.SemaphoreType.DMA((4,)),
        ],
        8,
        staged_out=False,
    )


def my_half(array, core, width):
    return lax.dynamic_slice_in_dim(array, core * width, width, axis=1)


def all_sum(value):
    for pairs in (ZS[1:], [FIRST, SECOND, BOTH]):
        one, two, three = (send(value, p) for p in pairs)
        value = (value + one) + (two + three)
    return value


WINDOWS = (0, 64, 192, 256)
SCALE = HD ** (-0.5)


def piece_copies(idx_ref, base, pieces, target, rows, sems, first_sem):
    copies = []
    for number in range(32):
        half = idx_ref[base + number]
        row = pl.multiple_of(idx_ref[base + 32 + number], 16)
        each = 32 // len(pieces)
        source = pieces[number // each].at[number % each]
        copies.append(
            pltpu.make_async_copy(
                source, target.at[half, pl.ds(row, rows), :], sems.at[first_sem + number]
            )
        )
    return copies


def window_bias(seg_row, seg_col, b):
    w = WINDOWS[b]
    same = seg_col[b * 128 : (b + 1) * 128, :] == seg_row[:, w : w + 256]
    bias = jnp.where(same, 0.0, -1e30)
    return jnp.concatenate([bias, bias], 0)


def two_heads(block):
    left = lax.broadcasted_iota(jnp.int32, block.shape, 1) < HD
    none = jnp.zeros_like(block)
    return jnp.concatenate([jnp.where(left, block, none), jnp.where(left, none, block)], 0)


def nt_dot(a, b):
    return lax.dot_general(a, b, (((1,), (1,)), ((), ())), preferred_element_type=f32)


def tn_dot(a, b):
    return lax.dot_general(a, b, (((0,), (0,)), ((), ())), preferred_element_type=f32)


def nn_dot(a, b):
    return jnp.dot(a, b, preferred_element_type=f32)


def row_norm(v):
    center = v - jnp.mean(v, -1, keepdims=True)
    inv = lax.rsqrt(jnp.mean(center * center, -1, keepdims=True) + norm_eps)
    return center * inv, inv


def attention_kernel(ready, idx_ref, seg_row_ref, seg_col_ref, *refs):
    e_in, pieces = refs[:4], refs[4:12]
    (e_ref, qkv_ref, lse_ref, mixed_ref, unit_ref, inv_ref, low_ref, par_ref, side_ref) = refs[12:21]
    et_ref, w_ref, bias_ref, attended_ref, sems = refs[21:]
    e_copies = [
        pltpu.make_async_copy(
            e_in[j].at[:, pl.ds(0, 512)],
            et_ref.at[pl.ds(pl.multiple_of(idx_ref[j], 16), 192), :],
            sems.at[j],
        )
        for j in range(4)
    ]
    w_copies = piece_copies(idx_ref, 4, pieces, w_ref, 48, sems, 4)
    for copy in e_copies + w_copies:
        copy.start()
    ready()
    for b in range(4):
        bias_ref[b] = window_bias(seg_row_ref[...], seg_col_ref[...], b)
    for copy in e_copies:
        copy.wait()
    e_ref[...] = et_ref[...].T
    ready.put(0)
    for copy in w_copies:
        copy.wait()
    par_ref[...] = w_ref[0, :, 1536:1664].T.astype(f32)[:8]
    side_ref[...] = w_ref[:, :, 1536:1664]
    for k in range(2):
        for t in range(3):
            part = nn_dot(e_ref[...], w_ref[k, :, t * 384 : (t + 1) * 384])
            if t == 0:
                part = part.astype(bf16).astype(f32) * SCALE
            part = part.astype(bf16)
            for i in range(3):
                qkv_ref[t * 6 + k * 3 + i] = part[:, i * 128 : (i + 1) * 128]
    ready.put(1, 7, 8)
    lse_ref[...] = jnp.zeros_like(lse_ref)
    lane = lax.broadcasted_iota(jnp.int32, (128, 128), 1)
    left = lane < HD

    @pl.loop(0, 6, unroll=3)
    def _(pair):
        for b in range(4):
            rows = pl.ds(b * 128, 128)
            keys = pl.ds(WINDOWS[b], 256)
            q = qkv_ref[pair, rows, :]
            k = qkv_ref[pair + 6, keys, :]
            v = qkv_ref[pair + 12, keys, :]
            s = nt_dot(two_heads(q), k) + bias_ref[b]
            top = jnp.max(s, -1, keepdims=True)
            e = jnp.exp(s - top)
            total = jnp.sum(e, -1, keepdims=True)
            log = top + jnp.log(total)
            lse = jnp.where(lane == pair * 2, log[:128], lse_ref[rows, :])
            lse_ref[rows, :] = jnp.where(lane == pair * 2 + 1, log[128:], lse)
            mixed = nn_dot((e * (1.0 / total)).astype(bf16), v)
            cols = pl.ds(pl.multiple_of(pair * 128, 128), 128)
            mixed_ref[rows, cols] = jnp.where(left, mixed[:128], mixed[128:]).astype(bf16)

    ready.put(2, 3)
    for k in range(2):
        attended_ref[:, k * 384 : (k + 1) * 384] = nn_dot(mixed_ref[...], w_ref[k, :, 1152:1536])
    for b in range(4):
        rows = slice(b * 128, (b + 1) * 128)
        unit, inv = row_norm(e_ref[rows, :].astype(f32) + attended_ref[rows, :])
        unit_ref[rows, :] = unit
        inv_ref[rows, :] = jnp.broadcast_to(inv, (128, 128))
        low_ref[rows, :] = (unit * par_ref[0:1, :] + par_ref[1:2, :]).astype(bf16)


def attention_forward(index, seg_row, seg_col, columns, pieces):
    return staged_call(
        attention_kernel,
        [(index, Z_ROWS)],
        [seg_row, seg_col],
        [*columns, *pieces],
        [
            shaped(bf16, 512, 768),
            shaped(bf16, 18, 512, 128),
            shaped(f32, 512, 128),
            shaped(bf16, 512, 768),
            shaped(f32, 512, 768),
            shaped(f32, 512, 128),
            shaped(bf16, 512, 768),
            shaped(f32, 8, 768),
            shaped(bf16, 2, 768, 128),
        ],
        [
            pltpu.VMEM((768, 512), bf16),
            pltpu.VMEM((2, 768, 1664), bf16),
            pltpu.VMEM((4, 256, 256), f32),
            pltpu.VMEM((512, 768), f32),
            pltpu.SemaphoreType.DMA((36,)),
        ],
        17,
    )


def gelu_and_slope(u):
    bell = jnp.exp(-0.5 * u * u)
    base = 1.0 + (0.3275911 * 0.5**0.5) * jnp.abs(u)
    t = pl.reciprocal(base, approx=True)
    t = t * (2.0 - base * t)
    poly = -0.07032334059476852
    for factor in (
        0.24725385010242462,
        -0.2008872926235199,
        0.2245105654001236,
        0.013965459540486336,
        0.10251718759536743,
        0.09044301509857178,
        0.09252061694860458,
    ):
        poly = factor + t * poly
    tail = (t * poly) * bell
    phi = jnp.where(u < 0, tail, 1.0 - tail)
    return u * phi, phi + (u * 0.3989422804014327) * bell


def up_kernel(ready, idx_ref, low_ref, *refs):
    pieces, act_ref, slope_ref, w_ref, sems = refs[:8], refs[8], refs[9], refs[10], refs[11]
    copies = piece_copies(idx_ref, 0, pieces, w_ref, 48, sems, 0)
    for copy in copies:
        copy.start()
    ready()
    core = idx_ref[0]
    for side in range(2):
        half = core if side == 0 else 1 - core
        for copy in copies[side * 16 : side * 16 + 16]:
            copy.wait()

        @pl.loop(0, 6, unroll=3)
        def _(n):
            cols = pl.ds(pl.multiple_of(n * 256, 256), 256)
            u = nn_dot(low_ref[...], w_ref[half, :, cols])
            value, slope = gelu_and_slope(u)
            out_cols = pl.ds(pl.multiple_of(half * 1536 + n * 256, 256), 256)
            act_ref[:, out_cols] = value.astype(bf16)
            slope_ref[:, out_cols] = slope.astype(bf16)

        ready.put_half(side, half, (0, 1), 1536)


def up_forward(index, low, pieces):
    return staged_call(
        up_kernel,
        [(index, BY_FLIP)],
        [low],
        pieces,
        [
            shaped(bf16, 512, 3072),
            shaped(bf16, 512, 3072),
        ],
        [
            pltpu.VMEM((2, 768, 1536), bf16),
            pltpu.SemaphoreType.DMA((32,)),
        ],
        18,
    )


def thirds(v):
    high = v.astype(bf16)
    rest = v - high.astype(f32)
    middle = rest.astype(bf16)
    return high, middle, (rest - middle.astype(f32)).astype(bf16)


def down_kernel(ready, idx_ref, seg_row_ref, act_ref, unit_one_ref, par_ref, *refs):
    unit_ref, inv_ref, frag_ref, frag_low_ref, size_ref, w_ref, result_ref, sems = refs[4:]
    copies = piece_copies(idx_ref, 0, refs[:4], w_ref, 192, sems, 0)
    for copy in copies:
        copy.start()
    ready()
    for copy in copies:
        copy.wait()
    for k in range(2):
        result_ref[:, k * 384 : (k + 1) * 384] = nn_dot(act_ref[...], w_ref[k])
    pooled = jnp.zeros((32, 768), f32)
    for b in range(4):
        rows = slice(b * 128, (b + 1) * 128)
        one = unit_one_ref[rows, :] * par_ref[0:1, :] + par_ref[1:2, :]
        unit, inv = row_norm(one + result_ref[rows, :])
        unit_ref[rows, :] = unit
        inv_ref[rows, :] = jnp.broadcast_to(inv, (128, 128))
        two = unit * par_ref[2:3, :] + par_ref[3:4, :]
        member = lax.broadcasted_iota(jnp.int32, (32, 128), 0) == seg_row_ref[:, rows]
        member = jnp.where(member, 1.0, 0.0).astype(bf16)
        for part in thirds(two):
            pooled += nn_dot(member, part)
    size = lax.rsqrt(jnp.sum(pooled * pooled, -1, keepdims=True) + unit_eps)
    frag = pooled * size
    frag_ref[...] = frag
    frag_low_ref[...] = frag.astype(bf16)
    size_ref[...] = jnp.broadcast_to(size, (32, 128))


def down_forward(index, seg_row, act, unit_one, params, pieces):
    return staged_call(
        down_kernel,
        [(index, BY_PAIR)],
        [seg_row, act, unit_one, params],
        pieces,
        [
            shaped(f32, 512, 768),
            shaped(f32, 512, 128),
            shaped(f32, 32, 768),
            shaped(bf16, 32, 768),
            shaped(f32, 32, 128),
        ],
        [
            pltpu.VMEM((2, 3072, 384), bf16),
            pltpu.VMEM((512, 768), f32),
            pltpu.SemaphoreType.DMA((32,)),
        ],
        10,
    )


def back_norm(upstream, unit, inv, gain):
    scaled = upstream * gain
    return inv * (
        scaled
        - jnp.mean(scaled, -1, keepdims=True)
        - unit * jnp.mean(scaled * unit, -1, keepdims=True)
    )


def loss_kernel(
    ready, idx_ref, heat_ref, seg_col_ref, partner_ref, own_weight_ref, side_ref,
    frag_ref, size_ref, unit_ref, inv_ref, par_ref, slope_ref, *refs
):
    blocks, down_pieces = refs[:8], refs[8:12]
    loss_ref, low_own_ref, low_other_ref, gup_own_ref, gup_other_ref, two_ref, gains_ref = refs[12:19]
    all_ref, down_ref, low_ref, spread_ref, sems, w_sems = refs[19:]
    copies = []
    for number in range(32):
        row = pl.multiple_of(idx_ref[1 + number], 16)
        copies.append(
            pltpu.make_async_copy(
                blocks[number // 4].at[number % 4], all_ref.at[pl.ds(row, 32), :], sems.at[number]
            )
        )
    core = idx_ref[33]
    down_copies = piece_copies(idx_ref, 34, down_pieces, down_ref, 192, w_sems, 0)
    for copy in copies:
        copy.start()
    for copy in copies:
        copy.wait()
    ready(1, 2, 3)
    ready.copies_in[9].start()
    for copy in down_copies:
        copy.start()
    base = idx_ref[0]
    inv_heat = 1.0 / heat_ref[0]
    tally = 1024
    mine = all_ref[pl.ds(pl.multiple_of(base, 16), 32), :]
    grid = (nt_dot(mine, all_ref[...]) - 1.0) * inv_heat
    across = lax.broadcasted_iota(jnp.int32, (32, tally), 1)
    down = lax.broadcasted_iota(jnp.int32, (32, tally), 0) + base
    powers = jnp.where(across == down, 0.0, jnp.exp(grid))
    total = jnp.sum(powers, -1, keepdims=True)
    eye = lax.broadcasted_iota(jnp.int32, (32, 32), 0) == lax.broadcasted_iota(jnp.int32, (32, 32), 1)
    partner = jnp.sum(jnp.where(eye, partner_ref[...].astype(f32), 0.0), -1, keepdims=True)
    own_weight = jnp.sum(jnp.where(eye, own_weight_ref[...], 0.0), -1, keepdims=True)
    chosen = across == partner.astype(jnp.int32)
    target = jnp.sum(jnp.where(chosen, grid, 0.0), -1, keepdims=True)
    terms = own_weight * (jnp.log(total) - target)
    loss_ref[...] = jnp.broadcast_to(jnp.sum(terms, 0, keepdims=True) / tally, (8, 128))
    picked = jnp.where(chosen, 1.0, 0.0)
    pull = (powers / total - picked) * (own_weight * (inv_heat / tally))
    totals = [jnp.zeros((1, 128), f32) for _ in range(8)]
    number = lax.broadcasted_iota(jnp.int32, (128, 128), 0)
    same = number == lax.broadcasted_iota(jnp.int32, (128, 128), 1)
    weights = []
    for big in range(2):
        spread_ref[...] = nt_dot(all_ref[big * 512 : (big + 1) * 512, :], all_ref[...])
        for b in range(big * 4, big * 4 + 4):
            inside = slice((b - big * 4) * 128, (b - big * 4 + 1) * 128)
            for n in range(8):
                spread = jnp.exp((spread_ref[inside, n * 128 : (n + 1) * 128] - 1.0) * inv_heat)
                if n == b:
                    spread = jnp.where(same, 0.0, spread)
                totals[n] += jnp.sum(spread, 0, keepdims=True)
            side = jnp.concatenate(
                [
                    side_ref[n % 2, (n // 2) * 48 : (n // 2) * 48 + 32, :].astype(f32)
                    for n in range(b * 4, b * 4 + 4)
                ],
                0,
            ).T
            weights.append(side[4:5] + side[5:6] + side[6:7])
    totals, weights = jnp.concatenate(totals, 1), jnp.concatenate(weights, 1)
    column_pull = (powers / totals - picked) * (weights * (inv_heat / tally))
    both = jnp.concatenate([pull.astype(bf16), column_pull.astype(bf16)], 0)
    both = nn_dot(both, all_ref[...])
    grad = both[:32] + both[32:]
    ready(0, 4, 5, 6, 7, 8)
    frag = frag_ref[...]
    pooled = size_ref[:, 0:1] * (grad - frag * jnp.sum(grad * frag, -1, keepdims=True))
    stacked = jnp.concatenate(thirds(pooled), 0)
    gain_two = jnp.zeros((1, 768), f32)
    shift_two = jnp.zeros((1, 768), f32)
    for b in range(4):
        rows = slice(b * 128, (b + 1) * 128)
        slot = lax.broadcasted_iota(jnp.int32, (128, 96), 1) % 32
        member = jnp.where(slot == seg_col_ref[rows, :], 1.0, 0.0).astype(bf16)
        upstream = nn_dot(member, stacked)
        unit = unit_ref[rows, :]
        back = back_norm(upstream, unit, inv_ref[rows, 0:1], par_ref[2:3, :])
        two_ref[rows, :] = back
        low_ref[rows, :] = back.astype(bf16)
        gain_two += jnp.sum(upstream * unit, 0, keepdims=True)
        shift_two += jnp.sum(upstream, 0, keepdims=True)
    halves = (core, 1 - core)
    for half, ref in zip(halves, (low_own_ref, low_other_ref)):
        ref[...] = low_ref[:, pl.ds(pl.multiple_of(half * 384, 128), 384)]
    ready.put(0, 1, 2, 5)
    ready(9)
    for copy in down_copies:
        copy.wait()
    for half, gup_ref in zip(halves, (gup_own_ref, gup_other_ref)):

        @pl.loop(0, 6, unroll=3)
        def _(n):
            cols = pl.ds(pl.multiple_of(n * 256, 256), 256)
            wide = pl.ds(pl.multiple_of(half * 1536 + n * 256, 256), 256)
            g = sum(
                nt_dot(low_ref[:, k * 384 : (k + 1) * 384], down_ref[k, wide, :])
                for k in range(2)
            )
            gup_ref[:, cols] = (g * slope_ref[:, wide].astype(f32)).astype(bf16)

        if gup_ref is gup_own_ref:
            ready.put(3)

    gains_ref[...] = jnp.concatenate([gain_two, shift_two, jnp.zeros((6, 768), f32)], 0)


def loss_backward(index, heat, arrays, pieces):
    return staged_call(
        loss_kernel,
        [(index, FRAGMENTS), (heat, 0)],
        arrays,
        pieces,
        [
            shaped(f32, 8, 128),
            shaped(bf16, 512, 384),
            shaped(bf16, 512, 384),
            shaped(bf16, 512, 1536),
            shaped(bf16, 512, 1536),
            shaped(f32, 512, 768),
            shaped(f32, 8, 768),
        ],
        [
            pltpu.VMEM((1024, 768), bf16),
            pltpu.VMEM((2, 3072, 384), bf16),
            pltpu.VMEM((512, 768), bf16),
            pltpu.VMEM((512, 1024), f32),
            pltpu.SemaphoreType.DMA((32,)),
            pltpu.SemaphoreType.DMA((32,)),
        ],
        18,
        (9,),
    )


def ffn_back_kernel(
    ready, idx_ref, gup_own_ref, gup_other_ref, two_ref, unit_ref, inv_ref, par_ref, gains_two_ref, *refs
):
    pieces = refs[:8]
    resid_ref, att_ref, own_ref, other_ref, gains_ref, up_ref, sems = refs[8:]
    copies = piece_copies(idx_ref, 0, pieces, up_ref, 48, sems, 0)
    for copy in copies:
        copy.start()
    ready()
    for copy in copies:
        copy.wait()
    core = idx_ref[0]
    for n in range(3):
        cols = slice(n * 256, (n + 1) * 256)
        resid_ref[:, cols] = (
            two_ref[:, cols]
            + nt_dot(gup_own_ref[...], up_ref[core, cols, :])
            + nt_dot(gup_other_ref[...], up_ref[1 - core, cols, :])
        )
    gain_sum = jnp.zeros((1, 768), f32)
    shift_sum = jnp.zeros((1, 768), f32)
    for b in range(4):
        rows = slice(b * 128, (b + 1) * 128)
        one = resid_ref[rows, :]
        unit = unit_ref[rows, :]
        back = back_norm(one, unit, inv_ref[rows, 0:1], par_ref[0:1, :])
        resid_ref[rows, :] = back
        att_ref[rows, :] = back.astype(bf16)
        gain_sum += jnp.sum(one * unit, 0, keepdims=True)
        shift_sum += jnp.sum(one, 0, keepdims=True)
    for half, ref in ((core, own_ref), (1 - core, other_ref)):
        ref[...] = att_ref[:, pl.ds(pl.multiple_of(half * 384, 128), 384)]
    gains_ref[...] = jnp.concatenate(
        [gain_sum, shift_sum, gains_two_ref[0:2, :], jnp.zeros((4, 768), f32)], 0
    )


def ffn_backward(index, arrays, pieces):
    return staged_call(
        ffn_back_kernel,
        [(index, BY_FLIP)],
        arrays,
        pieces,
        [
            shaped(f32, 512, 768),
            shaped(bf16, 512, 768),
            shaped(bf16, 512, 384),
            shaped(bf16, 512, 384),
            shaped(f32, 8, 768),
        ],
        [pltpu.VMEM((2, 768, 1536), bf16), pltpu.SemaphoreType.DMA((32,))],
        9,
    )


def heads_back(half, gm_ref, qkv_ref, lse_ref, bias_ref, gqkv_ref, gk_ref, gv_ref):
    lane = lax.broadcasted_iota(jnp.int32, (128, 128), 1)
    left = lane < HD
    gk_ref[...] = jnp.zeros_like(gk_ref)
    gv_ref[...] = jnp.zeros_like(gv_ref)

    @pl.loop(0, 3, unroll=3)
    def _(spot):
        pair = half * 3 + spot
        for b in range(4):
            rows = pl.ds(b * 128, 128)
            keys = pl.ds(WINDOWS[b], 256)
            q = qkv_ref[pair, rows, :]
            k = qkv_ref[pair + 6, keys, :]
            v = qkv_ref[pair + 12, keys, :]
            gm = gm_ref[rows, pl.ds(pl.multiple_of(spot * 128, 128), 128)]
            q, gm = two_heads(q), two_heads(gm)
            stats = lse_ref[rows, :]
            lse = jnp.concatenate(
                [
                    jnp.sum(jnp.where(lane == pair * 2 + h, stats, 0.0), -1, keepdims=True)
                    for h in range(2)
                ],
                0,
            )
            p = jnp.exp(nt_dot(q, k) + bias_ref[b] - lse)
            gp = nt_dot(gm, v)
            gs = (p * (gp - jnp.sum(gp * p, -1, keepdims=True))).astype(bf16)
            gq = nn_dot(gs, k)
            gq = (jnp.where(left, gq[:128], gq[128:]) * SCALE).astype(bf16)
            gqkv_ref[rows, pl.ds(pl.multiple_of(spot * 128, 128), 128)] = gq
            gk_ref[spot, keys, :] += tn_dot(gs, q)
            gv_ref[spot, keys, :] += tn_dot(p.astype(bf16), gm)
        for third, ref in ((1, gk_ref), (2, gv_ref)):
            cols = pl.ds(pl.multiple_of(third * 384 + spot * 128, 128), 128)
            gqkv_ref[:, cols] = ref[spot].astype(bf16)


def other_heads_kernel(ready, idx_ref, seg_row_ref, seg_col_ref, qkv_ref, lse_ref, att_ref, resid_ref, *refs
):
    pieces = refs[:8]
    gqkv_ref, gm_own_ref, part_ref = refs[8:11]
    w_ref, bias_ref, gm_ref, gk_ref, gv_ref, sems = refs[11:]
    copies = piece_copies(idx_ref, 4, pieces, w_ref, 48, sems, 0)
    for copy in copies:
        copy.start()
    ready()
    for b in range(4):
        bias_ref[b] = window_bias(seg_row_ref[...], seg_col_ref[...], b)
    for copy in copies:
        copy.wait()
    core = idx_ref[4]
    half = 1 - core
    for side, ref in ((half, gm_ref), (core, gm_own_ref)):
        rows = pl.ds(pl.multiple_of(side * 384, 128), 384)
        ref[...] = sum(
            nt_dot(att_ref[:, k * 384 : (k + 1) * 384], w_ref[k, rows, 1152:1536])
            for k in range(2)
        ).astype(bf16)
    heads_back(half, gm_ref, qkv_ref, lse_ref, bias_ref, gqkv_ref, gk_ref, gv_ref)
    ready.put(0, 1)
    for n in range(3):
        cols = slice(n * 256, (n + 1) * 256)
        part_ref[:, cols] = resid_ref[:, cols] + nt_dot(gqkv_ref[...], w_ref[half, cols, :1152])


def other_heads(index, arrays, pieces):
    return staged_call(
        other_heads_kernel,
        [(index, Z_ROWS)],
        arrays,
        pieces,
        [
            shaped(bf16, 512, 1152),
            shaped(bf16, 512, 384),
            shaped(f32, 512, 768),
        ],
        [
            pltpu.VMEM((2, 768, 1664), bf16),
            pltpu.VMEM((4, 256, 256), f32),
            pltpu.VMEM((512, 384), bf16),
            pltpu.VMEM((3, 512, 128), f32),
            pltpu.VMEM((3, 512, 128), f32),
            pltpu.SemaphoreType.DMA((32,)),
        ],
        17,
    )


def own_heads_kernel(ready, idx_ref, seg_row_ref, seg_col_ref, qkv_ref, lse_ref, gm_ref, part_ref, *refs
):
    pieces = refs[:4]
    gqkv_ref, outs = refs[4], refs[5:9]
    w_ref, bias_ref, gk_ref, gv_ref, et_ref, sems = refs[9:]
    copies = []
    for number in range(16):
        row = pl.multiple_of(idx_ref[36 + number], 16)
        copies.append(
            pltpu.make_async_copy(
                pieces[number // 4].at[number % 4], w_ref.at[pl.ds(row, 48), :], sems.at[number]
            )
        )
    for copy in copies:
        copy.start()
    ready()
    for b in range(4):
        bias_ref[b] = window_bias(seg_row_ref[...], seg_col_ref[...], b)
    core = idx_ref[4]
    heads_back(core, gm_ref, qkv_ref, lse_ref, bias_ref, gqkv_ref, gk_ref, gv_ref)
    ready.put(0)
    for copy in copies:
        copy.wait()
    for n in range(3):
        cols = slice(n * 256, (n + 1) * 256)
        total = part_ref[:, cols] + nt_dot(gqkv_ref[...], w_ref[cols, :1152])
        et_ref[cols, :] = total.astype(bf16).T
    for j in range(4):
        outs[j][...] = et_ref[pl.ds(pl.multiple_of(idx_ref[j], 16), 192), :]


def own_heads(index, arrays, pieces):
    return staged_call(
        own_heads_kernel,
        [(index, Z_ROWS)],
        arrays,
        pieces,
        [
            shaped(bf16, 512, 1152),
            shaped(bf16, 192, 512),
            shaped(bf16, 192, 512),
            shaped(bf16, 192, 512),
            shaped(bf16, 192, 512),
        ],
        [
            pltpu.VMEM((768, 1664), bf16),
            pltpu.VMEM((4, 256, 256), f32),
            pltpu.VMEM((3, 512, 128), f32),
            pltpu.VMEM((3, 512, 128), f32),
            pltpu.VMEM((768, 512), bf16),
            pltpu.SemaphoreType.DMA((16,)),
        ],
        15,
    )


def to_slots(idx_ref, whole_ref, keep_ref, away_ref, sems):
    copies = []
    for start, ref in ((8, away_ref), (0, keep_ref)):
        for slot in range(8):
            source = whole_ref.at[idx_ref[start + slot]]
            copies.append(pltpu.make_async_copy(source, ref.at[slot], sems.at[start + slot]))
    for copy in copies:
        copy.start()
    for copy in copies:
        copy.wait()


def down_grad_kernel(ready, idx_ref, act_ref, act_o_ref, g_ref, g_o_ref, keep_ref, away_ref, whole_ref, sems):
    ready()
    for n in range(8):
        cols = slice(n * 384, (n + 1) * 384)
        total = tn_dot(act_ref[:, cols], g_ref[...]) + tn_dot(act_o_ref[:, cols], g_o_ref[...])
        total = total.astype(bf16)
        whole_ref[2 * n] = total[:192]
        whole_ref[2 * n + 1] = total[192:]
    to_slots(idx_ref, whole_ref, keep_ref, away_ref, sems)


def down_grad(index, arrays):
    return staged_call(
        down_grad_kernel,
        [(index, SLOTS)],
        arrays,
        [],
        [shaped(bf16, 8, 192, 384)] * 2,
        [pltpu.VMEM((16, 192, 384), bf16), pltpu.SemaphoreType.DMA((16,))],
        7,
        staged_out=False,
    )


def store_chunks(whole_ref, cols, total):
    for f in range(16):
        whole_ref[f, :, cols] = total[f * 48 : (f + 1) * 48]


def up_out_grad_kernel(
    ready, idx_ref, low_ref, low_o_ref, g_ref, g_o_ref, mixed_ref, mixed_o_ref, ga_ref, ga_o_ref, norms_ref,
    norms_o_ref, keep_ref, away_ref, whole_ref, t_ref, sems,
):
    ready()
    t_ref[0] = low_ref[...].T
    t_ref[1] = low_o_ref[...].T
    for n in range(3):
        cols = slice(n * 512, (n + 1) * 512)
        total = nn_dot(t_ref[0], g_ref[:, cols]) + nn_dot(t_ref[1], g_o_ref[:, cols])
        store_chunks(whole_ref, cols, total.astype(bf16))
    t_ref[0] = mixed_ref[...].T
    t_ref[1] = mixed_o_ref[...].T
    total = nn_dot(t_ref[0], ga_ref[...]) + nn_dot(t_ref[1], ga_o_ref[...])
    store_chunks(whole_ref, slice(1536, 1920), total.astype(bf16))
    norms = (norms_ref[...] + norms_o_ref[...]).T.astype(bf16)
    norms = jnp.concatenate([norms, jnp.zeros((768, 120), bf16)], 1)
    store_chunks(whole_ref, slice(1920, 2048), norms)
    to_slots(idx_ref, whole_ref, keep_ref, away_ref, sems)


def up_out_grad(index, arrays):
    return staged_call(
        up_out_grad_kernel,
        [(index, SLOTS)],
        arrays,
        [],
        [
            shaped(bf16, 8, 48, 2048),
            shaped(bf16, 8, 48, 2048),
        ],
        [
            pltpu.VMEM((16, 48, 2048), bf16),
            pltpu.VMEM((2, 768, 512), bf16),
            pltpu.SemaphoreType.DMA((16,)),
        ],
        8,
        staged_out=False,
    )


def in_grad_kernel(ready, idx_ref, e_ref, e_o_ref, g_ref, g_o_ref, keep_ref, away_ref, whole_ref, t_ref, sems):
    ready()
    t_ref[0] = e_ref[...].T
    t_ref[1] = e_o_ref[...].T
    for t in range(3):
        cols = slice(t * 384, (t + 1) * 384)
        total = nn_dot(t_ref[0], g_ref[:, cols]) + nn_dot(t_ref[1], g_o_ref[:, cols])
        store_chunks(whole_ref, cols, total.astype(bf16))
    to_slots(idx_ref, whole_ref, keep_ref, away_ref, sems)


def in_grad(index, arrays):
    return staged_call(
        in_grad_kernel,
        [(index, SLOTS)],
        arrays,
        [],
        [
            shaped(bf16, 8, 48, 1152),
            shaped(bf16, 8, 48, 1152),
        ],
        [
            pltpu.VMEM((16, 48, 1152), bf16),
            pltpu.VMEM((2, 768, 512), bf16),
            pltpu.SemaphoreType.DMA((16,)),
        ],
        6,
        staged_out=False,
    )


def optimizer_kernel(ready, core_ref, fix_ref, totals_ref, totals_o_ref, *refs):
    ready(*range(10))
    own, other = refs[:4], refs[4:8]
    params, outs = refs[8:26], refs[26:46]
    table_ref = refs[46]
    core = core_ref[0]
    totals = totals_ref[...] + totals_o_ref[...]
    norm = jnp.sqrt(totals[:, 0:1])
    outs[0][...] = totals[:, 1:2]
    outs[1][...] = norm
    factor = clip_norm / jnp.maximum(norm, clip_norm)
    fix_one, fix_two = 1.0 / fix_ref[0], 1.0 / fix_ref[1]

    def update(number, spot, grad, rate, decay):
        w_ref, first_ref, second_ref = params[3 * number : 3 * number + 3]
        grad = grad.astype(f32) * factor
        weight = w_ref[spot]
        first = beta_one * first_ref[spot] + (1.0 - beta_one) * grad
        second = beta_two * second_ref[spot] + (1.0 - beta_two) * grad * grad
        step = (first * fix_one) / (jnp.sqrt(second * fix_two) + adam_eps)
        outs[2 + 3 * number][spot] = weight - rate * (step + decay * weight)
        outs[3 + 3 * number][spot] = first
        outs[4 + 3 * number][spot] = second

    every = slice(None)
    halves = ((core, own), (1 - core, other))

    def columns(half, width, start=0):
        return pl.ds(pl.multiple_of(half * width + start, 128), width)

    def opened(number):
        ready(*range(10 + 3 * number, 13 + 3 * number))

    def done(number):
        ready.put(*range(2 + 3 * number, 5 + 3 * number))

    opened(3)
    for half, (_, _, up_out, _) in halves:
        for t in range(3):
            spot = pl.ds(pl.multiple_of(half * 1536 + t * 512, 128), 512)
            update(3, (every, spot), up_out[:, t * 512 : (t + 1) * 512], rate_matrix, decay_rate)
    done(3)
    opened(4)
    for half, (_, _, _, down) in halves:
        for t in range(4):
            rows = slice(t * 48, (t + 1) * 48)
            update(4, (rows, columns(half, 384)), down[rows, :], rate_matrix, decay_rate)
    done(4)
    opened(1)
    for half, (_, into, _, _) in halves:
        for t in range(3):
            update(
                1,
                (every, columns(half, 384, t * 768)),
                into[:, t * 384 : (t + 1) * 384],
                rate_matrix,
                decay_rate,
            )
    done(1)
    opened(0)
    for half, (table, _, _, _) in halves:
        table_ref[:, columns(half, VOCAB_HALF)] = table[...]
    vocab = params[0].shape[1]
    for low in range(0, vocab, 512):
        spot = slice(low, min(vocab, low + 512))
        update(0, (every, spot), table_ref[:, spot], rate_embed, decay_rate)
    done(0)
    opened(2)
    for half, (_, _, up_out, _) in halves:
        update(2, (every, columns(half, 384)), up_out[:, 1536:1920], rate_matrix, decay_rate)
    done(2)
    opened(5)
    norms = jnp.where(core == 0, own[2][:, 1920:].astype(f32), other[2][:, 1920:].astype(f32))
    update(5, (every, every), norms.T[:4], rate_norm, 0.0)


def optimizer(core, fixes, totals, totals_o, own, other, params):
    return staged_call(
        optimizer_kernel,
        [(core, MY_CORE), (fixes, 0)],
        [totals, totals_o, *own, *other, *params],
        [],
        [
            shaped(f32, 1, 1),
            shaped(f32, 1, 1),
            *[shaped(f32, *p.shape) for p in params],
        ],
        [
            pltpu.VMEM((48, VOCAB_PAD), bf16),
        ],
        8,
    )


def per_device_links(
    kmer_identifiers,
    slot_fragment_ids,
    mirror_fragment_index,
    fragment_weight,
    affinity_heat,
    optimizer_iteration,
    lexicon_table,
    lexicon_first_moment,
    lexicon_raw_moment,
    query_key_value_maps,
    qkv_first_moment,
    qkv_raw_moment,
    attention_exit_map,
    exit_first_moment,
    exit_raw_moment,
    widening_matrix_in,
    widening_first_moment,
    widening_raw_moment,
    narrowing_matrix_out,
    narrowing_first_moment,
    narrowing_raw_moment,
    layernorm_scale_bias,
    layernorm_first_moment,
    layernorm_raw_moment,
):
    place = Place()
    core = place.core
    vocab = lexicon_table.shape[0]
    index = index_vector(place)
    both_cut, table_cut, table_half, down_half = prepare(
        index,
        [
            lexicon_table.T,
            query_key_value_maps,
            attention_exit_map,
            widening_matrix_in,
            narrowing_matrix_out,
            layernorm_scale_bias,
            kmer_identifiers,
            fragment_weight.reshape(1, 32),
        ],
    )
    near = [send(table_half, FIRST), send(table_half, SECOND)]
    near.append(send(near[0], SECOND))
    both_far = z_sends(both_cut)
    down_first = send(after(down_half, near[0]), FIRST)
    others = send(after(jnp.stack(near), down_first, *both_far), CORE)
    id_parts = jnp.stack([p[:8, 3200:] for p in both_far]).astype(f32)
    ids_z = (id_parts[:, :4] * 64.0 + id_parts[:, 4:]).astype(jnp.int32)
    in_out_column = jnp.stack([p[:, :1664] for p in both_far])
    in_out_mine = plane_sends(in_out_column, True)
    found = lookup(index, ids_z, [down_half, down_first], [table_cut] + near + [others])
    up_column = after(jnp.stack([p[:, 1664:3200] for p in both_far]), *found)
    columns = [found[0]] + [send(found[j], ZS[j]) for j in (1, 2, 3)]
    in_out = both_cores(together(in_out_mine, *columns))
    up_mine = plane_sends(after(up_column, in_out_mine[3]), True)
    down_pair = jnp.stack([down_half, after(down_first, *found)])
    down_pair = after(down_pair, *columns)
    d_two, d_three = (send(down_pair, ZS[j]) for j in (2, 3))
    seg_row = slot_fragment_ids
    seg_col = slot_fragment_ids.reshape(512, 1)
    embedded, qkv, lse, mixed, unit_one, inv_one, normed_low, params, side = attention_forward(
        index, seg_row, seg_col, columns, in_out
    )
    *up_mine, d_two, d_three = together(up_mine + [d_two, d_three], normed_low)
    d_one = jnp.stack([columns[1][:, 512:896], columns[1][:, 896:]])
    down_one = jnp.stack([down_pair, d_one, d_two, d_three]).reshape(8, 192, 384)
    down_two = send(down_one, SECOND)
    down_one_o = send(down_one, CORE)
    up_w = both_cores(up_mine)
    activated, slope = up_forward(index, normed_low, up_w)
    down_two, down_one_o = together([down_two, down_one_o], activated)
    down_w = [down_one, down_two, down_one_o, send(down_two, CORE)]
    unit_two, inv_two, unit_rows, unit_low, unit_scale = down_forward(
        index, seg_row, activated, unit_one, params, down_w
    )
    embedded_o, mixed_o, normed_o, activated_o = (
        send(a, CORE) for a in (embedded, mixed, normed_low, activated)
    )
    column = jnp.stack([unit_low] + [send(unit_low, ZS[j]) for j in (1, 2, 3)])
    blocks = [column, send(column, FIRST), send(column, SECOND), send(column, BOTH)]
    blocks = blocks + [send(block, CORE) for block in blocks]
    (
        loss_tile, grad_result_own, grad_result_x, grad_up_own, grad_up_x, grad_two, gains_two,
    ) = loss_backward(
        index,
        affinity_heat.reshape(1),
        [
            seg_col,
            mirror_fragment_index.reshape(1, 32),
            fragment_weight.reshape(1, 32),
            side,
            unit_rows,
            unit_scale,
            unit_two,
            inv_two,
            params,
            slope,
        ],
        blocks + down_w,
    )
    grad_result_o = send(grad_result_x, CORE)
    ids_o = send(ids_z, CORE)
    grad_up_o = send(grad_up_x, CORE)
    spare = [embedded_o, mixed_o, normed_o, ids_o]
    down_keep, down_away = down_grad(
        index, [after(activated, *spare), activated_o, grad_result_own, grad_result_o]
    )
    down_came = send(down_away, SECOND)
    grad_resid, grad_attended, grad_att_own, grad_att_x, norms = ffn_backward(
        index,
        [after(grad_up_own, down_away), grad_up_x, grad_two, unit_one, inv_one, params, gains_two],
        up_w,
    )
    grad_att_o = send(grad_att_x, CORE)
    norms_o = send(norms, CORE)
    up_out_keep, up_out_away = up_out_grad(
        index,
        [
            normed_low,
            normed_o,
            grad_up_own,
            grad_up_o,
            mixed,
            mixed_o,
            grad_att_own,
            grad_att_o,
            norms,
            norms_o,
        ],
    )
    up_out_came = send(up_out_away, SECOND)
    down_came = after(down_came, up_out_away)
    down_across = scatter_add(down_keep, down_came)
    down_came_two = send(down_across, FIRST)
    grad_qkv_x, grad_mixed_own, part = other_heads(
        index,
        [seg_row, seg_col, qkv, lse, after(grad_attended, down_across), grad_resid],
        in_out,
    )
    grad_qkv_o = send(grad_qkv_x, CORE)
    down_came_two = after(down_came_two, part)
    down_here, down_far = scatter_here(down_keep, down_came, down_came_two)
    down_far_came = line_sends(down_far)
    grad_qkv_own, *outs = own_heads(
        index,
        [seg_row, seg_col, qkv, lse, grad_mixed_own, after(part, *down_far)],
        in_out[:4],
    )
    far_cols = [send(outs[j], ZS[j]) for j in (1, 2, 3)]
    *down_far_came, up_out_came, grad_qkv_o = together(
        down_far_came + [up_out_came, grad_qkv_o], grad_qkv_own
    )
    up_out_across = scatter_add(up_out_keep, up_out_came)
    up_out_came_two = send(up_out_across, FIRST)
    in_keep, in_away = in_grad(
        index, [embedded, embedded_o, after(grad_qkv_own, up_out_across), grad_qkv_o]
    )
    far_cols = together(far_cols, in_away)
    in_came = send(in_away, SECOND)
    token_cols = jnp.stack([outs[0]] + far_cols)
    token_cols_o = send(token_cols, CORE)
    up_out_here, up_out_far = scatter_here(
        up_out_keep, up_out_came, after(up_out_came_two, token_cols)
    )
    up_out_far_came = line_sends(up_out_far)
    keep, away = token_sum(
        index,
        after(ids_z, *up_out_far),
        ids_o,
        token_cols,
        token_cols_o,
    )
    came = send(away, SECOND)
    in_came = after(in_came, away)
    in_across = scatter_add(in_keep, in_came)
    in_came_two = send(in_across, FIRST)
    across = (keep[1].astype(f32) + came[1].astype(f32)).astype(bf16)
    came_two = send(across, FIRST)
    up_out_far_came = together(up_out_far_came, across)
    in_here, in_far = scatter_here(
        in_keep, in_came, after(in_came_two, across, *up_out_far_came)
    )
    in_far_came = line_sends(in_far)
    down_sum = line_sum(after(down_here, came_two), down_far_came)
    up_out_sum = line_sum(up_out_here, together(up_out_far_came, came_two))
    table_sum = keep[0].astype(f32) + came[0].astype(f32) + came_two.astype(f32)
    table_sum = table_sum.astype(bf16)
    early = [table_sum, up_out_sum, down_sum]
    norm_own = up_out_sum[:, 1920:1924].astype(f32)
    squares = sum(
        jnp.sum(jnp.square(p.astype(f32))) for p in (table_sum, up_out_sum[:, :1920], down_sum)
    ) + jnp.where(core == 0, jnp.sum(norm_own * norm_own), 0.0)
    early_o = [send(s, CORE) for s in early]
    in_sum = line_sum(in_here, together(in_far_came, squares))
    in_o = send(in_sum, CORE)
    squares += jnp.sum(jnp.square(in_sum.astype(f32)))
    lane = lax.broadcasted_iota(jnp.int32, (1, 128), 1)
    totals = jnp.where(lane == 0, squares, loss_tile[0:1])
    totals = all_sum(after(totals, *early_o))
    sums = [table_sum, in_sum, up_out_sum, down_sum]
    sums_o = [early_o[0], in_o, early_o[1], early_o[2]]
    count_now = optimizer_iteration.astype(f32)
    fixes = jnp.stack([1.0 - jnp.power(beta_one, count_now), 1.0 - jnp.power(beta_two, count_now)])
    results = optimizer(
        index,
        fixes,
        totals,
        send(totals, CORE),
        sums,
        sums_o,
        [
            lexicon_table.T,
            lexicon_first_moment.T,
            lexicon_raw_moment.T,
            query_key_value_maps,
            qkv_first_moment,
            qkv_raw_moment,
            attention_exit_map,
            exit_first_moment,
            exit_raw_moment,
            widening_matrix_in,
            widening_first_moment,
            widening_raw_moment,
            narrowing_matrix_out,
            narrowing_first_moment,
            narrowing_raw_moment,
            layernorm_scale_bias,
            layernorm_first_moment,
            layernorm_raw_moment,
        ],
    )
    results = list(results)
    results[:2] = [r[0, 0] for r in results[:2]]
    results[2:5] = [r.T for r in results[2:5]]
    return tuple(results)


def solution(mesh):
    in_specs = (
        P(("fsdp", "dp"), None),
        P(("fsdp", "dp"), None),
        P(("fsdp", "dp")),
        P(("fsdp", "dp")),
        P(),
        P(),
        P(None, "fsdp"),
        P(None, "fsdp"),
        P(None, "fsdp"),
        P("fsdp", None),
        P("fsdp", None),
        P("fsdp", None),
        P("fsdp", None),
        P("fsdp", None),
        P("fsdp", None),
        P("fsdp", None),
        P("fsdp", None),
        P("fsdp", None),
        P("fsdp", None),
        P("fsdp", None),
        P("fsdp", None),
        P(None, "fsdp"),
        P(None, "fsdp"),
        P(None, "fsdp"),
    )
    out_specs = (
        P(),
        P(),
        P(None, "fsdp"),
        P(None, "fsdp"),
        P(None, "fsdp"),
        P("fsdp", None),
        P("fsdp", None),
        P("fsdp", None),
        P("fsdp", None),
        P("fsdp", None),
        P("fsdp", None),
        P("fsdp", None),
        P("fsdp", None),
        P("fsdp", None),
        P("fsdp", None),
        P("fsdp", None),
        P("fsdp", None),
        P(None, "fsdp"),
        P(None, "fsdp"),
        P(None, "fsdp"),
    )
    own_plan = dict(mesh.shape) == {"fsdp": 16, "dp": 2}
    return jax.shard_map(
        per_device_links if own_plan else per_device, mesh=mesh, in_specs=in_specs, out_specs=out_specs, check_vma=False
    )
```

```python
import jax
import jax.numpy as jnp
from jax import lax
from jax.experimental import pallas as pl
from jax.experimental.pallas import tpu as pltpu
from jax.sharding import PartitionSpec as P

MODEL_WIDTH = 768
H = 12
HD = 64
SEG_ROW = 32


largest_value = lax.Precision.HIGHEST
beta_one = 0.9
beta_two = 0.999
adam_eps = 1e-12
decay_rate = 0.01
rate_matrix = 0.1
rate_embed = 1.0
rate_norm = 1.0
clip_norm = 0.001
norm_eps = 1e-05
unit_eps = 1e-06


def layer_norm(inputs, gain_row, shifts):
    center = inputs - jnp.mean(inputs, -1, keepdims=True)
    inv_std = lax.rsqrt(jnp.mean(center * center, -1, keepdims=True) + norm_eps)
    normed = center * inv_std
    return (normed * gain_row + shifts, normed, inv_std)


def norm_back(upstream, normed, inv_std, gain_row):
    scaled = upstream * gain_row
    grad_in = inv_std * (
        scaled
        - jnp.mean(scaled, -1, keepdims=True)
        - normed * jnp.mean(scaled * normed, -1, keepdims=True)
    )
    return (grad_in, jnp.sum(upstream * normed, 0), jnp.sum(upstream, 0))


def masked_scores(query_rows, key_rows, segment_rows):
    raw_scores = jnp.einsum(
        "bqhd,bkhd->bhqk", query_rows, key_rows, preferred_element_type=jnp.float32
    )
    same_segment = segment_rows[:, None, :, None] == segment_rows[:, None, None, :]
    return jnp.where(same_segment, raw_scores * HD ** (-0.5), -1e30)


def layer_forward(gathered, token_rows, segment_rows):
    (
        lexicon_table,
        query_key_value_maps,
        attention_exit_map,
        widening_matrix_in,
        narrowing_matrix_out,
        layernorm_scale_bias,
    ) = gathered
    batch_row_list, sequence_length = token_rows.shape
    embedded = jnp.take(lexicon_table, token_rows.reshape(-1), axis=0)
    qkv_all = jnp.dot(embedded, query_key_value_maps, preferred_element_type=jnp.float32).astype(
        jnp.bfloat16
    )
    qkv_all = qkv_all.reshape(batch_row_list, sequence_length, 3, H, HD)
    query_rows, key_rows, value_rows = (qkv_all[:, :, 0], qkv_all[:, :, 1], qkv_all[:, :, 2])
    scores = masked_scores(query_rows, key_rows, segment_rows)
    row_max = jnp.max(scores, -1, keepdims=True)
    log_total = row_max + jnp.log(jnp.sum(jnp.exp(scores - row_max), -1, keepdims=True))
    attn_probs = jnp.exp(scores - log_total).astype(jnp.bfloat16)
    mixed_heads = jnp.einsum(
        "bhqk,bkhd->bqhd", attn_probs, value_rows, preferred_element_type=jnp.float32
    )
    mixed_heads = mixed_heads.reshape(batch_row_list * sequence_length, MODEL_WIDTH).astype(
        jnp.bfloat16
    )
    attended = jnp.dot(mixed_heads, attention_exit_map, preferred_element_type=jnp.float32)
    normed_one, unit_one, inv_one = layer_norm(
        embedded.astype(jnp.float32) + attended, layernorm_scale_bias[0], layernorm_scale_bias[1]
    )
    normed_low = normed_one.astype(jnp.bfloat16)
    up_proj = jnp.dot(normed_low, widening_matrix_in, preferred_element_type=jnp.float32)
    activated = jax.nn.gelu(up_proj, approximate=False).astype(jnp.bfloat16)
    ffn_result = jnp.dot(activated, narrowing_matrix_out, preferred_element_type=jnp.float32)
    second_normalized, unit_two, inv_two = layer_norm(
        normed_one + ffn_result, layernorm_scale_bias[2], layernorm_scale_bias[3]
    )
    group_member = (
        segment_rows[:, None, :] == jnp.arange(SEG_ROW, dtype=jnp.int32)[None, :, None]
    ).astype(jnp.float32)
    pooled_state = jnp.einsum(
        "nkz,nzh->nkh",
        group_member,
        second_normalized.reshape(batch_row_list, sequence_length, MODEL_WIDTH),
        precision=largest_value,
    )
    saved_state = (
        embedded,
        query_rows,
        key_rows,
        value_rows,
        log_total,
        mixed_heads,
        unit_one,
        inv_one,
        normed_low,
        up_proj,
        activated,
        unit_two,
        inv_two,
        group_member,
    )
    return (pooled_state.reshape(batch_row_list * SEG_ROW, MODEL_WIDTH), saved_state)


def layer_backward(gathered, saved_state, token_rows, segment_rows, pooled_gradient):
    (
        lexicon_table,
        query_key_value_maps,
        attention_exit_map,
        widening_matrix_in,
        narrowing_matrix_out,
        layernorm_scale_bias,
    ) = gathered
    (
        embedded,
        query_rows,
        key_rows,
        value_rows,
        log_total,
        mixed_heads,
        unit_one,
        inv_one,
        normed_low,
        up_proj,
        activated,
        unit_two,
        inv_two,
        group_member,
    ) = saved_state
    batch_row_list, sequence_length = token_rows.shape
    pooled_gradient = pooled_gradient.reshape(batch_row_list, SEG_ROW, MODEL_WIDTH)
    second_gradient = jnp.einsum(
        "got,goy->gty", group_member, pooled_gradient, precision=largest_value
    ).reshape(batch_row_list * sequence_length, MODEL_WIDTH)
    grad_resid_two, grad_gain_two, grad_shift_two = norm_back(
        second_gradient, unit_two, inv_two, layernorm_scale_bias[2]
    )
    grad_result = grad_resid_two.astype(jnp.bfloat16)
    grad_ffn_down = jnp.einsum(
        "nf,nd->fd", activated, grad_result, preferred_element_type=jnp.float32
    )
    grad_act = jnp.einsum(
        "nd,fd->nf", grad_result, narrowing_matrix_out, preferred_element_type=jnp.float32
    )
    gelu_value, gelu_pull = jax.vjp(
        lambda pre_act: jax.nn.gelu(pre_act, approximate=False), up_proj
    )
    grad_up = gelu_pull(grad_act)[0].astype(jnp.bfloat16)
    grad_ffn_up = jnp.einsum("nd,nf->df", normed_low, grad_up, preferred_element_type=jnp.float32)
    grad_one = grad_resid_two + jnp.einsum(
        "nf,df->nd", grad_up, widening_matrix_in, preferred_element_type=jnp.float32
    )
    grad_resid_one, grad_gain_one, grad_shift_one = norm_back(
        grad_one, unit_one, inv_one, layernorm_scale_bias[0]
    )
    grad_attended = grad_resid_one.astype(jnp.bfloat16)
    grad_project_out = jnp.einsum(
        "nc,nd->cd", mixed_heads, grad_attended, preferred_element_type=jnp.float32
    )
    grad_mixed = jnp.einsum(
        "nd,cd->nc", grad_attended, attention_exit_map, preferred_element_type=jnp.float32
    )
    grad_mixed = grad_mixed.astype(jnp.bfloat16).reshape(batch_row_list, sequence_length, H, HD)
    scores = masked_scores(query_rows, key_rows, segment_rows)
    attn_probs = jnp.exp(scores - log_total)
    probs_low = attn_probs.astype(jnp.bfloat16)
    grad_values = jnp.einsum(
        "bhqk,bqhd->bkhd", probs_low, grad_mixed, preferred_element_type=jnp.float32
    )
    grad_probs = jnp.einsum(
        "bqhd,bkhd->bhqk", grad_mixed, value_rows, preferred_element_type=jnp.float32
    )
    grad_scores = attn_probs * (grad_probs - jnp.sum(grad_probs * attn_probs, -1, keepdims=True))
    grad_scores = grad_scores.astype(jnp.bfloat16)
    grad_query = jnp.einsum(
        "bhqk,bkhd->bqhd", grad_scores, key_rows, preferred_element_type=jnp.float32
    ) * HD ** (-0.5)
    grad_keys = jnp.einsum(
        "bhqk,bqhd->bkhd", grad_scores, query_rows, preferred_element_type=jnp.float32
    ) * HD ** (-0.5)
    grad_qkv = (
        jnp.stack([grad_query, grad_keys, grad_values], 2)
        .reshape(batch_row_list * sequence_length, 3 * MODEL_WIDTH)
        .astype(jnp.bfloat16)
    )
    grad_project_in = jnp.einsum(
        "nd,nc->dc", embedded, grad_qkv, preferred_element_type=jnp.float32
    )
    grad_embedded = grad_resid_one + jnp.einsum(
        "nc,dc->nd", grad_qkv, query_key_value_maps, preferred_element_type=jnp.float32
    )
    grad_norms = jnp.stack([grad_gain_one, grad_shift_one, grad_gain_two, grad_shift_two])
    return (
        grad_embedded,
        grad_project_in,
        grad_project_out,
        grad_ffn_up,
        grad_ffn_down,
        grad_norms,
    )


def adam_update(weight, first, second, grad, fix_first, fix_second, rate, decay):
    first_new = beta_one * first + (1.0 - beta_one) * grad
    second_new = beta_two * second + (1.0 - beta_two) * grad * grad
    step_size = first_new / fix_first / (jnp.sqrt(second_new / fix_second) + adam_eps)
    return (weight - rate * (step_size + decay * weight), first_new, second_new)


def per_device(
    kmer_identifiers,
    slot_fragment_ids,
    mirror_fragment_index,
    fragment_weight,
    affinity_heat,
    optimizer_iteration,
    lexicon_table,
    lexicon_first_moment,
    lexicon_raw_moment,
    query_key_value_maps,
    qkv_first_moment,
    qkv_raw_moment,
    attention_exit_map,
    exit_first_moment,
    exit_raw_moment,
    widening_matrix_in,
    widening_first_moment,
    widening_raw_moment,
    narrowing_matrix_out,
    narrowing_first_moment,
    narrowing_raw_moment,
    layernorm_scale_bias,
    layernorm_first_moment,
    layernorm_raw_moment,
):
    masters = (
        lexicon_table,
        query_key_value_maps,
        attention_exit_map,
        widening_matrix_in,
        narrowing_matrix_out,
        layernorm_scale_bias,
    )
    firsts = (
        lexicon_first_moment,
        qkv_first_moment,
        exit_first_moment,
        widening_first_moment,
        narrowing_first_moment,
        layernorm_first_moment,
    )
    seconds = (
        lexicon_raw_moment,
        qkv_raw_moment,
        exit_raw_moment,
        widening_raw_moment,
        narrowing_raw_moment,
        layernorm_raw_moment,
    )
    rates = (rate_embed, rate_matrix, rate_matrix, rate_matrix, rate_matrix, rate_norm)
    decays = (decay_rate, decay_rate, decay_rate, decay_rate, decay_rate, 0.0)
    lowered = tuple((piece.astype(jnp.bfloat16) for piece in masters))
    gathered = (
        lax.all_gather(lowered[0], "fsdp", axis=1, tiled=True),
        lax.all_gather(lowered[1], "fsdp", axis=0, tiled=True),
        lax.all_gather(lowered[2], "fsdp", axis=0, tiled=True),
        lax.all_gather(lowered[3], "fsdp", axis=0, tiled=True),
        lax.all_gather(lowered[4], "fsdp", axis=0, tiled=True),
        lax.all_gather(lowered[5], "fsdp", axis=1, tiled=True),
    )
    pooled_state, saved_state = layer_forward(gathered, kmer_identifiers, slot_fragment_ids)
    unit_scale = lax.rsqrt(jnp.sum(pooled_state * pooled_state, -1, keepdims=True) + unit_eps)
    unit_rows = pooled_state * unit_scale
    unit_low = unit_rows.astype(jnp.bfloat16)
    every_unit = lax.all_gather(unit_low, ("fsdp", "dp"), axis=0, tiled=True)
    cosine_affinity_grid = jnp.einsum(
        "sd,td->st", unit_low, every_unit, preferred_element_type=jnp.float32
    )
    seg_local = pooled_state.shape[0]
    fragment_tally = every_unit.shape[0]
    shard_fragment_lines = lax.axis_index(("fsdp", "dp")) * seg_local + jnp.arange(
        seg_local, dtype=jnp.int32
    )
    field_sequence_array = jnp.arange(fragment_tally, dtype=jnp.int32)
    raw_affinity_values = jnp.where(
        shard_fragment_lines[:, None] == field_sequence_array[None, :],
        -1e30,
        cosine_affinity_grid / affinity_heat,
    )
    row_max = jnp.max(raw_affinity_values, -1, keepdims=True)
    log_total = row_max[:, 0] + jnp.log(jnp.sum(jnp.exp(raw_affinity_values - row_max), -1))
    chosen = mirror_fragment_index[:, None] == field_sequence_array[None, :]
    chosen_real_entry = chosen.astype(jnp.float32)
    target = jnp.sum(jnp.where(chosen, raw_affinity_values, 0.0), -1)
    contrast_objective = (
        lax.psum(jnp.sum(fragment_weight * (log_total - target)), ("fsdp", "dp")) / fragment_tally
    )
    exponent_probabilities = jnp.exp(raw_affinity_values - log_total[:, None])
    similarity_gradient = (
        (exponent_probabilities - chosen_real_entry)
        * fragment_weight[:, None]
        / (fragment_tally * affinity_heat)
    ).astype(jnp.bfloat16)
    grad_rows = jnp.dot(similarity_gradient, every_unit, preferred_element_type=jnp.float32)
    column_terms = jnp.einsum(
        "st,sd->td", similarity_gradient, unit_low, preferred_element_type=jnp.float32
    )
    grad_cols = lax.psum_scatter(column_terms, ("fsdp", "dp"), scatter_dimension=0, tiled=True)
    grad_unit = grad_rows + grad_cols
    pooled_gradient = unit_scale * (
        grad_unit - unit_rows * jnp.sum(grad_unit * unit_rows, -1, keepdims=True)
    )
    again = (
        lax.all_gather(lowered[0], "fsdp", axis=1, tiled=True),
        lax.all_gather(lowered[1], "fsdp", axis=0, tiled=True),
        lax.all_gather(lowered[2], "fsdp", axis=0, tiled=True),
        lax.all_gather(lowered[3], "fsdp", axis=0, tiled=True),
        lax.all_gather(lowered[4], "fsdp", axis=0, tiled=True),
        lax.all_gather(lowered[5], "fsdp", axis=1, tiled=True),
    )
    grads = layer_backward(again, saved_state, kmer_identifiers, slot_fragment_ids, pooled_gradient)
    vocab = lexicon_table.shape[0]
    rest = (
        lax.psum_scatter(grads[1], "fsdp", scatter_dimension=0, tiled=True),
        lax.psum_scatter(grads[2], "fsdp", scatter_dimension=0, tiled=True),
        lax.psum_scatter(grads[3], "fsdp", scatter_dimension=0, tiled=True),
        lax.psum_scatter(grads[4], "fsdp", scatter_dimension=0, tiled=True),
        lax.psum_scatter(grads[5], "fsdp", scatter_dimension=1, tiled=True),
    )
    column_rows = lax.all_to_all(
        grads[0].astype(jnp.bfloat16), "fsdp", split_axis=1, concat_axis=0, tiled=True
    ).astype(jnp.float32)
    all_tokens = lax.all_gather(kmer_identifiers.reshape(-1), "fsdp", axis=0, tiled=True)
    table_shard = jax.ops.segment_sum(column_rows, all_tokens, num_segments=vocab)
    shards = (table_shard, rest[0], rest[1], rest[2], rest[3], rest[4])
    shards = (
        lax.psum(shards[0].astype(jnp.bfloat16), "dp").astype(jnp.float32),
        lax.psum(shards[1].astype(jnp.bfloat16), "dp").astype(jnp.float32),
        lax.psum(shards[2].astype(jnp.bfloat16), "dp").astype(jnp.float32),
        lax.psum(shards[3].astype(jnp.bfloat16), "dp").astype(jnp.float32),
        lax.psum(shards[4].astype(jnp.bfloat16), "dp").astype(jnp.float32),
        lax.psum(shards[5].astype(jnp.bfloat16), "dp").astype(jnp.float32),
    )
    squares = sum((jnp.sum(piece * piece) for piece in shards))
    grad_norm = jnp.sqrt(lax.psum(squares, "fsdp"))
    factor = clip_norm / jnp.maximum(grad_norm, clip_norm)
    count_now = optimizer_iteration.astype(jnp.float32)
    fix_first = 1.0 - jnp.power(beta_one, count_now)
    fix_second = 1.0 - jnp.power(beta_two, count_now)
    updated = [
        adam_update(
            masters[number],
            firsts[number],
            seconds[number],
            shards[number] * factor,
            fix_first,
            fix_second,
            rates[number],
            decays[number],
        )
        for number in range(6)
    ]
    return (
        contrast_objective,
        grad_norm,
        updated[0][0],
        updated[0][1],
        updated[0][2],
        updated[1][0],
        updated[1][1],
        updated[1][2],
        updated[2][0],
        updated[2][1],
        updated[2][2],
        updated[3][0],
        updated[3][1],
        updated[3][2],
        updated[4][0],
        updated[4][1],
        updated[4][2],
        updated[5][0],
        updated[5][1],
        updated[5][2],
    )


AXES = ("fsdp", "dp")
VOCAB_PAD = 4352
VOCAB_HALF = VOCAB_PAD // 2
BIG_VMEM = pltpu.CompilerParams(vmem_limit_bytes=60 * 1024 * 1024)
bf16 = jnp.bfloat16
f32 = jnp.float32


def pairs_of(moved):
    spots = [(z, y, x, c) for z in range(4) for y in range(2) for x in range(2) for c in range(2)]

    def linear(spot):
        z, y, x, c = spot
        return ((z * 2 + y) * 2 + x) * 2 + c

    return [(linear(spot), linear(moved(*spot))) for spot in spots]


FIRST = pairs_of(lambda z, y, x, c: (z, y, x ^ 1, c) if c == 0 else (z, y ^ 1, x, c))
SECOND = pairs_of(lambda z, y, x, c: (z, y ^ 1, x, c) if c == 0 else (z, y, x ^ 1, c))
BOTH = pairs_of(lambda z, y, x, c: (z, y ^ 1, x ^ 1, c))
CORE = pairs_of(lambda z, y, x, c: (z, y, x, 1 - c))
ZS = [None] + [pairs_of(lambda z, y, x, c, j=j: (z ^ j, y, x, c)) for j in (1, 2, 3)]


def send(array, pairs):
    return lax.ppermute(array, AXES, pairs)


def after(array, *others):
    return lax.optimization_barrier((array,) + others)[0]


def together(arrays, *others):
    arrays = list(arrays)
    return list(lax.optimization_barrier((*arrays, *others)))[: len(arrays)]


class Place:
    def __init__(self):
        f = lax.axis_index("fsdp")
        self.core = lax.axis_index("dp")
        self.z, self.y, self.x = f // 4, (f // 2) % 2, f % 2

    def plane_slot(self, core, a, b):
        dy = jnp.where(core == 0, b, a)
        dx = jnp.where(core == 0, a, b)
        return (self.y ^ dy) * 2 + (self.x ^ dx)

    def chip(self, core, j, a, b):
        return (self.z ^ j) * 4 + self.plane_slot(core, a, b)


def z_sends(piece):
    return [piece] + [send(piece, ZS[j]) for j in (1, 2, 3)]


def z_column(piece):
    return jnp.stack(z_sends(piece))


def plane_sends(column, direct=False, gate=()):
    one = send(column, FIRST)
    two = send(column, SECOND)
    three = send(column, BOTH) if direct else send(after(one, *gate), SECOND)
    return [column, one, two, three]


def both_cores(mine):
    return mine + [send(block, CORE) for block in mine]


Z_ROWS, BY_FLIP, FRAGMENTS, BY_PAIR, SLOTS, LOOKUP, PLANE = 0, 4, 68, 102, 166, 182, 191
MY_CORE = FRAGMENTS + 33


def index_vector(place):
    core, other = place.core, 1 - place.core
    n = jnp.arange(32, dtype=jnp.int32)
    who, m = jnp.where(n < 16, core, other), n % 16
    chips = place.chip(who, m % 4, (m // 4) % 2, m // 8)
    pairs = place.chip(who, (m // 2) % 4, m % 2, m // 8)
    base = (lax.axis_index("fsdp") * 2 + core) * 32
    k = jnp.arange(7, dtype=jnp.int32)
    side, flips = jnp.where(k < 4, core, other), jnp.where(k < 4, k, k - 3)
    reached = place.plane_slot(side, flips % 2, flips // 2)
    parts = [
        (place.z ^ jnp.arange(4, dtype=jnp.int32)) * 192,
        who,
        chips * 48,
        base,
        (chips * 2 + who) * 32,
        core,
        who,
        pairs * 192,
        chips[:16],
        reached * 48,
        core * VOCAB_HALF,
        other * VOCAB_HALF,
        core * VOCAB_HALF,
        reached[:4] * 48,
    ]
    return jnp.concatenate([jnp.atleast_1d(p).astype(jnp.int32) for p in parts])


class Part:
    def __init__(self, ref, start):
        self.ref, self.start = ref, start

    def __getitem__(self, number):
        return self.ref[self.start + number]


def scatter_add(keep, came):
    return (keep[4:].astype(f32) + came[4:].astype(f32)).astype(bf16)


def scatter_here(keep, came, came_two):
    here = [
        keep[j].astype(f32) + came[j].astype(f32) + came_two[j].astype(f32) for j in range(4)
    ]
    return here[0], [h.astype(bf16) for h in here[1:]]


def line_sends(far):
    return [send(h, ZS[j]) for h, j in zip(far, (1, 2, 3))]


def line_sum(here, far):
    return (here + far[0].astype(f32) + far[1].astype(f32) + far[2].astype(f32)).astype(bf16)


def whole_copies(sources, targets, sems):
    return [
        pltpu.make_async_copy(source, target, sems.at[number])
        for number, (source, target) in enumerate(zip(sources, targets))
    ]


class Stage:
    def __init__(self, copies_in, copies_out, pairs, sems):
        self.copies_in, self.copies_out = dict(enumerate(copies_in)), dict(enumerate(copies_out))
        self.started, self.pairs, self.sems = [], pairs, sems

    def __call__(self, *which):
        for number in which or tuple(self.copies_in):
            self.copies_in.pop(number).wait()

    def put(self, *which):
        for number in which or tuple(self.copies_out):
            copy = self.copies_out.pop(number)
            copy.start()
            self.started.append(copy)

    def put_half(self, side, half, which, width):
        cols = pl.ds(pl.multiple_of(half * width, 128), width)
        for number in which:
            self.copies_out.pop(number, None)
            source, target = self.pairs[number]
            copy = pltpu.make_async_copy(
                source.at[:, cols], target.at[:, cols], self.sems.at[side * len(which) + number]
            )
            copy.start()
            self.started.append(copy)

    def finish(self):
        self.put(*tuple(self.copies_out))
        for copy in self.started:
            copy.wait()


def staged_call(body, scalars, arrays, pieces, shapes, scratch, cost, late=(), staged_out=True):
    n_s, n_a, n_p, n_o = len(scalars), len(arrays), len(pieces), len(shapes)

    def kernel(*refs):
        smem, refs = [Part(r, s) for r, (_, s) in zip(refs, scalars)], refs[n_s:]
        hbm, refs = refs[:n_a], refs[n_a:]
        far, refs = refs[:n_p], refs[n_p:]
        out, refs = refs[:n_o], refs[n_o:]
        near_in, refs = refs[:n_a], refs[n_a:]
        if staged_out:
            near_out, refs = refs[:n_o], refs[n_o:]
        else:
            near_out, out = out, []
        in_sems, out_sems, half_sems, refs = refs[0], refs[1], refs[2], refs[3:]
        copies = whole_copies(hbm, near_in, in_sems)
        for number, copy in enumerate(copies):
            if number not in late:
                copy.start()
        pairs = list(zip(near_out, out))
        stage = Stage(copies, whole_copies(near_out, out, out_sems), pairs, half_sems)
        body(stage, *smem, *near_in, *far, *near_out, *refs)
        stage.finish()

    in_hbm = pl.BlockSpec(memory_space=pltpu.HBM)
    return pl.pallas_call(
        kernel,
        out_shape=shapes,
        in_specs=[pl.BlockSpec(memory_space=pltpu.SMEM)] * n_s + [in_hbm] * (n_a + n_p),
        out_specs=[in_hbm] * n_o,
        scratch_shapes=[pltpu.VMEM(a.shape, a.dtype) for a in arrays]
        + [pltpu.VMEM(s.shape, s.dtype) for s in shapes if staged_out]
        + [pltpu.SemaphoreType.DMA((n,)) for n in (n_a, n_o, 4)]
        + scratch,
        cost_estimate=pl.CostEstimate(flops=int(cost * 1e9), bytes_accessed=0, transcendentals=0),
        compiler_params=BIG_VMEM,
    )(*[vector for vector, _ in scalars], *arrays, *pieces)


def shaped(dtype, *dims):
    return jax.ShapeDtypeStruct(dims, dtype)


def one_hot(ids_row, start, count):
    spots = lax.broadcasted_iota(jnp.int32, (count, ids_row.shape[1]), 0) + start
    return jnp.where(spots == ids_row, 1.0, 0.0).astype(bf16)


def prepare_kernel(
    ready, table_ref, in_ref, out_ref, up_ref, down_ref, norm_ref, ids_ref, weight_ref,
    both_ref, cut_ref, half_ref, down_half_ref,
):
    core = lax.axis_index("dp")

    def mine(ref, width, start=0):
        return ref[:, pl.ds(pl.multiple_of(start + core * width, 128), width)].astype(bf16)

    ready(1, 2, 3, 5, 6, 7)
    for t in range(3):
        both_ref[:, t * 384 : (t + 1) * 384] = mine(in_ref, 384, t * 768)
    both_ref[:, 1152:1536] = mine(out_ref, 384)
    rest = jnp.zeros((1, 16), f32)
    heavy = [jnp.concatenate([w.astype(f32), rest], 1) for w in thirds(weight_ref[...])]
    extra = jnp.concatenate([norm_ref[...]] + heavy + [jnp.zeros((121, 48), f32)], 0)
    both_ref[:, 1536:1664] = extra.T.astype(bf16)
    both_ref[:, 1664:3200] = mine(up_ref, 1536)
    ids = jnp.concatenate([ids_ref[:, k * 128 : (k + 1) * 128] for k in range(4)], 0)
    high = lax.shift_right_logical(ids, 6)
    ids = jnp.concatenate([high, ids - high * 64], 0).astype(f32).astype(bf16)
    both_ref[:, 3200:3328] = jnp.concatenate([ids, jnp.zeros((40, 128), bf16)], 0)
    ready.put(0)
    ready(0, 4)
    vocab = table_ref.shape[1]
    even = vocab - vocab % 128
    cut_ref[:, :even] = table_ref[:, :even].astype(bf16)
    last = [table_ref[:, even:], jnp.zeros((48, VOCAB_PAD - vocab), f32)]
    cut_ref[:, even:] = jnp.concatenate(last, 1).astype(bf16)
    half_ref[...] = cut_ref[:, pl.ds(pl.multiple_of(core * VOCAB_HALF, 128), VOCAB_HALF)]
    down_half_ref[...] = mine(down_ref, 384)


def prepare(arrays):
    return staged_call(
        prepare_kernel,
        [],
        arrays,
        [],
        [
            shaped(bf16, 48, 3328),
            shaped(bf16, 48, VOCAB_PAD),
            shaped(bf16, 48, VOCAB_HALF),
            shaped(bf16, 192, 384),
        ],
        [],
        3,
    )


def id_row(ids_ref, j):
    rows = ids_ref[j]
    return jnp.concatenate([rows[k : k + 1] for k in range(4)], 1)


def lookup_kernel(ready, idx_ref, ids_ref, down_ref, down_first_ref, *refs):
    ins = list(refs[:4]) + [refs[4].at[k] for k in range(3)]
    outs, table, sems = refs[5:9], refs[9], refs[10]
    copies = [
        pltpu.make_async_copy(
            ins[0], table.at[pl.ds(pl.multiple_of(idx_ref[0], 16), 48), :], sems.at[0]
        )
    ]
    for number in range(1, 7):
        column = pl.multiple_of(idx_ref[7 + (number - 1) // 3], 128)
        row = pl.multiple_of(idx_ref[number], 16)
        copies.append(
            pltpu.make_async_copy(
                ins[number],
                table.at[pl.ds(row, 48), pl.ds(column, VOCAB_HALF)],
                sems.at[number],
            )
        )
    for copy in copies:
        copy.start()
    ready()
    for copy in copies:
        copy.wait()
    for j in range(4):
        total = jnp.zeros((192, 512), f32)
        for k in range(VOCAB_PAD // 256):
            total += jnp.dot(
                table[:, k * 256 : (k + 1) * 256],
                one_hot(id_row(ids_ref, j), k * 256, 256),
                preferred_element_type=f32,
            )
        outs[j][:, :512] = total.astype(bf16)
    outs[1][:, 512:896] = down_ref[...]
    outs[1][:, 896:] = down_first_ref[...]


def lookup(index, ids_z, down_pair, arrays):
    return staged_call(
        lookup_kernel,
        [(index, LOOKUP)],
        [ids_z, *down_pair],
        arrays,
        [
            shaped(bf16, 192, 512),
            shaped(bf16, 192, 1280),
            shaped(bf16, 192, 512),
            shaped(bf16, 192, 512),
        ],
        [
            pltpu.VMEM((192, VOCAB_PAD), bf16),
            pltpu.SemaphoreType.DMA((7,)),
        ],
        6,
    )


def token_sum_kernel(
    ready, idx_ref, ids_ref, other_ids_ref, mine_ref, other_ref, keep_ref, away_ref, whole_ref, sems
):
    ready()
    start = idx_ref[0]
    for low in range(0, VOCAB_HALF, 256):
        count = min(256, VOCAB_HALF - low)
        total = jnp.zeros((192, count), f32)
        for ids, block in ((ids_ref, mine_ref), (other_ids_ref, other_ref)):
            for j in range(4):
                total += lax.dot_general(
                    block[j],
                    one_hot(id_row(ids, j), start + low, count),
                    (((1,), (1,)), ((), ())),
                    preferred_element_type=f32,
                )
        whole_ref[:, low : low + count] = total.astype(bf16)
    copies = []
    for k in range(4):
        rows = pl.ds(pl.multiple_of(idx_ref[1 + k], 16), 48)
        ref = keep_ref if k < 2 else away_ref
        copies.append(pltpu.make_async_copy(whole_ref.at[rows, :], ref.at[k % 2], sems.at[k]))
    for copy in copies[::-1]:
        copy.start()
    for copy in copies:
        copy.wait()


def token_sum(index, ids_z, other_ids, mine, other):
    return staged_call(
        token_sum_kernel,
        [(index, PLANE)],
        [ids_z, other_ids, mine, other],
        [],
        [
            shaped(bf16, 2, 48, VOCAB_HALF),
            shaped(bf16, 2, 48, VOCAB_HALF),
        ],
        [
            pltpu.VMEM((192, VOCAB_HALF), bf16),
            pltpu.SemaphoreType.DMA((4,)),
        ],
        8,
        staged_out=False,
    )


def my_half(array, core, width):
    return lax.dynamic_slice_in_dim(array, core * width, width, axis=1)


def all_sum(value):
    for pairs in (ZS[1:], [FIRST, SECOND, BOTH]):
        one, two, three = (send(value, p) for p in pairs)
        value = (value + one) + (two + three)
    return value


WINDOWS = (0, 64, 192, 256)
SCALE = HD ** (-0.5)


def piece_copies(idx_ref, base, pieces, target, rows, sems, first_sem):
    copies = []
    for number in range(32):
        half = idx_ref[base + number]
        row = pl.multiple_of(idx_ref[base + 32 + number], 16)
        each = 32 // len(pieces)
        source = pieces[number // each].at[number % each]
        copies.append(
            pltpu.make_async_copy(
                source, target.at[half, pl.ds(row, rows), :], sems.at[first_sem + number]
            )
        )
    return copies


def window_bias(seg_row, seg_col, b):
    w = WINDOWS[b]
    same = seg_col[b * 128 : (b + 1) * 128, :] == seg_row[:, w : w + 256]
    bias = jnp.where(same, 0.0, -1e30)
    return jnp.concatenate([bias, bias], 0)


def two_heads(block):
    left = lax.broadcasted_iota(jnp.int32, block.shape, 1) < HD
    none = jnp.zeros_like(block)
    return jnp.concatenate([jnp.where(left, block, none), jnp.where(left, none, block)], 0)


def nt_dot(a, b):
    return lax.dot_general(a, b, (((1,), (1,)), ((), ())), preferred_element_type=f32)


def tn_dot(a, b):
    return lax.dot_general(a, b, (((0,), (0,)), ((), ())), preferred_element_type=f32)


def nn_dot(a, b):
    return jnp.dot(a, b, preferred_element_type=f32)


def row_norm(v):
    center = v - jnp.mean(v, -1, keepdims=True)
    inv = lax.rsqrt(jnp.mean(center * center, -1, keepdims=True) + norm_eps)
    return center * inv, inv


def attention_kernel(ready, idx_ref, seg_row_ref, seg_col_ref, *refs):
    e_in, pieces = refs[:4], refs[4:12]
    (e_ref, qkv_ref, lse_ref, mixed_ref, unit_ref, inv_ref, low_ref, par_ref, side_ref) = refs[12:21]
    et_ref, w_ref, bias_ref, attended_ref, sems = refs[21:]
    e_copies = [
        pltpu.make_async_copy(
            e_in[j].at[:, pl.ds(0, 512)],
            et_ref.at[pl.ds(pl.multiple_of(idx_ref[j], 16), 192), :],
            sems.at[j],
        )
        for j in range(4)
    ]
    w_copies = piece_copies(idx_ref, 4, pieces, w_ref, 48, sems, 4)
    for copy in e_copies + w_copies:
        copy.start()
    ready()
    for b in range(4):
        bias_ref[b] = window_bias(seg_row_ref[...], seg_col_ref[...], b)
    for copy in e_copies:
        copy.wait()
    e_ref[...] = et_ref[...].T
    ready.put(0)
    for copy in w_copies:
        copy.wait()
    par_ref[...] = w_ref[0, :, 1536:1664].T.astype(f32)[:8]
    side_ref[...] = w_ref[:, :, 1536:1664]
    for k in range(2):
        for t in range(3):
            part = nn_dot(e_ref[...], w_ref[k, :, t * 384 : (t + 1) * 384])
            if t == 0:
                part = part.astype(bf16).astype(f32) * SCALE
            part = part.astype(bf16)
            for i in range(3):
                qkv_ref[t * 6 + k * 3 + i] = part[:, i * 128 : (i + 1) * 128]
    ready.put(1, 7, 8)
    lse_ref[...] = jnp.zeros_like(lse_ref)
    lane = lax.broadcasted_iota(jnp.int32, (128, 128), 1)
    left = lane < HD

    @pl.loop(0, 6, unroll=3)
    def _(pair):
        for b in range(4):
            rows = pl.ds(b * 128, 128)
            keys = pl.ds(WINDOWS[b], 256)
            q = qkv_ref[pair, rows, :]
            k = qkv_ref[pair + 6, keys, :]
            v = qkv_ref[pair + 12, keys, :]
            s = nt_dot(two_heads(q), k) + bias_ref[b]
            top = jnp.max(s, -1, keepdims=True)
            e = jnp.exp(s - top)
            total = jnp.sum(e, -1, keepdims=True)
            log = top + jnp.log(total)
            lse = jnp.where(lane == pair * 2, log[:128], lse_ref[rows, :])
            lse_ref[rows, :] = jnp.where(lane == pair * 2 + 1, log[128:], lse)
            mixed = nn_dot((e * (1.0 / total)).astype(bf16), v)
            cols = pl.ds(pl.multiple_of(pair * 128, 128), 128)
            mixed_ref[rows, cols] = jnp.where(left, mixed[:128], mixed[128:]).astype(bf16)

    ready.put(2, 3)
    for k in range(2):
        attended_ref[:, k * 384 : (k + 1) * 384] = nn_dot(mixed_ref[...], w_ref[k, :, 1152:1536])
    for b in range(4):
        rows = slice(b * 128, (b + 1) * 128)
        unit, inv = row_norm(e_ref[rows, :].astype(f32) + attended_ref[rows, :])
        unit_ref[rows, :] = unit
        inv_ref[rows, :] = jnp.broadcast_to(inv, (128, 128))
        low_ref[rows, :] = (unit * par_ref[0:1, :] + par_ref[1:2, :]).astype(bf16)


def attention_forward(index, seg_row, seg_col, columns, pieces):
    return staged_call(
        attention_kernel,
        [(index, Z_ROWS)],
        [seg_row, seg_col],
        [*columns, *pieces],
        [
            shaped(bf16, 512, 768),
            shaped(bf16, 18, 512, 128),
            shaped(f32, 512, 128),
            shaped(bf16, 512, 768),
            shaped(f32, 512, 768),
            shaped(f32, 512, 128),
            shaped(bf16, 512, 768),
            shaped(f32, 8, 768),
            shaped(bf16, 2, 768, 128),
        ],
        [
            pltpu.VMEM((768, 512), bf16),
            pltpu.VMEM((2, 768, 1664), bf16),
            pltpu.VMEM((4, 256, 256), f32),
            pltpu.VMEM((512, 768), f32),
            pltpu.SemaphoreType.DMA((36,)),
        ],
        17,
    )


def gelu_and_slope(u):
    bell = jnp.exp(-0.5 * u * u)
    base = 1.0 + (0.3275911 * 0.5**0.5) * jnp.abs(u)
    t = pl.reciprocal(base, approx=True)
    t = t * (2.0 - base * t)
    poly = -0.07032334059476852
    for factor in (
        0.24725385010242462,
        -0.2008872926235199,
        0.2245105654001236,
        0.013965459540486336,
        0.10251718759536743,
        0.09044301509857178,
        0.09252061694860458,
    ):
        poly = factor + t * poly
    tail = (t * poly) * bell
    phi = jnp.where(u < 0, tail, 1.0 - tail)
    return u * phi, phi + (u * 0.3989422804014327) * bell


def up_kernel(ready, idx_ref, low_ref, *refs):
    pieces, act_ref, slope_ref, w_ref, sems = refs[:8], refs[8], refs[9], refs[10], refs[11]
    copies = piece_copies(idx_ref, 0, pieces, w_ref, 48, sems, 0)
    for copy in copies:
        copy.start()
    ready()
    core = idx_ref[0]
    for side in range(2):
        half = core if side == 0 else 1 - core
        for copy in copies[side * 16 : side * 16 + 16]:
            copy.wait()

        @pl.loop(0, 6, unroll=3)
        def _(n):
            cols = pl.ds(pl.multiple_of(n * 256, 256), 256)
            u = nn_dot(low_ref[...], w_ref[half, :, cols])
            value, slope = gelu_and_slope(u)
            out_cols = pl.ds(pl.multiple_of(half * 1536 + n * 256, 256), 256)
            act_ref[:, out_cols] = value.astype(bf16)
            slope_ref[:, out_cols] = slope.astype(bf16)

        ready.put_half(side, half, (0, 1), 1536)


def up_forward(index, low, pieces):
    return staged_call(
        up_kernel,
        [(index, BY_FLIP)],
        [low],
        pieces,
        [
            shaped(bf16, 512, 3072),
            shaped(bf16, 512, 3072),
        ],
        [
            pltpu.VMEM((2, 768, 1536), bf16),
            pltpu.SemaphoreType.DMA((32,)),
        ],
        18,
    )


def thirds(v):
    high = v.astype(bf16)
    rest = v - high.astype(f32)
    middle = rest.astype(bf16)
    return high, middle, (rest - middle.astype(f32)).astype(bf16)


def down_kernel(ready, idx_ref, seg_row_ref, act_ref, unit_one_ref, par_ref, *refs):
    unit_ref, inv_ref, frag_ref, frag_low_ref, size_ref, w_ref, result_ref, sems = refs[4:]
    copies = piece_copies(idx_ref, 0, refs[:4], w_ref, 192, sems, 0)
    for copy in copies:
        copy.start()
    ready()
    for copy in copies:
        copy.wait()
    for k in range(2):
        result_ref[:, k * 384 : (k + 1) * 384] = nn_dot(act_ref[...], w_ref[k])
    pooled = jnp.zeros((32, 768), f32)
    for b in range(4):
        rows = slice(b * 128, (b + 1) * 128)
        one = unit_one_ref[rows, :] * par_ref[0:1, :] + par_ref[1:2, :]
        unit, inv = row_norm(one + result_ref[rows, :])
        unit_ref[rows, :] = unit
        inv_ref[rows, :] = jnp.broadcast_to(inv, (128, 128))
        two = unit * par_ref[2:3, :] + par_ref[3:4, :]
        member = lax.broadcasted_iota(jnp.int32, (32, 128), 0) == seg_row_ref[:, rows]
        member = jnp.where(member, 1.0, 0.0).astype(bf16)
        for part in thirds(two):
            pooled += nn_dot(member, part)
    size = lax.rsqrt(jnp.sum(pooled * pooled, -1, keepdims=True) + unit_eps)
    frag = pooled * size
    frag_ref[...] = frag
    frag_low_ref[...] = frag.astype(bf16)
    size_ref[...] = jnp.broadcast_to(size, (32, 128))


def down_forward(index, seg_row, act, unit_one, params, pieces):
    return staged_call(
        down_kernel,
        [(index, BY_PAIR)],
        [seg_row, act, unit_one, params],
        pieces,
        [
            shaped(f32, 512, 768),
            shaped(f32, 512, 128),
            shaped(f32, 32, 768),
            shaped(bf16, 32, 768),
            shaped(f32, 32, 128),
        ],
        [
            pltpu.VMEM((2, 3072, 384), bf16),
            pltpu.VMEM((512, 768), f32),
            pltpu.SemaphoreType.DMA((32,)),
        ],
        10,
    )


def back_norm(upstream, unit, inv, gain):
    scaled = upstream * gain
    return inv * (
        scaled
        - jnp.mean(scaled, -1, keepdims=True)
        - unit * jnp.mean(scaled * unit, -1, keepdims=True)
    )


def loss_kernel(
    ready, idx_ref, heat_ref, seg_col_ref, partner_ref, own_weight_ref, side_ref,
    frag_ref, size_ref, unit_ref, inv_ref, par_ref, slope_ref, *refs
):
    blocks, down_pieces = refs[:8], refs[8:12]
    loss_ref, low_own_ref, low_other_ref, gup_own_ref, gup_other_ref, two_ref, gains_ref = refs[12:19]
    all_ref, down_ref, low_ref, spread_ref, sems, w_sems = refs[19:]
    copies = []
    for number in range(32):
        row = pl.multiple_of(idx_ref[1 + number], 16)
        copies.append(
            pltpu.make_async_copy(
                blocks[number // 4].at[number % 4], all_ref.at[pl.ds(row, 32), :], sems.at[number]
            )
        )
    core = idx_ref[33]
    down_copies = piece_copies(idx_ref, 34, down_pieces, down_ref, 192, w_sems, 0)
    for copy in copies:
        copy.start()
    for copy in copies:
        copy.wait()
    ready(1, 2, 3)
    ready.copies_in[9].start()
    for copy in down_copies:
        copy.start()
    base = idx_ref[0]
    inv_heat = 1.0 / heat_ref[0]
    tally = 1024
    mine = all_ref[pl.ds(pl.multiple_of(base, 16), 32), :]
    grid = (nt_dot(mine, all_ref[...]) - 1.0) * inv_heat
    across = lax.broadcasted_iota(jnp.int32, (32, tally), 1)
    down = lax.broadcasted_iota(jnp.int32, (32, tally), 0) + base
    powers = jnp.where(across == down, 0.0, jnp.exp(grid))
    total = jnp.sum(powers, -1, keepdims=True)
    eye = lax.broadcasted_iota(jnp.int32, (32, 32), 0) == lax.broadcasted_iota(jnp.int32, (32, 32), 1)
    partner = jnp.sum(jnp.where(eye, partner_ref[...].astype(f32), 0.0), -1, keepdims=True)
    own_weight = jnp.sum(jnp.where(eye, own_weight_ref[...], 0.0), -1, keepdims=True)
    chosen = across == partner.astype(jnp.int32)
    target = jnp.sum(jnp.where(chosen, grid, 0.0), -1, keepdims=True)
    terms = own_weight * (jnp.log(total) - target)
    loss_ref[...] = jnp.broadcast_to(jnp.sum(terms, 0, keepdims=True) / tally, (8, 128))
    picked = jnp.where(chosen, 1.0, 0.0)
    pull = (powers / total - picked) * (own_weight * (inv_heat / tally))
    totals = [jnp.zeros((1, 128), f32) for _ in range(8)]
    number = lax.broadcasted_iota(jnp.int32, (128, 128), 0)
    same = number == lax.broadcasted_iota(jnp.int32, (128, 128), 1)
    weights = []
    for big in range(2):
        spread_ref[...] = nt_dot(all_ref[big * 512 : (big + 1) * 512, :], all_ref[...])
        for b in range(big * 4, big * 4 + 4):
            inside = slice((b - big * 4) * 128, (b - big * 4 + 1) * 128)
            for n in range(8):
                spread = jnp.exp((spread_ref[inside, n * 128 : (n + 1) * 128] - 1.0) * inv_heat)
                if n == b:
                    spread = jnp.where(same, 0.0, spread)
                totals[n] += jnp.sum(spread, 0, keepdims=True)
            side = jnp.concatenate(
                [
                    side_ref[n % 2, (n // 2) * 48 : (n // 2) * 48 + 32, :].astype(f32)
                    for n in range(b * 4, b * 4 + 4)
                ],
                0,
            ).T
            weights.append(side[4:5] + side[5:6] + side[6:7])
    totals, weights = jnp.concatenate(totals, 1), jnp.concatenate(weights, 1)
    column_pull = (powers / totals - picked) * (weights * (inv_heat / tally))
    both = jnp.concatenate([pull.astype(bf16), column_pull.astype(bf16)], 0)
    both = nn_dot(both, all_ref[...])
    grad = both[:32] + both[32:]
    ready(0, 4, 5, 6, 7, 8)
    frag = frag_ref[...]
    pooled = size_ref[:, 0:1] * (grad - frag * jnp.sum(grad * frag, -1, keepdims=True))
    stacked = jnp.concatenate(thirds(pooled), 0)
    gain_two = jnp.zeros((1, 768), f32)
    shift_two = jnp.zeros((1, 768), f32)
    for b in range(4):
        rows = slice(b * 128, (b + 1) * 128)
        slot = lax.broadcasted_iota(jnp.int32, (128, 96), 1) % 32
        member = jnp.where(slot == seg_col_ref[rows, :], 1.0, 0.0).astype(bf16)
        upstream = nn_dot(member, stacked)
        unit = unit_ref[rows, :]
        back = back_norm(upstream, unit, inv_ref[rows, 0:1], par_ref[2:3, :])
        two_ref[rows, :] = back
        low_ref[rows, :] = back.astype(bf16)
        gain_two += jnp.sum(upstream * unit, 0, keepdims=True)
        shift_two += jnp.sum(upstream, 0, keepdims=True)
    halves = (core, 1 - core)
    for half, ref in zip(halves, (low_own_ref, low_other_ref)):
        ref[...] = low_ref[:, pl.ds(pl.multiple_of(half * 384, 128), 384)]
    ready.put(0, 1, 2, 5)
    ready(9)
    for copy in down_copies:
        copy.wait()
    for half, gup_ref in zip(halves, (gup_own_ref, gup_other_ref)):

        @pl.loop(0, 6, unroll=3)
        def _(n):
            cols = pl.ds(pl.multiple_of(n * 256, 256), 256)
            wide = pl.ds(pl.multiple_of(half * 1536 + n * 256, 256), 256)
            g = sum(
                nt_dot(low_ref[:, k * 384 : (k + 1) * 384], down_ref[k, wide, :])
                for k in range(2)
            )
            gup_ref[:, cols] = (g * slope_ref[:, wide].astype(f32)).astype(bf16)

        if gup_ref is gup_own_ref:
            ready.put(3)

    gains_ref[...] = jnp.concatenate([gain_two, shift_two, jnp.zeros((6, 768), f32)], 0)


def loss_backward(index, heat, arrays, pieces):
    return staged_call(
        loss_kernel,
        [(index, FRAGMENTS), (heat, 0)],
        arrays,
        pieces,
        [
            shaped(f32, 8, 128),
            shaped(bf16, 512, 384),
            shaped(bf16, 512, 384),
            shaped(bf16, 512, 1536),
            shaped(bf16, 512, 1536),
            shaped(f32, 512, 768),
            shaped(f32, 8, 768),
        ],
        [
            pltpu.VMEM((1024, 768), bf16),
            pltpu.VMEM((2, 3072, 384), bf16),
            pltpu.VMEM((512, 768), bf16),
            pltpu.VMEM((512, 1024), f32),
            pltpu.SemaphoreType.DMA((32,)),
            pltpu.SemaphoreType.DMA((32,)),
        ],
        18,
        (9,),
    )


def ffn_back_kernel(
    ready, idx_ref, gup_own_ref, gup_other_ref, two_ref, unit_ref, inv_ref, par_ref, gains_two_ref, *refs
):
    pieces = refs[:8]
    resid_ref, att_ref, own_ref, other_ref, gains_ref, up_ref, sems = refs[8:]
    copies = piece_copies(idx_ref, 0, pieces, up_ref, 48, sems, 0)
    for copy in copies:
        copy.start()
    ready()
    for copy in copies:
        copy.wait()
    core = idx_ref[0]
    for n in range(3):
        cols = slice(n * 256, (n + 1) * 256)
        resid_ref[:, cols] = (
            two_ref[:, cols]
            + nt_dot(gup_own_ref[...], up_ref[core, cols, :])
            + nt_dot(gup_other_ref[...], up_ref[1 - core, cols, :])
        )
    gain_sum = jnp.zeros((1, 768), f32)
    shift_sum = jnp.zeros((1, 768), f32)
    for b in range(4):
        rows = slice(b * 128, (b + 1) * 128)
        one = resid_ref[rows, :]
        unit = unit_ref[rows, :]
        back = back_norm(one, unit, inv_ref[rows, 0:1], par_ref[0:1, :])
        resid_ref[rows, :] = back
        att_ref[rows, :] = back.astype(bf16)
        gain_sum += jnp.sum(one * unit, 0, keepdims=True)
        shift_sum += jnp.sum(one, 0, keepdims=True)
    for half, ref in ((core, own_ref), (1 - core, other_ref)):
        ref[...] = att_ref[:, pl.ds(pl.multiple_of(half * 384, 128), 384)]
    gains_ref[...] = jnp.concatenate(
        [gain_sum, shift_sum, gains_two_ref[0:2, :], jnp.zeros((4, 768), f32)], 0
    )


def ffn_backward(index, arrays, pieces):
    return staged_call(
        ffn_back_kernel,
        [(index, BY_FLIP)],
        arrays,
        pieces,
        [
            shaped(f32, 512, 768),
            shaped(bf16, 512, 768),
            shaped(bf16, 512, 384),
            shaped(bf16, 512, 384),
            shaped(f32, 8, 768),
        ],
        [pltpu.VMEM((2, 768, 1536), bf16), pltpu.SemaphoreType.DMA((32,))],
        9,
    )


def heads_back(half, gm_ref, qkv_ref, lse_ref, bias_ref, gqkv_ref, gk_ref, gv_ref):
    lane = lax.broadcasted_iota(jnp.int32, (128, 128), 1)
    left = lane < HD
    gk_ref[...] = jnp.zeros_like(gk_ref)
    gv_ref[...] = jnp.zeros_like(gv_ref)

    @pl.loop(0, 3, unroll=3)
    def _(spot):
        pair = half * 3 + spot
        for b in range(4):
            rows = pl.ds(b * 128, 128)
            keys = pl.ds(WINDOWS[b], 256)
            q = qkv_ref[pair, rows, :]
            k = qkv_ref[pair + 6, keys, :]
            v = qkv_ref[pair + 12, keys, :]
            gm = gm_ref[rows, pl.ds(pl.multiple_of(spot * 128, 128), 128)]
            q, gm = two_heads(q), two_heads(gm)
            stats = lse_ref[rows, :]
            lse = jnp.concatenate(
                [
                    jnp.sum(jnp.where(lane == pair * 2 + h, stats, 0.0), -1, keepdims=True)
                    for h in range(2)
                ],
                0,
            )
            p = jnp.exp(nt_dot(q, k) + bias_ref[b] - lse)
            gp = nt_dot(gm, v)
            gs = (p * (gp - jnp.sum(gp * p, -1, keepdims=True))).astype(bf16)
            gq = nn_dot(gs, k)
            gq = (jnp.where(left, gq[:128], gq[128:]) * SCALE).astype(bf16)
            gqkv_ref[rows, pl.ds(pl.multiple_of(spot * 128, 128), 128)] = gq
            gk_ref[spot, keys, :] += tn_dot(gs, q)
            gv_ref[spot, keys, :] += tn_dot(p.astype(bf16), gm)
        for third, ref in ((1, gk_ref), (2, gv_ref)):
            cols = pl.ds(pl.multiple_of(third * 384 + spot * 128, 128), 128)
            gqkv_ref[:, cols] = ref[spot].astype(bf16)


def other_heads_kernel(ready, idx_ref, seg_row_ref, seg_col_ref, qkv_ref, lse_ref, att_ref, resid_ref, *refs
):
    pieces = refs[:8]
    gqkv_ref, gm_own_ref, part_ref = refs[8:11]
    w_ref, bias_ref, gm_ref, gk_ref, gv_ref, sems = refs[11:]
    copies = piece_copies(idx_ref, 4, pieces, w_ref, 48, sems, 0)
    for copy in copies:
        copy.start()
    ready()
    for b in range(4):
        bias_ref[b] = window_bias(seg_row_ref[...], seg_col_ref[...], b)
    for copy in copies:
        copy.wait()
    core = idx_ref[4]
    half = 1 - core
    for side, ref in ((half, gm_ref), (core, gm_own_ref)):
        rows = pl.ds(pl.multiple_of(side * 384, 128), 384)
        ref[...] = sum(
            nt_dot(att_ref[:, k * 384 : (k + 1) * 384], w_ref[k, rows, 1152:1536])
            for k in range(2)
        ).astype(bf16)
    heads_back(half, gm_ref, qkv_ref, lse_ref, bias_ref, gqkv_ref, gk_ref, gv_ref)
    ready.put(0, 1)
    for n in range(3):
        cols = slice(n * 256, (n + 1) * 256)
        part_ref[:, cols] = resid_ref[:, cols] + nt_dot(gqkv_ref[...], w_ref[half, cols, :1152])


def other_heads(index, arrays, pieces):
    return staged_call(
        other_heads_kernel,
        [(index, Z_ROWS)],
        arrays,
        pieces,
        [
            shaped(bf16, 512, 1152),
            shaped(bf16, 512, 384),
            shaped(f32, 512, 768),
        ],
        [
            pltpu.VMEM((2, 768, 1664), bf16),
            pltpu.VMEM((4, 256, 256), f32),
            pltpu.VMEM((512, 384), bf16),
            pltpu.VMEM((3, 512, 128), f32),
            pltpu.VMEM((3, 512, 128), f32),
            pltpu.SemaphoreType.DMA((32,)),
        ],
        17,
    )


def own_heads_kernel(ready, idx_ref, seg_row_ref, seg_col_ref, qkv_ref, lse_ref, gm_ref, part_ref, *refs
):
    pieces = refs[:4]
    gqkv_ref, outs = refs[4], refs[5:9]
    w_ref, bias_ref, gk_ref, gv_ref, et_ref, sems = refs[9:]
    copies = []
    for number in range(16):
        row = pl.multiple_of(idx_ref[36 + number], 16)
        copies.append(
            pltpu.make_async_copy(
                pieces[number // 4].at[number % 4], w_ref.at[pl.ds(row, 48), :], sems.at[number]
            )
        )
    for copy in copies:
        copy.start()
    ready()
    for b in range(4):
        bias_ref[b] = window_bias(seg_row_ref[...], seg_col_ref[...], b)
    core = idx_ref[4]
    heads_back(core, gm_ref, qkv_ref, lse_ref, bias_ref, gqkv_ref, gk_ref, gv_ref)
    ready.put(0)
    for copy in copies:
        copy.wait()
    for n in range(3):
        cols = slice(n * 256, (n + 1) * 256)
        total = part_ref[:, cols] + nt_dot(gqkv_ref[...], w_ref[cols, :1152])
        et_ref[cols, :] = total.astype(bf16).T
    for j in range(4):
        outs[j][...] = et_ref[pl.ds(pl.multiple_of(idx_ref[j], 16), 192), :]


def own_heads(index, arrays, pieces):
    return staged_call(
        own_heads_kernel,
        [(index, Z_ROWS)],
        arrays,
        pieces,
        [
            shaped(bf16, 512, 1152),
            shaped(bf16, 192, 512),
            shaped(bf16, 192, 512),
            shaped(bf16, 192, 512),
            shaped(bf16, 192, 512),
        ],
        [
            pltpu.VMEM((768, 1664), bf16),
            pltpu.VMEM((4, 256, 256), f32),
            pltpu.VMEM((3, 512, 128), f32),
            pltpu.VMEM((3, 512, 128), f32),
            pltpu.VMEM((768, 512), bf16),
            pltpu.SemaphoreType.DMA((16,)),
        ],
        15,
    )


def to_slots(idx_ref, whole_ref, keep_ref, away_ref, sems):
    copies = []
    for start, ref in ((8, away_ref), (0, keep_ref)):
        for slot in range(8):
            source = whole_ref.at[idx_ref[start + slot]]
            copies.append(pltpu.make_async_copy(source, ref.at[slot], sems.at[start + slot]))
    for copy in copies:
        copy.start()
    for copy in copies:
        copy.wait()


def down_grad_kernel(ready, idx_ref, act_ref, act_o_ref, g_ref, g_o_ref, keep_ref, away_ref, whole_ref, sems):
    ready()
    for n in range(8):
        cols = slice(n * 384, (n + 1) * 384)
        total = tn_dot(act_ref[:, cols], g_ref[...]) + tn_dot(act_o_ref[:, cols], g_o_ref[...])
        total = total.astype(bf16)
        whole_ref[2 * n] = total[:192]
        whole_ref[2 * n + 1] = total[192:]
    to_slots(idx_ref, whole_ref, keep_ref, away_ref, sems)


def down_grad(index, arrays):
    return staged_call(
        down_grad_kernel,
        [(index, SLOTS)],
        arrays,
        [],
        [shaped(bf16, 8, 192, 384)] * 2,
        [pltpu.VMEM((16, 192, 384), bf16), pltpu.SemaphoreType.DMA((16,))],
        7,
        staged_out=False,
    )


def store_chunks(whole_ref, cols, total):
    for f in range(16):
        whole_ref[f, :, cols] = total[f * 48 : (f + 1) * 48]


def up_out_grad_kernel(
    ready, idx_ref, low_ref, low_o_ref, g_ref, g_o_ref, mixed_ref, mixed_o_ref, ga_ref, ga_o_ref, norms_ref,
    norms_o_ref, keep_ref, away_ref, whole_ref, t_ref, sems,
):
    ready()
    t_ref[0] = low_ref[...].T
    t_ref[1] = low_o_ref[...].T
    for n in range(3):
        cols = slice(n * 512, (n + 1) * 512)
        total = nn_dot(t_ref[0], g_ref[:, cols]) + nn_dot(t_ref[1], g_o_ref[:, cols])
        store_chunks(whole_ref, cols, total.astype(bf16))
    t_ref[0] = mixed_ref[...].T
    t_ref[1] = mixed_o_ref[...].T
    total = nn_dot(t_ref[0], ga_ref[...]) + nn_dot(t_ref[1], ga_o_ref[...])
    store_chunks(whole_ref, slice(1536, 1920), total.astype(bf16))
    norms = (norms_ref[...] + norms_o_ref[...]).T.astype(bf16)
    norms = jnp.concatenate([norms, jnp.zeros((768, 120), bf16)], 1)
    store_chunks(whole_ref, slice(1920, 2048), norms)
    to_slots(idx_ref, whole_ref, keep_ref, away_ref, sems)


def up_out_grad(index, arrays):
    return staged_call(
        up_out_grad_kernel,
        [(index, SLOTS)],
        arrays,
        [],
        [
            shaped(bf16, 8, 48, 2048),
            shaped(bf16, 8, 48, 2048),
        ],
        [
            pltpu.VMEM((16, 48, 2048), bf16),
            pltpu.VMEM((2, 768, 512), bf16),
            pltpu.SemaphoreType.DMA((16,)),
        ],
        8,
        staged_out=False,
    )


def in_grad_kernel(ready, idx_ref, e_ref, e_o_ref, g_ref, g_o_ref, keep_ref, away_ref, whole_ref, t_ref, sems):
    ready()
    t_ref[0] = e_ref[...].T
    t_ref[1] = e_o_ref[...].T
    for t in range(3):
        cols = slice(t * 384, (t + 1) * 384)
        total = nn_dot(t_ref[0], g_ref[:, cols]) + nn_dot(t_ref[1], g_o_ref[:, cols])
        store_chunks(whole_ref, cols, total.astype(bf16))
    to_slots(idx_ref, whole_ref, keep_ref, away_ref, sems)


def in_grad(index, arrays):
    return staged_call(
        in_grad_kernel,
        [(index, SLOTS)],
        arrays,
        [],
        [
            shaped(bf16, 8, 48, 1152),
            shaped(bf16, 8, 48, 1152),
        ],
        [
            pltpu.VMEM((16, 48, 1152), bf16),
            pltpu.VMEM((2, 768, 512), bf16),
            pltpu.SemaphoreType.DMA((16,)),
        ],
        6,
        staged_out=False,
    )


def optimizer_kernel(ready, core_ref, fix_ref, totals_ref, totals_o_ref, *refs):
    ready(*range(10))
    own, other = refs[:4], refs[4:8]
    params, outs = refs[8:26], refs[26:46]
    table_ref = refs[46]
    core = core_ref[0]
    totals = totals_ref[...] + totals_o_ref[...]
    norm = jnp.sqrt(totals[:, 0:1])
    outs[0][...] = totals[:, 1:2]
    outs[1][...] = norm
    factor = clip_norm / jnp.maximum(norm, clip_norm)
    fix_one, fix_two = 1.0 / fix_ref[0], 1.0 / fix_ref[1]

    def update(number, spot, grad, rate, decay):
        w_ref, first_ref, second_ref = params[3 * number : 3 * number + 3]
        grad = grad.astype(f32) * factor
        weight = w_ref[spot]
        first = beta_one * first_ref[spot] + (1.0 - beta_one) * grad
        second = beta_two * second_ref[spot] + (1.0 - beta_two) * grad * grad
        step = (first * fix_one) / (jnp.sqrt(second * fix_two) + adam_eps)
        outs[2 + 3 * number][spot] = weight - rate * (step + decay * weight)
        outs[3 + 3 * number][spot] = first
        outs[4 + 3 * number][spot] = second

    every = slice(None)
    halves = ((core, own), (1 - core, other))

    def columns(half, width, start=0):
        return pl.ds(pl.multiple_of(half * width + start, 128), width)

    def opened(number):
        ready(*range(10 + 3 * number, 13 + 3 * number))

    def done(number):
        ready.put(*range(2 + 3 * number, 5 + 3 * number))

    opened(3)
    for half, (_, _, up_out, _) in halves:
        for t in range(3):
            spot = pl.ds(pl.multiple_of(half * 1536 + t * 512, 128), 512)
            update(3, (every, spot), up_out[:, t * 512 : (t + 1) * 512], rate_matrix, decay_rate)
    done(3)
    opened(4)
    for half, (_, _, _, down) in halves:
        for t in range(4):
            rows = slice(t * 48, (t + 1) * 48)
            update(4, (rows, columns(half, 384)), down[rows, :], rate_matrix, decay_rate)
    done(4)
    opened(1)
    for half, (_, into, _, _) in halves:
        for t in range(3):
            update(
                1,
                (every, columns(half, 384, t * 768)),
                into[:, t * 384 : (t + 1) * 384],
                rate_matrix,
                decay_rate,
            )
    done(1)
    opened(0)
    for half, (table, _, _, _) in halves:
        table_ref[:, columns(half, VOCAB_HALF)] = table[...]
    vocab = params[0].shape[1]
    for low in range(0, vocab, 512):
        spot = slice(low, min(vocab, low + 512))
        update(0, (every, spot), table_ref[:, spot], rate_embed, decay_rate)
    done(0)
    opened(2)
    for half, (_, _, up_out, _) in halves:
        update(2, (every, columns(half, 384)), up_out[:, 1536:1920], rate_matrix, decay_rate)
    done(2)
    opened(5)
    norms = jnp.where(core == 0, own[2][:, 1920:].astype(f32), other[2][:, 1920:].astype(f32))
    update(5, (every, every), norms.T[:4], rate_norm, 0.0)


def optimizer(core, fixes, totals, totals_o, own, other, params):
    return staged_call(
        optimizer_kernel,
        [(core, MY_CORE), (fixes, 0)],
        [totals, totals_o, *own, *other, *params],
        [],
        [
            shaped(f32, 1, 1),
            shaped(f32, 1, 1),
            *[shaped(f32, *p.shape) for p in params],
        ],
        [
            pltpu.VMEM((48, VOCAB_PAD), bf16),
        ],
        8,
    )


def per_device_links(
    kmer_identifiers,
    slot_fragment_ids,
    mirror_fragment_index,
    fragment_weight,
    affinity_heat,
    optimizer_iteration,
    lexicon_table,
    lexicon_first_moment,
    lexicon_raw_moment,
    query_key_value_maps,
    qkv_first_moment,
    qkv_raw_moment,
    attention_exit_map,
    exit_first_moment,
    exit_raw_moment,
    widening_matrix_in,
    widening_first_moment,
    widening_raw_moment,
    narrowing_matrix_out,
    narrowing_first_moment,
    narrowing_raw_moment,
    layernorm_scale_bias,
    layernorm_first_moment,
    layernorm_raw_moment,
):
    place = Place()
    core = place.core
    vocab = lexicon_table.shape[0]
    index = index_vector(place)
    both_cut, table_cut, table_half, down_half = prepare(
        [
            lexicon_table.T,
            query_key_value_maps,
            attention_exit_map,
            widening_matrix_in,
            narrowing_matrix_out,
            layernorm_scale_bias,
            kmer_identifiers,
            fragment_weight.reshape(1, 32),
        ],
    )
    near = [send(table_half, FIRST), send(table_half, SECOND)]
    near.append(send(near[0], SECOND))
    both_far = z_sends(both_cut)
    down_first = send(after(down_half, near[0]), FIRST)
    others = send(after(jnp.stack(near), down_first, *both_far), CORE)
    id_parts = jnp.stack([p[:8, 3200:] for p in both_far]).astype(f32)
    ids_z = (id_parts[:, :4] * 64.0 + id_parts[:, 4:]).astype(jnp.int32)
    in_out_column = jnp.stack([p[:, :1664] for p in both_far])
    in_out_mine = plane_sends(in_out_column, True)
    found = lookup(index, ids_z, [down_half, down_first], [table_cut] + near + [others])
    up_column = after(jnp.stack([p[:, 1664:3200] for p in both_far]), *found)
    columns = [found[0]] + [send(found[j], ZS[j]) for j in (1, 2, 3)]
    in_out = both_cores(together(in_out_mine, *columns))
    up_mine = plane_sends(after(up_column, in_out_mine[3]), True)
    down_pair = jnp.stack([down_half, after(down_first, *found)])
    down_pair = after(down_pair, *columns)
    d_two, d_three = (send(down_pair, ZS[j]) for j in (2, 3))
    seg_row = slot_fragment_ids
    seg_col = slot_fragment_ids.reshape(512, 1)
    embedded, qkv, lse, mixed, unit_one, inv_one, normed_low, params, side = attention_forward(
        index, seg_row, seg_col, columns, in_out
    )
    *up_mine, d_two, d_three = together(up_mine + [d_two, d_three], normed_low)
    d_one = jnp.stack([columns[1][:, 512:896], columns[1][:, 896:]])
    down_one = jnp.stack([down_pair, d_one, d_two, d_three]).reshape(8, 192, 384)
    down_two = send(down_one, SECOND)
    down_one_o = send(down_one, CORE)
    up_w = both_cores(up_mine)
    activated, slope = up_forward(index, normed_low, up_w)
    down_two, down_one_o = together([down_two, down_one_o], activated)
    down_w = [down_one, down_two, down_one_o, send(down_two, CORE)]
    unit_two, inv_two, unit_rows, unit_low, unit_scale = down_forward(
        index, seg_row, activated, unit_one, params, down_w
    )
    embedded_o, mixed_o, normed_o, activated_o = (
        send(a, CORE) for a in (embedded, mixed, normed_low, activated)
    )
    column = jnp.stack([unit_low] + [send(unit_low, ZS[j]) for j in (1, 2, 3)])
    blocks = [column, send(column, FIRST), send(column, SECOND), send(column, BOTH)]
    blocks = blocks + [send(block, CORE) for block in blocks]
    (
        loss_tile, grad_result_own, grad_result_x, grad_up_own, grad_up_x, grad_two, gains_two,
    ) = loss_backward(
        index,
        affinity_heat.reshape(1),
        [
            seg_col,
            mirror_fragment_index.reshape(1, 32),
            fragment_weight.reshape(1, 32),
            side,
            unit_rows,
            unit_scale,
            unit_two,
            inv_two,
            params,
            slope,
        ],
        blocks + down_w,
    )
    grad_result_o = send(grad_result_x, CORE)
    ids_o = send(ids_z, CORE)
    grad_up_o = send(grad_up_x, CORE)
    spare = [embedded_o, mixed_o, normed_o, ids_o]
    down_keep, down_away = down_grad(
        index, [after(activated, *spare), activated_o, grad_result_own, grad_result_o]
    )
    down_came = send(down_away, SECOND)
    grad_resid, grad_attended, grad_att_own, grad_att_x, norms = ffn_backward(
        index,
        [after(grad_up_own, down_away), grad_up_x, grad_two, unit_one, inv_one, params, gains_two],
        up_w,
    )
    grad_att_o = send(grad_att_x, CORE)
    norms_o = send(norms, CORE)
    up_out_keep, up_out_away = up_out_grad(
        index,
        [
            normed_low,
            normed_o,
            grad_up_own,
            grad_up_o,
            mixed,
            mixed_o,
            grad_att_own,
            grad_att_o,
            norms,
            norms_o,
        ],
    )
    up_out_came = send(up_out_away, SECOND)
    down_came = after(down_came, up_out_away)
    down_across = scatter_add(down_keep, down_came)
    down_came_two = send(down_across, FIRST)
    grad_qkv_x, grad_mixed_own, part = other_heads(
        index,
        [seg_row, seg_col, qkv, lse, after(grad_attended, down_across), grad_resid],
        in_out,
    )
    grad_qkv_o = send(grad_qkv_x, CORE)
    down_came_two = after(down_came_two, part)
    down_here, down_far = scatter_here(down_keep, down_came, down_came_two)
    down_far_came = line_sends(down_far)
    grad_qkv_own, *outs = own_heads(
        index,
        [seg_row, seg_col, qkv, lse, grad_mixed_own, after(part, *down_far)],
        in_out[:4],
    )
    far_cols = [send(outs[j], ZS[j]) for j in (1, 2, 3)]
    *down_far_came, up_out_came, grad_qkv_o = together(
        down_far_came + [up_out_came, grad_qkv_o], grad_qkv_own
    )
    up_out_across = scatter_add(up_out_keep, up_out_came)
    up_out_came_two = send(up_out_across, FIRST)
    in_keep, in_away = in_grad(
        index, [embedded, embedded_o, after(grad_qkv_own, up_out_across), grad_qkv_o]
    )
    far_cols = together(far_cols, in_away)
    in_came = send(in_away, SECOND)
    token_cols = jnp.stack([outs[0]] + far_cols)
    token_cols_o = send(token_cols, CORE)
    up_out_here, up_out_far = scatter_here(
        up_out_keep, up_out_came, after(up_out_came_two, token_cols)
    )
    up_out_far_came = line_sends(up_out_far)
    keep, away = token_sum(
        index,
        after(ids_z, *up_out_far),
        ids_o,
        token_cols,
        token_cols_o,
    )
    came = send(away, SECOND)
    in_came = after(in_came, away)
    in_across = scatter_add(in_keep, in_came)
    in_came_two = send(in_across, FIRST)
    across = (keep[1].astype(f32) + came[1].astype(f32)).astype(bf16)
    came_two = send(across, FIRST)
    up_out_far_came = together(up_out_far_came, across)
    in_here, in_far = scatter_here(
        in_keep, in_came, after(in_came_two, across, *up_out_far_came)
    )
    in_far_came = line_sends(in_far)
    down_sum = line_sum(after(down_here, came_two), down_far_came)
    up_out_sum = line_sum(up_out_here, together(up_out_far_came, came_two))
    table_sum = keep[0].astype(f32) + came[0].astype(f32) + came_two.astype(f32)
    table_sum = table_sum.astype(bf16)
    early = [table_sum, up_out_sum, down_sum]
    norm_own = up_out_sum[:, 1920:1924].astype(f32)
    squares = sum(
        jnp.sum(jnp.square(p.astype(f32))) for p in (table_sum, up_out_sum[:, :1920], down_sum)
    ) + jnp.where(core == 0, jnp.sum(norm_own * norm_own), 0.0)
    early_o = [send(s, CORE) for s in early]
    in_sum = line_sum(in_here, together(in_far_came, squares))
    in_o = send(in_sum, CORE)
    squares += jnp.sum(jnp.square(in_sum.astype(f32)))
    lane = lax.broadcasted_iota(jnp.int32, (1, 128), 1)
    totals = jnp.where(lane == 0, squares, loss_tile[0:1])
    totals = all_sum(after(totals, *early_o))
    sums = [table_sum, in_sum, up_out_sum, down_sum]
    sums_o = [early_o[0], in_o, early_o[1], early_o[2]]
    count_now = optimizer_iteration.astype(f32)
    fixes = jnp.stack([1.0 - jnp.power(beta_one, count_now), 1.0 - jnp.power(beta_two, count_now)])
    results = optimizer(
        index,
        fixes,
        totals,
        send(totals, CORE),
        sums,
        sums_o,
        [
            lexicon_table.T,
            lexicon_first_moment.T,
            lexicon_raw_moment.T,
            query_key_value_maps,
            qkv_first_moment,
            qkv_raw_moment,
            attention_exit_map,
            exit_first_moment,
            exit_raw_moment,
            widening_matrix_in,
            widening_first_moment,
            widening_raw_moment,
            narrowing_matrix_out,
            narrowing_first_moment,
            narrowing_raw_moment,
            layernorm_scale_bias,
            layernorm_first_moment,
            layernorm_raw_moment,
        ],
    )
    results = list(results)
    results[:2] = [r[0, 0] for r in results[:2]]
    results[2:5] = [r.T for r in results[2:5]]
    return tuple(results)


def solution(mesh):
    in_specs = (
        P(("fsdp", "dp"), None),
        P(("fsdp", "dp"), None),
        P(("fsdp", "dp")),
        P(("fsdp", "dp")),
        P(),
        P(),
        P(None, "fsdp"),
        P(None, "fsdp"),
        P(None, "fsdp"),
        P("fsdp", None),
        P("fsdp", None),
        P("fsdp", None),
        P("fsdp", None),
        P("fsdp", None),
        P("fsdp", None),
        P("fsdp", None),
        P("fsdp", None),
        P("fsdp", None),
        P("fsdp", None),
        P("fsdp", None),
        P("fsdp", None),
        P(None, "fsdp"),
        P(None, "fsdp"),
        P(None, "fsdp"),
    )
    out_specs = (
        P(),
        P(),
        P(None, "fsdp"),
        P(None, "fsdp"),
        P(None, "fsdp"),
        P("fsdp", None),
        P("fsdp", None),
        P("fsdp", None),
        P("fsdp", None),
        P("fsdp", None),
        P("fsdp", None),
        P("fsdp", None),
        P("fsdp", None),
        P("fsdp", None),
        P("fsdp", None),
        P("fsdp", None),
        P("fsdp", None),
        P(None, "fsdp"),
        P(None, "fsdp"),
        P(None, "fsdp"),
    )
    own_plan = dict(mesh.shape) == {"fsdp": 16, "dp": 2}
    return jax.shard_map(
        per_device_links if own_plan else per_device, mesh=mesh, in_specs=in_specs, out_specs=out_specs, check_vma=False
    )
```

```python
import jax
import jax.numpy as jnp
from jax import lax
from jax.experimental import pallas as pl
from jax.experimental.pallas import tpu as pltpu
from jax.sharding import PartitionSpec as P

MODEL_WIDTH = 768
H = 12
HD = 64
SEG_ROW = 32


largest_value = lax.Precision.HIGHEST
beta_one = 0.9
beta_two = 0.999
adam_eps = 1e-12
decay_rate = 0.01
rate_matrix = 0.1
rate_embed = 1.0
rate_norm = 1.0
clip_norm = 0.001
norm_eps = 1e-05
unit_eps = 1e-06


def layer_norm(inputs, gain_row, shifts):
    center = inputs - jnp.mean(inputs, -1, keepdims=True)
    inv_std = lax.rsqrt(jnp.mean(center * center, -1, keepdims=True) + norm_eps)
    normed = center * inv_std
    return (normed * gain_row + shifts, normed, inv_std)


def norm_back(upstream, normed, inv_std, gain_row):
    scaled = upstream * gain_row
    grad_in = inv_std * (
        scaled
        - jnp.mean(scaled, -1, keepdims=True)
        - normed * jnp.mean(scaled * normed, -1, keepdims=True)
    )
    return (grad_in, jnp.sum(upstream * normed, 0), jnp.sum(upstream, 0))


def masked_scores(query_rows, key_rows, segment_rows):
    raw_scores = jnp.einsum(
        "bqhd,bkhd->bhqk", query_rows, key_rows, preferred_element_type=jnp.float32
    )
    same_segment = segment_rows[:, None, :, None] == segment_rows[:, None, None, :]
    return jnp.where(same_segment, raw_scores * HD ** (-0.5), -1e30)


def layer_forward(gathered, token_rows, segment_rows):
    (
        lexicon_table,
        query_key_value_maps,
        attention_exit_map,
        widening_matrix_in,
        narrowing_matrix_out,
        layernorm_scale_bias,
    ) = gathered
    batch_row_list, sequence_length = token_rows.shape
    embedded = jnp.take(lexicon_table, token_rows.reshape(-1), axis=0)
    qkv_all = jnp.dot(embedded, query_key_value_maps, preferred_element_type=jnp.float32).astype(
        jnp.bfloat16
    )
    qkv_all = qkv_all.reshape(batch_row_list, sequence_length, 3, H, HD)
    query_rows, key_rows, value_rows = (qkv_all[:, :, 0], qkv_all[:, :, 1], qkv_all[:, :, 2])
    scores = masked_scores(query_rows, key_rows, segment_rows)
    row_max = jnp.max(scores, -1, keepdims=True)
    log_total = row_max + jnp.log(jnp.sum(jnp.exp(scores - row_max), -1, keepdims=True))
    attn_probs = jnp.exp(scores - log_total).astype(jnp.bfloat16)
    mixed_heads = jnp.einsum(
        "bhqk,bkhd->bqhd", attn_probs, value_rows, preferred_element_type=jnp.float32
    )
    mixed_heads = mixed_heads.reshape(batch_row_list * sequence_length, MODEL_WIDTH).astype(
        jnp.bfloat16
    )
    attended = jnp.dot(mixed_heads, attention_exit_map, preferred_element_type=jnp.float32)
    normed_one, unit_one, inv_one = layer_norm(
        embedded.astype(jnp.float32) + attended, layernorm_scale_bias[0], layernorm_scale_bias[1]
    )
    normed_low = normed_one.astype(jnp.bfloat16)
    up_proj = jnp.dot(normed_low, widening_matrix_in, preferred_element_type=jnp.float32)
    activated = jax.nn.gelu(up_proj, approximate=False).astype(jnp.bfloat16)
    ffn_result = jnp.dot(activated, narrowing_matrix_out, preferred_element_type=jnp.float32)
    second_normalized, unit_two, inv_two = layer_norm(
        normed_one + ffn_result, layernorm_scale_bias[2], layernorm_scale_bias[3]
    )
    group_member = (
        segment_rows[:, None, :] == jnp.arange(SEG_ROW, dtype=jnp.int32)[None, :, None]
    ).astype(jnp.float32)
    pooled_state = jnp.einsum(
        "nkz,nzh->nkh",
        group_member,
        second_normalized.reshape(batch_row_list, sequence_length, MODEL_WIDTH),
        precision=largest_value,
    )
    saved_state = (
        embedded,
        query_rows,
        key_rows,
        value_rows,
        log_total,
        mixed_heads,
        unit_one,
        inv_one,
        normed_low,
        up_proj,
        activated,
        unit_two,
        inv_two,
        group_member,
    )
    return (pooled_state.reshape(batch_row_list * SEG_ROW, MODEL_WIDTH), saved_state)


def layer_backward(gathered, saved_state, token_rows, segment_rows, pooled_gradient):
    (
        lexicon_table,
        query_key_value_maps,
        attention_exit_map,
        widening_matrix_in,
        narrowing_matrix_out,
        layernorm_scale_bias,
    ) = gathered
    (
        embedded,
        query_rows,
        key_rows,
        value_rows,
        log_total,
        mixed_heads,
        unit_one,
        inv_one,
        normed_low,
        up_proj,
        activated,
        unit_two,
        inv_two,
        group_member,
    ) = saved_state
    batch_row_list, sequence_length = token_rows.shape
    pooled_gradient = pooled_gradient.reshape(batch_row_list, SEG_ROW, MODEL_WIDTH)
    second_gradient = jnp.einsum(
        "got,goy->gty", group_member, pooled_gradient, precision=largest_value
    ).reshape(batch_row_list * sequence_length, MODEL_WIDTH)
    grad_resid_two, grad_gain_two, grad_shift_two = norm_back(
        second_gradient, unit_two, inv_two, layernorm_scale_bias[2]
    )
    grad_result = grad_resid_two.astype(jnp.bfloat16)
    grad_ffn_down = jnp.einsum(
        "nf,nd->fd", activated, grad_result, preferred_element_type=jnp.float32
    )
    grad_act = jnp.einsum(
        "nd,fd->nf", grad_result, narrowing_matrix_out, preferred_element_type=jnp.float32
    )
    gelu_value, gelu_pull = jax.vjp(
        lambda pre_act: jax.nn.gelu(pre_act, approximate=False), up_proj
    )
    grad_up = gelu_pull(grad_act)[0].astype(jnp.bfloat16)
    grad_ffn_up = jnp.einsum("nd,nf->df", normed_low, grad_up, preferred_element_type=jnp.float32)
    grad_one = grad_resid_two + jnp.einsum(
        "nf,df->nd", grad_up, widening_matrix_in, preferred_element_type=jnp.float32
    )
    grad_resid_one, grad_gain_one, grad_shift_one = norm_back(
        grad_one, unit_one, inv_one, layernorm_scale_bias[0]
    )
    grad_attended = grad_resid_one.astype(jnp.bfloat16)
    grad_project_out = jnp.einsum(
        "nc,nd->cd", mixed_heads, grad_attended, preferred_element_type=jnp.float32
    )
    grad_mixed = jnp.einsum(
        "nd,cd->nc", grad_attended, attention_exit_map, preferred_element_type=jnp.float32
    )
    grad_mixed = grad_mixed.astype(jnp.bfloat16).reshape(batch_row_list, sequence_length, H, HD)
    scores = masked_scores(query_rows, key_rows, segment_rows)
    attn_probs = jnp.exp(scores - log_total)
    probs_low = attn_probs.astype(jnp.bfloat16)
    grad_values = jnp.einsum(
        "bhqk,bqhd->bkhd", probs_low, grad_mixed, preferred_element_type=jnp.float32
    )
    grad_probs = jnp.einsum(
        "bqhd,bkhd->bhqk", grad_mixed, value_rows, preferred_element_type=jnp.float32
    )
    grad_scores = attn_probs * (grad_probs - jnp.sum(grad_probs * attn_probs, -1, keepdims=True))
    grad_scores = grad_scores.astype(jnp.bfloat16)
    grad_query = jnp.einsum(
        "bhqk,bkhd->bqhd", grad_scores, key_rows, preferred_element_type=jnp.float32
    ) * HD ** (-0.5)
    grad_keys = jnp.einsum(
        "bhqk,bqhd->bkhd", grad_scores, query_rows, preferred_element_type=jnp.float32
    ) * HD ** (-0.5)
    grad_qkv = (
        jnp.stack([grad_query, grad_keys, grad_values], 2)
        .reshape(batch_row_list * sequence_length, 3 * MODEL_WIDTH)
        .astype(jnp.bfloat16)
    )
    grad_project_in = jnp.einsum(
        "nd,nc->dc", embedded, grad_qkv, preferred_element_type=jnp.float32
    )
    grad_embedded = grad_resid_one + jnp.einsum(
        "nc,dc->nd", grad_qkv, query_key_value_maps, preferred_element_type=jnp.float32
    )
    grad_norms = jnp.stack([grad_gain_one, grad_shift_one, grad_gain_two, grad_shift_two])
    return (
        grad_embedded,
        grad_project_in,
        grad_project_out,
        grad_ffn_up,
        grad_ffn_down,
        grad_norms,
    )


def adam_update(weight, first, second, grad, fix_first, fix_second, rate, decay):
    first_new = beta_one * first + (1.0 - beta_one) * grad
    second_new = beta_two * second + (1.0 - beta_two) * grad * grad
    step_size = first_new / fix_first / (jnp.sqrt(second_new / fix_second) + adam_eps)
    return (weight - rate * (step_size + decay * weight), first_new, second_new)


def per_device(
    kmer_identifiers,
    slot_fragment_ids,
    mirror_fragment_index,
    fragment_weight,
    affinity_heat,
    optimizer_iteration,
    lexicon_table,
    lexicon_first_moment,
    lexicon_raw_moment,
    query_key_value_maps,
    qkv_first_moment,
    qkv_raw_moment,
    attention_exit_map,
    exit_first_moment,
    exit_raw_moment,
    widening_matrix_in,
    widening_first_moment,
    widening_raw_moment,
    narrowing_matrix_out,
    narrowing_first_moment,
    narrowing_raw_moment,
    layernorm_scale_bias,
    layernorm_first_moment,
    layernorm_raw_moment,
):
    masters = (
        lexicon_table,
        query_key_value_maps,
        attention_exit_map,
        widening_matrix_in,
        narrowing_matrix_out,
        layernorm_scale_bias,
    )
    firsts = (
        lexicon_first_moment,
        qkv_first_moment,
        exit_first_moment,
        widening_first_moment,
        narrowing_first_moment,
        layernorm_first_moment,
    )
    seconds = (
        lexicon_raw_moment,
        qkv_raw_moment,
        exit_raw_moment,
        widening_raw_moment,
        narrowing_raw_moment,
        layernorm_raw_moment,
    )
    rates = (rate_embed, rate_matrix, rate_matrix, rate_matrix, rate_matrix, rate_norm)
    decays = (decay_rate, decay_rate, decay_rate, decay_rate, decay_rate, 0.0)
    lowered = tuple((piece.astype(jnp.bfloat16) for piece in masters))
    gathered = (
        lax.all_gather(lowered[0], "fsdp", axis=1, tiled=True),
        lax.all_gather(lowered[1], "fsdp", axis=0, tiled=True),
        lax.all_gather(lowered[2], "fsdp", axis=0, tiled=True),
        lax.all_gather(lowered[3], "fsdp", axis=0, tiled=True),
        lax.all_gather(lowered[4], "fsdp", axis=0, tiled=True),
        lax.all_gather(lowered[5], "fsdp", axis=1, tiled=True),
    )
    pooled_state, saved_state = layer_forward(gathered, kmer_identifiers, slot_fragment_ids)
    unit_scale = lax.rsqrt(jnp.sum(pooled_state * pooled_state, -1, keepdims=True) + unit_eps)
    unit_rows = pooled_state * unit_scale
    unit_low = unit_rows.astype(jnp.bfloat16)
    every_unit = lax.all_gather(unit_low, ("fsdp", "dp"), axis=0, tiled=True)
    cosine_affinity_grid = jnp.einsum(
        "sd,td->st", unit_low, every_unit, preferred_element_type=jnp.float32
    )
    seg_local = pooled_state.shape[0]
    fragment_tally = every_unit.shape[0]
    shard_fragment_lines = lax.axis_index(("fsdp", "dp")) * seg_local + jnp.arange(
        seg_local, dtype=jnp.int32
    )
    field_sequence_array = jnp.arange(fragment_tally, dtype=jnp.int32)
    raw_affinity_values = jnp.where(
        shard_fragment_lines[:, None] == field_sequence_array[None, :],
        -1e30,
        cosine_affinity_grid / affinity_heat,
    )
    row_max = jnp.max(raw_affinity_values, -1, keepdims=True)
    log_total = row_max[:, 0] + jnp.log(jnp.sum(jnp.exp(raw_affinity_values - row_max), -1))
    chosen = mirror_fragment_index[:, None] == field_sequence_array[None, :]
    chosen_real_entry = chosen.astype(jnp.float32)
    target = jnp.sum(jnp.where(chosen, raw_affinity_values, 0.0), -1)
    contrast_objective = (
        lax.psum(jnp.sum(fragment_weight * (log_total - target)), ("fsdp", "dp")) / fragment_tally
    )
    exponent_probabilities = jnp.exp(raw_affinity_values - log_total[:, None])
    similarity_gradient = (
        (exponent_probabilities - chosen_real_entry)
        * fragment_weight[:, None]
        / (fragment_tally * affinity_heat)
    ).astype(jnp.bfloat16)
    grad_rows = jnp.dot(similarity_gradient, every_unit, preferred_element_type=jnp.float32)
    column_terms = jnp.einsum(
        "st,sd->td", similarity_gradient, unit_low, preferred_element_type=jnp.float32
    )
    grad_cols = lax.psum_scatter(column_terms, ("fsdp", "dp"), scatter_dimension=0, tiled=True)
    grad_unit = grad_rows + grad_cols
    pooled_gradient = unit_scale * (
        grad_unit - unit_rows * jnp.sum(grad_unit * unit_rows, -1, keepdims=True)
    )
    again = (
        lax.all_gather(lowered[0], "fsdp", axis=1, tiled=True),
        lax.all_gather(lowered[1], "fsdp", axis=0, tiled=True),
        lax.all_gather(lowered[2], "fsdp", axis=0, tiled=True),
        lax.all_gather(lowered[3], "fsdp", axis=0, tiled=True),
        lax.all_gather(lowered[4], "fsdp", axis=0, tiled=True),
        lax.all_gather(lowered[5], "fsdp", axis=1, tiled=True),
    )
    grads = layer_backward(again, saved_state, kmer_identifiers, slot_fragment_ids, pooled_gradient)
    vocab = lexicon_table.shape[0]
    rest = (
        lax.psum_scatter(grads[1], "fsdp", scatter_dimension=0, tiled=True),
        lax.psum_scatter(grads[2], "fsdp", scatter_dimension=0, tiled=True),
        lax.psum_scatter(grads[3], "fsdp", scatter_dimension=0, tiled=True),
        lax.psum_scatter(grads[4], "fsdp", scatter_dimension=0, tiled=True),
        lax.psum_scatter(grads[5], "fsdp", scatter_dimension=1, tiled=True),
    )
    column_rows = lax.all_to_all(
        grads[0].astype(jnp.bfloat16), "fsdp", split_axis=1, concat_axis=0, tiled=True
    ).astype(jnp.float32)
    all_tokens = lax.all_gather(kmer_identifiers.reshape(-1), "fsdp", axis=0, tiled=True)
    table_shard = jax.ops.segment_sum(column_rows, all_tokens, num_segments=vocab)
    shards = (table_shard, rest[0], rest[1], rest[2], rest[3], rest[4])
    shards = (
        lax.psum(shards[0].astype(jnp.bfloat16), "dp").astype(jnp.float32),
        lax.psum(shards[1].astype(jnp.bfloat16), "dp").astype(jnp.float32),
        lax.psum(shards[2].astype(jnp.bfloat16), "dp").astype(jnp.float32),
        lax.psum(shards[3].astype(jnp.bfloat16), "dp").astype(jnp.float32),
        lax.psum(shards[4].astype(jnp.bfloat16), "dp").astype(jnp.float32),
        lax.psum(shards[5].astype(jnp.bfloat16), "dp").astype(jnp.float32),
    )
    squares = sum((jnp.sum(piece * piece) for piece in shards))
    grad_norm = jnp.sqrt(lax.psum(squares, "fsdp"))
    factor = clip_norm / jnp.maximum(grad_norm, clip_norm)
    count_now = optimizer_iteration.astype(jnp.float32)
    fix_first = 1.0 - jnp.power(beta_one, count_now)
    fix_second = 1.0 - jnp.power(beta_two, count_now)
    updated = [
        adam_update(
            masters[number],
            firsts[number],
            seconds[number],
            shards[number] * factor,
            fix_first,
            fix_second,
            rates[number],
            decays[number],
        )
        for number in range(6)
    ]
    return (
        contrast_objective,
        grad_norm,
        updated[0][0],
        updated[0][1],
        updated[0][2],
        updated[1][0],
        updated[1][1],
        updated[1][2],
        updated[2][0],
        updated[2][1],
        updated[2][2],
        updated[3][0],
        updated[3][1],
        updated[3][2],
        updated[4][0],
        updated[4][1],
        updated[4][2],
        updated[5][0],
        updated[5][1],
        updated[5][2],
    )


AXES = ("fsdp", "dp")
VOCAB_PAD = 4352
VOCAB_HALF = VOCAB_PAD // 2
BIG_VMEM = pltpu.CompilerParams(vmem_limit_bytes=60 * 1024 * 1024)
bf16 = jnp.bfloat16
f32 = jnp.float32


def pairs_of(moved):
    spots = [(z, y, x, c) for z in range(4) for y in range(2) for x in range(2) for c in range(2)]

    def linear(spot):
        z, y, x, c = spot
        return ((z * 2 + y) * 2 + x) * 2 + c

    return [(linear(spot), linear(moved(*spot))) for spot in spots]


FIRST = pairs_of(lambda z, y, x, c: (z, y, x ^ 1, c) if c == 0 else (z, y ^ 1, x, c))
SECOND = pairs_of(lambda z, y, x, c: (z, y ^ 1, x, c) if c == 0 else (z, y, x ^ 1, c))
BOTH = pairs_of(lambda z, y, x, c: (z, y ^ 1, x ^ 1, c))
CORE = pairs_of(lambda z, y, x, c: (z, y, x, 1 - c))
ZS = [None] + [pairs_of(lambda z, y, x, c, j=j: (z ^ j, y, x, c)) for j in (1, 2, 3)]


def send(array, pairs):
    return lax.ppermute(array, AXES, pairs)


def after(array, *others):
    return lax.optimization_barrier((array,) + others)[0]


def together(arrays, *others):
    arrays = list(arrays)
    return list(lax.optimization_barrier((*arrays, *others)))[: len(arrays)]


class Place:
    def __init__(self):
        f = lax.axis_index("fsdp")
        self.core = lax.axis_index("dp")
        self.z, self.y, self.x = f // 4, (f // 2) % 2, f % 2

    def plane_slot(self, core, a, b):
        dy = jnp.where(core == 0, b, a)
        dx = jnp.where(core == 0, a, b)
        return (self.y ^ dy) * 2 + (self.x ^ dx)

    def chip(self, core, j, a, b):
        return (self.z ^ j) * 4 + self.plane_slot(core, a, b)


def z_sends(piece):
    return [piece] + [send(piece, ZS[j]) for j in (1, 2, 3)]


def z_column(piece):
    return jnp.stack(z_sends(piece))


def plane_sends(column, direct=False, gate=()):
    one = send(column, FIRST)
    two = send(column, SECOND)
    three = send(column, BOTH) if direct else send(after(one, *gate), SECOND)
    return [column, one, two, three]


def both_cores(mine):
    return mine + [send(block, CORE) for block in mine]


Z_ROWS, BY_FLIP, FRAGMENTS, BY_PAIR, SLOTS, LOOKUP, PLANE = 0, 4, 68, 102, 166, 182, 191
MY_CORE = FRAGMENTS + 33


def index_vector(place):
    core, other = place.core, 1 - place.core
    n = jnp.arange(32, dtype=jnp.int32)
    who, m = jnp.where(n < 16, core, other), n % 16
    chips = place.chip(who, m % 4, (m // 4) % 2, m // 8)
    pairs = place.chip(who, (m // 2) % 4, m % 2, m // 8)
    base = (lax.axis_index("fsdp") * 2 + core) * 32
    k = jnp.arange(7, dtype=jnp.int32)
    side, flips = jnp.where(k < 4, core, other), jnp.where(k < 4, k, k - 3)
    reached = place.plane_slot(side, flips % 2, flips // 2)
    parts = [
        (place.z ^ jnp.arange(4, dtype=jnp.int32)) * 192,
        who,
        chips * 48,
        base,
        (chips * 2 + who) * 32,
        core,
        who,
        pairs * 192,
        chips[:16],
        reached * 48,
        core * VOCAB_HALF,
        other * VOCAB_HALF,
        core * VOCAB_HALF,
        reached[:4] * 48,
    ]
    return jnp.concatenate([jnp.atleast_1d(p).astype(jnp.int32) for p in parts])


class Part:
    def __init__(self, ref, start):
        self.ref, self.start = ref, start

    def __getitem__(self, number):
        return self.ref[self.start + number]


def scatter_add(keep, came):
    return (keep[4:].astype(f32) + came[4:].astype(f32)).astype(bf16)


def scatter_here(keep, came, came_two):
    here = [
        keep[j].astype(f32) + came[j].astype(f32) + came_two[j].astype(f32) for j in range(4)
    ]
    return here[0], [h.astype(bf16) for h in here[1:]]


def line_sends(far):
    return [send(h, ZS[j]) for h, j in zip(far, (1, 2, 3))]


def line_sum(here, far):
    return (here + far[0].astype(f32) + far[1].astype(f32) + far[2].astype(f32)).astype(bf16)


def whole_copies(sources, targets, sems):
    return [
        pltpu.make_async_copy(source, target, sems.at[number])
        for number, (source, target) in enumerate(zip(sources, targets))
    ]


class Stage:
    def __init__(self, copies_in, copies_out, pairs, sems):
        self.copies_in, self.copies_out = dict(enumerate(copies_in)), dict(enumerate(copies_out))
        self.started, self.pairs, self.sems = [], pairs, sems

    def __call__(self, *which):
        for number in which or tuple(self.copies_in):
            self.copies_in.pop(number).wait()

    def put(self, *which):
        for number in which or tuple(self.copies_out):
            copy = self.copies_out.pop(number)
            copy.start()
            self.started.append(copy)

    def put_half(self, side, half, which, width):
        cols = pl.ds(pl.multiple_of(half * width, 128), width)
        for number in which:
            self.copies_out.pop(number, None)
            source, target = self.pairs[number]
            copy = pltpu.make_async_copy(
                source.at[:, cols], target.at[:, cols], self.sems.at[side * len(which) + number]
            )
            copy.start()
            self.started.append(copy)

    def finish(self):
        self.put(*tuple(self.copies_out))
        for copy in self.started:
            copy.wait()


def staged_call(body, scalars, arrays, pieces, shapes, scratch, cost, late=(), staged_out=True):
    n_s, n_a, n_p, n_o = len(scalars), len(arrays), len(pieces), len(shapes)

    def kernel(*refs):
        smem, refs = [Part(r, s) for r, (_, s) in zip(refs, scalars)], refs[n_s:]
        hbm, refs = refs[:n_a], refs[n_a:]
        far, refs = refs[:n_p], refs[n_p:]
        out, refs = refs[:n_o], refs[n_o:]
        near_in, refs = refs[:n_a], refs[n_a:]
        if staged_out:
            near_out, refs = refs[:n_o], refs[n_o:]
        else:
            near_out, out = out, []
        in_sems, out_sems, half_sems, refs = refs[0], refs[1], refs[2], refs[3:]
        copies = whole_copies(hbm, near_in, in_sems)
        for number, copy in enumerate(copies):
            if number not in late:
                copy.start()
        pairs = list(zip(near_out, out))
        stage = Stage(copies, whole_copies(near_out, out, out_sems), pairs, half_sems)
        body(stage, *smem, *near_in, *far, *near_out, *refs)
        stage.finish()

    in_hbm = pl.BlockSpec(memory_space=pltpu.HBM)
    return pl.pallas_call(
        kernel,
        out_shape=shapes,
        in_specs=[pl.BlockSpec(memory_space=pltpu.SMEM)] * n_s + [in_hbm] * (n_a + n_p),
        out_specs=[in_hbm] * n_o,
        scratch_shapes=[pltpu.VMEM(a.shape, a.dtype) for a in arrays]
        + [pltpu.VMEM(s.shape, s.dtype) for s in shapes if staged_out]
        + [pltpu.SemaphoreType.DMA((n,)) for n in (n_a, n_o, 4)]
        + scratch,
        cost_estimate=pl.CostEstimate(flops=int(cost * 1e9), bytes_accessed=0, transcendentals=0),
        compiler_params=BIG_VMEM,
    )(*[vector for vector, _ in scalars], *arrays, *pieces)


def shaped(dtype, *dims):
    return jax.ShapeDtypeStruct(dims, dtype)


def one_hot(ids_row, start, count):
    spots = lax.broadcasted_iota(jnp.int32, (count, ids_row.shape[1]), 0) + start
    return jnp.where(spots == ids_row, 1.0, 0.0).astype(bf16)


def prepare_kernel(
    ready, table_ref, in_ref, out_ref, up_ref, down_ref, norm_ref, ids_ref, weight_ref,
    both_ref, cut_ref, half_ref, down_half_ref,
):
    core = lax.axis_index("dp")

    def mine(ref, width, start=0):
        return ref[:, pl.ds(pl.multiple_of(start + core * width, 128), width)].astype(bf16)

    ready(1, 2, 3, 5, 6, 7)
    for t in range(3):
        both_ref[:, t * 384 : (t + 1) * 384] = mine(in_ref, 384, t * 768)
    both_ref[:, 1152:1536] = mine(out_ref, 384)
    rest = jnp.zeros((1, 16), f32)
    heavy = [jnp.concatenate([w.astype(f32), rest], 1) for w in thirds(weight_ref[...])]
    extra = jnp.concatenate([norm_ref[...]] + heavy + [jnp.zeros((121, 48), f32)], 0)
    both_ref[:, 1536:1664] = extra.T.astype(bf16)
    both_ref[:, 1664:3200] = mine(up_ref, 1536)
    ids = jnp.concatenate([ids_ref[:, k * 128 : (k + 1) * 128] for k in range(4)], 0)
    high = lax.shift_right_logical(ids, 6)
    ids = jnp.concatenate([high, ids - high * 64], 0).astype(f32).astype(bf16)
    both_ref[:, 3200:3328] = jnp.concatenate([ids, jnp.zeros((40, 128), bf16)], 0)
    ready.put(0)
    ready(0, 4)
    vocab = table_ref.shape[1]
    even = vocab - vocab % 128
    cut_ref[:, :even] = table_ref[:, :even].astype(bf16)
    last = [table_ref[:, even:], jnp.zeros((48, VOCAB_PAD - vocab), f32)]
    cut_ref[:, even:] = jnp.concatenate(last, 1).astype(bf16)
    half_ref[...] = cut_ref[:, pl.ds(pl.multiple_of(core * VOCAB_HALF, 128), VOCAB_HALF)]
    down_half_ref[...] = mine(down_ref, 384)


def prepare(arrays):
    return staged_call(
        prepare_kernel,
        [],
        arrays,
        [],
        [
            shaped(bf16, 48, 3328),
            shaped(bf16, 48, VOCAB_PAD),
            shaped(bf16, 48, VOCAB_HALF),
            shaped(bf16, 192, 384),
        ],
        [],
        3,
    )


def id_row(ids_ref, j):
    rows = ids_ref[j]
    return jnp.concatenate([rows[k : k + 1] for k in range(4)], 1)


def lookup_kernel(ready, idx_ref, ids_ref, down_ref, down_first_ref, *refs):
    ins = list(refs[:4]) + [refs[4].at[k] for k in range(3)]
    outs, table, sems = refs[5:9], refs[9], refs[10]
    copies = [
        pltpu.make_async_copy(
            ins[0], table.at[pl.ds(pl.multiple_of(idx_ref[0], 16), 48), :], sems.at[0]
        )
    ]
    for number in range(1, 7):
        column = pl.multiple_of(idx_ref[7 + (number - 1) // 3], 128)
        row = pl.multiple_of(idx_ref[number], 16)
        copies.append(
            pltpu.make_async_copy(
                ins[number],
                table.at[pl.ds(row, 48), pl.ds(column, VOCAB_HALF)],
                sems.at[number],
            )
        )
    for copy in copies:
        copy.start()
    ready()
    for copy in copies:
        copy.wait()
    for j in range(4):
        total = jnp.zeros((192, 512), f32)
        for k in range(VOCAB_PAD // 256):
            total += jnp.dot(
                table[:, k * 256 : (k + 1) * 256],
                one_hot(id_row(ids_ref, j), k * 256, 256),
                preferred_element_type=f32,
            )
        outs[j][:, :512] = total.astype(bf16)
    outs[1][:, 512:896] = down_ref[...]
    outs[1][:, 896:] = down_first_ref[...]


def lookup(index, ids_z, down_pair, arrays):
    return staged_call(
        lookup_kernel,
        [(index, LOOKUP)],
        [ids_z, *down_pair],
        arrays,
        [
            shaped(bf16, 192, 512),
            shaped(bf16, 192, 1280),
            shaped(bf16, 192, 512),
            shaped(bf16, 192, 512),
        ],
        [
            pltpu.VMEM((192, VOCAB_PAD), bf16),
            pltpu.SemaphoreType.DMA((7,)),
        ],
        6,
    )


def token_sum_kernel(
    ready, idx_ref, ids_ref, other_ids_ref, mine_ref, other_ref, keep_ref, away_ref, whole_ref, sems
):
    ready()
    start = idx_ref[0]
    for low in range(0, VOCAB_HALF, 256):
        count = min(256, VOCAB_HALF - low)
        total = jnp.zeros((192, count), f32)
        for ids, block in ((ids_ref, mine_ref), (other_ids_ref, other_ref)):
            for j in range(4):
                total += lax.dot_general(
                    block[j],
                    one_hot(id_row(ids, j), start + low, count),
                    (((1,), (1,)), ((), ())),
                    preferred_element_type=f32,
                )
        whole_ref[:, low : low + count] = total.astype(bf16)
    copies = []
    for k in range(4):
        rows = pl.ds(pl.multiple_of(idx_ref[1 + k], 16), 48)
        ref = keep_ref if k < 2 else away_ref
        copies.append(pltpu.make_async_copy(whole_ref.at[rows, :], ref.at[k % 2], sems.at[k]))
    for copy in copies[::-1]:
        copy.start()
    for copy in copies:
        copy.wait()


def token_sum(index, ids_z, other_ids, mine, other):
    return staged_call(
        token_sum_kernel,
        [(index, PLANE)],
        [ids_z, other_ids, mine, other],
        [],
        [
            shaped(bf16, 2, 48, VOCAB_HALF),
            shaped(bf16, 2, 48, VOCAB_HALF),
        ],
        [
            pltpu.VMEM((192, VOCAB_HALF), bf16),
            pltpu.SemaphoreType.DMA((4,)),
        ],
        8,
        staged_out=False,
    )


def my_half(array, core, width):
    return lax.dynamic_slice_in_dim(array, core * width, width, axis=1)


def all_sum(value):
    for pairs in (ZS[1:], [FIRST, SECOND, BOTH]):
        one, two, three = (send(value, p) for p in pairs)
        value = (value + one) + (two + three)
    return value


WINDOWS = (0, 64, 192, 256)
SCALE = HD ** (-0.5)


def piece_copies(idx_ref, base, pieces, target, rows, sems, first_sem):
    copies = []
    for number in range(32):
        half = idx_ref[base + number]
        row = pl.multiple_of(idx_ref[base + 32 + number], 16)
        each = 32 // len(pieces)
        source = pieces[number // each].at[number % each]
        copies.append(
            pltpu.make_async_copy(
                source, target.at[half, pl.ds(row, rows), :], sems.at[first_sem + number]
            )
        )
    return copies


def window_bias(seg_row, seg_col, b):
    w = WINDOWS[b]
    same = seg_col[b * 128 : (b + 1) * 128, :] == seg_row[:, w : w + 256]
    bias = jnp.where(same, 0.0, -1e30)
    return jnp.concatenate([bias, bias], 0)


def two_heads(block):
    left = lax.broadcasted_iota(jnp.int32, block.shape, 1) < HD
    none = jnp.zeros_like(block)
    return jnp.concatenate([jnp.where(left, block, none), jnp.where(left, none, block)], 0)


def nt_dot(a, b):
    return lax.dot_general(a, b, (((1,), (1,)), ((), ())), preferred_element_type=f32)


def tn_dot(a, b):
    return lax.dot_general(a, b, (((0,), (0,)), ((), ())), preferred_element_type=f32)


def nn_dot(a, b):
    return jnp.dot(a, b, preferred_element_type=f32)


def row_norm(v):
    center = v - jnp.mean(v, -1, keepdims=True)
    inv = lax.rsqrt(jnp.mean(center * center, -1, keepdims=True) + norm_eps)
    return center * inv, inv


def attention_kernel(ready, idx_ref, seg_row_ref, seg_col_ref, *refs):
    e_in, pieces = refs[:4], refs[4:12]
    (e_ref, qkv_ref, lse_ref, mixed_ref, unit_ref, inv_ref, low_ref, par_ref, side_ref) = refs[12:21]
    et_ref, w_ref, bias_ref, attended_ref, sems = refs[21:]
    e_copies = [
        pltpu.make_async_copy(
            e_in[j].at[:, pl.ds(0, 512)],
            et_ref.at[pl.ds(pl.multiple_of(idx_ref[j], 16), 192), :],
            sems.at[j],
        )
        for j in range(4)
    ]
    w_copies = piece_copies(idx_ref, 4, pieces, w_ref, 48, sems, 4)
    for copy in e_copies + w_copies:
        copy.start()
    ready()
    for b in range(4):
        bias_ref[b] = window_bias(seg_row_ref[...], seg_col_ref[...], b)
    for copy in e_copies:
        copy.wait()
    e_ref[...] = et_ref[...].T
    ready.put(0)
    for copy in w_copies:
        copy.wait()
    par_ref[...] = w_ref[0, :, 1536:1664].T.astype(f32)[:8]
    side_ref[...] = w_ref[:, :, 1536:1664]
    for k in range(2):
        for t in range(3):
            part = nn_dot(e_ref[...], w_ref[k, :, t * 384 : (t + 1) * 384])
            if t == 0:
                part = part.astype(bf16).astype(f32) * SCALE
            part = part.astype(bf16)
            for i in range(3):
                qkv_ref[t * 6 + k * 3 + i] = part[:, i * 128 : (i + 1) * 128]
    ready.put(1, 7, 8)
    lse_ref[...] = jnp.zeros_like(lse_ref)
    lane = lax.broadcasted_iota(jnp.int32, (128, 128), 1)
    left = lane < HD

    @pl.loop(0, 6, unroll=3)
    def _(pair):
        for b in range(4):
            rows = pl.ds(b * 128, 128)
            keys = pl.ds(WINDOWS[b], 256)
            q = qkv_ref[pair, rows, :]
            k = qkv_ref[pair + 6, keys, :]
            v = qkv_ref[pair + 12, keys, :]
            s = nt_dot(two_heads(q), k) + bias_ref[b]
            top = jnp.max(s, -1, keepdims=True)
            e = jnp.exp(s - top)
            total = jnp.sum(e, -1, keepdims=True)
            log = top + jnp.log(total)
            lse = jnp.where(lane == pair * 2, log[:128], lse_ref[rows, :])
            lse_ref[rows, :] = jnp.where(lane == pair * 2 + 1, log[128:], lse)
            mixed = nn_dot((e * (1.0 / total)).astype(bf16), v)
            cols = pl.ds(pl.multiple_of(pair * 128, 128), 128)
            mixed_ref[rows, cols] = jnp.where(left, mixed[:128], mixed[128:]).astype(bf16)

    ready.put(2, 3)
    for k in range(2):
        attended_ref[:, k * 384 : (k + 1) * 384] = nn_dot(mixed_ref[...], w_ref[k, :, 1152:1536])
    for b in range(4):
        rows = slice(b * 128, (b + 1) * 128)
        unit, inv = row_norm(e_ref[rows, :].astype(f32) + attended_ref[rows, :])
        unit_ref[rows, :] = unit
        inv_ref[rows, :] = jnp.broadcast_to(inv, (128, 128))
        low_ref[rows, :] = (unit * par_ref[0:1, :] + par_ref[1:2, :]).astype(bf16)


def attention_forward(index, seg_row, seg_col, columns, pieces):
    return staged_call(
        attention_kernel,
        [(index, Z_ROWS)],
        [seg_row, seg_col],
        [*columns, *pieces],
        [
            shaped(bf16, 512, 768),
            shaped(bf16, 18, 512, 128),
            shaped(f32, 512, 128),
            shaped(bf16, 512, 768),
            shaped(f32, 512, 768),
            shaped(f32, 512, 128),
            shaped(bf16, 512, 768),
            shaped(f32, 8, 768),
            shaped(bf16, 2, 768, 128),
        ],
        [
            pltpu.VMEM((768, 512), bf16),
            pltpu.VMEM((2, 768, 1664), bf16),
            pltpu.VMEM((4, 256, 256), f32),
            pltpu.VMEM((512, 768), f32),
            pltpu.SemaphoreType.DMA((36,)),
        ],
        17,
    )


def gelu_and_slope(u):
    bell = jnp.exp(-0.5 * u * u)
    base = 1.0 + (0.3275911 * 0.5**0.5) * jnp.abs(u)
    t = pl.reciprocal(base, approx=True)
    t = t * (2.0 - base * t)
    poly = -0.07032334059476852
    for factor in (
        0.24725385010242462,
        -0.2008872926235199,
        0.2245105654001236,
        0.013965459540486336,
        0.10251718759536743,
        0.09044301509857178,
        0.09252061694860458,
    ):
        poly = factor + t * poly
    tail = (t * poly) * bell
    phi = jnp.where(u < 0, tail, 1.0 - tail)
    return u * phi, phi + (u * 0.3989422804014327) * bell


def up_kernel(ready, idx_ref, low_ref, *refs):
    pieces, act_ref, slope_ref, w_ref, sems = refs[:8], refs[8], refs[9], refs[10], refs[11]
    copies = piece_copies(idx_ref, 0, pieces, w_ref, 48, sems, 0)
    for copy in copies:
        copy.start()
    ready()
    core = idx_ref[0]
    for side in range(2):
        half = core if side == 0 else 1 - core
        for copy in copies[side * 16 : side * 16 + 16]:
            copy.wait()

        @pl.loop(0, 6, unroll=3)
        def _(n):
            cols = pl.ds(pl.multiple_of(n * 256, 256), 256)
            u = nn_dot(low_ref[...], w_ref[half, :, cols])
            value, slope = gelu_and_slope(u)
            out_cols = pl.ds(pl.multiple_of(half * 1536 + n * 256, 256), 256)
            act_ref[:, out_cols] = value.astype(bf16)
            slope_ref[:, out_cols] = slope.astype(bf16)

        ready.put_half(side, half, (0, 1), 1536)


def up_forward(index, low, pieces):
    return staged_call(
        up_kernel,
        [(index, BY_FLIP)],
        [low],
        pieces,
        [
            shaped(bf16, 512, 3072),
            shaped(bf16, 512, 3072),
        ],
        [
            pltpu.VMEM((2, 768, 1536), bf16),
            pltpu.SemaphoreType.DMA((32,)),
        ],
        18,
    )


def thirds(v):
    high = v.astype(bf16)
    rest = v - high.astype(f32)
    middle = rest.astype(bf16)
    return high, middle, (rest - middle.astype(f32)).astype(bf16)


def down_kernel(ready, idx_ref, seg_row_ref, act_ref, unit_one_ref, par_ref, *refs):
    unit_ref, inv_ref, frag_ref, frag_low_ref, size_ref, w_ref, result_ref, parts_ref, sems = refs[4:]
    copies = piece_copies(idx_ref, 0, refs[:4], w_ref, 192, sems, 0)
    for copy in copies:
        copy.start()
    ready()
    for copy in copies:
        copy.wait()
    for k in range(2):
        result_ref[:, k * 384 : (k + 1) * 384] = nn_dot(act_ref[...], w_ref[k])
    for b in range(4):
        rows = slice(b * 128, (b + 1) * 128)
        one = unit_one_ref[rows, :] * par_ref[0:1, :] + par_ref[1:2, :]
        unit, inv = row_norm(one + result_ref[rows, :])
        unit_ref[rows, :] = unit
        inv_ref[rows, :] = jnp.broadcast_to(inv, (128, 128))
        two = unit * par_ref[2:3, :] + par_ref[3:4, :]
        for number, part in enumerate(thirds(two)):
            parts_ref[number, rows, :] = part
    ready.put(0, 1)
    member = lax.broadcasted_iota(jnp.int32, (32, 512), 0) == seg_row_ref[...]
    member = jnp.where(member, 1.0, 0.0).astype(bf16)
    pooled = sum(nn_dot(member, parts_ref[number]) for number in range(3))
    size = lax.rsqrt(jnp.sum(pooled * pooled, -1, keepdims=True) + unit_eps)
    frag = pooled * size
    frag_ref[...] = frag
    frag_low_ref[...] = frag.astype(bf16)
    size_ref[...] = jnp.broadcast_to(size, (32, 128))


def down_forward(index, seg_row, act, unit_one, params, pieces):
    return staged_call(
        down_kernel,
        [(index, BY_PAIR)],
        [seg_row, act, unit_one, params],
        pieces,
        [
            shaped(f32, 512, 768),
            shaped(f32, 512, 128),
            shaped(f32, 32, 768),
            shaped(bf16, 32, 768),
            shaped(f32, 32, 128),
        ],
        [
            pltpu.VMEM((2, 3072, 384), bf16),
            pltpu.VMEM((512, 768), f32),
            pltpu.VMEM((3, 512, 768), bf16),
            pltpu.SemaphoreType.DMA((32,)),
        ],
        10,
    )


def back_norm(upstream, unit, inv, gain):
    scaled = upstream * gain
    return inv * (
        scaled
        - jnp.mean(scaled, -1, keepdims=True)
        - unit * jnp.mean(scaled * unit, -1, keepdims=True)
    )


def loss_kernel(
    ready, idx_ref, heat_ref, seg_col_ref, partner_ref, own_weight_ref, side_ref,
    frag_ref, size_ref, unit_ref, inv_ref, par_ref, slope_ref, *refs
):
    blocks, down_pieces = refs[:8], refs[8:12]
    loss_ref, low_own_ref, low_other_ref, gup_own_ref, gup_other_ref, two_ref, gains_ref = refs[12:19]
    all_ref, down_ref, low_ref, spread_ref, sems, w_sems = refs[19:]
    copies = []
    for number in range(32):
        row = pl.multiple_of(idx_ref[1 + number], 16)
        copies.append(
            pltpu.make_async_copy(
                blocks[number // 4].at[number % 4], all_ref.at[pl.ds(row, 32), :], sems.at[number]
            )
        )
    core = idx_ref[33]
    down_copies = piece_copies(idx_ref, 34, down_pieces, down_ref, 192, w_sems, 0)
    for copy in copies:
        copy.start()
    for copy in copies:
        copy.wait()
    ready(1, 2, 3)
    ready.copies_in[9].start()
    for copy in down_copies:
        copy.start()
    base = idx_ref[0]
    inv_heat = 1.0 / heat_ref[0]
    tally = 1024
    mine = all_ref[pl.ds(pl.multiple_of(base, 16), 32), :]
    grid = (nt_dot(mine, all_ref[...]) - 1.0) * inv_heat
    across = lax.broadcasted_iota(jnp.int32, (32, tally), 1)
    down = lax.broadcasted_iota(jnp.int32, (32, tally), 0) + base
    powers = jnp.where(across == down, 0.0, jnp.exp(grid))
    total = jnp.sum(powers, -1, keepdims=True)
    eye = lax.broadcasted_iota(jnp.int32, (32, 32), 0) == lax.broadcasted_iota(jnp.int32, (32, 32), 1)
    partner = jnp.sum(jnp.where(eye, partner_ref[...].astype(f32), 0.0), -1, keepdims=True)
    own_weight = jnp.sum(jnp.where(eye, own_weight_ref[...], 0.0), -1, keepdims=True)
    chosen = across == partner.astype(jnp.int32)
    target = jnp.sum(jnp.where(chosen, grid, 0.0), -1, keepdims=True)
    terms = own_weight * (jnp.log(total) - target)
    loss_ref[...] = jnp.broadcast_to(jnp.sum(terms, 0, keepdims=True) / tally, (8, 128))
    picked = jnp.where(chosen, 1.0, 0.0)
    pull = (powers / total - picked) * (own_weight * (inv_heat / tally))
    totals = [jnp.zeros((1, 128), f32) for _ in range(8)]
    number = lax.broadcasted_iota(jnp.int32, (128, 128), 0)
    same = number == lax.broadcasted_iota(jnp.int32, (128, 128), 1)
    weights = []
    for big in range(2):
        spread_ref[...] = nt_dot(all_ref[big * 512 : (big + 1) * 512, :], all_ref[...])
        for b in range(big * 4, big * 4 + 4):
            inside = slice((b - big * 4) * 128, (b - big * 4 + 1) * 128)
            for n in range(8):
                spread = jnp.exp((spread_ref[inside, n * 128 : (n + 1) * 128] - 1.0) * inv_heat)
                if n == b:
                    spread = jnp.where(same, 0.0, spread)
                totals[n] += jnp.sum(spread, 0, keepdims=True)
            side = jnp.concatenate(
                [
                    side_ref[n % 2, (n // 2) * 48 : (n // 2) * 48 + 32, :].astype(f32)
                    for n in range(b * 4, b * 4 + 4)
                ],
                0,
            ).T
            weights.append(side[4:5] + side[5:6] + side[6:7])
    totals, weights = jnp.concatenate(totals, 1), jnp.concatenate(weights, 1)
    column_pull = (powers / totals - picked) * (weights * (inv_heat / tally))
    both = jnp.concatenate([pull.astype(bf16), column_pull.astype(bf16)], 0)
    both = nn_dot(both, all_ref[...])
    grad = both[:32] + both[32:]
    ready(0, 4, 5, 6, 7, 8)
    frag = frag_ref[...]
    pooled = size_ref[:, 0:1] * (grad - frag * jnp.sum(grad * frag, -1, keepdims=True))
    stacked = jnp.concatenate(thirds(pooled), 0)
    gain_two = jnp.zeros((1, 768), f32)
    shift_two = jnp.zeros((1, 768), f32)
    for b in range(4):
        rows = slice(b * 128, (b + 1) * 128)
        slot = lax.broadcasted_iota(jnp.int32, (128, 96), 1) % 32
        member = jnp.where(slot == seg_col_ref[rows, :], 1.0, 0.0).astype(bf16)
        upstream = nn_dot(member, stacked)
        unit = unit_ref[rows, :]
        back = back_norm(upstream, unit, inv_ref[rows, 0:1], par_ref[2:3, :])
        two_ref[rows, :] = back
        low_ref[rows, :] = back.astype(bf16)
        gain_two += jnp.sum(upstream * unit, 0, keepdims=True)
        shift_two += jnp.sum(upstream, 0, keepdims=True)
    halves = (core, 1 - core)
    for half, ref in zip(halves, (low_own_ref, low_other_ref)):
        ref[...] = low_ref[:, pl.ds(pl.multiple_of(half * 384, 128), 384)]
    ready.put(0, 1, 2, 5)
    ready(9)
    for copy in down_copies:
        copy.wait()
    for half, gup_ref in zip(halves, (gup_own_ref, gup_other_ref)):

        @pl.loop(0, 6, unroll=3)
        def _(n):
            cols = pl.ds(pl.multiple_of(n * 256, 256), 256)
            wide = pl.ds(pl.multiple_of(half * 1536 + n * 256, 256), 256)
            g = sum(
                nt_dot(low_ref[:, k * 384 : (k + 1) * 384], down_ref[k, wide, :])
                for k in range(2)
            )
            gup_ref[:, cols] = (g * slope_ref[:, wide].astype(f32)).astype(bf16)

        if gup_ref is gup_own_ref:
            ready.put(3)

    gains_ref[...] = jnp.concatenate([gain_two, shift_two, jnp.zeros((6, 768), f32)], 0)


def loss_backward(index, heat, arrays, pieces):
    return staged_call(
        loss_kernel,
        [(index, FRAGMENTS), (heat, 0)],
        arrays,
        pieces,
        [
            shaped(f32, 8, 128),
            shaped(bf16, 512, 384),
            shaped(bf16, 512, 384),
            shaped(bf16, 512, 1536),
            shaped(bf16, 512, 1536),
            shaped(f32, 512, 768),
            shaped(f32, 8, 768),
        ],
        [
            pltpu.VMEM((1024, 768), bf16),
            pltpu.VMEM((2, 3072, 384), bf16),
            pltpu.VMEM((512, 768), bf16),
            pltpu.VMEM((512, 1024), f32),
            pltpu.SemaphoreType.DMA((32,)),
            pltpu.SemaphoreType.DMA((32,)),
        ],
        18,
        (9,),
    )


def ffn_back_kernel(
    ready, idx_ref, gup_own_ref, gup_other_ref, two_ref, unit_ref, inv_ref, par_ref, gains_two_ref, *refs
):
    pieces = refs[:8]
    resid_ref, att_ref, own_ref, other_ref, gains_ref, up_ref, sems = refs[8:]
    copies = piece_copies(idx_ref, 0, pieces, up_ref, 48, sems, 0)
    for copy in copies:
        copy.start()
    ready()
    for copy in copies:
        copy.wait()
    core = idx_ref[0]
    for n in range(3):
        cols = slice(n * 256, (n + 1) * 256)
        resid_ref[:, cols] = (
            two_ref[:, cols]
            + nt_dot(gup_own_ref[...], up_ref[core, cols, :])
            + nt_dot(gup_other_ref[...], up_ref[1 - core, cols, :])
        )
    gain_sum = jnp.zeros((1, 768), f32)
    shift_sum = jnp.zeros((1, 768), f32)
    for b in range(4):
        rows = slice(b * 128, (b + 1) * 128)
        one = resid_ref[rows, :]
        unit = unit_ref[rows, :]
        back = back_norm(one, unit, inv_ref[rows, 0:1], par_ref[0:1, :])
        resid_ref[rows, :] = back
        att_ref[rows, :] = back.astype(bf16)
        gain_sum += jnp.sum(one * unit, 0, keepdims=True)
        shift_sum += jnp.sum(one, 0, keepdims=True)
    for half, ref in ((core, own_ref), (1 - core, other_ref)):
        ref[...] = att_ref[:, pl.ds(pl.multiple_of(half * 384, 128), 384)]
    gains_ref[...] = jnp.concatenate(
        [gain_sum, shift_sum, gains_two_ref[0:2, :], jnp.zeros((4, 768), f32)], 0
    )


def ffn_backward(index, arrays, pieces):
    return staged_call(
        ffn_back_kernel,
        [(index, BY_FLIP)],
        arrays,
        pieces,
        [
            shaped(f32, 512, 768),
            shaped(bf16, 512, 768),
            shaped(bf16, 512, 384),
            shaped(bf16, 512, 384),
            shaped(f32, 8, 768),
        ],
        [pltpu.VMEM((2, 768, 1536), bf16), pltpu.SemaphoreType.DMA((32,))],
        9,
    )


def heads_back(half, gm_ref, qkv_ref, lse_ref, bias_ref, gqkv_ref, gk_ref, gv_ref):
    lane = lax.broadcasted_iota(jnp.int32, (128, 128), 1)
    left = lane < HD
    gk_ref[...] = jnp.zeros_like(gk_ref)
    gv_ref[...] = jnp.zeros_like(gv_ref)

    @pl.loop(0, 3, unroll=3)
    def _(spot):
        pair = half * 3 + spot
        for b in range(4):
            rows = pl.ds(b * 128, 128)
            keys = pl.ds(WINDOWS[b], 256)
            q = qkv_ref[pair, rows, :]
            k = qkv_ref[pair + 6, keys, :]
            v = qkv_ref[pair + 12, keys, :]
            gm = gm_ref[rows, pl.ds(pl.multiple_of(spot * 128, 128), 128)]
            q, gm = two_heads(q), two_heads(gm)
            stats = lse_ref[rows, :]
            lse = jnp.concatenate(
                [
                    jnp.sum(jnp.where(lane == pair * 2 + h, stats, 0.0), -1, keepdims=True)
                    for h in range(2)
                ],
                0,
            )
            p = jnp.exp(nt_dot(q, k) + bias_ref[b] - lse)
            gp = nt_dot(gm, v)
            gs = (p * (gp - jnp.sum(gp * p, -1, keepdims=True))).astype(bf16)
            gq = nn_dot(gs, k)
            gq = (jnp.where(left, gq[:128], gq[128:]) * SCALE).astype(bf16)
            gqkv_ref[rows, pl.ds(pl.multiple_of(spot * 128, 128), 128)] = gq
            gk_ref[spot, keys, :] += tn_dot(gs, q)
            gv_ref[spot, keys, :] += tn_dot(p.astype(bf16), gm)
        for third, ref in ((1, gk_ref), (2, gv_ref)):
            cols = pl.ds(pl.multiple_of(third * 384 + spot * 128, 128), 128)
            gqkv_ref[:, cols] = ref[spot].astype(bf16)


def other_heads_kernel(ready, idx_ref, seg_row_ref, seg_col_ref, qkv_ref, lse_ref, att_ref, resid_ref, *refs
):
    pieces = refs[:8]
    gqkv_ref, gm_own_ref, part_ref = refs[8:11]
    w_ref, bias_ref, gm_ref, gk_ref, gv_ref, sems = refs[11:]
    copies = piece_copies(idx_ref, 4, pieces, w_ref, 48, sems, 0)
    for copy in copies:
        copy.start()
    ready()
    for b in range(4):
        bias_ref[b] = window_bias(seg_row_ref[...], seg_col_ref[...], b)
    for copy in copies:
        copy.wait()
    core = idx_ref[4]
    half = 1 - core
    for side, ref in ((half, gm_ref), (core, gm_own_ref)):
        rows = pl.ds(pl.multiple_of(side * 384, 128), 384)
        ref[...] = sum(
            nt_dot(att_ref[:, k * 384 : (k + 1) * 384], w_ref[k, rows, 1152:1536])
            for k in range(2)
        ).astype(bf16)
    heads_back(half, gm_ref, qkv_ref, lse_ref, bias_ref, gqkv_ref, gk_ref, gv_ref)
    ready.put(0, 1)
    for n in range(3):
        cols = slice(n * 256, (n + 1) * 256)
        part_ref[:, cols] = resid_ref[:, cols] + nt_dot(gqkv_ref[...], w_ref[half, cols, :1152])


def other_heads(index, arrays, pieces):
    return staged_call(
        other_heads_kernel,
        [(index, Z_ROWS)],
        arrays,
        pieces,
        [
            shaped(bf16, 512, 1152),
            shaped(bf16, 512, 384),
            shaped(f32, 512, 768),
        ],
        [
            pltpu.VMEM((2, 768, 1664), bf16),
            pltpu.VMEM((4, 256, 256), f32),
            pltpu.VMEM((512, 384), bf16),
            pltpu.VMEM((3, 512, 128), f32),
            pltpu.VMEM((3, 512, 128), f32),
            pltpu.SemaphoreType.DMA((32,)),
        ],
        17,
    )


def own_heads_kernel(ready, idx_ref, seg_row_ref, seg_col_ref, qkv_ref, lse_ref, gm_ref, part_ref, *refs
):
    pieces = refs[:4]
    gqkv_ref, outs = refs[4], refs[5:9]
    w_ref, bias_ref, gk_ref, gv_ref, et_ref, sems = refs[9:]
    copies = []
    for number in range(16):
        row = pl.multiple_of(idx_ref[36 + number], 16)
        copies.append(
            pltpu.make_async_copy(
                pieces[number // 4].at[number % 4], w_ref.at[pl.ds(row, 48), :], sems.at[number]
            )
        )
    for copy in copies:
        copy.start()
    ready()
    for b in range(4):
        bias_ref[b] = window_bias(seg_row_ref[...], seg_col_ref[...], b)
    core = idx_ref[4]
    heads_back(core, gm_ref, qkv_ref, lse_ref, bias_ref, gqkv_ref, gk_ref, gv_ref)
    ready.put(0)
    for copy in copies:
        copy.wait()
    for n in range(3):
        cols = slice(n * 256, (n + 1) * 256)
        total = part_ref[:, cols] + nt_dot(gqkv_ref[...], w_ref[cols, :1152])
        et_ref[cols, :] = total.astype(bf16).T
    for j in range(4):
        outs[j][...] = et_ref[pl.ds(pl.multiple_of(idx_ref[j], 16), 192), :]


def own_heads(index, arrays, pieces):
    return staged_call(
        own_heads_kernel,
        [(index, Z_ROWS)],
        arrays,
        pieces,
        [
            shaped(bf16, 512, 1152),
            shaped(bf16, 192, 512),
            shaped(bf16, 192, 512),
            shaped(bf16, 192, 512),
            shaped(bf16, 192, 512),
        ],
        [
            pltpu.VMEM((768, 1664), bf16),
            pltpu.VMEM((4, 256, 256), f32),
            pltpu.VMEM((3, 512, 128), f32),
            pltpu.VMEM((3, 512, 128), f32),
            pltpu.VMEM((768, 512), bf16),
            pltpu.SemaphoreType.DMA((16,)),
        ],
        15,
    )


def to_slots(idx_ref, whole_ref, keep_ref, away_ref, sems):
    copies = []
    for start, ref in ((8, away_ref), (0, keep_ref)):
        for slot in range(8):
            source = whole_ref.at[idx_ref[start + slot]]
            copies.append(pltpu.make_async_copy(source, ref.at[slot], sems.at[start + slot]))
    for copy in copies:
        copy.start()
    for copy in copies:
        copy.wait()


def down_grad_kernel(ready, idx_ref, act_ref, act_o_ref, g_ref, g_o_ref, keep_ref, away_ref, whole_ref, sems):
    ready()
    for n in range(8):
        cols = slice(n * 384, (n + 1) * 384)
        total = tn_dot(act_ref[:, cols], g_ref[...]) + tn_dot(act_o_ref[:, cols], g_o_ref[...])
        total = total.astype(bf16)
        whole_ref[2 * n] = total[:192]
        whole_ref[2 * n + 1] = total[192:]
    to_slots(idx_ref, whole_ref, keep_ref, away_ref, sems)


def down_grad(index, arrays):
    return staged_call(
        down_grad_kernel,
        [(index, SLOTS)],
        arrays,
        [],
        [shaped(bf16, 8, 192, 384)] * 2,
        [pltpu.VMEM((16, 192, 384), bf16), pltpu.SemaphoreType.DMA((16,))],
        7,
        staged_out=False,
    )


def store_chunks(whole_ref, cols, total):
    for f in range(16):
        whole_ref[f, :, cols] = total[f * 48 : (f + 1) * 48]


def up_out_grad_kernel(
    ready, idx_ref, low_ref, low_o_ref, g_ref, g_o_ref, mixed_ref, mixed_o_ref, ga_ref, ga_o_ref, norms_ref,
    norms_o_ref, keep_ref, away_ref, whole_ref, t_ref, sems,
):
    ready()
    t_ref[0] = low_ref[...].T
    t_ref[1] = low_o_ref[...].T
    for n in range(3):
        cols = slice(n * 512, (n + 1) * 512)
        total = nn_dot(t_ref[0], g_ref[:, cols]) + nn_dot(t_ref[1], g_o_ref[:, cols])
        store_chunks(whole_ref, cols, total.astype(bf16))
    t_ref[0] = mixed_ref[...].T
    t_ref[1] = mixed_o_ref[...].T
    total = nn_dot(t_ref[0], ga_ref[...]) + nn_dot(t_ref[1], ga_o_ref[...])
    store_chunks(whole_ref, slice(1536, 1920), total.astype(bf16))
    norms = (norms_ref[...] + norms_o_ref[...]).T.astype(bf16)
    norms = jnp.concatenate([norms, jnp.zeros((768, 120), bf16)], 1)
    store_chunks(whole_ref, slice(1920, 2048), norms)
    to_slots(idx_ref, whole_ref, keep_ref, away_ref, sems)


def up_out_grad(index, arrays):
    return staged_call(
        up_out_grad_kernel,
        [(index, SLOTS)],
        arrays,
        [],
        [
            shaped(bf16, 8, 48, 2048),
            shaped(bf16, 8, 48, 2048),
        ],
        [
            pltpu.VMEM((16, 48, 2048), bf16),
            pltpu.VMEM((2, 768, 512), bf16),
            pltpu.SemaphoreType.DMA((16,)),
        ],
        8,
        staged_out=False,
    )


def in_grad_kernel(ready, idx_ref, e_ref, e_o_ref, g_ref, g_o_ref, keep_ref, away_ref, whole_ref, t_ref, sems):
    ready()
    t_ref[0] = e_ref[...].T
    t_ref[1] = e_o_ref[...].T
    for t in range(3):
        cols = slice(t * 384, (t + 1) * 384)
        total = nn_dot(t_ref[0], g_ref[:, cols]) + nn_dot(t_ref[1], g_o_ref[:, cols])
        store_chunks(whole_ref, cols, total.astype(bf16))
    to_slots(idx_ref, whole_ref, keep_ref, away_ref, sems)


def in_grad(index, arrays):
    return staged_call(
        in_grad_kernel,
        [(index, SLOTS)],
        arrays,
        [],
        [
            shaped(bf16, 8, 48, 1152),
            shaped(bf16, 8, 48, 1152),
        ],
        [
            pltpu.VMEM((16, 48, 1152), bf16),
            pltpu.VMEM((2, 768, 512), bf16),
            pltpu.SemaphoreType.DMA((16,)),
        ],
        6,
        staged_out=False,
    )


def optimizer_kernel(ready, core_ref, fix_ref, totals_ref, totals_o_ref, *refs):
    ready(*range(10))
    own, other = refs[:4], refs[4:8]
    params, outs = refs[8:26], refs[26:46]
    table_ref = refs[46]
    core = core_ref[0]
    totals = totals_ref[...] + totals_o_ref[...]
    norm = jnp.sqrt(totals[:, 0:1])
    outs[0][...] = totals[:, 1:2]
    outs[1][...] = norm
    factor = clip_norm / jnp.maximum(norm, clip_norm)
    fix_one, fix_two = 1.0 / fix_ref[0], 1.0 / fix_ref[1]

    def update(number, spot, grad, rate, decay):
        w_ref, first_ref, second_ref = params[3 * number : 3 * number + 3]
        grad = grad.astype(f32) * factor
        weight = w_ref[spot]
        first = beta_one * first_ref[spot] + (1.0 - beta_one) * grad
        second = beta_two * second_ref[spot] + (1.0 - beta_two) * grad * grad
        step = (first * fix_one) / (jnp.sqrt(second * fix_two) + adam_eps)
        outs[2 + 3 * number][spot] = weight - rate * (step + decay * weight)
        outs[3 + 3 * number][spot] = first
        outs[4 + 3 * number][spot] = second

    every = slice(None)
    halves = ((core, own), (1 - core, other))

    def columns(half, width, start=0):
        return pl.ds(pl.multiple_of(half * width + start, 128), width)

    def opened(number):
        ready(*range(10 + 3 * number, 13 + 3 * number))

    def done(number):
        ready.put(*range(2 + 3 * number, 5 + 3 * number))

    opened(3)
    for half, (_, _, up_out, _) in halves:
        for t in range(3):
            spot = pl.ds(pl.multiple_of(half * 1536 + t * 512, 128), 512)
            update(3, (every, spot), up_out[:, t * 512 : (t + 1) * 512], rate_matrix, decay_rate)
    done(3)
    opened(4)
    for half, (_, _, _, down) in halves:
        for t in range(4):
            rows = slice(t * 48, (t + 1) * 48)
            update(4, (rows, columns(half, 384)), down[rows, :], rate_matrix, decay_rate)
    done(4)
    opened(1)
    for half, (_, into, _, _) in halves:
        for t in range(3):
            update(
                1,
                (every, columns(half, 384, t * 768)),
                into[:, t * 384 : (t + 1) * 384],
                rate_matrix,
                decay_rate,
            )
    done(1)
    opened(0)
    for half, (table, _, _, _) in halves:
        table_ref[:, columns(half, VOCAB_HALF)] = table[...]
    vocab = params[0].shape[1]
    for low in range(0, vocab, 512):
        spot = slice(low, min(vocab, low + 512))
        update(0, (every, spot), table_ref[:, spot], rate_embed, decay_rate)
    done(0)
    opened(2)
    for half, (_, _, up_out, _) in halves:
        update(2, (every, columns(half, 384)), up_out[:, 1536:1920], rate_matrix, decay_rate)
    done(2)
    opened(5)
    norms = jnp.where(core == 0, own[2][:, 1920:].astype(f32), other[2][:, 1920:].astype(f32))
    update(5, (every, every), norms.T[:4], rate_norm, 0.0)


def optimizer(core, fixes, totals, totals_o, own, other, params):
    return staged_call(
        optimizer_kernel,
        [(core, MY_CORE), (fixes, 0)],
        [totals, totals_o, *own, *other, *params],
        [],
        [
            shaped(f32, 1, 1),
            shaped(f32, 1, 1),
            *[shaped(f32, *p.shape) for p in params],
        ],
        [
            pltpu.VMEM((48, VOCAB_PAD), bf16),
        ],
        8,
    )


def per_device_links(
    kmer_identifiers,
    slot_fragment_ids,
    mirror_fragment_index,
    fragment_weight,
    affinity_heat,
    optimizer_iteration,
    lexicon_table,
    lexicon_first_moment,
    lexicon_raw_moment,
    query_key_value_maps,
    qkv_first_moment,
    qkv_raw_moment,
    attention_exit_map,
    exit_first_moment,
    exit_raw_moment,
    widening_matrix_in,
    widening_first_moment,
    widening_raw_moment,
    narrowing_matrix_out,
    narrowing_first_moment,
    narrowing_raw_moment,
    layernorm_scale_bias,
    layernorm_first_moment,
    layernorm_raw_moment,
):
    place = Place()
    core = place.core
    vocab = lexicon_table.shape[0]
    index = index_vector(place)
    both_cut, table_cut, table_half, down_half = prepare(
        [
            lexicon_table.T,
            query_key_value_maps,
            attention_exit_map,
            widening_matrix_in,
            narrowing_matrix_out,
            layernorm_scale_bias,
            kmer_identifiers,
            fragment_weight.reshape(1, 32),
        ],
    )
    near = [send(table_half, FIRST), send(table_half, SECOND)]
    near.append(send(near[0], SECOND))
    both_far = z_sends(both_cut)
    down_first = send(after(down_half, near[0]), FIRST)
    others = send(after(jnp.stack(near), down_first, *both_far), CORE)
    id_parts = jnp.stack([p[:8, 3200:] for p in both_far]).astype(f32)
    ids_z = (id_parts[:, :4] * 64.0 + id_parts[:, 4:]).astype(jnp.int32)
    in_out_column = jnp.stack([p[:, :1664] for p in both_far])
    in_out_mine = plane_sends(in_out_column, True)
    found = lookup(index, ids_z, [down_half, down_first], [table_cut] + near + [others])
    up_column = after(jnp.stack([p[:, 1664:3200] for p in both_far]), *found)
    columns = [found[0]] + [send(found[j], ZS[j]) for j in (1, 2, 3)]
    in_out = both_cores(together(in_out_mine, *columns))
    up_mine = plane_sends(after(up_column, in_out_mine[3]), True)
    down_pair = jnp.stack([down_half, after(down_first, *found)])
    down_pair = after(down_pair, *columns)
    d_two, d_three = (send(down_pair, ZS[j]) for j in (2, 3))
    seg_row = slot_fragment_ids
    seg_col = slot_fragment_ids.reshape(512, 1)
    embedded, qkv, lse, mixed, unit_one, inv_one, normed_low, params, side = attention_forward(
        index, seg_row, seg_col, columns, in_out
    )
    *up_mine, d_two, d_three = together(up_mine + [d_two, d_three], normed_low)
    d_one = jnp.stack([columns[1][:, 512:896], columns[1][:, 896:]])
    down_one = jnp.stack([down_pair, d_one, d_two, d_three]).reshape(8, 192, 384)
    down_two = send(down_one, SECOND)
    down_one_o = send(down_one, CORE)
    up_w = both_cores(up_mine)
    activated, slope = up_forward(index, normed_low, up_w)
    down_two, down_one_o = together([down_two, down_one_o], activated)
    down_w = [down_one, down_two, down_one_o, send(down_two, CORE)]
    unit_two, inv_two, unit_rows, unit_low, unit_scale = down_forward(
        index, seg_row, activated, unit_one, params, down_w
    )
    embedded_o, mixed_o, normed_o, activated_o = (
        send(a, CORE) for a in (embedded, mixed, normed_low, activated)
    )
    column = jnp.stack([unit_low] + [send(unit_low, ZS[j]) for j in (1, 2, 3)])
    blocks = [column, send(column, FIRST), send(column, SECOND), send(column, BOTH)]
    blocks = blocks + [send(block, CORE) for block in blocks]
    (
        loss_tile, grad_result_own, grad_result_x, grad_up_own, grad_up_x, grad_two, gains_two,
    ) = loss_backward(
        index,
        affinity_heat.reshape(1),
        [
            seg_col,
            mirror_fragment_index.reshape(1, 32),
            fragment_weight.reshape(1, 32),
            side,
            unit_rows,
            unit_scale,
            unit_two,
            inv_two,
            params,
            slope,
        ],
        blocks + down_w,
    )
    grad_result_o = send(grad_result_x, CORE)
    ids_o = send(ids_z, CORE)
    grad_up_o = send(grad_up_x, CORE)
    spare = [embedded_o, mixed_o, normed_o, ids_o]
    down_keep, down_away = down_grad(
        index, [after(activated, *spare), activated_o, grad_result_own, grad_result_o]
    )
    down_came = send(down_away, SECOND)
    grad_resid, grad_attended, grad_att_own, grad_att_x, norms = ffn_backward(
        index,
        [after(grad_up_own, down_away), grad_up_x, grad_two, unit_one, inv_one, params, gains_two],
        up_w,
    )
    grad_att_o = send(grad_att_x, CORE)
    norms_o = send(norms, CORE)
    up_out_keep, up_out_away = up_out_grad(
        index,
        [
            normed_low,
            normed_o,
            grad_up_own,
            grad_up_o,
            mixed,
            mixed_o,
            grad_att_own,
            grad_att_o,
            norms,
            norms_o,
        ],
    )
    up_out_came = send(up_out_away, SECOND)
    down_came = after(down_came, up_out_away)
    down_across = scatter_add(down_keep, down_came)
    down_came_two = send(down_across, FIRST)
    grad_qkv_x, grad_mixed_own, part = other_heads(
        index,
        [seg_row, seg_col, qkv, lse, after(grad_attended, down_across), grad_resid],
        in_out,
    )
    grad_qkv_o = send(grad_qkv_x, CORE)
    down_came_two = after(down_came_two, part)
    down_here, down_far = scatter_here(down_keep, down_came, down_came_two)
    down_far_came = line_sends(down_far)
    grad_qkv_own, *outs = own_heads(
        index,
        [seg_row, seg_col, qkv, lse, grad_mixed_own, after(part, *down_far)],
        in_out[:4],
    )
    far_cols = [send(outs[j], ZS[j]) for j in (1, 2, 3)]
    *down_far_came, up_out_came, grad_qkv_o = together(
        down_far_came + [up_out_came, grad_qkv_o], grad_qkv_own
    )
    up_out_across = scatter_add(up_out_keep, up_out_came)
    up_out_came_two = send(up_out_across, FIRST)
    in_keep, in_away = in_grad(
        index, [embedded, embedded_o, after(grad_qkv_own, up_out_across), grad_qkv_o]
    )
    far_cols = together(far_cols, in_away)
    in_came = send(in_away, SECOND)
    token_cols = jnp.stack([outs[0]] + far_cols)
    token_cols_o = send(token_cols, CORE)
    up_out_here, up_out_far = scatter_here(
        up_out_keep, up_out_came, after(up_out_came_two, token_cols)
    )
    up_out_far_came = line_sends(up_out_far)
    keep, away = token_sum(
        index,
        after(ids_z, *up_out_far),
        ids_o,
        token_cols,
        token_cols_o,
    )
    came = send(away, SECOND)
    in_came = after(in_came, away)
    in_across = scatter_add(in_keep, in_came)
    in_came_two = send(in_across, FIRST)
    across = (keep[1].astype(f32) + came[1].astype(f32)).astype(bf16)
    came_two = send(across, FIRST)
    up_out_far_came = together(up_out_far_came, across)
    in_here, in_far = scatter_here(
        in_keep, in_came, after(in_came_two, across, *up_out_far_came)
    )
    in_far_came = line_sends(in_far)
    down_sum = line_sum(after(down_here, came_two), down_far_came)
    up_out_sum = line_sum(up_out_here, together(up_out_far_came, came_two))
    table_sum = keep[0].astype(f32) + came[0].astype(f32) + came_two.astype(f32)
    table_sum = table_sum.astype(bf16)
    early = [table_sum, up_out_sum, down_sum]
    norm_own = up_out_sum[:, 1920:1924].astype(f32)
    squares = sum(
        jnp.sum(jnp.square(p.astype(f32))) for p in (table_sum, up_out_sum[:, :1920], down_sum)
    ) + jnp.where(core == 0, jnp.sum(norm_own * norm_own), 0.0)
    early_o = [send(s, CORE) for s in early]
    in_sum = line_sum(in_here, together(in_far_came, squares))
    in_o = send(in_sum, CORE)
    squares += jnp.sum(jnp.square(in_sum.astype(f32)))
    lane = lax.broadcasted_iota(jnp.int32, (1, 128), 1)
    totals = jnp.where(lane == 0, squares, loss_tile[0:1])
    totals = all_sum(after(totals, *early_o))
    sums = [table_sum, in_sum, up_out_sum, down_sum]
    sums_o = [early_o[0], in_o, early_o[1], early_o[2]]
    count_now = optimizer_iteration.astype(f32)
    fixes = jnp.stack([1.0 - jnp.power(beta_one, count_now), 1.0 - jnp.power(beta_two, count_now)])
    results = optimizer(
        index,
        fixes,
        totals,
        send(totals, CORE),
        sums,
        sums_o,
        [
            lexicon_table.T,
            lexicon_first_moment.T,
            lexicon_raw_moment.T,
            query_key_value_maps,
            qkv_first_moment,
            qkv_raw_moment,
            attention_exit_map,
            exit_first_moment,
            exit_raw_moment,
            widening_matrix_in,
            widening_first_moment,
            widening_raw_moment,
            narrowing_matrix_out,
            narrowing_first_moment,
            narrowing_raw_moment,
            layernorm_scale_bias,
            layernorm_first_moment,
            layernorm_raw_moment,
        ],
    )
    results = list(results)
    results[:2] = [r[0, 0] for r in results[:2]]
    results[2:5] = [r.T for r in results[2:5]]
    return tuple(results)


def solution(mesh):
    in_specs = (
        P(("fsdp", "dp"), None),
        P(("fsdp", "dp"), None),
        P(("fsdp", "dp")),
        P(("fsdp", "dp")),
        P(),
        P(),
        P(None, "fsdp"),
        P(None, "fsdp"),
        P(None, "fsdp"),
        P("fsdp", None),
        P("fsdp", None),
        P("fsdp", None),
        P("fsdp", None),
        P("fsdp", None),
        P("fsdp", None),
        P("fsdp", None),
        P("fsdp", None),
        P("fsdp", None),
        P("fsdp", None),
        P("fsdp", None),
        P("fsdp", None),
        P(None, "fsdp"),
        P(None, "fsdp"),
        P(None, "fsdp"),
    )
    out_specs = (
        P(),
        P(),
        P(None, "fsdp"),
        P(None, "fsdp"),
        P(None, "fsdp"),
        P("fsdp", None),
        P("fsdp", None),
        P("fsdp", None),
        P("fsdp", None),
        P("fsdp", None),
        P("fsdp", None),
        P("fsdp", None),
        P("fsdp", None),
        P("fsdp", None),
        P("fsdp", None),
        P("fsdp", None),
        P("fsdp", None),
        P(None, "fsdp"),
        P(None, "fsdp"),
        P(None, "fsdp"),
    )
    own_plan = dict(mesh.shape) == {"fsdp": 16, "dp": 2}
    return jax.shard_map(
        per_device_links if own_plan else per_device, mesh=mesh, in_specs=in_specs, out_specs=out_specs, check_vma=False
    )
```
